512 devices in a mesh: gx: 8 (over z), gy: 4 (over x), gz: 16 (over y, core).
Axes of the slice: x: 4, y: 8, z: 8, core: 2. Of those that a mesh axis runs over, the one named last changes fastest.
Arguments:
- initial_edge_intensity: float32 [3, 128, 64, 2048], P(None, 'gx', 'gy', 'gz'), may hold values from -3 to 3
- source_amperage: float32 [3, 128, 64, 2048], P(None, 'gx', 'gy', 'gz'), may hold values from -24 to 24
- electric_sigma: float32 [128, 64, 2048], P('gx', 'gy', 'gz'), may hold values from 0.1 to 3
- earlier_warmth: float32 [128, 64, 2048], P('gx', 'gy', 'gz'), may hold values from -6 to 6
- storage_coefficient: float32 [128, 64, 2048], P('gx', 'gy', 'gz'), may hold values from 0.5 to 4
- receiving_partition_rank: int32 [8, 4, 16, 256, 1], P('gx', 'gy', 'gz'), may hold values from 0 to 63; in each aligned block of 256 rows (0 to 255, 256 to 511, ..., all dimensions but the last counted through in order) at most 8 rows name the same one
- receiving_node_column: int32 [8, 4, 16, 256], P('gx', 'gy', 'gz'), may hold values from 0 to 255
Outputs:
- final_edge_intensity: float32 [3, 128, 64, 2048], P(None, 'gx', 'gy', 'gz')
- updated_warmth: float32 [128, 64, 2048], P('gx', 'gy', 'gz')
The draws below stay inside these ranges and needn't reach their ends.
Inputs may be any that keep to these rules, and one draw needn't show every extreme that they name: `receiving_partition_rank`: in the 256 element columns of one device no thermal partition is named more than 8 times, and in every draw one is named exactly 8 times in some device's columns.
All inputs are finite; a program needn't handle non-finite values.
Results may differ from the reference program's by a relative error of at most 0.00027.
Values sent between devices are 32-bit elements; how exact they have to be, the bound alone decides.
No kernel may reach another device: no remote copies, remote signals or barrier semaphores. Data moves between devices by JAX's collectives and lax.ppermute only.
A program may use at most 64 MiB of HBM per device.

```python
import math
import jax
import jax.numpy as jnp
import numpy as np

CX = 16
CY = 16
CZ = 128
EM_SWEEPS = 4
HEAT_SWEEPS = 2
LINES = 256
CAP = 8
MESH_COUNT_FIRST = 128
MESH_COUNT_MID = 64
MESH_COUNT_LAST = 2048
N_GX = 8
N_GY = 4
N_GZ = 16


def with_ends(drawn, rng, smallest, high):
    spot = [jax.random.randint(jax.random.fold_in(rng, axis), (), 0, length) for axis, length in enumerate(drawn.shape)]
    widest = drawn.shape.index(max(drawn.shape))
    beside = spot[:widest] + [(spot[widest] + 1) % drawn.shape[widest]] + spot[widest + 1:]
    return drawn.at[tuple(spot)].set(smallest).at[tuple(beside)].set(high)


def levels(key, dims, pieces, least, top_value):
    gain = 1.0
    for axis_at, parts in pieces:
        steps = jax.random.uniform(jax.random.fold_in(jax.random.fold_in(key, 6), axis_at), (parts,), jnp.float32, least / len(pieces), top_value / len(pieces))
        gain = gain * jnp.repeat(jnp.exp(steps), dims[axis_at] // parts).reshape((-1,) + (1,) * (len(dims) - 1 - axis_at))
    return gain


def routed_block(key, own, number, rows, number_of, top, most, lean):
    ranking = jax.random.permutation(key, number_of)
    crowded, ordinary = shares(number_of, rows * top, most, lean, True), shares(number_of, rows * top, most, lean, False)
    places = jnp.arange(number_of)

    def named(lengths, rotation):
        used = int((lengths > 0).sum())
        fixed = max(1, used // 4)
        moved = fixed + (places - fixed + rotation * (used - fixed)) % max(1, number_of - fixed)
        return jnp.zeros((number_of,), jnp.int32).at[ranking[jnp.where(places < fixed, places, moved)]].set(jnp.asarray(lengths, jnp.int32))

    lengths = jnp.where(number % 4 == 0, named(crowded, number // 4), named(ordinary, number - number // 4 - 1))
    mixed = jax.random.permutation(jax.random.fold_in(own, 3), number_of)
    source_of, sink = mixed[0:number_of // 2 * 2:2], mixed[1:number_of // 2 * 2:2]
    margin = jnp.minimum(lengths[source_of] - 1, most - lengths[sink]) // 2
    margin = jnp.where((source_of == ranking[0]) | (sink == ranking[0]) | (lengths[sink] == 0), 0, jnp.maximum(margin, 0))
    moved = jax.random.randint(jax.random.fold_in(own, 4), (number_of // 2,), 0, 1 << 20) % (margin + 1)
    lengths = lengths.at[source_of].add(-moved).at[sink].add(moved)
    items = jnp.searchsorted(jnp.cumsum(lengths), jnp.arange(rows * top), side="right").astype(jnp.int32)
    listing = items.reshape(top, rows).T
    listing = listing[jax.random.permutation(jax.random.fold_in(own, 1), rows)]
    rotation = jax.random.randint(jax.random.fold_in(own, 2), (rows, 1), 0, top)
    return jnp.take_along_axis(listing, (jnp.arange(top)[None, :] + rotation) % top, axis=1)


def shares(amount, total, bound, skew, full):
    portions = [(1 << 20) // math.isqrt(standing ** skew) + 1 for standing in range(1, amount + 1)]
    largest = bound if full else min(bound, max(-(-total // amount), total * portions[0] // sum(portions)))
    least = 1 if total - largest >= amount - 1 else 0
    holding, rest = [largest] + [least] * (amount - 1), total - largest - least * (amount - 1)
    while rest > 0:
        free = [i for i in range(1, amount) if holding[i] < largest] or [i for i in range(1, amount) if holding[i] < bound]
        mass, left = sum([portions[i] for i in free]), rest
        for i in free:
            extra = min(bound - holding[i], max(1, left * portions[i] // mass), rest)
            holding[i] = holding[i] + extra
            rest = rest - extra
    return np.array(holding)


def normal_values(own_key, shape, deviation, limit, cuts=(), kind=jnp.bfloat16):
    gain = levels(own_key, shape, cuts, -0.22, 0.18) if cuts else 1.0
    result = jax.random.normal(own_key, shape, jnp.float32) * deviation * gain
    return jnp.minimum(jnp.maximum(result, -limit), limit).astype(kind)


def setup_inputs(seed: int = 0) -> dict:
    key_of = jax.random.split(jax.random.key(seed), 8)
    initial_edge_intensity = normal_values(key_of[0], (3, MESH_COUNT_FIRST, MESH_COUNT_MID, MESH_COUNT_LAST), 0.5, 3.0, ((1, 8), (2, 4), (3, 16)), jnp.float32)
    source_amperage = normal_values(key_of[1], (3, MESH_COUNT_FIRST, MESH_COUNT_MID, MESH_COUNT_LAST), 4.0, 24.0, ((1, 8), (2, 4), (3, 16)), jnp.float32)
    electric_sigma = jnp.clip(jnp.exp(math.log(3.0) - 3.4011974 * jax.random.uniform(key_of[2], (MESH_COUNT_FIRST, MESH_COUNT_MID, MESH_COUNT_LAST), jnp.float32) ** levels(key_of[2], (MESH_COUNT_FIRST, MESH_COUNT_MID, MESH_COUNT_LAST), ((0, 8), (1, 4), (2, 16)), -0.2, 0.2)), 0.1, 3.0)
    earlier_warmth = normal_values(key_of[3], (MESH_COUNT_FIRST, MESH_COUNT_MID, MESH_COUNT_LAST), 1.0, 6.0, ((0, 8), (1, 4), (2, 16)), jnp.float32)
    storage_coefficient = jnp.clip(jnp.exp(math.log(4.0) - 2.0794415 * jax.random.uniform(key_of[4], (MESH_COUNT_FIRST, MESH_COUNT_MID, MESH_COUNT_LAST), jnp.float32) ** levels(key_of[4], (MESH_COUNT_FIRST, MESH_COUNT_MID, MESH_COUNT_LAST), ((0, 8), (1, 4), (2, 16)), -0.2, 0.2)), 0.5, 4.0)
    receiving_partition_rank_keys = jax.random.split(jax.random.fold_in(key_of[5], 1), N_GX * N_GY * N_GZ * LINES // LINES)
    receiving_partition_rank_turns = jax.random.permutation(jax.random.fold_in(key_of[5], 3), N_GX * N_GY * N_GZ * LINES // LINES)
    receiving_partition_rank = jax.vmap(lambda own, number: routed_block(jax.random.fold_in(key_of[5], 2), own, number, LINES, N_GY * N_GZ, 1, CAP, 2))(receiving_partition_rank_keys, receiving_partition_rank_turns).reshape((N_GX, N_GY, N_GZ, LINES, 1))
    receiving_node_column = with_ends(jax.random.randint(key_of[6], (N_GX, N_GY, N_GZ, LINES), 0, LINES), jax.random.fold_in(key_of[6], 1), 0, LINES - 1).astype(jnp.int32)
    return dict(initial_edge_intensity=initial_edge_intensity, source_amperage=source_amperage, electric_sigma=electric_sigma, earlier_warmth=earlier_warmth, storage_coefficient=storage_coefficient, receiving_partition_rank=receiving_partition_rank, receiving_node_column=receiving_node_column)


em_lower = 0.02
em_upper = 3.0
heat_lower = 0.07
heat_upper = 2.0
edge_offsets = (((0, 0, 0), (0, 1, 0), (0, 0, 1), (0, 1, 1)), ((0, 0, 0), (1, 0, 0), (0, 0, 1), (1, 0, 1)), ((0, 0, 0), (1, 0, 0), (0, 1, 0), (1, 1, 0)))


def chebyshev_weights(lower_end, upper_end, sweep_count):
    middle = 0.5 * (upper_end + lower_end)
    radius = 0.5 * (upper_end - lower_end)
    return [1.0 / (middle + radius * math.cos(math.pi * (2 * number + 1) / (2 * sweep_count))) for number in range(sweep_count)]


def step_up(values, dimension):
    shifted = [slice(0, -1), slice(0, -1), slice(0, -1)]
    shifted[dimension] = slice(1, None)
    return values[tuple(shifted)] - values[:-1, :-1, :-1]


def step_down(values, dimension):
    shifted = [slice(1, None), slice(1, None), slice(1, None)]
    shifted[dimension] = slice(0, -1)
    return values[1:, 1:, 1:] - values[tuple(shifted)]


def curl_curl(bordered_entries):
    field_x, field_y, field_z = bordered_entries[0], bordered_entries[1], bordered_entries[2]
    curl_x = step_up(field_z, 1) - step_up(field_y, 2)
    curl_y = step_up(field_x, 2) - step_up(field_z, 0)
    curl_z = step_up(field_y, 0) - step_up(field_x, 1)
    back_x = step_down(curl_z, 1) - step_down(curl_y, 2)
    back_y = step_down(curl_x, 2) - step_down(curl_z, 0)
    back_z = step_down(curl_y, 0) - step_down(curl_x, 1)
    return jnp.stack([back_x, back_y, back_z])


def corner_cut(values, offsets):
    extent = values.shape
    return values[1 + offsets[0]:extent[0] - 1 + offsets[0], 1 + offsets[1]:extent[1] - 1 + offsets[1], 1 + offsets[2]:extent[2] - 1 + offsets[2]]


def joule_heat(bordered_entries, electric_sigma):
    summed = jnp.zeros(electric_sigma.shape, jnp.float32)
    for component in range(3):
        squares = bordered_entries[component] * bordered_entries[component]
        for offsets in edge_offsets[component]:
            summed = summed + corner_cut(squares, offsets)
    return electric_sigma * (0.25 * summed)


def neighbour_total(bordered_entries):
    summed = bordered_entries[2:, 1:-1, 1:-1] + bordered_entries[:-2, 1:-1, 1:-1]
    summed = summed + bordered_entries[1:-1, 2:, 1:-1] + bordered_entries[1:-1, :-2, 1:-1]
    summed = summed + bordered_entries[1:-1, 1:-1, 2:] + bordered_entries[1:-1, 1:-1, :-2]
    return summed


def reference(initial_edge_intensity, source_amperage, electric_sigma, earlier_warmth, storage_coefficient, receiving_partition_rank, receiving_node_column):
    diagonal = 4.0 + electric_sigma
    final_edge_intensity = initial_edge_intensity
    for relaxing_factor in chebyshev_weights(em_lower, em_upper, EM_SWEEPS):
        bordered_entries = jnp.pad(final_edge_intensity, ((0, 0), (1, 1), (1, 1), (1, 1)))
        driving_excitation = curl_curl(bordered_entries) + electric_sigma * final_edge_intensity
        final_edge_intensity = final_edge_intensity + relaxing_factor * (source_amperage - driving_excitation) / diagonal
    cell_heat = joule_heat(jnp.pad(final_edge_intensity, ((0, 0), (1, 1), (1, 1), (1, 1))), electric_sigma)
    blocks = cell_heat.reshape(N_GX, CX, N_GY, CY, N_GZ, CZ).transpose(0, 2, 4, 1, 3, 5).reshape(N_GX * N_GY * N_GZ * CX * CY, CZ)
    planes = jnp.arange(N_GX, dtype=jnp.int32)[:, None, None, None]
    target = (planes * (N_GY * N_GZ) + receiving_partition_rank[..., 0].astype(jnp.int32)) * (CX * CY) + receiving_node_column.astype(jnp.int32)
    collected = jax.ops.segment_sum(blocks, target.reshape(-1), num_segments=N_GX * N_GY * N_GZ * CX * CY)
    dissipated_power = collected.reshape(N_GX, N_GY, N_GZ, CX, CY, CZ).transpose(0, 3, 1, 4, 2, 5).reshape(CX * N_GX, CY * N_GY, CZ * N_GZ)
    warmth_matrix_pivot = 6.0 + storage_coefficient
    linear_forcing_vector = storage_coefficient * earlier_warmth + dissipated_power
    updated_warmth = earlier_warmth
    for relaxing_factor in chebyshev_weights(heat_lower, heat_upper, HEAT_SWEEPS):
        bordered_entries = jnp.pad(updated_warmth, 1)
        driving_excitation = warmth_matrix_pivot * updated_warmth - neighbour_total(bordered_entries)
        updated_warmth = updated_warmth + relaxing_factor * (linear_forcing_vector - driving_excitation) / warmth_matrix_pivot
    return final_edge_intensity, updated_warmth
```

```python
import math

import jax
import jax.numpy as jnp
from jax import lax
from jax.experimental import pallas as pl
from jax.experimental.pallas import tpu as pltpu
from jax.sharding import PartitionSpec as P

EM_SWEEPS = 4
HEAT_SWEEPS = 2
CAP = 8
LOW, HIGH = 4, 5
F32 = jnp.float32

em_lower = 0.02
em_upper = 3.0
heat_lower = 0.07
heat_upper = 2.0

UP_LAYERS = ((0, 12, 4), (1, 12, 4), (2, 12, 4), (3, 13, 3), (4, 13, 3), (5, 13, 3), (6, 13, 3), (7, 15, 1))
DOWN_LAYERS = ((0, 0, 4), (1, 0, 5), (2, 0, 5), (3, 0, 3), (4, 0, 4), (5, 0, 4), (6, 0, 4), (7, 0, 1))


def spots(layers, shift):
    where, at = {}, 0
    for field, first, count in layers:
        for x in range(first, first + count):
            where[field, x + shift] = at
            at += 1
    return where, at


UP_AT, UP_COUNT = spots(UP_LAYERS, -16)
DOWN_AT, DOWN_COUNT = spots(DOWN_LAYERS, 16)
X_LAYERS = max(UP_COUNT, DOWN_COUNT)


def chebyshev_weights(lower_end, upper_end, sweep_count):
    middle = 0.5 * (upper_end + lower_end)
    radius = 0.5 * (upper_end - lower_end)
    return [
        1.0 / (middle + radius * math.cos(math.pi * (2 * number + 1) / (2 * sweep_count)))
        for number in range(sweep_count)
    ]


EM_WEIGHTS = chebyshev_weights(em_lower, em_upper, EM_SWEEPS)
HEAT_WEIGHTS = chebyshev_weights(heat_lower, heat_upper, HEAT_SWEEPS)


def on_first_core():
    return lax.rem(lax.axis_index("gz"), 2) == 0


def lanes(shape):
    return lax.broadcasted_iota(jnp.int32, shape, len(shape) - 1)


def rows(shape):
    return lax.broadcasted_iota(jnp.int32, shape, len(shape) - 2)


def roll(values, by, axis):
    size = values.shape[axis]
    by = by % size
    return values if by == 0 else pltpu.roll(values, by, axis)


def call(body, out_shapes, scratch=(), name=None):
    return pl.pallas_call(
        body,
        out_shape=[jax.ShapeDtypeStruct(s, F32) for s in out_shapes],
        scratch_shapes=[pltpu.VMEM(s, F32) for s in scratch],
        compiler_params=pltpu.CompilerParams(vmem_limit_bytes=40 << 20),
        name=name,
    )


def swap_store(first, fwd, bwd, at, up, down):
    fwd[at] = jnp.where(first, up, down)
    bwd[at] = jnp.where(first, down, up)


def pack_x(field, source, sigma, warmth, fwd, bwd, scaled):
    first = on_first_core()
    inverse = 1.0 / (4.0 + sigma[...])
    scaled[3] = inverse
    for c in range(3):
        scaled[c] = source[c] * inverse

    def layer(f, x):
        if f < 3:
            return field[f, x]
        return warmth[x] if f == 7 else scaled[f - 3, x]

    ups = [(f, x) for f, start, n in UP_LAYERS for x in range(start, start + n)]
    downs = [(f, x) for f, start, n in DOWN_LAYERS for x in range(start, start + n)]
    for at in range(X_LAYERS):
        up = layer(*ups[min(at, len(ups) - 1)])
        down = layer(*downs[min(at, len(downs) - 1)])
        swap_store(first, fwd, bwd, at, up, down)


class Slabs:
    def __init__(self, field, scaled, warmth, got_fwd, got_bwd):
        self.field, self.scaled, self.warmth = field, scaled, warmth
        self.got_fwd, self.got_bwd = got_fwd, got_bwd
        self.first = on_first_core()
        gx = lax.axis_index("gx")
        self.below, self.above = gx > 0, gx < lax.axis_size("gx") - 1

    def own(self, f, x):
        if f < 3:
            return self.field[f, x]
        return self.warmth[x] if f == 7 else self.scaled[f - 3, x]

    def beside(self, f, x):
        fwd, bwd = self.got_fwd, self.got_bwd
        if x < 0:
            at = UP_AT.get((f, x))
            if at is None:
                return None
            value = jnp.where(self.first, fwd[at], bwd[at])
            return jnp.where(self.below, value, 0.0)
        at = DOWN_AT.get((f, x))
        if at is None:
            return None
        value = jnp.where(self.first, bwd[at], fwd[at])
        return jnp.where(self.above, value, 0.0)

    def every(self, emit):
        zero = jnp.zeros((16, 128), F32)
        for x in list(range(-LOW, 0)) + list(range(16, 16 + HIGH)):
            values = [self.beside(f, x) for f in range(7)]
            emit(x + LOW, [zero if v is None else v for v in values] + [zero])

        def step(x, carry):
            emit(x + LOW, [self.own(f, x) for f in range(8)])
            return carry

        lax.fori_loop(0, 16, step, 0)


def pack_y(field, scaled, warmth, got_fwd, got_bwd, fwd, bwd):
    slabs = Slabs(field, scaled, warmth, got_fwd, got_bwd)
    row = rows((8, 128))
    low_half = row < 4

    def emit(at, v):
        tops = [a[8:16] for a in v]
        ends = [a[0:8] for a in v]
        for pair in range(4):
            a, b = 2 * pair, 2 * pair + 1
            up = jnp.where(low_half, roll(tops[b], 4, 0), tops[a])
            down = jnp.where(low_half, ends[a], roll(ends[b], 4, 0))
            if pair == 3:
                down = jnp.where(row == 5, roll(ends[0], 1, 0), down)
                down = jnp.where(row == 6, roll(ends[2], 2, 0), down)
            part = pl.ds(8 * pair, 8)
            fwd[at, part] = jnp.where(slabs.first, up, down)
            bwd[at, part] = jnp.where(slabs.first, down, up)

    slabs.every(emit)


def y_halo(first, got_fwd, got_bwd, at, pair):
    gy = lax.axis_index("gy")
    part = pl.ds(8 * pair, 8)
    f, b = got_fwd[at, part], got_bwd[at, part]
    lower = jnp.where(gy > 0, jnp.where(first, f, b), 0.0)
    upper = jnp.where(gy < lax.axis_size("gy") - 1, jnp.where(first, b, f), 0.0)
    return lower, upper


X_ALL = LOW + 16 + HIGH
X_PAIRS = (X_ALL + 1) // 2


def pack_z(field, scaled, warmth, xf, xb, yf, yb, whole, up, down, packed):
    slabs = Slabs(field, scaled, warmth, xf, xb)
    first = slabs.first
    low_half = rows((8, 128)) < 4
    window = lanes((24, 128)) // 16

    def emit(at, v):
        acc = None
        for pair in range(4):
            lower, upper = y_halo(first, yf, yb, at, pair)
            last = []
            last.append(jnp.where(low_half, upper, lower))
            if pair < 3:
                last.append(roll(jnp.where(low_half, lower, upper), 4, 0))
            else:
                last.append(roll(upper, 3, 0))
            for f, tile in zip((2 * pair, 2 * pair + 1), last):
                slab = jnp.concatenate([v[f], tile], axis=0)
                if f < 7:
                    whole[f, at] = slab
                moved = roll(slab, 16 * f + 8, 1)
                acc = moved if acc is None else jnp.where(window == f, moved, acc)
        packed[at] = acc

    slabs.every(emit)
    packed[X_ALL] = jnp.zeros((24, 128), F32)
    half = (lanes((24, 128)) // 8) % 2 == 0

    def pair_up(k, carry):
        a, b = packed[2 * k], packed[2 * k + 1]
        up[k] = jnp.where(half, a, roll(b, 8, 1))
        down[k] = jnp.where(half, roll(a, -8, 1), b)
        return carry

    lax.fori_loop(0, X_PAIRS, pair_up, 0)


def up_z(main, tail):
    last = lanes(main.shape) == 127
    a, b = roll(main, -1, 1), roll(tail, -1, 1)
    return jnp.where(last, b, a), jnp.where(last, a, b)


def down_z(main, tail):
    start = lanes(main.shape) == 0
    a, b = roll(main, 1, 1), roll(tail, 1, 1)
    return jnp.where(start, b, a), jnp.where(start, a, b)


def both(function, *pairs):
    return tuple(function(*parts) for parts in zip(*pairs))


def relax(
    whole, xf, xb, yf, yb, below_z, above_z, sigma, warmth, storage, position, nodes,
    out, send, partial, main, tail, heat, extra,
):
    first = on_first_core()
    gx, gz = lax.axis_index("gx"), lax.axis_index("gz")
    lane = lanes((24, 128))
    row = rows((24, 128))
    half = (lane // 8) % 2 == 0
    edge = (lane < 8) | (lane >= 120)
    has_below, has_above = gz > 0, gz < lax.axis_size("gz") - 1

    def unpack_one(at, packed):
        for f in range(7):
            tail[f, at] = jnp.where(edge, roll(packed, -(16 * f + 8), 1), 0.0)
        tail[7, at] = roll(packed, 8, 1)
        _, upper = y_halo(first, yf, yb, at, 3)
        for n, place in enumerate((5, 6)):
            extra[n, at, 0:8] = jnp.broadcast_to(upper[place : place + 1], (8, 128))
            extra[n, at, 8:16] = jnp.broadcast_to(tail[7, at, 16 + n : 17 + n, :], (8, 128))
        for f in range(3):
            main[f, at] = whole[f, at]

    def unpack(k, carry):
        lower = jnp.where(has_below, below_z[k], 0.0)
        upper = jnp.where(has_above, above_z[k], 0.0)
        unpack_one(2 * k, jnp.where(half, lower, roll(upper, 8, 1)))
        second = jnp.where(half, roll(lower, -8, 1), upper)

        @pl.when(2 * k + 1 < X_ALL)
        def _():
            unpack_one(2 * k + 1, second)

        return carry

    lax.fori_loop(0, X_PAIRS, unpack, 0)

    def up_y(v):
        return roll(v, -1, 0)

    def down_y(v):
        return roll(v, 1, 0)

    def load(f, at):
        return main[f, at], tail[f, at]

    def up_y_edge(v, n, at):
        moved = both(up_y, v)
        edges = (extra[n, at, 0:8], extra[n, at, 8:16])
        return tuple(
            jnp.where(row == 19, jnp.concatenate([e, e, e], axis=0), m)
            for m, e in zip(moved, edges)
        )

    def curls(at, ahead, e, outer):
        ex, ey, ez = e
        ey_ahead, ez_ahead = ahead
        if outer:
            ex_up, ez_up = up_y_edge(ex, 0, at), up_y_edge(ez, 1, at)
        else:
            ex_up, ez_up = both(up_y, ex), both(up_y, ez)
        cx = both(lambda a, b, c, d: (a - b) - (c - d), ez_up, ez, up_z(*ey), ey)
        cy = both(lambda a, b, c, d: (a - b) - (c - d), up_z(*ex), ex, ez_ahead, ez)
        cz = both(lambda a, b, c, d: (a - b) - (c - d), ey_ahead, ey, ex_up, ex)
        return cx, cy, cz

    for number, weight in enumerate(EM_WEIGHTS):
        begin = 1 + number
        outer = number == 0

        def curls_at(at, outer=outer):
            e = [load(f, at) for f in range(3)]
            ahead = (load(1, at + 1), load(2, at + 1))
            return e, curls(at, ahead, e, outer)

        def step(at, carry, weight=weight, curls_at=curls_at):
            cy_before, cz_before = carry
            e, (cx, cy, cz) = curls_at(at)
            kx = both(
                lambda a, b, c, d: (a - b) - (c - d), cz, both(down_y, cz), cy, down_z(*cy)
            )
            ky = both(lambda a, b, c, d: (a - b) - (c - d), cx, down_z(*cx), cz, cz_before)
            kz = both(
                lambda a, b, c, d: (a - b) - (c - d), cy, cy_before, cx, both(down_y, cx)
            )
            g = (whole[6, at] * weight, tail[6, at] * weight)
            keep = both(lambda v: (1.0 - weight) + 4.0 * v, g)
            for f, k in enumerate((kx, ky, kz)):
                h = (whole[3 + f, at], tail[3 + f, at])
                new = both(
                    lambda p, v, s, w, d: p * v + weight * s - w * d, keep, e[f], h, g, k
                )
                main[f, at], tail[f, at] = new
            return cy, cz

        _, (_, cy, cz) = curls_at(begin - 1)
        lax.fori_loop(begin, X_ALL - begin, step, (cy, cz))

    def joule(x, carry):
        at = x + LOW
        ex, ey, ez = (both(lambda v: v * v, load(f, at)) for f in range(3))
        ey_ahead, ez_ahead = (both(lambda v: v * v, load(f, at + 1)) for f in (1, 2))
        a = both(lambda v: v + up_y(v), ex)
        c = both(lambda p, q, r: p + (q + r), a, ey, ey_ahead)
        c = c[0] + up_z(*c)[0]
        d = ez[0] + ez_ahead[0]
        s = c + (d + up_y(d))
        heat[x] = sigma[x] * (0.25 * s[0:16])
        for f in range(3):
            out[f, x] = main[f, at, 0:16, :]
        return carry

    lax.fori_loop(0, 16, joule, 0)

    count = send.shape[0]
    spread = (rows((count, 256)) == position[...]).astype(jnp.bfloat16)
    left = heat[...].reshape(256, 128)
    total = nodes[...]
    for _ in range(3):
        piece = left.astype(jnp.bfloat16)
        left = left - piece.astype(F32)
        total = total + jnp.dot(spread, piece, preferred_element_type=F32)
    send[...] = total

    row16 = rows((16, 128))
    low_at, high_at = UP_AT[7, -1], DOWN_AT[7, 16]
    under = jnp.where(gx > 0, jnp.where(first, xf[low_at], xb[low_at]), 0.0)
    over = jnp.where(
        gx < lax.axis_size("gx") - 1, jnp.where(first, xb[high_at], xf[high_at]), 0.0
    )
    for x in range(16):
        t = warmth[x]
        ends = tail[7, x + LOW, 0:16, :]
        lower, upper = y_halo(first, yf, yb, x + LOW, 3)
        total = (warmth[x - 1] if x else under) + (warmth[x + 1] if x < 15 else over)
        total = total + jnp.where(row16 == 0, lower[3:4], roll(t, 1, 0))
        total = total + jnp.where(row16 == 15, upper[4:5], roll(t, -1, 0))
        total = total + up_z(t, ends)[0] + down_z(t, ends)[0]
        partial[x] = t + HEAT_WEIGHTS[0] * (total - 6.0 * t) / (6.0 + storage[x])


def place(owners, columns, position, nodes):
    groups = lax.axis_size("gy") * lax.axis_size("gz")
    owner, column = owners[...], columns[...]
    member = rows((groups, 256)) == owner
    earlier = (rows((256, 256)) < lanes((256, 256))).astype(jnp.bfloat16)
    before = jnp.dot(member.astype(jnp.bfloat16), earlier, preferred_element_type=F32)
    rank = jnp.sum(jnp.where(member, before, 0.0), axis=0, keepdims=True).astype(jnp.int32)
    position[...] = owner * (CAP + 1) + rank
    count = nodes.shape[0]
    spread = (rows((count, 256)) == owner * (CAP + 1) + CAP).astype(jnp.bfloat16)
    listed = jnp.where(rows((128, 256)) == rank, column + 1, 0).astype(F32).astype(jnp.bfloat16)
    nodes[...] = lax.dot_general(
        spread, listed, (((1,), (1,)), ((), ())), preferred_element_type=F32
    )


def warm(got, partial, warmth, storage, xf, xb, yf, yb, up, down, rest, heat, mid):
    first = on_first_core()
    groups = got.shape[0] // (CAP + 1)
    ids = got[pl.ds(CAP, groups, stride=CAP + 1), :]
    lane = lanes((groups, 256))
    total = None
    for r in range(CAP):
        hit = (ids[:, r : r + 1] == (lane + 1).astype(F32)).astype(jnp.bfloat16)
        left = got[pl.ds(r, groups, stride=CAP + 1), :]
        for _ in range(3):
            piece = left.astype(jnp.bfloat16)
            left = left - piece.astype(F32)
            term = lax.dot_general(
                hit, piece, (((0,), (0,)), ((), ())), preferred_element_type=F32
            )
            total = term if total is None else total + term
    heat[...] = total.reshape(16, 16, 128)
    lane = lanes((16, 128))
    row = rows((16, 128))
    for x in range(16):
        mid[x] = partial[x] + HEAT_WEIGHTS[0] * heat[x] / (6.0 + storage[x])
    xf[...] = jnp.where(first, mid[15], mid[0])
    xb[...] = jnp.where(first, mid[0], mid[15])
    ups = downs = jnp.zeros((16, 128), F32)
    for x in range(16):
        t = mid[x]
        top, end = t[15:16], t[0:1]
        yf[x : x + 1] = jnp.where(first, top, end)
        yb[x : x + 1] = jnp.where(first, end, top)
        ups = jnp.where(lane == 8 * x, roll(t, 8 * x + 1, 1), ups)
        downs = jnp.where(lane == 8 * x, roll(t, 8 * x, 1), downs)
        near = jnp.where(row == 0, 0.0, roll(t, 1, 0)) + jnp.where(row == 15, 0.0, roll(t, -1, 0))
        near = near + jnp.where(lane == 0, 0.0, roll(t, 1, 1))
        near = near + jnp.where(lane == 127, 0.0, roll(t, -1, 1))
        if x > 0:
            near = near + mid[x - 1]
        if x < 15:
            near = near + mid[x + 1]
        s = storage[x]
        push = s * warmth[x] + heat[x] - (6.0 + s) * t + near
        rest[x] = t + HEAT_WEIGHTS[1] * push / (6.0 + s)
    up[...] = ups
    down[...] = downs


def finish(rest, storage, xf, xb, yf, yb, from_below, from_above, out):
    first = on_first_core()
    gx, gy, gz = (lax.axis_index(a) for a in ("gx", "gy", "gz"))
    ends = [a > 0 for a in (gx, gy, gz)]
    tops = [a < lax.axis_size(n) - 1 for a, n in ((gx, "gx"), (gy, "gy"), (gz, "gz"))]
    f, b = xf[...], xb[...]
    x_low = jnp.where(ends[0], jnp.where(first, f, b), 0.0)
    x_high = jnp.where(tops[0], jnp.where(first, b, f), 0.0)
    f, b = yf[...], yb[...]
    y_low = jnp.where(ends[1], jnp.where(first, f, b), 0.0)
    y_high = jnp.where(tops[1], jnp.where(first, b, f), 0.0)
    z_low = jnp.where(ends[2], from_below[...], 0.0)
    z_high = jnp.where(tops[2], from_above[...], 0.0)
    lane = lanes((16, 128))
    row = rows((16, 128))
    for x in range(16):
        near = jnp.where(row == 0, y_low[x : x + 1], 0.0)
        near = near + jnp.where(row == 15, y_high[x : x + 1], 0.0)
        near = near + jnp.where(lane == 0, roll(z_low, -8 * x, 1), 0.0)
        near = near + jnp.where(lane == 127, roll(z_high, 127 - 8 * x, 1), 0.0)
        if x == 0:
            near = near + x_low
        if x == 15:
            near = near + x_high
        out[x] = rest[x] + HEAT_WEIGHTS[1] * near / (6.0 + storage[x])


def around(axis):
    n, m = lax.axis_size(axis), lax.axis_size("gz")

    def target(a, c):
        to = a + (1 if c % 2 == 0 else -1)
        return (to, c) if 0 <= to < n else (a, c ^ 1)

    forward = []
    for a in range(n):
        for c in range(m):
            to = target(a, c)
            forward.append((a * m + c, to[0] * m + to[1]))
    return forward, [(j, i) for i, j in forward]


def exchange(axis, fwd, bwd):
    forward, backward = around(axis)
    names = (axis, "gz")
    return lax.ppermute(fwd, names, forward), lax.ppermute(bwd, names, backward)


def exchange_z(up, down):
    m = lax.axis_size("gz")
    ring = [(i, (i + 1) % m) for i in range(m)]
    return lax.ppermute(up, "gz", ring), lax.ppermute(down, "gz", [(j, i) for i, j in ring])


def local(field, source, sigma, warmth, storage, partition, column):
    groups = lax.axis_size("gy") * lax.axis_size("gz")
    count = groups * (CAP + 1)
    cube = (16, 16, 128)
    face = (16, 128)
    fwd, bwd, scaled = call(
        pack_x, [(X_LAYERS, 16, 128), (X_LAYERS, 16, 128), (4, 16, 16, 128)], name="pack_x"
    )(field, source, sigma, warmth)
    xf, xb = exchange("gx", fwd, bwd)
    position, nodes = pl.pallas_call(
        place,
        out_shape=[
            jax.ShapeDtypeStruct((1, 256), jnp.int32),
            jax.ShapeDtypeStruct((count, 128), F32),
        ],
        name="place",
    )(partition.reshape(1, 256), column.reshape(1, 256))
    fwd, bwd = call(pack_y, [(X_ALL, 32, 128), (X_ALL, 32, 128)], name="pack_y")(
        field, scaled, warmth, xf, xb
    )
    yf, yb = exchange("gy", fwd, bwd)
    whole, up, down = call(
        pack_z,
        [(7, X_ALL, 24, 128), (X_PAIRS, 24, 128), (X_PAIRS, 24, 128)],
        [(X_ALL + 1, 24, 128)],
        name="pack_z",
    )(field, scaled, warmth, xf, xb, yf, yb)
    below_z, above_z = exchange_z(up, down)
    out, send, partial = call(
        relax,
        [(3, *cube), (count, 128), cube],
        [(3, X_ALL, 24, 128), (8, X_ALL, 24, 128), cube, (2, X_ALL, 16, 128)],
        name="relax",
    )(whole, xf, xb, yf, yb, below_z, above_z, sigma, warmth, storage, position, nodes)
    got = lax.all_to_all(
        send.reshape(count, 1, 128), ("gy", "gz"), split_axis=0, concat_axis=0, tiled=True
    ).reshape(count, 128)
    xf, xb, yf, yb, up, down, rest = call(
        warm, [face, face, face, face, face, face, cube], [cube, cube], name="warm"
    )(got, partial, warmth, storage)
    xf, xb = exchange("gx", xf, xb)
    yf, yb = exchange("gy", yf, yb)
    below_z, above_z = exchange_z(up, down)
    (updated,) = call(finish, [cube], name="finish")(
        rest, storage, xf, xb, yf, yb, below_z, above_z
    )
    return out, updated


def solution(mesh):
    in_specs = (
        P(None, "gx", "gy", "gz"),
        P(None, "gx", "gy", "gz"),
        P("gx", "gy", "gz"),
        P("gx", "gy", "gz"),
        P("gx", "gy", "gz"),
        P("gx", "gy", "gz", None, None),
        P("gx", "gy", "gz", None),
    )
    out_specs = (P(None, "gx", "gy", "gz"), P("gx", "gy", "gz"))
    return jax.shard_map(local, mesh=mesh, in_specs=in_specs, out_specs=out_specs, check_vma=False)
```

```python
import math

import jax
import jax.numpy as jnp
from jax import lax
from jax.experimental import pallas as pl
from jax.experimental.pallas import tpu as pltpu
from jax.sharding import PartitionSpec as P

EM_SWEEPS = 4
HEAT_SWEEPS = 2
CAP = 8
LOW, HIGH = 4, 5
F32 = jnp.float32

em_lower = 0.02
em_upper = 3.0
heat_lower = 0.07
heat_upper = 2.0

UP_LAYERS = ((0, 12, 4), (1, 12, 4), (2, 12, 4), (3, 13, 3), (4, 13, 3), (5, 13, 3), (6, 13, 3), (7, 15, 1))
DOWN_LAYERS = ((0, 0, 4), (1, 0, 5), (2, 0, 5), (3, 0, 3), (4, 0, 4), (5, 0, 4), (6, 0, 4), (7, 0, 1))


def spots(layers, shift):
    where, at = {}, 0
    for field, first, count in layers:
        for x in range(first, first + count):
            where[field, x + shift] = at
            at += 1
    return where, at


UP_AT, UP_COUNT = spots(UP_LAYERS, -16)
DOWN_AT, DOWN_COUNT = spots(DOWN_LAYERS, 16)
X_LAYERS = max(UP_COUNT, DOWN_COUNT)


def chebyshev_weights(lower_end, upper_end, sweep_count):
    middle = 0.5 * (upper_end + lower_end)
    radius = 0.5 * (upper_end - lower_end)
    return [
        1.0 / (middle + radius * math.cos(math.pi * (2 * number + 1) / (2 * sweep_count)))
        for number in range(sweep_count)
    ]


EM_WEIGHTS = chebyshev_weights(em_lower, em_upper, EM_SWEEPS)
HEAT_WEIGHTS = chebyshev_weights(heat_lower, heat_upper, HEAT_SWEEPS)


def on_first_core():
    return lax.rem(lax.axis_index("gz"), 2) == 0


def lanes(shape):
    return lax.broadcasted_iota(jnp.int32, shape, len(shape) - 1)


def rows(shape):
    return lax.broadcasted_iota(jnp.int32, shape, len(shape) - 2)


def roll(values, by, axis):
    size = values.shape[axis]
    by = by % size
    return values if by == 0 else pltpu.roll(values, by, axis)


def call(body, out_shapes, scratch=(), name=None, **options):
    return pl.pallas_call(
        body,
        out_shape=[jax.ShapeDtypeStruct(s, F32) for s in out_shapes],
        scratch_shapes=[pltpu.VMEM(s, F32) if isinstance(s, tuple) else s for s in scratch],
        compiler_params=pltpu.CompilerParams(vmem_limit_bytes=40 << 20),
        name=name,
        **options,
    )


def swap_store(first, fwd, bwd, at, up, down):
    fwd[at] = jnp.where(first, up, down)
    bwd[at] = jnp.where(first, down, up)


def pack_x(*refs):
    far, (fwd, bwd, scaled, field, sigma, warmth, storage, source, arrived) = refs[:5], refs[5:]
    near = (field, source, sigma, warmth, storage)
    copies = [
        pltpu.make_async_copy(a, b, arrived.at[n]) for n, (a, b) in enumerate(zip(far, near))
    ]
    for copy in copies:
        copy.start()
    for copy in copies:
        copy.wait()
    first = on_first_core()
    inverse = 1.0 / (4.0 + sigma[...])
    scaled[3] = inverse
    for c in range(3):
        scaled[c] = source[c] * inverse

    def layer(f, x):
        if f < 3:
            return field[f, x]
        return warmth[x] if f == 7 else scaled[f - 3, x]

    ups = [(f, x) for f, start, n in UP_LAYERS for x in range(start, start + n)]
    downs = [(f, x) for f, start, n in DOWN_LAYERS for x in range(start, start + n)]
    for at in range(X_LAYERS):
        up = layer(*ups[min(at, len(ups) - 1)])
        down = layer(*downs[min(at, len(downs) - 1)])
        swap_store(first, fwd, bwd, at, up, down)


class Slabs:
    def __init__(self, field, scaled, warmth, got_fwd, got_bwd):
        self.field, self.scaled, self.warmth = field, scaled, warmth
        self.got_fwd, self.got_bwd = got_fwd, got_bwd
        self.first = on_first_core()
        gx = lax.axis_index("gx")
        self.below, self.above = gx > 0, gx < lax.axis_size("gx") - 1

    def own(self, f, x):
        if f < 3:
            return self.field[f, x]
        return self.warmth[x] if f == 7 else self.scaled[f - 3, x]

    def beside(self, f, x):
        fwd, bwd = self.got_fwd, self.got_bwd
        if x < 0:
            at = UP_AT.get((f, x))
            if at is None:
                return None
            value = jnp.where(self.first, fwd[at], bwd[at])
            return jnp.where(self.below, value, 0.0)
        at = DOWN_AT.get((f, x))
        if at is None:
            return None
        value = jnp.where(self.first, bwd[at], fwd[at])
        return jnp.where(self.above, value, 0.0)

    def every(self, emit, unroll=4):
        zero = jnp.zeros((16, 128), F32)
        for x in list(range(-LOW, 0)) + list(range(16, 16 + HIGH)):
            values = [self.beside(f, x) for f in range(7)]
            emit(x + LOW, [zero if v is None else v for v in values] + [zero])

        def step(x, carry):
            emit(x + LOW, [self.own(f, x) for f in range(8)])
            return carry

        lax.fori_loop(0, 16, step, 0, unroll=unroll)


def pack_y(field, scaled, warmth, got_fwd, got_bwd, fwd, bwd):
    slabs = Slabs(field, scaled, warmth, got_fwd, got_bwd)
    row = rows((8, 128))
    low_half = row < 4

    def emit(at, v):
        tops = [a[8:16] for a in v]
        ends = [a[0:8] for a in v]
        for pair in range(4):
            a, b = 2 * pair, 2 * pair + 1
            up = jnp.where(low_half, roll(tops[b], 4, 0), tops[a])
            down = jnp.where(low_half, ends[a], roll(ends[b], 4, 0))
            if pair == 3:
                down = jnp.where(row == 5, roll(ends[0], 1, 0), down)
                down = jnp.where(row == 6, roll(ends[2], 2, 0), down)
            part = pl.ds(8 * pair, 8)
            fwd[at, part] = jnp.where(slabs.first, up, down)
            bwd[at, part] = jnp.where(slabs.first, down, up)

    slabs.every(emit)


def y_halo(first, got_fwd, got_bwd, at, pair):
    gy = lax.axis_index("gy")
    part = pl.ds(8 * pair, 8)
    f, b = got_fwd[at, part], got_bwd[at, part]
    lower = jnp.where(gy > 0, jnp.where(first, f, b), 0.0)
    upper = jnp.where(gy < lax.axis_size("gy") - 1, jnp.where(first, b, f), 0.0)
    return lower, upper


X_ALL = LOW + 16 + HIGH
X_PAIRS = (X_ALL + 1) // 2


def pack_z(field, scaled, warmth, xf, xb, yf, yb, whole, up, down, packed):
    slabs = Slabs(field, scaled, warmth, xf, xb)
    first = slabs.first
    low_half = rows((8, 128)) < 4
    window = lanes((24, 128)) // 16

    def emit(at, v):
        acc = None
        for pair in range(4):
            lower, upper = y_halo(first, yf, yb, at, pair)
            last = []
            last.append(jnp.where(low_half, upper, lower))
            if pair < 3:
                last.append(roll(jnp.where(low_half, lower, upper), 4, 0))
            else:
                last.append(roll(upper, 3, 0))
            for f, tile in zip((2 * pair, 2 * pair + 1), last):
                slab = jnp.concatenate([v[f], tile], axis=0)
                if f < 7:
                    whole[f, at] = slab
                moved = roll(slab, 16 * f + 8, 1)
                acc = moved if acc is None else jnp.where(window == f, moved, acc)
        packed[at] = acc

    slabs.every(emit)
    packed[X_ALL] = jnp.zeros((24, 128), F32)
    half = (lanes((24, 128)) // 8) % 2 == 0

    def pair_up(k, carry):
        a, b = packed[2 * k], packed[2 * k + 1]
        up[k] = jnp.where(half, a, roll(b, 8, 1))
        down[k] = jnp.where(half, roll(a, -8, 1), b)
        return carry

    lax.fori_loop(0, X_PAIRS, pair_up, 0, unroll=True)


def up_z(main, tail):
    last = lanes(main.shape) == 127
    a, b = roll(main, -1, 1), roll(tail, -1, 1)
    return jnp.where(last, b, a), jnp.where(last, a, b)


def down_z(main, tail):
    start = lanes(main.shape) == 0
    a, b = roll(main, 1, 1), roll(tail, 1, 1)
    return jnp.where(start, b, a), jnp.where(start, a, b)


def both(function, *pairs):
    return tuple(function(*parts) for parts in zip(*pairs))


def relax(
    whole, xf, xb, yf, yb, below_z, above_z, sigma, warmth, storage, position, nodes,
    out, send, partial, main, tail, other, far, heat, extra,
):
    first = on_first_core()
    gx, gz = lax.axis_index("gx"), lax.axis_index("gz")
    lane = lanes((24, 128))
    row = rows((24, 128))
    half = (lane // 8) % 2 == 0
    edge = (lane < 8) | (lane >= 120)
    has_below, has_above = gz > 0, gz < lax.axis_size("gz") - 1

    def unpack_one(at, packed):
        for f in range(7):
            tail[f, at] = jnp.where(edge, roll(packed, -(16 * f + 8), 1), 0.0)
        tail[7, at] = roll(packed, 8, 1)
        _, upper = y_halo(first, yf, yb, at, 3)
        for n, place in enumerate((5, 6)):
            extra[n, at, 0:8] = jnp.broadcast_to(upper[place : place + 1], (8, 128))
            extra[n, at, 8:16] = jnp.broadcast_to(tail[7, at, 16 + n : 17 + n, :], (8, 128))

    def unpack(k, carry):
        lower = jnp.where(has_below, below_z[k], 0.0)
        upper = jnp.where(has_above, above_z[k], 0.0)
        unpack_one(2 * k, jnp.where(half, lower, roll(upper, 8, 1)))
        second = jnp.where(half, roll(lower, -8, 1), upper)

        unpack_one(2 * k + 1, second)
        return carry

    lax.fori_loop(0, X_ALL // 2, unpack, 0, unroll=4)
    lower = jnp.where(has_below, below_z[X_PAIRS - 1], 0.0)
    upper = jnp.where(has_above, above_z[X_PAIRS - 1], 0.0)
    unpack_one(X_ALL - 1, jnp.where(half, lower, roll(upper, 8, 1)))

    def up_y(v):
        return roll(v, -1, 0)

    def down_y(v):
        return roll(v, 1, 0)

    buffers = [(whole, tail), (main, far), (other, tail), (main, far), (other, tail)]

    def load(number, f, at):
        return buffers[number][0][f, at], buffers[number][1][f, at]

    def up_y_edge(v, n, at):
        moved = both(up_y, v)
        edges = (extra[n, at, 0:8], extra[n, at, 8:16])
        return tuple(
            jnp.where(row == 19, jnp.concatenate([e, e, e], axis=0), m)
            for m, e in zip(moved, edges)
        )

    def curls(at, ahead, e, outer):
        ex, ey, ez = e
        ey_ahead, ez_ahead = ahead
        if outer:
            ex_up, ez_up = up_y_edge(ex, 0, at), up_y_edge(ez, 1, at)
        else:
            ex_up, ez_up = both(up_y, ex), both(up_y, ez)
        cx = both(lambda a, b, c, d: (a - b) - (c - d), ez_up, ez, up_z(*ey), ey)
        cy = both(lambda a, b, c, d: (a - b) - (c - d), up_z(*ex), ex, ez_ahead, ez)
        cz = both(lambda a, b, c, d: (a - b) - (c - d), ey_ahead, ey, ex_up, ex)
        return cx, cy, cz

    for number, weight in enumerate(EM_WEIGHTS):
        begin = 1 + number
        outer = number == 0

        def curls_at(at, number=number, outer=outer):
            e = [load(number, f, at) for f in range(3)]
            ahead = (load(number, 1, at + 1), load(number, 2, at + 1))
            return e, curls(at, ahead, e, outer)

        def step(at, carry, number=number, weight=weight, curls_at=curls_at):
            cy_before, cz_before = carry
            e, (cx, cy, cz) = curls_at(at)
            kx = both(
                lambda a, b, c, d: (a - b) - (c - d), cz, both(down_y, cz), cy, down_z(*cy)
            )
            ky = both(lambda a, b, c, d: (a - b) - (c - d), cx, down_z(*cx), cz, cz_before)
            kz = both(
                lambda a, b, c, d: (a - b) - (c - d), cy, cy_before, cx, both(down_y, cx)
            )
            g = (whole[6, at] * weight, tail[6, at] * weight)
            keep = both(lambda v: (1.0 - weight) + 4.0 * v, g)
            for f, k in enumerate((kx, ky, kz)):
                h = (whole[3 + f, at], tail[3 + f, at])
                new = both(
                    lambda p, v, s, w, d: p * v + weight * s - w * d, keep, e[f], h, g, k
                )
                buffers[number + 1][0][f, at], buffers[number + 1][1][f, at] = new
            return cy, cz

        _, (_, cy, cz) = curls_at(begin - 1)
        lax.fori_loop(begin, X_ALL - begin, step, (cy, cz), unroll=4)

    def joule(x, carry):
        at = x + LOW
        ex, ey, ez = (both(lambda v: v * v, load(EM_SWEEPS, f, at)) for f in range(3))
        ey_ahead, ez_ahead = (both(lambda v: v * v, load(EM_SWEEPS, f, at + 1)) for f in (1, 2))
        a = both(lambda v: v + up_y(v), ex)
        c = both(lambda p, q, r: p + (q + r), a, ey, ey_ahead)
        c = c[0] + up_z(*c)[0]
        d = ez[0] + ez_ahead[0]
        s = c + (d + up_y(d))
        heat[x] = sigma[x] * (0.25 * s[0:16])
        for f in range(3):
            out[f, x] = other[f, at, 0:16, :]
        return carry

    lax.fori_loop(0, 16, joule, 0, unroll=4)

    count = send.shape[0]
    spread = (rows((count, 256)) == position[...]).astype(jnp.bfloat16)
    left = heat[...].reshape(256, 128)
    total = nodes[...]
    for _ in range(3):
        piece = left.astype(jnp.bfloat16)
        left = left - piece.astype(F32)
        total = total + jnp.dot(spread, piece, preferred_element_type=F32)
    send[...] = total

    row16 = rows((16, 128))
    low_at, high_at = UP_AT[7, -1], DOWN_AT[7, 16]
    under = jnp.where(gx > 0, jnp.where(first, xf[low_at], xb[low_at]), 0.0)
    over = jnp.where(
        gx < lax.axis_size("gx") - 1, jnp.where(first, xb[high_at], xf[high_at]), 0.0
    )
    for x in range(16):
        t = warmth[x]
        ends = tail[7, x + LOW, 0:16, :]
        lower, upper = y_halo(first, yf, yb, x + LOW, 3)
        total = (warmth[x - 1] if x else under) + (warmth[x + 1] if x < 15 else over)
        total = total + jnp.where(row16 == 0, lower[3:4], roll(t, 1, 0))
        total = total + jnp.where(row16 == 15, upper[4:5], roll(t, -1, 0))
        total = total + up_z(t, ends)[0] + down_z(t, ends)[0]
        partial[x] = t + HEAT_WEIGHTS[0] * (total - 6.0 * t) / (6.0 + storage[x])


def place(owners, columns, position, nodes):
    groups = lax.axis_size("gy") * lax.axis_size("gz")
    owner, column = owners[...], columns[...]
    member = rows((groups, 256)) == owner
    earlier = (rows((256, 256)) < lanes((256, 256))).astype(jnp.bfloat16)
    before = jnp.dot(member.astype(jnp.bfloat16), earlier, preferred_element_type=F32)
    rank = jnp.sum(jnp.where(member, before, 0.0), axis=0, keepdims=True).astype(jnp.int32)
    position[...] = owner * (CAP + 1) + rank
    count = nodes.shape[0]
    spread = (rows((count, 256)) == owner * (CAP + 1) + CAP).astype(jnp.bfloat16)
    listed = jnp.where(rows((128, 256)) == rank, column + 1, 0).astype(F32).astype(jnp.bfloat16)
    nodes[...] = lax.dot_general(
        spread, listed, (((1,), (1,)), ((), ())), preferred_element_type=F32
    )


def warm(got, partial, warmth, storage, xf, xb, yf, yb, up, down, rest, heat, mid):
    first = on_first_core()
    groups = got.shape[0] // (CAP + 1)
    ids = got[pl.ds(CAP, groups, stride=CAP + 1), :]
    lane = lanes((groups, 256))
    total = None
    for r in range(CAP):
        hit = (ids[:, r : r + 1] == (lane + 1).astype(F32)).astype(jnp.bfloat16)
        left = got[pl.ds(r, groups, stride=CAP + 1), :]
        for _ in range(3):
            piece = left.astype(jnp.bfloat16)
            left = left - piece.astype(F32)
            term = lax.dot_general(
                hit, piece, (((0,), (0,)), ((), ())), preferred_element_type=F32
            )
            total = term if total is None else total + term
    heat[...] = total.reshape(16, 16, 128)
    lane = lanes((16, 128))
    row = rows((16, 128))
    for x in range(16):
        mid[x] = partial[x] + HEAT_WEIGHTS[0] * heat[x] / (6.0 + storage[x])
    xf[...] = jnp.where(first, mid[15], mid[0])
    xb[...] = jnp.where(first, mid[0], mid[15])
    ups = downs = jnp.zeros((16, 128), F32)
    for x in range(16):
        t = mid[x]
        top, end = t[15:16], t[0:1]
        yf[x : x + 1] = jnp.where(first, top, end)
        yb[x : x + 1] = jnp.where(first, end, top)
        ups = jnp.where(lane == 8 * x, roll(t, 8 * x + 1, 1), ups)
        downs = jnp.where(lane == 8 * x, roll(t, 8 * x, 1), downs)
        near = jnp.where(row == 0, 0.0, roll(t, 1, 0)) + jnp.where(row == 15, 0.0, roll(t, -1, 0))
        near = near + jnp.where(lane == 0, 0.0, roll(t, 1, 1))
        near = near + jnp.where(lane == 127, 0.0, roll(t, -1, 1))
        if x > 0:
            near = near + mid[x - 1]
        if x < 15:
            near = near + mid[x + 1]
        s = storage[x]
        push = s * warmth[x] + heat[x] - (6.0 + s) * t + near
        rest[x] = t + HEAT_WEIGHTS[1] * push / (6.0 + s)
    up[...] = ups
    down[...] = downs


def finish(rest, storage, xf, xb, yf, yb, from_below, from_above, out):
    first = on_first_core()
    gx, gy, gz = (lax.axis_index(a) for a in ("gx", "gy", "gz"))
    ends = [a > 0 for a in (gx, gy, gz)]
    tops = [a < lax.axis_size(n) - 1 for a, n in ((gx, "gx"), (gy, "gy"), (gz, "gz"))]
    f, b = xf[...], xb[...]
    x_low = jnp.where(ends[0], jnp.where(first, f, b), 0.0)
    x_high = jnp.where(tops[0], jnp.where(first, b, f), 0.0)
    f, b = yf[...], yb[...]
    y_low = jnp.where(ends[1], jnp.where(first, f, b), 0.0)
    y_high = jnp.where(tops[1], jnp.where(first, b, f), 0.0)
    z_low = jnp.where(ends[2], from_below[...], 0.0)
    z_high = jnp.where(tops[2], from_above[...], 0.0)
    lane = lanes((16, 128))
    row = rows((16, 128))
    for x in range(16):
        near = jnp.where(row == 0, y_low[x : x + 1], 0.0)
        near = near + jnp.where(row == 15, y_high[x : x + 1], 0.0)
        near = near + jnp.where(lane == 0, roll(z_low, -8 * x, 1), 0.0)
        near = near + jnp.where(lane == 127, roll(z_high, 127 - 8 * x, 1), 0.0)
        if x == 0:
            near = near + x_low
        if x == 15:
            near = near + x_high
        out[x] = rest[x] + HEAT_WEIGHTS[1] * near / (6.0 + storage[x])


def around(axis):
    n, m = lax.axis_size(axis), lax.axis_size("gz")

    def target(a, c):
        to = a + (1 if c % 2 == 0 else -1)
        return (to, c) if 0 <= to < n else (a, c ^ 1)

    forward = []
    for a in range(n):
        for c in range(m):
            to = target(a, c)
            forward.append((a * m + c, to[0] * m + to[1]))
    return forward, [(j, i) for i, j in forward]


def exchange(axis, fwd, bwd):
    forward, backward = around(axis)
    names = (axis, "gz")
    return lax.ppermute(fwd, names, forward), lax.ppermute(bwd, names, backward)


def exchange_z(up, down):
    m = lax.axis_size("gz")
    ring = [(i, (i + 1) % m) for i in range(m)]
    return lax.ppermute(up, "gz", ring), lax.ppermute(down, "gz", [(j, i) for i, j in ring])


def local(field, source, sigma, warmth, storage, partition, column):
    groups = lax.axis_size("gy") * lax.axis_size("gz")
    count = groups * (CAP + 1)
    cube = (16, 16, 128)
    face = (16, 128)
    fwd, bwd, scaled, field, sigma, warmth, storage = call(
        pack_x,
        [(X_LAYERS, 16, 128), (X_LAYERS, 16, 128), (4, *cube), (3, *cube), cube, cube, cube],
        [(3, *cube), pltpu.SemaphoreType.DMA((5,))],
        name="pack_x",
        in_specs=[pl.BlockSpec(memory_space=pltpu.HBM)] * 5,
    )(field, source, sigma, warmth, storage)
    xf, xb = exchange("gx", fwd, bwd)
    position, nodes = pl.pallas_call(
        place,
        out_shape=[
            jax.ShapeDtypeStruct((1, 256), jnp.int32),
            jax.ShapeDtypeStruct((count, 128), F32),
        ],
        name="place",
    )(partition.reshape(1, 256), column.reshape(1, 256))
    fwd, bwd = call(pack_y, [(X_ALL, 32, 128), (X_ALL, 32, 128)], name="pack_y")(
        field, scaled, warmth, xf, xb
    )
    yf, yb = exchange("gy", fwd, bwd)
    whole, up, down = call(
        pack_z,
        [(7, X_ALL, 24, 128), (X_PAIRS, 24, 128), (X_PAIRS, 24, 128)],
        [(X_ALL + 1, 24, 128)],
        name="pack_z",
    )(field, scaled, warmth, xf, xb, yf, yb)
    below_z, above_z = exchange_z(up, down)
    out, send, partial = call(
        relax,
        [(3, *cube), (count, 128), cube],
        [
            (3, X_ALL, 24, 128),
            (8, X_ALL, 24, 128),
            (3, X_ALL, 24, 128),
            (3, X_ALL, 24, 128),
            cube,
            (2, X_ALL, 16, 128),
        ],
        name="relax",
    )(whole, xf, xb, yf, yb, below_z, above_z, sigma, warmth, storage, position, nodes)
    got = lax.all_to_all(
        send.reshape(count, 1, 128), ("gy", "gz"), split_axis=0, concat_axis=0, tiled=True
    ).reshape(count, 128)
    xf, xb, yf, yb, up, down, rest = call(
        warm, [face, face, face, face, face, face, cube], [cube, cube], name="warm"
    )(got, partial, warmth, storage)
    xf, xb = exchange("gx", xf, xb)
    yf, yb = exchange("gy", yf, yb)
    below_z, above_z = exchange_z(up, down)
    (updated,) = call(finish, [cube], name="finish")(
        rest, storage, xf, xb, yf, yb, below_z, above_z
    )
    return out, updated


def solution(mesh):
    in_specs = (
        P(None, "gx", "gy", "gz"),
        P(None, "gx", "gy", "gz"),
        P("gx", "gy", "gz"),
        P("gx", "gy", "gz"),
        P("gx", "gy", "gz"),
        P("gx", "gy", "gz", None, None),
        P("gx", "gy", "gz", None),
    )
    out_specs = (P(None, "gx", "gy", "gz"), P("gx", "gy", "gz"))
    return jax.shard_map(local, mesh=mesh, in_specs=in_specs, out_specs=out_specs, check_vma=False)
```

```python
import functools
import math

import jax
import jax.numpy as jnp
from jax import lax
from jax.experimental import pallas as pl
from jax.experimental.pallas import tpu as pltpu
from jax.sharding import PartitionSpec as P

EM_SWEEPS = 4
HEAT_SWEEPS = 2
CAP = 8
LOW, HIGH = 4, 5
F32 = jnp.float32
FIRST_LIMIT = 62 << 20

em_lower = 0.02
em_upper = 3.0
heat_lower = 0.07
heat_upper = 2.0

UP_LAYERS = ((0, 12, 4), (1, 12, 4), (2, 12, 4), (3, 13, 3), (4, 13, 3), (5, 13, 3), (6, 13, 3), (7, 15, 1))
DOWN_LAYERS = ((0, 0, 4), (1, 0, 5), (2, 0, 5), (3, 0, 3), (4, 0, 4), (5, 0, 4), (6, 0, 4), (7, 0, 1))


def spots(layers, shift):
    where, at = {}, 0
    for field, first, count in layers:
        for x in range(first, first + count):
            where[field, x + shift] = at
            at += 1
    return where, at


UP_AT, UP_COUNT = spots(UP_LAYERS, -16)
DOWN_AT, DOWN_COUNT = spots(DOWN_LAYERS, 16)
X_LAYERS = max(UP_COUNT, DOWN_COUNT)


def chebyshev_weights(lower_end, upper_end, sweep_count):
    middle = 0.5 * (upper_end + lower_end)
    radius = 0.5 * (upper_end - lower_end)
    return [
        1.0 / (middle + radius * math.cos(math.pi * (2 * number + 1) / (2 * sweep_count)))
        for number in range(sweep_count)
    ]


EM_WEIGHTS = chebyshev_weights(em_lower, em_upper, EM_SWEEPS)
HEAT_WEIGHTS = chebyshev_weights(heat_lower, heat_upper, HEAT_SWEEPS)


def on_first_core():
    return lax.rem(lax.axis_index("gz"), 2) == 0


def lanes(shape):
    return lax.broadcasted_iota(jnp.int32, shape, len(shape) - 1)


def rows(shape):
    return lax.broadcasted_iota(jnp.int32, shape, len(shape) - 2)


def roll(values, by, axis):
    size = values.shape[axis]
    by = by % size
    return values if by == 0 else pltpu.roll(values, by, axis)


def call(body, out_shapes, scratch=(), name=None, limit=8 << 20, **options):
    return pl.pallas_call(
        body,
        out_shape=[jax.ShapeDtypeStruct(s, F32) for s in out_shapes],
        scratch_shapes=[pltpu.VMEM(s, F32) if isinstance(s, tuple) else s for s in scratch],
        compiler_params=pltpu.CompilerParams(vmem_limit_bytes=limit),
        name=name,
        **options,
    )


def swap_store(first, fwd, bwd, at, up, down):
    fwd[at] = jnp.where(first, up, down)
    bwd[at] = jnp.where(first, down, up)


def y_tiles(v, first, fwd, bwd, at):
    row = rows((8, 128))
    low_half = row < 4
    tops = [a[8:16] for a in v]
    ends = [a[0:8] for a in v]
    for pair in range(4):
        a, b = 2 * pair, 2 * pair + 1
        up = jnp.where(low_half, roll(tops[b], 4, 0), tops[a])
        down = jnp.where(low_half, ends[a], roll(ends[b], 4, 0))
        if pair == 3:
            down = jnp.where(row == 5, roll(ends[0], 1, 0), down)
            down = jnp.where(row == 6, roll(ends[2], 2, 0), down)
        part = pl.ds(8 * pair, 8)
        fwd[at, part] = jnp.where(first, up, down)
        bwd[at, part] = jnp.where(first, down, up)


def pack_xy(*refs):
    far, (xf, xb, yf, yb), near, (scaled, arrived) = refs[:4], refs[4:8], refs[8:12], refs[12:]
    copies = [
        pltpu.make_async_copy(a, b, arrived.at[n]) for n, (a, b) in enumerate(zip(far, near))
    ]
    for copy in copies:
        copy.start()
    for copy in copies:
        copy.wait()
    field, source, sigma, warmth = near
    first = on_first_core()
    inverse = 1.0 / (4.0 + sigma[...])
    scaled[3] = inverse
    for c in range(3):
        scaled[c] = source[c] * inverse

    def layer(f, x):
        if f < 3:
            return field[f, x]
        return warmth[x] if f == 7 else scaled[f - 3, x]

    ups = [(f, x) for f, start, n in UP_LAYERS for x in range(start, start + n)]
    downs = [(f, x) for f, start, n in DOWN_LAYERS for x in range(start, start + n)]
    for at in range(X_LAYERS):
        up = layer(*ups[min(at, len(ups) - 1)])
        down = layer(*downs[min(at, len(downs) - 1)])
        swap_store(first, xf, xb, at, up, down)

    def step(x, carry):
        y_tiles([layer(f, x) for f in range(8)], first, yf, yb, x)
        return carry

    lax.fori_loop(0, 16, step, 0, unroll=4)


def scale(source, sigma, scaled):
    inverse = 1.0 / (4.0 + sigma[...])
    scaled[3] = inverse
    for c in range(3):
        scaled[c] = source[c] * inverse


class Slabs:
    def __init__(self, field, scaled, warmth, got_fwd, got_bwd):
        self.field, self.scaled, self.warmth = field, scaled, warmth
        self.got_fwd, self.got_bwd = got_fwd, got_bwd
        self.first = on_first_core()
        gx = lax.axis_index("gx")
        self.below, self.above = gx > 0, gx < lax.axis_size("gx") - 1

    def own(self, f, x):
        if f < 3:
            return self.field[f, x]
        return self.warmth[x] if f == 7 else self.scaled[f - 3, x]

    def beside(self, f, x):
        fwd, bwd = self.got_fwd, self.got_bwd
        if x < 0:
            at = UP_AT.get((f, x))
            if at is None:
                return None
            value = jnp.where(self.first, fwd[at], bwd[at])
            return jnp.where(self.below, value, 0.0)
        at = DOWN_AT.get((f, x))
        if at is None:
            return None
        value = jnp.where(self.first, bwd[at], fwd[at])
        return jnp.where(self.above, value, 0.0)

    def halo(self, emit):
        zero = jnp.zeros((16, 128), F32)
        for number, x in enumerate(HALO_X):
            values = [self.beside(f, x) for f in range(7)]
            emit(number, x + LOW, [zero if v is None else v for v in values] + [zero])

    def inner(self, emit):
        def step(x, carry):
            emit(x, x + LOW, [self.own(f, x) for f in range(8)])
            return carry

        lax.fori_loop(0, 16, step, 0, unroll=4)


def pack_corners(xf, xb, fwd, bwd):
    slabs = Slabs(None, None, None, xf, xb)
    slabs.halo(lambda number, at, v: y_tiles(v, slabs.first, fwd, bwd, number))


def y_halo(first, got, at, pair):
    gy = lax.axis_index("gy")
    part = pl.ds(8 * pair, 8)
    f, b = got[0][at, part], got[1][at, part]
    lower = jnp.where(gy > 0, jnp.where(first, f, b), 0.0)
    upper = jnp.where(gy < lax.axis_size("gy") - 1, jnp.where(first, b, f), 0.0)
    return lower, upper


HALO_X = tuple(range(-LOW, 0)) + tuple(range(16, 16 + HIGH))
X_ALL = LOW + 16 + HIGH
X_PAIRS = (X_ALL + 1) // 2


def pack_z(field, scaled, warmth, xf, xb, yf, yb, cf, cb, whole, up, down, packed):
    slabs = Slabs(field, scaled, warmth, xf, xb)
    first = slabs.first
    low_half = rows((8, 128)) < 4
    window = lanes((24, 128)) // 16

    def emit(got, number, at, v):
        acc = None
        for pair in range(4):
            lower, upper = y_halo(first, got, number, pair)
            last = []
            last.append(jnp.where(low_half, upper, lower))
            if pair < 3:
                last.append(roll(jnp.where(low_half, lower, upper), 4, 0))
            else:
                last.append(roll(upper, 3, 0))
            for f, tile in zip((2 * pair, 2 * pair + 1), last):
                slab = jnp.concatenate([v[f], tile], axis=0)
                if f < 7:
                    whole[f, at] = slab
                moved = roll(slab, 16 * f + 8, 1)
                acc = moved if acc is None else jnp.where(window == f, moved, acc)
        packed[at] = acc

    slabs.halo(functools.partial(emit, (cf, cb)))
    slabs.inner(functools.partial(emit, (yf, yb)))
    packed[X_ALL] = jnp.zeros((24, 128), F32)
    half = (lanes((24, 128)) // 8) % 2 == 0

    def pair_up(k, carry):
        a, b = packed[2 * k], packed[2 * k + 1]
        up[k] = jnp.where(half, a, roll(b, 8, 1))
        down[k] = jnp.where(half, roll(a, -8, 1), b)
        return carry

    lax.fori_loop(0, X_PAIRS, pair_up, 0, unroll=True)


def up_z(main, tail):
    last = lanes(main.shape) == 127
    a, b = roll(main, -1, 1), roll(tail, -1, 1)
    return jnp.where(last, b, a), jnp.where(last, a, b)


def down_z(main, tail):
    start = lanes(main.shape) == 0
    a, b = roll(main, 1, 1), roll(tail, 1, 1)
    return jnp.where(start, b, a), jnp.where(start, a, b)


def both(function, *pairs):
    return tuple(function(*parts) for parts in zip(*pairs))


def relax(
    whole, xf, xb, yf, yb, cf, cb, below_z, above_z, sigma, warmth, storage, position, nodes,
    out, send, partial, main, tail, other, far, heat, extra, sent,
):
    first = on_first_core()
    gx, gz = lax.axis_index("gx"), lax.axis_index("gz")
    lane = lanes((24, 128))
    row = rows((24, 128))
    half = (lane // 8) % 2 == 0
    edge = (lane < 8) | (lane >= 120)
    has_below, has_above = gz > 0, gz < lax.axis_size("gz") - 1

    def unpack_one(at, got, number, packed):
        for f in range(7):
            tail[f, at] = jnp.where(edge, roll(packed, -(16 * f + 8), 1), 0.0)
        tail[7, at] = roll(packed, 8, 1)
        _, upper = y_halo(first, got, number, 3)
        for n, place in enumerate((5, 6)):
            extra[n, at, 0:8] = jnp.broadcast_to(upper[place : place + 1], (8, 128))
            extra[n, at, 8:16] = jnp.broadcast_to(tail[7, at, 16 + n : 17 + n, :], (8, 128))

    def unpack(k, odd):
        lower = jnp.where(has_below, below_z[k], 0.0)
        upper = jnp.where(has_above, above_z[k], 0.0)
        if odd:
            return jnp.where(half, roll(lower, -8, 1), upper)
        return jnp.where(half, lower, roll(upper, 8, 1))

    for number, x in enumerate(HALO_X):
        at = x + LOW
        unpack_one(at, (cf, cb), number, unpack(at // 2, at % 2))

    def unpack_pair(k, carry):
        for odd in range(2):
            at = 2 * k + LOW + odd
            unpack_one(at, (yf, yb), 2 * k + odd, unpack(k + LOW // 2, odd))
        return carry

    lax.fori_loop(0, 8, unpack_pair, 0, unroll=4)

    def up_y(v):
        return roll(v, -1, 0)

    def down_y(v):
        return roll(v, 1, 0)

    buffers = [(whole, tail), (main, far), (other, tail), (main, far), (other, tail)]

    def load(number, f, at):
        return buffers[number][0][f, at], buffers[number][1][f, at]

    def up_y_edge(v, n, at):
        moved = both(up_y, v)
        edges = (extra[n, at, 0:8], extra[n, at, 8:16])
        return tuple(
            jnp.where(row == 19, jnp.concatenate([e, e, e], axis=0), m)
            for m, e in zip(moved, edges)
        )

    def curls(at, ahead, e, outer):
        ex, ey, ez = e
        ey_ahead, ez_ahead = ahead
        if outer:
            ex_up, ez_up = up_y_edge(ex, 0, at), up_y_edge(ez, 1, at)
        else:
            ex_up, ez_up = both(up_y, ex), both(up_y, ez)
        cx = both(lambda a, b, c, d: (a - b) - (c - d), ez_up, ez, up_z(*ey), ey)
        cy = both(lambda a, b, c, d: (a - b) - (c - d), up_z(*ex), ex, ez_ahead, ez)
        cz = both(lambda a, b, c, d: (a - b) - (c - d), ey_ahead, ey, ex_up, ex)
        return cx, cy, cz

    for number, weight in enumerate(EM_WEIGHTS):
        begin = 1 + number
        outer = number == 0

        def curls_at(at, number=number, outer=outer):
            e = [load(number, f, at) for f in range(3)]
            ahead = (load(number, 1, at + 1), load(number, 2, at + 1))
            return e, curls(at, ahead, e, outer)

        def step(at, carry, number=number, weight=weight, curls_at=curls_at):
            cy_before, cz_before = carry
            e, (cx, cy, cz) = curls_at(at)
            kx = both(
                lambda a, b, c, d: (a - b) - (c - d), cz, both(down_y, cz), cy, down_z(*cy)
            )
            ky = both(lambda a, b, c, d: (a - b) - (c - d), cx, down_z(*cx), cz, cz_before)
            kz = both(
                lambda a, b, c, d: (a - b) - (c - d), cy, cy_before, cx, both(down_y, cx)
            )
            g = (whole[6, at] * weight, tail[6, at] * weight)
            keep = both(lambda v: (1.0 - weight) + 4.0 * v, g)
            for f, k in enumerate((kx, ky, kz)):
                h = (whole[3 + f, at], tail[3 + f, at])
                new = both(
                    lambda p, v, s, w, d: p * v + weight * s - w * d, keep, e[f], h, g, k
                )
                buffers[number + 1][0][f, at], buffers[number + 1][1][f, at] = new
            return cy, cz

        _, (_, cy, cz) = curls_at(begin - 1)
        lax.fori_loop(begin, X_ALL - begin, step, (cy, cz), unroll=4)

    result = pltpu.make_async_copy(other.at[:, pl.ds(LOW, 16), pl.ds(0, 16), :], out, sent)
    result.start()

    def joule(x, carry):
        at = x + LOW
        ex, ey, ez = (both(lambda v: v * v, load(EM_SWEEPS, f, at)) for f in range(3))
        ey_ahead, ez_ahead = (both(lambda v: v * v, load(EM_SWEEPS, f, at + 1)) for f in (1, 2))
        a = both(lambda v: v + up_y(v), ex)
        c = both(lambda p, q, r: p + (q + r), a, ey, ey_ahead)
        c = c[0] + up_z(*c)[0]
        d = ez[0] + ez_ahead[0]
        s = c + (d + up_y(d))
        heat[x] = sigma[x] * (0.25 * s[0:16])
        return carry

    lax.fori_loop(0, 16, joule, 0, unroll=4)

    count = send.shape[0]
    spread = (rows((count, 256)) == position[...]).astype(jnp.bfloat16)
    left = heat[...].reshape(256, 128)
    total = nodes[...]
    for _ in range(3):
        piece = left.astype(jnp.bfloat16)
        left = left - piece.astype(F32)
        total = total + jnp.dot(spread, piece, preferred_element_type=F32)
    send[...] = total

    row16 = rows((16, 128))
    low_at, high_at = UP_AT[7, -1], DOWN_AT[7, 16]
    under = jnp.where(gx > 0, jnp.where(first, xf[low_at], xb[low_at]), 0.0)
    over = jnp.where(
        gx < lax.axis_size("gx") - 1, jnp.where(first, xb[high_at], xf[high_at]), 0.0
    )
    for x in range(16):
        t = warmth[x]
        ends = tail[7, x + LOW, 0:16, :]
        lower, upper = y_halo(first, (yf, yb), x, 3)
        total = (warmth[x - 1] if x else under) + (warmth[x + 1] if x < 15 else over)
        total = total + jnp.where(row16 == 0, lower[3:4], roll(t, 1, 0))
        total = total + jnp.where(row16 == 15, upper[4:5], roll(t, -1, 0))
        total = total + up_z(t, ends)[0] + down_z(t, ends)[0]
        partial[x] = t + HEAT_WEIGHTS[0] * (total - 6.0 * t) / (6.0 + storage[x])
    result.wait()


def place(owners, columns, position, nodes):
    groups = lax.axis_size("gy") * lax.axis_size("gz")
    owner, column = owners[...], columns[...]
    member = rows((groups, 256)) == owner
    earlier = (rows((256, 256)) < lanes((256, 256))).astype(jnp.bfloat16)
    before = jnp.dot(member.astype(jnp.bfloat16), earlier, preferred_element_type=F32)
    rank = jnp.sum(jnp.where(member, before, 0.0), axis=0, keepdims=True).astype(jnp.int32)
    position[...] = owner * (CAP + 1) + rank
    count = nodes.shape[0]
    spread = (rows((count, 256)) == owner * (CAP + 1) + CAP).astype(jnp.bfloat16)
    listed = jnp.where(rows((128, 256)) == rank, column + 1, 0).astype(F32).astype(jnp.bfloat16)
    nodes[...] = lax.dot_general(
        spread, listed, (((1,), (1,)), ((), ())), preferred_element_type=F32
    )


def warm(got, partial, warmth, storage, xf, xb, yf, yb, up, down, rest, heat, mid):
    first = on_first_core()
    groups = got.shape[0] // (CAP + 1)
    ids = got[pl.ds(CAP, groups, stride=CAP + 1), :]
    lane = lanes((groups, 256))
    total = None
    for r in range(CAP):
        hit = (ids[:, r : r + 1] == (lane + 1).astype(F32)).astype(jnp.bfloat16)
        left = got[pl.ds(r, groups, stride=CAP + 1), :]
        for _ in range(3):
            piece = left.astype(jnp.bfloat16)
            left = left - piece.astype(F32)
            term = lax.dot_general(
                hit, piece, (((0,), (0,)), ((), ())), preferred_element_type=F32
            )
            total = term if total is None else total + term
    heat[...] = total.reshape(16, 16, 128)
    lane = lanes((16, 128))
    row = rows((16, 128))
    for x in range(16):
        mid[x] = partial[x] + HEAT_WEIGHTS[0] * heat[x] / (6.0 + storage[x])
    xf[...] = jnp.where(first, mid[15], mid[0])
    xb[...] = jnp.where(first, mid[0], mid[15])
    ups = downs = jnp.zeros((16, 128), F32)
    for x in range(16):
        t = mid[x]
        top, end = t[15:16], t[0:1]
        yf[x : x + 1] = jnp.where(first, top, end)
        yb[x : x + 1] = jnp.where(first, end, top)
        ups = jnp.where(lane == 8 * x, roll(t, 8 * x + 1, 1), ups)
        downs = jnp.where(lane == 8 * x, roll(t, 8 * x, 1), downs)
        near = jnp.where(row == 0, 0.0, roll(t, 1, 0)) + jnp.where(row == 15, 0.0, roll(t, -1, 0))
        near = near + jnp.where(lane == 0, 0.0, roll(t, 1, 1))
        near = near + jnp.where(lane == 127, 0.0, roll(t, -1, 1))
        if x > 0:
            near = near + mid[x - 1]
        if x < 15:
            near = near + mid[x + 1]
        s = storage[x]
        push = s * warmth[x] + heat[x] - (6.0 + s) * t + near
        rest[x] = t + HEAT_WEIGHTS[1] * push / (6.0 + s)
    up[...] = ups
    down[...] = downs


def finish(rest, storage, xf, xb, yf, yb, from_below, from_above, out):
    first = on_first_core()
    gx, gy, gz = (lax.axis_index(a) for a in ("gx", "gy", "gz"))
    ends = [a > 0 for a in (gx, gy, gz)]
    tops = [a < lax.axis_size(n) - 1 for a, n in ((gx, "gx"), (gy, "gy"), (gz, "gz"))]
    f, b = xf[...], xb[...]
    x_low = jnp.where(ends[0], jnp.where(first, f, b), 0.0)
    x_high = jnp.where(tops[0], jnp.where(first, b, f), 0.0)
    f, b = yf[...], yb[...]
    y_low = jnp.where(ends[1], jnp.where(first, f, b), 0.0)
    y_high = jnp.where(tops[1], jnp.where(first, b, f), 0.0)
    z_low = jnp.where(ends[2], from_below[...], 0.0)
    z_high = jnp.where(tops[2], from_above[...], 0.0)
    lane = lanes((16, 128))
    row = rows((16, 128))
    for x in range(16):
        near = jnp.where(row == 0, y_low[x : x + 1], 0.0)
        near = near + jnp.where(row == 15, y_high[x : x + 1], 0.0)
        near = near + jnp.where(lane == 0, roll(z_low, -8 * x, 1), 0.0)
        near = near + jnp.where(lane == 127, roll(z_high, 127 - 8 * x, 1), 0.0)
        if x == 0:
            near = near + x_low
        if x == 15:
            near = near + x_high
        out[x] = rest[x] + HEAT_WEIGHTS[1] * near / (6.0 + storage[x])


def around(axis):
    n, m = lax.axis_size(axis), lax.axis_size("gz")

    def target(a, c):
        to = a + (1 if c % 2 == 0 else -1)
        return (to, c) if 0 <= to < n else (a, c ^ 1)

    forward = []
    for a in range(n):
        for c in range(m):
            to = target(a, c)
            forward.append((a * m + c, to[0] * m + to[1]))
    return forward, [(j, i) for i, j in forward]


def exchange(axis, fwd, bwd):
    forward, backward = around(axis)
    names = (axis, "gz")
    return lax.ppermute(fwd, names, forward), lax.ppermute(bwd, names, backward)


def exchange_z(up, down):
    m = lax.axis_size("gz")
    ring = [(i, (i + 1) % m) for i in range(m)]
    return lax.ppermute(up, "gz", ring), lax.ppermute(down, "gz", [(j, i) for i, j in ring])


def local(field, source, sigma, warmth, storage, partition, column):
    groups = lax.axis_size("gy") * lax.axis_size("gz")
    count = groups * (CAP + 1)
    cube = (16, 16, 128)
    face = (16, 128)
    x_message, y_message, corners = (X_LAYERS, 16, 128), (16, 32, 128), (len(HALO_X), 32, 128)
    xf, xb, yf, yb = call(
        pack_xy,
        [x_message, x_message, y_message, y_message],
        [(3, *cube), (3, *cube), cube, cube, (4, *cube), pltpu.SemaphoreType.DMA((4,))],
        name="pack_xy",
        limit=FIRST_LIMIT,
        in_specs=[pl.BlockSpec(memory_space=pltpu.HBM)] * 4,
    )(field, source, sigma, warmth)
    xf, xb = exchange("gx", xf, xb)
    yf, yb = exchange("gy", yf, yb)
    (scaled,) = call(scale, [(4, *cube)], name="scale")(source, sigma)
    position, nodes = pl.pallas_call(
        place,
        out_shape=[
            jax.ShapeDtypeStruct((1, 256), jnp.int32),
            jax.ShapeDtypeStruct((count, 128), F32),
        ],
        compiler_params=pltpu.CompilerParams(vmem_limit_bytes=8 << 20),
        name="place",
    )(partition.reshape(1, 256), column.reshape(1, 256))
    cf, cb = call(pack_corners, [corners, corners], name="pack_corners")(xf, xb)
    cf, cb = exchange("gy", cf, cb)
    whole, up, down = call(
        pack_z,
        [(7, X_ALL, 24, 128), (X_PAIRS, 24, 128), (X_PAIRS, 24, 128)],
        [(X_ALL + 1, 24, 128)],
        name="pack_z",
    )(field, scaled, warmth, xf, xb, yf, yb, cf, cb)
    below_z, above_z = exchange_z(up, down)
    out, send, partial = call(
        relax,
        [(3, *cube), (count, 128), cube],
        [
            (3, X_ALL, 24, 128),
            (8, X_ALL, 24, 128),
            (3, X_ALL, 24, 128),
            (3, X_ALL, 24, 128),
            cube,
            (2, X_ALL, 16, 128),
            pltpu.SemaphoreType.DMA,
        ],
        name="relax",
        limit=16 << 20,
        out_specs=[pl.BlockSpec(memory_space=pltpu.HBM)] + [pl.BlockSpec(memory_space=pltpu.VMEM)] * 2,
    )(whole, xf, xb, yf, yb, cf, cb, below_z, above_z, sigma, warmth, storage, position, nodes)
    got = lax.all_to_all(
        send.reshape(count, 1, 128), ("gy", "gz"), split_axis=0, concat_axis=0, tiled=True
    ).reshape(count, 128)
    xf, xb, yf, yb, up, down, rest = call(
        warm, [face, face, face, face, face, face, cube], [cube, cube], name="warm"
    )(got, partial, warmth, storage)
    xf, xb = exchange("gx", xf, xb)
    yf, yb = exchange("gy", yf, yb)
    below_z, above_z = exchange_z(up, down)
    (updated,) = call(finish, [cube], name="finish")(
        rest, storage, xf, xb, yf, yb, below_z, above_z
    )
    return out, updated


def solution(mesh):
    in_specs = (
        P(None, "gx", "gy", "gz"),
        P(None, "gx", "gy", "gz"),
        P("gx", "gy", "gz"),
        P("gx", "gy", "gz"),
        P("gx", "gy", "gz"),
        P("gx", "gy", "gz", None, None),
        P("gx", "gy", "gz", None),
    )
    out_specs = (P(None, "gx", "gy", "gz"), P("gx", "gy", "gz"))
    return jax.shard_map(local, mesh=mesh, in_specs=in_specs, out_specs=out_specs, check_vma=False)
```

```python
import functools
import math

import jax
import jax.numpy as jnp
from jax import lax
from jax.experimental import pallas as pl
from jax.experimental.pallas import tpu as pltpu
from jax.sharding import PartitionSpec as P

EM_SWEEPS = 4
HEAT_SWEEPS = 2
CAP = 8
LOW, HIGH = 4, 5
F32 = jnp.float32
FIRST_LIMIT = 62 << 20

em_lower = 0.02
em_upper = 3.0
heat_lower = 0.07
heat_upper = 2.0

UP_LAYERS = ((0, 12, 4), (1, 12, 4), (2, 12, 4), (3, 13, 3), (4, 13, 3), (5, 13, 3), (6, 13, 3), (7, 15, 1))
DOWN_LAYERS = ((0, 0, 4), (1, 0, 5), (2, 0, 5), (3, 0, 3), (4, 0, 4), (5, 0, 4), (6, 0, 4), (7, 0, 1))


def spots(layers, shift):
    where, at = {}, 0
    for field, first, count in layers:
        for x in range(first, first + count):
            where[field, x + shift] = at
            at += 1
    return where, at


UP_AT, UP_COUNT = spots(UP_LAYERS, -16)
DOWN_AT, DOWN_COUNT = spots(DOWN_LAYERS, 16)
X_LAYERS = max(UP_COUNT, DOWN_COUNT)


def chebyshev_weights(lower_end, upper_end, sweep_count):
    middle = 0.5 * (upper_end + lower_end)
    radius = 0.5 * (upper_end - lower_end)
    return [
        1.0 / (middle + radius * math.cos(math.pi * (2 * number + 1) / (2 * sweep_count)))
        for number in range(sweep_count)
    ]


EM_WEIGHTS = chebyshev_weights(em_lower, em_upper, EM_SWEEPS)
HEAT_WEIGHTS = chebyshev_weights(heat_lower, heat_upper, HEAT_SWEEPS)


def on_first_core():
    return lax.rem(lax.axis_index("gz"), 2) == 0


def lanes(shape):
    return lax.broadcasted_iota(jnp.int32, shape, len(shape) - 1)


def rows(shape):
    return lax.broadcasted_iota(jnp.int32, shape, len(shape) - 2)


def roll(values, by, axis):
    size = values.shape[axis]
    by = by % size
    return values if by == 0 else pltpu.roll(values, by, axis)


def call(body, out_shapes, scratch=(), name=None, limit=8 << 20, **options):
    return pl.pallas_call(
        body,
        out_shape=[jax.ShapeDtypeStruct(s, F32) for s in out_shapes],
        scratch_shapes=[pltpu.VMEM(s, F32) if isinstance(s, tuple) else s for s in scratch],
        compiler_params=pltpu.CompilerParams(vmem_limit_bytes=limit),
        name=name,
        **options,
    )


def swap_store(first, fwd, bwd, at, up, down):
    fwd[at] = jnp.where(first, up, down)
    bwd[at] = jnp.where(first, down, up)


def y_tiles(v, first, fwd, bwd, at):
    row = rows((8, 128))
    low_half = row < 4
    tops = [a[8:16] for a in v]
    ends = [a[0:8] for a in v]
    for pair in range(4):
        a, b = 2 * pair, 2 * pair + 1
        up = jnp.where(low_half, roll(tops[b], 4, 0), tops[a])
        down = jnp.where(low_half, ends[a], roll(ends[b], 4, 0))
        if pair == 3:
            down = jnp.where(row == 5, roll(ends[0], 1, 0), down)
            down = jnp.where(row == 6, roll(ends[2], 2, 0), down)
        part = pl.ds(8 * pair, 8)
        fwd[at, part] = jnp.where(first, up, down)
        bwd[at, part] = jnp.where(first, down, up)


def pack_xy(*refs):
    far, (xf, xb, yf, yb), near, (scaled, arrived) = refs[:4], refs[4:8], refs[8:12], refs[12:]
    copies = [
        pltpu.make_async_copy(a, b, arrived.at[n]) for n, (a, b) in enumerate(zip(far, near))
    ]
    for copy in copies:
        copy.start()
    for copy in copies:
        copy.wait()
    field, source, sigma, warmth = near
    first = on_first_core()
    inverse = 1.0 / (4.0 + sigma[...])
    scaled[3] = inverse
    for c in range(3):
        scaled[c] = source[c] * inverse

    def layer(f, x):
        if f < 3:
            return field[f, x]
        return warmth[x] if f == 7 else scaled[f - 3, x]

    ups = [(f, x) for f, start, n in UP_LAYERS for x in range(start, start + n)]
    downs = [(f, x) for f, start, n in DOWN_LAYERS for x in range(start, start + n)]
    for at in range(X_LAYERS):
        up = layer(*ups[min(at, len(ups) - 1)])
        down = layer(*downs[min(at, len(downs) - 1)])
        swap_store(first, xf, xb, at, up, down)

    def step(x, carry):
        y_tiles([layer(f, x) for f in range(8)], first, yf, yb, x)
        return carry

    lax.fori_loop(0, 16, step, 0, unroll=4)


def scale(source, sigma, scaled):
    inverse = 1.0 / (4.0 + sigma[...])
    scaled[3] = inverse
    for c in range(3):
        scaled[c] = source[c] * inverse


class Slabs:
    def __init__(self, field, scaled, warmth, got_fwd, got_bwd):
        self.field, self.scaled, self.warmth = field, scaled, warmth
        self.got_fwd, self.got_bwd = got_fwd, got_bwd
        self.first = on_first_core()
        gx = lax.axis_index("gx")
        self.below, self.above = gx > 0, gx < lax.axis_size("gx") - 1

    def own(self, f, x):
        if f < 3:
            return self.field[f, x]
        return self.warmth[x] if f == 7 else self.scaled[f - 3, x]

    def beside(self, f, x):
        fwd, bwd = self.got_fwd, self.got_bwd
        if x < 0:
            at = UP_AT.get((f, x))
            if at is None:
                return None
            value = jnp.where(self.first, fwd[at], bwd[at])
            return jnp.where(self.below, value, 0.0)
        at = DOWN_AT.get((f, x))
        if at is None:
            return None
        value = jnp.where(self.first, bwd[at], fwd[at])
        return jnp.where(self.above, value, 0.0)

    def halo(self, emit):
        zero = jnp.zeros((16, 128), F32)
        for number, x in enumerate(HALO_X):
            values = [self.beside(f, x) for f in range(7)]
            emit(number, x + LOW, [zero if v is None else v for v in values] + [zero])

    def inner(self, emit):
        def step(x, carry):
            emit(x, x + LOW, [self.own(f, x) for f in range(8)])
            return carry

        lax.fori_loop(0, 16, step, 0, unroll=4)


def pack_corners(xf, xb, fwd, bwd):
    slabs = Slabs(None, None, None, xf, xb)
    slabs.halo(lambda number, at, v: y_tiles(v, slabs.first, fwd, bwd, number))


def y_halo(first, got, at, pair):
    gy = lax.axis_index("gy")
    part = pl.ds(8 * pair, 8)
    f, b = got[0][at, part], got[1][at, part]
    lower = jnp.where(gy > 0, jnp.where(first, f, b), 0.0)
    upper = jnp.where(gy < lax.axis_size("gy") - 1, jnp.where(first, b, f), 0.0)
    return lower, upper


HALO_X = tuple(range(-LOW, 0)) + tuple(range(16, 16 + HIGH))
X_ALL = LOW + 16 + HIGH
GROUP_ALL = LOW + 4 + HIGH
SWEEP_UNROLL = 4
X_PAIRS = (X_ALL + 1) // 2


def pack_z(field, scaled, warmth, xf, xb, yf, yb, cf, cb, position, whole, packed, up, down):
    del position
    slabs = Slabs(field, scaled, warmth, xf, xb)
    first = slabs.first
    low_half = rows((8, 128)) < 4
    window = lanes((24, 128)) // 16

    def emit(got, number, at, v):
        acc = None
        for pair in range(4):
            lower, upper = y_halo(first, got, number, pair)
            last = []
            last.append(jnp.where(low_half, upper, lower))
            if pair < 3:
                last.append(roll(jnp.where(low_half, lower, upper), 4, 0))
            else:
                last.append(roll(upper, 3, 0))
            for f, tile in zip((2 * pair, 2 * pair + 1), last):
                slab = jnp.concatenate([v[f], tile], axis=0)
                whole[f, at] = slab
                moved = roll(slab, 16 * f + 8, 1)
                acc = moved if acc is None else jnp.where(window == f, moved, acc)
        packed[at] = acc

    slabs.halo(functools.partial(emit, (cf, cb)))
    slabs.inner(functools.partial(emit, (yf, yb)))
    packed[X_ALL] = jnp.zeros((24, 128), F32)
    half = (lanes((24, 128)) // 8) % 2 == 0

    def pair_up(k, carry):
        a, b = packed[2 * k], packed[2 * k + 1]
        up[k] = jnp.where(half, a, roll(b, 8, 1))
        down[k] = jnp.where(half, roll(a, -8, 1), b)
        return carry

    lax.fori_loop(0, X_PAIRS, pair_up, 0, unroll=True)


def up_y(v):
    return roll(v, -1, 0)


def down_y(v):
    return roll(v, 1, 0)


def up_z(v):
    return roll(v, -1, 1)


def down_z(v):
    return roll(v, 1, 1)


def twist(a, b, c, d):
    return (a - b) - (c - d)


def relax(fields, first, second, layers):
    row = rows((24, 128))
    buffers = (fields, first, second, first, second)

    def curls(source, at, outer):
        ex, ey, ez = (source[f, at] for f in range(3))
        ex_up, ez_up = up_y(ex), up_y(ez)
        if outer:
            ex_up = jnp.where(row == 19, fields[7, at, 16:17, :], ex_up)
            ez_up = jnp.where(row == 19, fields[7, at, 17:18, :], ez_up)
        cx = twist(ez_up, ez, up_z(ey), ey)
        cy = twist(up_z(ex), ex, source[2, at + 1], ez)
        cz = twist(source[1, at + 1], ey, ex_up, ex)
        return (ex, ey, ez), (cx, cy, cz)

    for number, weight in enumerate(EM_WEIGHTS):
        source, target, outer = buffers[number], buffers[number + 1], number == 0

        def step(at, carry, source=source, target=target, outer=outer, weight=weight):
            cy_before, cz_before = carry
            e, (cx, cy, cz) = curls(source, at, outer)
            kx = twist(cz, down_y(cz), cy, down_z(cy))
            ky = twist(cx, down_z(cx), cz, cz_before)
            kz = twist(cy, cy_before, cx, down_y(cx))
            g = fields[6, at] * weight
            keep = (1.0 - weight) + 4.0 * g
            for f, k in enumerate((kx, ky, kz)):
                target[f, at] = keep * e[f] + weight * fields[3 + f, at] - g * k
            return cy, cz

        begin = 1 + number
        _, (_, cy, cz) = curls(source, begin - 1, outer)
        lax.fori_loop(begin, layers - begin, step, (cy, cz), unroll=SWEEP_UNROLL)


def squares(field, at):
    ex, ey, ez = (field[f, at] * field[f, at] for f in range(3))
    ey_ahead, ez_ahead = (field[f, at + 1] * field[f, at + 1] for f in (1, 2))
    upright = ez + ez_ahead
    return (ex + up_y(ex)) + (ey + ey_ahead), upright + up_y(upright)


def bulk(whole, final, flat, upright, spare):
    relax(whole, spare, final, X_ALL)

    def step(x, carry):
        c, d = squares(final, x + LOW)
        flat[x], upright[x] = c[0:16], d[0:16]
        return carry

    lax.fori_loop(0, 16, step, 0, unroll=4)


def near_z(edge, group, inner):
    lane = lanes(inner.shape)
    high = roll(edge, 120 - 32 * group, 1)
    low = roll(edge, -(32 * group + 24), 1)
    return jnp.where(lane < 4, low, jnp.where(lane >= 124, high, inner)), high


def edge(
    packed, below_z, above_z, flat, upright, xf, xb, yf, yb, sigma, warmth, storage, position, nodes,
    final, send, partial, beside, faces, fields, spare, heat,
):
    first = on_first_core()
    gx, gz = lax.axis_index("gx"), lax.axis_index("gz")
    lane = lanes((24, 128))
    half = (lane // 8) % 2 == 0
    window = lane // 16
    has_below, has_above = gz > 0, gz < lax.axis_size("gz") - 1

    def unpack(k, odd):
        lower = jnp.where(has_below, below_z[k], 0.0)
        upper = jnp.where(has_above, above_z[k], 0.0)
        at = 2 * k + odd
        if odd:
            came = jnp.where(half, roll(lower, -8, 1), upper)
        else:
            came = jnp.where(half, lower, roll(upper, 8, 1))
        beside[at] = came
        faces[0, at] = jnp.where(half, packed[at], came)
        faces[1, at] = jnp.where(half, came, packed[at])

    def unpack_pair(k, carry):
        unpack(k, 0)
        unpack(k, 1)
        return carry

    lax.fori_loop(0, X_ALL // 2, unpack_pair, 0, unroll=4)
    unpack(X_ALL // 2, 0)

    def regroup(i, carry):
        v = [faces[j % 2, i + 4 * (j // 2)] for j in range(8)]
        for d in (1, 2, 4):
            plain = (window // d) % 2 == 0
            for a in range(8):
                if a & d == 0:
                    p, q = v[a], v[a + d]
                    v[a] = jnp.where(plain, p, roll(q, 16 * d, 1))
                    v[a + d] = jnp.where(plain, roll(p, -16 * d, 1), q)
        for f in range(8):
            fields[f, i] = v[f]
        return carry

    lax.fori_loop(0, GROUP_ALL, regroup, 0, unroll=2)
    relax(fields, spare, final, GROUP_ALL)
    lane = lanes((16, 128))
    for i in range(4):
        c, d = squares(final, i + LOW)
        c, d = c[0:16], d[0:16]
        for group in range(4):
            x = 4 * group + i
            c_all, c_high = near_z(c, group, flat[x])
            d_all, _ = near_z(d, group, upright[x])
            c_up = jnp.where(lane == 127, roll(c_high, -1, 1), roll(c_all, -1, 1))
            heat[x] = sigma[x] * (0.25 * ((c_all + c_up) + d_all))

    count = send.shape[0]
    spread = (rows((count, 256)) == position[...]).astype(jnp.bfloat16)
    left = heat[...].reshape(256, 128)
    total = nodes[...]
    for _ in range(3):
        piece = left.astype(jnp.bfloat16)
        left = left - piece.astype(F32)
        total = total + jnp.dot(spread, piece, preferred_element_type=F32)
    send[...] = total

    row = rows((16, 128))
    low_at, high_at = UP_AT[7, -1], DOWN_AT[7, 16]
    under = jnp.where(gx > 0, jnp.where(first, xf[low_at], xb[low_at]), 0.0)
    over = jnp.where(
        gx < lax.axis_size("gx") - 1, jnp.where(first, xb[high_at], xf[high_at]), 0.0
    )
    for x in range(16):
        t = warmth[x]
        ends = roll(beside[x + LOW, 0:16, :], 8, 1)
        lower, upper = y_halo(first, (yf, yb), x, 3)
        total = (warmth[x - 1] if x else under) + (warmth[x + 1] if x < 15 else over)
        total = total + jnp.where(row == 0, lower[3:4], down_y(t))
        total = total + jnp.where(row == 15, upper[4:5], up_y(t))
        total = total + jnp.where(lane == 0, down_z(ends), down_z(t))
        total = total + jnp.where(lane == 127, up_z(ends), up_z(t))
        partial[x] = t + HEAT_WEIGHTS[0] * (total - 6.0 * t) / (6.0 + storage[x])


def merge(final, near, out):
    for f in range(3):
        for i in range(4):
            windows = near[f, i + LOW, 0:16, :]
            for group in range(4):
                x = 4 * group + i
                out[f, x], _ = near_z(windows, group, final[f, x + LOW, 0:16, :])


def place(owners, columns, position, nodes):
    groups = lax.axis_size("gy") * lax.axis_size("gz")
    owner, column = owners[...], columns[...]
    member = rows((groups, 256)) == owner
    earlier = (rows((256, 256)) < lanes((256, 256))).astype(jnp.bfloat16)
    before = jnp.dot(member.astype(jnp.bfloat16), earlier, preferred_element_type=F32)
    rank = jnp.sum(jnp.where(member, before, 0.0), axis=0, keepdims=True).astype(jnp.int32)
    position[...] = owner * (CAP + 1) + rank
    count = nodes.shape[0]
    spread = (rows((count, 256)) == owner * (CAP + 1) + CAP).astype(jnp.bfloat16)
    listed = jnp.where(rows((128, 256)) == rank, column + 1, 0).astype(F32).astype(jnp.bfloat16)
    nodes[...] = lax.dot_general(
        spread, listed, (((1,), (1,)), ((), ())), preferred_element_type=F32
    )


def warm(got, partial, warmth, storage, xf, xb, yf, yb, up, down, rest, heat, mid):
    first = on_first_core()
    groups = got.shape[0] // (CAP + 1)
    ids = got[pl.ds(CAP, groups, stride=CAP + 1), :]
    lane = lanes((groups, 256))
    total = None
    for r in range(CAP):
        hit = (ids[:, r : r + 1] == (lane + 1).astype(F32)).astype(jnp.bfloat16)
        left = got[pl.ds(r, groups, stride=CAP + 1), :]
        for _ in range(3):
            piece = left.astype(jnp.bfloat16)
            left = left - piece.astype(F32)
            term = lax.dot_general(
                hit, piece, (((0,), (0,)), ((), ())), preferred_element_type=F32
            )
            total = term if total is None else total + term
    heat[...] = total.reshape(16, 16, 128)
    lane = lanes((16, 128))
    row = rows((16, 128))
    for x in range(16):
        mid[x] = partial[x] + HEAT_WEIGHTS[0] * heat[x] / (6.0 + storage[x])
    xf[...] = jnp.where(first, mid[15], mid[0])
    xb[...] = jnp.where(first, mid[0], mid[15])
    ups = downs = jnp.zeros((16, 128), F32)
    for x in range(16):
        t = mid[x]
        top, end = t[15:16], t[0:1]
        yf[x : x + 1] = jnp.where(first, top, end)
        yb[x : x + 1] = jnp.where(first, end, top)
        ups = jnp.where(lane == 8 * x, roll(t, 8 * x + 1, 1), ups)
        downs = jnp.where(lane == 8 * x, roll(t, 8 * x, 1), downs)
        near = jnp.where(row == 0, 0.0, roll(t, 1, 0)) + jnp.where(row == 15, 0.0, roll(t, -1, 0))
        near = near + jnp.where(lane == 0, 0.0, roll(t, 1, 1))
        near = near + jnp.where(lane == 127, 0.0, roll(t, -1, 1))
        if x > 0:
            near = near + mid[x - 1]
        if x < 15:
            near = near + mid[x + 1]
        s = storage[x]
        push = s * warmth[x] + heat[x] - (6.0 + s) * t + near
        rest[x] = t + HEAT_WEIGHTS[1] * push / (6.0 + s)
    up[...] = ups
    down[...] = downs


def finish(rest, storage, xf, xb, yf, yb, from_below, from_above, out):
    first = on_first_core()
    gx, gy, gz = (lax.axis_index(a) for a in ("gx", "gy", "gz"))
    ends = [a > 0 for a in (gx, gy, gz)]
    tops = [a < lax.axis_size(n) - 1 for a, n in ((gx, "gx"), (gy, "gy"), (gz, "gz"))]
    f, b = xf[...], xb[...]
    x_low = jnp.where(ends[0], jnp.where(first, f, b), 0.0)
    x_high = jnp.where(tops[0], jnp.where(first, b, f), 0.0)
    f, b = yf[...], yb[...]
    y_low = jnp.where(ends[1], jnp.where(first, f, b), 0.0)
    y_high = jnp.where(tops[1], jnp.where(first, b, f), 0.0)
    z_low = jnp.where(ends[2], from_below[...], 0.0)
    z_high = jnp.where(tops[2], from_above[...], 0.0)
    lane = lanes((16, 128))
    row = rows((16, 128))
    for x in range(16):
        near = jnp.where(row == 0, y_low[x : x + 1], 0.0)
        near = near + jnp.where(row == 15, y_high[x : x + 1], 0.0)
        near = near + jnp.where(lane == 0, roll(z_low, -8 * x, 1), 0.0)
        near = near + jnp.where(lane == 127, roll(z_high, 127 - 8 * x, 1), 0.0)
        if x == 0:
            near = near + x_low
        if x == 15:
            near = near + x_high
        out[x] = rest[x] + HEAT_WEIGHTS[1] * near / (6.0 + storage[x])


def around(axis):
    n, m = lax.axis_size(axis), lax.axis_size("gz")

    def target(a, c):
        to = a + (1 if c % 2 == 0 else -1)
        return (to, c) if 0 <= to < n else (a, c ^ 1)

    forward = []
    for a in range(n):
        for c in range(m):
            to = target(a, c)
            forward.append((a * m + c, to[0] * m + to[1]))
    return forward, [(j, i) for i, j in forward]


def exchange(axis, fwd, bwd):
    forward, backward = around(axis)
    names = (axis, "gz")
    return lax.ppermute(fwd, names, forward), lax.ppermute(bwd, names, backward)


def exchange_z(up, down):
    m = lax.axis_size("gz")
    ring = [(i, (i + 1) % m) for i in range(m)]
    return lax.ppermute(up, "gz", ring), lax.ppermute(down, "gz", [(j, i) for i, j in ring])


def local(field, source, sigma, warmth, storage, partition, column):
    groups = lax.axis_size("gy") * lax.axis_size("gz")
    count = groups * (CAP + 1)
    cube = (16, 16, 128)
    face = (16, 128)
    x_message, y_message, corners = (X_LAYERS, 16, 128), (16, 32, 128), (len(HALO_X), 32, 128)
    xf, xb, yf, yb = call(
        pack_xy,
        [x_message, x_message, y_message, y_message],
        [(3, *cube), (3, *cube), cube, cube, (4, *cube), pltpu.SemaphoreType.DMA((4,))],
        name="pack_xy",
        limit=FIRST_LIMIT,
        in_specs=[pl.BlockSpec(memory_space=pltpu.HBM)] * 4,
    )(field, source, sigma, warmth)
    xf, xb = exchange("gx", xf, xb)
    yf, yb = exchange("gy", yf, yb)
    (scaled,) = call(scale, [(4, *cube)], name="scale")(source, sigma)
    position, nodes = pl.pallas_call(
        place,
        out_shape=[
            jax.ShapeDtypeStruct((1, 256), jnp.int32),
            jax.ShapeDtypeStruct((count, 128), F32),
        ],
        compiler_params=pltpu.CompilerParams(vmem_limit_bytes=8 << 20),
        name="place",
    )(partition.reshape(1, 256), column.reshape(1, 256))
    cf, cb = call(pack_corners, [corners, corners], name="pack_corners")(xf, xb)
    cf, cb = exchange("gy", cf, cb)
    layer = (24, 128)
    whole, packed, up, down = call(
        pack_z,
        [(8, X_ALL, *layer), (X_ALL + 1, *layer), (X_PAIRS, *layer), (X_PAIRS, *layer)],
        name="pack_z",
    )(field, scaled, warmth, xf, xb, yf, yb, cf, cb, position)
    below_z, above_z = exchange_z(up, down)
    final, flat, upright = call(
        bulk,
        [(3, X_ALL, *layer), cube, cube],
        [(3, X_ALL, *layer)],
        name="bulk",
        cost_estimate=pl.CostEstimate(flops=10**9, bytes_accessed=10**7, transcendentals=0),
    )(whole)
    near, send, partial = call(
        edge,
        [(3, GROUP_ALL, *layer), (count, 128), cube],
        [
            (X_ALL, *layer),
            (2, X_ALL, *layer),
            (8, GROUP_ALL, *layer),
            (3, GROUP_ALL, *layer),
            cube,
        ],
        name="edge",
    )(
        packed, below_z, above_z, flat, upright, xf, xb, yf, yb, sigma, warmth, storage,
        position, nodes,
    )
    got = lax.all_to_all(
        send.reshape(count, 1, 128), ("gy", "gz"), split_axis=0, concat_axis=0, tiled=True
    ).reshape(count, 128)
    xf, xb, yf, yb, up, down, rest = call(
        warm, [face, face, face, face, face, face, cube], [cube, cube], name="warm"
    )(got, partial, warmth, storage)
    xf, xb = exchange("gx", xf, xb)
    yf, yb = exchange("gy", yf, yb)
    below_z, above_z = exchange_z(up, down)
    (updated,) = call(finish, [cube], name="finish")(
        rest, storage, xf, xb, yf, yb, below_z, above_z
    )
    (out,) = call(
        merge,
        [(3, *cube)],
        name="merge",
        cost_estimate=pl.CostEstimate(flops=10**9, bytes_accessed=10**6, transcendentals=0),
    )(final, near)
    return out, updated


def solution(mesh):
    in_specs = (
        P(None, "gx", "gy", "gz"),
        P(None, "gx", "gy", "gz"),
        P("gx", "gy", "gz"),
        P("gx", "gy", "gz"),
        P("gx", "gy", "gz"),
        P("gx", "gy", "gz", None, None),
        P("gx", "gy", "gz", None),
    )
    out_specs = (P(None, "gx", "gy", "gz"), P("gx", "gy", "gz"))
    return jax.shard_map(local, mesh=mesh, in_specs=in_specs, out_specs=out_specs, check_vma=False)
```

```python
import functools
import math

import jax
import jax.numpy as jnp
from jax import lax
from jax.experimental import pallas as pl
from jax.experimental.pallas import tpu as pltpu
from jax.sharding import PartitionSpec as P

EM_SWEEPS = 4
HEAT_SWEEPS = 2
CAP = 8
LOW, HIGH = 4, 5
F32 = jnp.float32

em_lower = 0.02
em_upper = 3.0
heat_lower = 0.07
heat_upper = 2.0

UP_LAYERS = ((0, 12, 4), (1, 12, 4), (2, 12, 4), (3, 13, 3), (4, 13, 3), (5, 13, 3), (6, 13, 3), (7, 15, 1))
DOWN_LAYERS = ((0, 0, 4), (1, 0, 5), (2, 0, 5), (3, 0, 3), (4, 0, 4), (5, 0, 4), (6, 0, 4), (7, 0, 1))


def spots(layers, shift):
    where, at = {}, 0
    for field, first, count in layers:
        for x in range(first, first + count):
            where[field, x + shift] = at
            at += 1
    return where, at


UP_AT, UP_COUNT = spots(UP_LAYERS, -16)
DOWN_AT, DOWN_COUNT = spots(DOWN_LAYERS, 16)
X_LAYERS = max(UP_COUNT, DOWN_COUNT)


def chebyshev_weights(lower_end, upper_end, sweep_count):
    middle = 0.5 * (upper_end + lower_end)
    radius = 0.5 * (upper_end - lower_end)
    return [
        1.0 / (middle + radius * math.cos(math.pi * (2 * number + 1) / (2 * sweep_count)))
        for number in range(sweep_count)
    ]


EM_WEIGHTS = chebyshev_weights(em_lower, em_upper, EM_SWEEPS)
HEAT_WEIGHTS = chebyshev_weights(heat_lower, heat_upper, HEAT_SWEEPS)


def on_first_core():
    return lax.rem(lax.axis_index("gz"), 2) == 0


def lanes(shape):
    return lax.broadcasted_iota(jnp.int32, shape, len(shape) - 1)


def rows(shape):
    return lax.broadcasted_iota(jnp.int32, shape, len(shape) - 2)


def roll(values, by, axis):
    size = values.shape[axis]
    by = by % size
    return values if by == 0 else pltpu.roll(values, by, axis)


def call(body, out_shapes, scratch=(), name=None, limit=8 << 20, near=False, **options):
    return pl.pallas_call(
        body,
        out_shape=[
            pltpu.VMEM(s, F32) if near else jax.ShapeDtypeStruct(s, F32) for s in out_shapes
        ],
        scratch_shapes=[pltpu.VMEM(s, F32) if isinstance(s, tuple) else s for s in scratch],
        compiler_params=pltpu.CompilerParams(vmem_limit_bytes=limit),
        name=name,
        **options,
    )


def swap_store(first, fwd, bwd, at, up, down):
    fwd[at] = jnp.where(first, up, down)
    bwd[at] = jnp.where(first, down, up)


def y_tiles(v, first, fwd, bwd, at):
    row = rows((8, 128))
    low_half = row < 4
    tops = [a[8:16] for a in v]
    ends = [a[0:8] for a in v]
    for pair in range(4):
        a, b = 2 * pair, 2 * pair + 1
        up = jnp.where(low_half, roll(tops[b], 4, 0), tops[a])
        down = jnp.where(low_half, ends[a], roll(ends[b], 4, 0))
        if pair == 3:
            down = jnp.where(row == 5, roll(ends[0], 1, 0), down)
            down = jnp.where(row == 6, roll(ends[2], 2, 0), down)
        part = pl.ds(8 * pair, 8)
        fwd[at, part] = jnp.where(first, up, down)
        bwd[at, part] = jnp.where(first, down, up)


def pack_xy(*refs):
    far, (xf, xb, yf, yb, scaled), near, arrived = refs[:4], refs[4:9], refs[9:13], refs[13]
    copies = [
        pltpu.make_async_copy(a, b, arrived.at[n]) for n, (a, b) in enumerate(zip(far, near))
    ]
    for copy in copies:
        copy.start()
    for copy in copies:
        copy.wait()
    field, source, sigma, warmth = near
    first = on_first_core()
    inverse = 1.0 / (4.0 + sigma[...])
    scaled[3] = inverse
    for c in range(3):
        scaled[c] = source[c] * inverse

    def layer(f, x):
        if f < 3:
            return field[f, x]
        return warmth[x] if f == 7 else scaled[f - 3, x]

    ups = [(f, x) for f, start, n in UP_LAYERS for x in range(start, start + n)]
    downs = [(f, x) for f, start, n in DOWN_LAYERS for x in range(start, start + n)]
    for at in range(X_LAYERS):
        up = layer(*ups[min(at, len(ups) - 1)])
        down = layer(*downs[min(at, len(downs) - 1)])
        swap_store(first, xf, xb, at, up, down)

    def step(x, carry):
        y_tiles([layer(f, x) for f in range(8)], first, yf, yb, x)
        return carry

    lax.fori_loop(0, 16, step, 0, unroll=4)


class Slabs:
    def __init__(self, field, scaled, warmth, got_fwd, got_bwd):
        self.field, self.scaled, self.warmth = field, scaled, warmth
        self.got_fwd, self.got_bwd = got_fwd, got_bwd
        self.first = on_first_core()
        gx = lax.axis_index("gx")
        self.below, self.above = gx > 0, gx < lax.axis_size("gx") - 1

    def own(self, f, x):
        if f < 3:
            return self.field[f, x]
        return self.warmth[x] if f == 7 else self.scaled[f - 3, x]

    def beside(self, f, x):
        fwd, bwd = self.got_fwd, self.got_bwd
        if x < 0:
            at = UP_AT.get((f, x))
            if at is None:
                return None
            value = jnp.where(self.first, fwd[at], bwd[at])
            return jnp.where(self.below, value, 0.0)
        at = DOWN_AT.get((f, x))
        if at is None:
            return None
        value = jnp.where(self.first, bwd[at], fwd[at])
        return jnp.where(self.above, value, 0.0)

    def halo(self, emit):
        zero = jnp.zeros((16, 128), F32)
        for number, x in enumerate(HALO_X):
            values = [self.beside(f, x) for f in range(7)]
            emit(number, x + LOW, [zero if v is None else v for v in values] + [zero])

    def inner(self, emit):
        def step(x, carry):
            emit(x, x + LOW, [self.own(f, x) for f in range(8)])
            return carry

        lax.fori_loop(0, 16, step, 0, unroll=4)


def pack_corners(xf, xb, fwd, bwd):
    slabs = Slabs(None, None, None, xf, xb)
    slabs.halo(lambda number, at, v: y_tiles(v, slabs.first, fwd, bwd, number))


def y_halo(first, got, at, pair):
    gy = lax.axis_index("gy")
    part = pl.ds(8 * pair, 8)
    f, b = got[0][at, part], got[1][at, part]
    lower = jnp.where(gy > 0, jnp.where(first, f, b), 0.0)
    upper = jnp.where(gy < lax.axis_size("gy") - 1, jnp.where(first, b, f), 0.0)
    return lower, upper


HALO_X = tuple(range(-LOW, 0)) + tuple(range(16, 16 + HIGH))
X_ALL = LOW + 16 + HIGH
BLOCKS = 5
Y_LANES = LOW + 16 + HIGH
X_PAIRS = (X_ALL + 1) // 2


def pack_z(field, scaled, warmth, xf, xb, yf, yb, cf, cb, position, whole, packed, up, down):
    del position
    slabs = Slabs(field, scaled, warmth, xf, xb)
    first = slabs.first
    low_half = rows((8, 128)) < 4
    window = lanes((24, 128)) // 16

    def emit(got, number, at, v):
        acc = None
        for pair in range(4):
            lower, upper = y_halo(first, got, number, pair)
            last = []
            last.append(jnp.where(low_half, upper, lower))
            if pair < 3:
                last.append(roll(jnp.where(low_half, lower, upper), 4, 0))
            else:
                last.append(roll(upper, 3, 0))
            for f, tile in zip((2 * pair, 2 * pair + 1), last):
                slab = jnp.concatenate([v[f], tile], axis=0)
                whole[f, at] = slab
                moved = roll(slab, 16 * f + 8, 1)
                acc = moved if acc is None else jnp.where(window == f, moved, acc)
        packed[at] = acc

    slabs.halo(functools.partial(emit, (cf, cb)))
    slabs.inner(functools.partial(emit, (yf, yb)))
    packed[X_ALL] = jnp.zeros((24, 128), F32)
    half = (lanes((24, 128)) // 8) % 2 == 0

    def pair_up(k, carry):
        a, b = packed[2 * k], packed[2 * k + 1]
        up[k] = jnp.where(half, a, roll(b, 8, 1))
        down[k] = jnp.where(half, roll(a, -8, 1), b)
        return carry

    lax.fori_loop(0, X_PAIRS, pair_up, 0, unroll=True)


def twist(a, b, c, d):
    return (a - b) - (c - d)


def curls(e, e_up_y, e_up_z, e_up_x):
    (ex, ey, ez), (ex_y, ez_y), (ex_z, ey_z), (ey_x, ez_x) = e, e_up_y, e_up_z, e_up_x
    return twist(ez_y, ez, ey_z, ey), twist(ex_z, ex, ez_x, ez), twist(ey_x, ey, ex_y, ex)


def relaxed(weight, e, h, g, c, c_down_x, c_down_y, c_down_z):
    (cx, cy, cz), (cy_x, cz_x), (cx_y, cz_y), (cx_z, cy_z) = c, c_down_x, c_down_y, c_down_z
    k = twist(cz, cz_y, cy, cy_z), twist(cx, cx_z, cz, cz_x), twist(cy, cy_x, cx, cx_y)
    g = g * weight
    keep = (1.0 - weight) + 4.0 * g
    return [keep * e[f] + weight * h[f] - g * k[f] for f in range(3)]


def bulk(whole, final, whole_sum, shifted, spare):
    row = rows((24, 128))
    buffers = (whole, spare, final, spare, final)

    def curls_at(source, at, outer):
        e = [source[f, at] for f in range(3)]
        up_y = [roll(e[0], -1, 0), roll(e[2], -1, 0)]
        if outer:
            up_y = [jnp.where(row == 19, whole[7, at, pl.ds(16 + n, 1), :], up_y[n]) for n in range(2)]
        up_z = roll(e[0], -1, 1), roll(e[1], -1, 1)
        return e, curls(e, up_y, up_z, (source[1, at + 1], source[2, at + 1]))

    for number, weight in enumerate(EM_WEIGHTS):
        source, target, outer = buffers[number], buffers[number + 1], number == 0

        def step(at, carry, source=source, target=target, outer=outer, weight=weight):
            e, c = curls_at(source, at, outer)
            h, g = [whole[3 + f, at] for f in range(3)], whole[6, at]
            down_y = roll(c[0], 1, 0), roll(c[2], 1, 0)
            down_z = roll(c[0], 1, 1), roll(c[1], 1, 1)
            new = relaxed(weight, e, h, g, c, carry, down_y, down_z)
            for f in range(3):
                target[f, at] = new[f]
            return c[1], c[2]

        begin = 1 + number
        _, c = curls_at(source, begin - 1, outer)
        lax.fori_loop(begin, X_ALL - begin, step, (c[1], c[2]), unroll=4)

    def step(x, carry):
        at = x + LOW
        ex, ey, ez = (final[f, at] * final[f, at] for f in range(3))
        ey_x, ez_x = (final[f, at + 1] * final[f, at + 1] for f in (1, 2))
        flat, upright = (ex + roll(ex, -1, 0)) + (ey + ey_x), ez + ez_x
        upright = upright + roll(upright, -1, 0)
        whole_sum[x] = flat[0:16] + upright[0:16]
        shifted[x] = roll(flat[0:16], -1, 1)
        return carry

    lax.fori_loop(0, 16, step, 0, unroll=4)


def of_layer(at):
    return at % BLOCKS, Y_LANES * (at // BLOCKS)


def edge(
    packed, below_z, above_z, whole_sum, shifted, xf, xb, yf, yb, sigma, warmth, storage, position, nodes,
    final, send, partial, beside, stack, fields, spare, last, heat,
):
    first = on_first_core()
    gx, gz = lax.axis_index("gx"), lax.axis_index("gz")
    half = (lanes((24, 128)) // 8) % 2 == 0
    has_below, has_above = gz > 0, gz < lax.axis_size("gz") - 1
    nothing = jnp.zeros((1, 128), F32)
    for block in range(BLOCKS):
        for face in range(2):
            for n in range(BLOCKS):
                stack[block, face, Y_LANES * n + 24 : Y_LANES * n + 25, :] = nothing
            stack[block, face, 125:128, :] = jnp.zeros((3, 128), F32)
    for k in range(X_PAIRS):
        lower = jnp.where(has_below, below_z[k], 0.0)
        upper = jnp.where(has_above, above_z[k], 0.0)
        for at in range(2 * k, min(2 * k + 2, X_ALL)):
            if at % 2:
                came = jnp.where(half, roll(lower, -8, 1), upper)
            else:
                came = jnp.where(half, lower, roll(upper, 8, 1))
            beside[at] = came
            block, lane_at = of_layer(at)
            own = packed[at]
            for face in range(2):
                window = jnp.where(half, came, own) if face else jnp.where(half, own, came)
                stack[block, face, lane_at : lane_at + 24, :] = roll(window, 4, 0)
    for block in range(BLOCKS):
        for face in range(2):
            turned = stack[block, face].T
            for f in range(8):
                fields[block, f, 16 * face : 16 * face + 16, :] = turned[16 * f : 16 * f + 16]
    top = lanes((32, 128)) % Y_LANES == 24
    for block in range(BLOCKS):
        extra = fields[block, 7]
        for f, by in ((0, 4), (2, 3)):
            fields[block, f] = jnp.where(top, roll(extra, by, 1), fields[block, f])

    buffers = (fields, spare, final, spare, final)

    def ahead(source, block, f):
        if block < BLOCKS - 1:
            return source[block + 1, f]
        return roll(source[0, f], -Y_LANES, 1)

    def curls_at(source, block):
        e = [source[block, f] for f in range(3)]
        up_y = roll(e[0], -1, 1), roll(e[2], -1, 1)
        up_z = roll(e[0], -1, 0), roll(e[1], -1, 0)
        return e, curls(e, up_y, up_z, (ahead(source, block, 1), ahead(source, block, 2)))

    for number, weight in enumerate(EM_WEIGHTS):
        source, target = buffers[number], buffers[number + 1]
        _, c = curls_at(source, BLOCKS - 1)
        for f in range(3):
            last[f] = c[f]
        before = roll(c[1], Y_LANES, 1), roll(c[2], Y_LANES, 1)
        for block in range(BLOCKS):
            if block < BLOCKS - 1:
                e, c = curls_at(source, block)
            else:
                e, c = [source[block, f] for f in range(3)], [last[f] for f in range(3)]
            h, g = [fields[block, 3 + f] for f in range(3)], fields[block, 6]
            down_y = roll(c[0], 1, 1), roll(c[2], 1, 1)
            down_z = roll(c[0], 1, 0), roll(c[1], 1, 0)
            new = relaxed(weight, e, h, g, c, before, down_y, down_z)
            for f in range(3):
                target[block, f] = new[f]
            before = c[1], c[2]

    for block in range(BLOCKS):
        ex, ey, ez = (final[block, f] * final[block, f] for f in range(3))
        ey_x, ez_x = (ahead(final, block, f) for f in (1, 2))
        flat, upright = (ex + roll(ex, -1, 1)) + (ey + ey_x * ey_x), ez + ez_x * ez_x
        both = flat + (upright + roll(upright, -1, 1))
        stack[block, 0, 0:8, :] = both[24:32]
        stack[block, 0, 120:128, :] = both[0:8]
        stack[block, 0, 59:64, :] = flat[4:9]
        stack[block, 0, 64:67, :] = flat[25:28]
    for block in range(BLOCKS):
        stack[block, 1] = stack[block, 0].T
    lane = lanes((16, 128))
    for x in range(16):
        block, lane_at = of_layer(x + LOW)
        near = stack[block, 1, lane_at + LOW : lane_at + LOW + 16, :]
        here = jnp.where((lane < 4) | (lane >= 124), near, whole_sum[x])
        above = jnp.where((lane < 3) | (lane >= 123), roll(near, 64, 1), shifted[x])
        heat[x] = sigma[x] * (0.25 * (here + above))

    count = send.shape[0]
    spread = (rows((count, 256)) == position[...]).astype(jnp.bfloat16)
    left = heat[...].reshape(256, 128)
    total = nodes[...]
    for _ in range(3):
        piece = left.astype(jnp.bfloat16)
        left = left - piece.astype(F32)
        total = total + jnp.dot(spread, piece, preferred_element_type=F32)
    send[...] = total

    row = rows((16, 128))
    low_at, high_at = UP_AT[7, -1], DOWN_AT[7, 16]
    under = jnp.where(gx > 0, jnp.where(first, xf[low_at], xb[low_at]), 0.0)
    over = jnp.where(
        gx < lax.axis_size("gx") - 1, jnp.where(first, xb[high_at], xf[high_at]), 0.0
    )
    for x in range(16):
        t = warmth[x]
        ends = roll(beside[x + LOW, 0:16, :], 8, 1)
        lower, upper = y_halo(first, (yf, yb), x, 3)
        total = (warmth[x - 1] if x else under) + (warmth[x + 1] if x < 15 else over)
        total = total + jnp.where(row == 0, lower[3:4], roll(t, 1, 0))
        total = total + jnp.where(row == 15, upper[4:5], roll(t, -1, 0))
        total = total + roll(jnp.where(lane == 127, ends, t), 1, 1)
        total = total + roll(jnp.where(lane == 0, ends, t), -1, 1)
        partial[x] = t + HEAT_WEIGHTS[0] * (total - 6.0 * t) / (6.0 + storage[x])


def merge(final, near, out, stack):
    for block in range(BLOCKS):
        for f in range(3):
            stack[block, 32 * f : 32 * f + 8, :] = near[block, f, 24:32, :]
            at = (32 * f - 8) % 128
            stack[block, at : at + 8, :] = near[block, f, 0:8, :]
    for block in range(BLOCKS):
        stack[block] = stack[block].T
    lane = lanes((16, 128))
    outer = (lane < 4) | (lane >= 124)
    for x in range(16):
        block, lane_at = of_layer(x + LOW)
        windows = stack[block, lane_at + LOW : lane_at + LOW + 16, :]
        for f in range(3):
            inner = final[f, x + LOW, 0:16, :]
            out[f, x] = jnp.where(outer, roll(windows, -32 * f, 1), inner)


def place(owners, columns, position, nodes):
    groups = lax.axis_size("gy") * lax.axis_size("gz")
    owner, column = owners[...], columns[...]
    member = rows((groups, 256)) == owner
    earlier = (rows((256, 256)) < lanes((256, 256))).astype(jnp.bfloat16)
    before = jnp.dot(member.astype(jnp.bfloat16), earlier, preferred_element_type=F32)
    rank = jnp.sum(jnp.where(member, before, 0.0), axis=0, keepdims=True).astype(jnp.int32)
    position[...] = owner * (CAP + 1) + rank
    count = nodes.shape[0]
    spread = (rows((count, 256)) == owner * (CAP + 1) + CAP).astype(jnp.bfloat16)
    listed = jnp.where(rows((128, 256)) == rank, column + 1, 0).astype(F32).astype(jnp.bfloat16)
    nodes[...] = lax.dot_general(
        spread, listed, (((1,), (1,)), ((), ())), preferred_element_type=F32
    )


def warm(got, partial, warmth, storage, xf, xb, yf, yb, up, down, rest, heat, mid):
    first = on_first_core()
    groups = got.shape[0] // (CAP + 1)
    ids = got[pl.ds(CAP, groups, stride=CAP + 1), :]
    lane = lanes((groups, 256))
    total = None
    for r in range(CAP):
        hit = (ids[:, r : r + 1] == (lane + 1).astype(F32)).astype(jnp.bfloat16)
        left = got[pl.ds(r, groups, stride=CAP + 1), :]
        for _ in range(3):
            piece = left.astype(jnp.bfloat16)
            left = left - piece.astype(F32)
            term = lax.dot_general(
                hit, piece, (((0,), (0,)), ((), ())), preferred_element_type=F32
            )
            total = term if total is None else total + term
    heat[...] = total.reshape(16, 16, 128)
    lane = lanes((16, 128))
    row = rows((16, 128))
    for x in range(16):
        mid[x] = partial[x] + HEAT_WEIGHTS[0] * heat[x] / (6.0 + storage[x])
    xf[...] = jnp.where(first, mid[15], mid[0])
    xb[...] = jnp.where(first, mid[0], mid[15])
    ups = downs = jnp.zeros((16, 128), F32)
    for x in range(16):
        t = mid[x]
        top, end = t[15:16], t[0:1]
        yf[x : x + 1] = jnp.where(first, top, end)
        yb[x : x + 1] = jnp.where(first, end, top)
        ups = jnp.where(lane == 8 * x, roll(t, 8 * x + 1, 1), ups)
        downs = jnp.where(lane == 8 * x, roll(t, 8 * x, 1), downs)
        near = jnp.where(row == 0, 0.0, roll(t, 1, 0)) + jnp.where(row == 15, 0.0, roll(t, -1, 0))
        near = near + jnp.where(lane == 0, 0.0, roll(t, 1, 1))
        near = near + jnp.where(lane == 127, 0.0, roll(t, -1, 1))
        if x > 0:
            near = near + mid[x - 1]
        if x < 15:
            near = near + mid[x + 1]
        s = storage[x]
        push = s * warmth[x] + heat[x] - (6.0 + s) * t + near
        rest[x] = t + HEAT_WEIGHTS[1] * push / (6.0 + s)
    up[...] = ups
    down[...] = downs


def finish(rest, storage, xf, xb, yf, yb, from_below, from_above, out):
    first = on_first_core()
    gx, gy, gz = (lax.axis_index(a) for a in ("gx", "gy", "gz"))
    ends = [a > 0 for a in (gx, gy, gz)]
    tops = [a < lax.axis_size(n) - 1 for a, n in ((gx, "gx"), (gy, "gy"), (gz, "gz"))]
    f, b = xf[...], xb[...]
    x_low = jnp.where(ends[0], jnp.where(first, f, b), 0.0)
    x_high = jnp.where(tops[0], jnp.where(first, b, f), 0.0)
    f, b = yf[...], yb[...]
    y_low = jnp.where(ends[1], jnp.where(first, f, b), 0.0)
    y_high = jnp.where(tops[1], jnp.where(first, b, f), 0.0)
    z_low = jnp.where(ends[2], from_below[...], 0.0)
    z_high = jnp.where(tops[2], from_above[...], 0.0)
    lane = lanes((16, 128))
    row = rows((16, 128))
    for x in range(16):
        near = jnp.where(row == 0, y_low[x : x + 1], 0.0)
        near = near + jnp.where(row == 15, y_high[x : x + 1], 0.0)
        near = near + jnp.where(lane == 0, roll(z_low, -8 * x, 1), 0.0)
        near = near + jnp.where(lane == 127, roll(z_high, 127 - 8 * x, 1), 0.0)
        if x == 0:
            near = near + x_low
        if x == 15:
            near = near + x_high
        out[x] = rest[x] + HEAT_WEIGHTS[1] * near / (6.0 + storage[x])


def around(axis):
    n, m = lax.axis_size(axis), lax.axis_size("gz")

    def target(a, c):
        to = a + (1 if c % 2 == 0 else -1)
        return (to, c) if 0 <= to < n else (a, c ^ 1)

    forward = []
    for a in range(n):
        for c in range(m):
            to = target(a, c)
            forward.append((a * m + c, to[0] * m + to[1]))
    return forward, [(j, i) for i, j in forward]


def exchange(axis, fwd, bwd):
    forward, backward = around(axis)
    names = (axis, "gz")
    return lax.ppermute(fwd, names, forward), lax.ppermute(bwd, names, backward)


def exchange_z(up, down):
    m = lax.axis_size("gz")
    ring = [(i, (i + 1) % m) for i in range(m)]
    return lax.ppermute(up, "gz", ring), lax.ppermute(down, "gz", [(j, i) for i, j in ring])


def local(field, source, sigma, warmth, storage, partition, column):
    groups = lax.axis_size("gy") * lax.axis_size("gz")
    count = groups * (CAP + 1)
    cube = (16, 16, 128)
    face = (16, 128)
    x_message, y_message, corners = (X_LAYERS, 16, 128), (16, 32, 128), (len(HALO_X), 32, 128)
    here = [pltpu.with_memory_space_constraint(v, pltpu.HBM) for v in (field, source, sigma, warmth)]
    xf, xb, yf, yb, scaled = call(
        pack_xy,
        [x_message, x_message, y_message, y_message, (4, *cube)],
        [(3, *cube), (3, *cube), cube, cube, pltpu.SemaphoreType.DMA((4,))],
        name="pack_xy",
        near=True,
        in_specs=[pl.BlockSpec(memory_space=pltpu.HBM)] * 4,
    )(*here)
    xf, xb = exchange("gx", xf, xb)
    yf, yb = exchange("gy", yf, yb)
    position, nodes = pl.pallas_call(
        place,
        out_shape=[
            jax.ShapeDtypeStruct((1, 256), jnp.int32),
            jax.ShapeDtypeStruct((count, 128), F32),
        ],
        compiler_params=pltpu.CompilerParams(vmem_limit_bytes=8 << 20),
        name="place",
    )(partition.reshape(1, 256), column.reshape(1, 256))
    cf, cb = call(pack_corners, [corners, corners], name="pack_corners")(xf, xb)
    cf, cb = exchange("gy", cf, cb)
    layer = (24, 128)
    whole, packed, up, down = call(
        pack_z,
        [(8, X_ALL, *layer), (X_ALL + 1, *layer), (X_PAIRS, *layer), (X_PAIRS, *layer)],
        name="pack_z",
    )(field, scaled, warmth, xf, xb, yf, yb, cf, cb, position)
    below_z, above_z = exchange_z(up, down)
    final, whole_sum, shifted = call(
        bulk,
        [(3, X_ALL, *layer), cube, cube],
        [(3, X_ALL, *layer)],
        name="bulk",
        cost_estimate=pl.CostEstimate(flops=10**9, bytes_accessed=10**7, transcendentals=0),
    )(whole)
    near, send, partial = call(
        edge,
        [(BLOCKS, 3, 32, 128), (count, 128), cube],
        [
            (X_ALL, *layer),
            (BLOCKS, 2, 128, 128),
            (BLOCKS, 8, 32, 128),
            (BLOCKS, 3, 32, 128),
            (3, 32, 128),
            cube,
        ],
        name="edge",
    )(
        packed, below_z, above_z, whole_sum, shifted, xf, xb, yf, yb, sigma, warmth, storage,
        position, nodes,
    )
    got = lax.all_to_all(
        send.reshape(count, 1, 128), ("gy", "gz"), split_axis=0, concat_axis=0, tiled=True
    ).reshape(count, 128)
    xf, xb, yf, yb, up, down, rest = call(
        warm, [face, face, face, face, face, face, cube], [cube, cube], name="warm"
    )(got, partial, warmth, storage)
    xf, xb = exchange("gx", xf, xb)
    yf, yb = exchange("gy", yf, yb)
    below_z, above_z = exchange_z(up, down)
    (updated,) = call(finish, [cube], name="finish")(
        rest, storage, xf, xb, yf, yb, below_z, above_z
    )
    (out,) = call(
        merge,
        [(3, *cube)],
        [(BLOCKS, 128, 128)],
        name="merge",
        cost_estimate=pl.CostEstimate(flops=10**9, bytes_accessed=10**6, transcendentals=0),
    )(final, near)
    return out, updated


def solution(mesh):
    in_specs = (
        P(None, "gx", "gy", "gz"),
        P(None, "gx", "gy", "gz"),
        P("gx", "gy", "gz"),
        P("gx", "gy", "gz"),
        P("gx", "gy", "gz"),
        P("gx", "gy", "gz", None, None),
        P("gx", "gy", "gz", None),
    )
    out_specs = (P(None, "gx", "gy", "gz"), P("gx", "gy", "gz"))
    return jax.shard_map(local, mesh=mesh, in_specs=in_specs, out_specs=out_specs, check_vma=False)
```

```python
import functools
import math

import jax
import jax.numpy as jnp
from jax import lax
from jax.experimental import pallas as pl
from jax.experimental.pallas import tpu as pltpu
from jax.sharding import PartitionSpec as P

EM_SWEEPS = 4
HEAT_SWEEPS = 2
CAP = 8
LOW, HIGH = 4, 5
F32 = jnp.float32

em_lower = 0.02
em_upper = 3.0
heat_lower = 0.07
heat_upper = 2.0

UP_LAYERS = ((0, 12, 4), (1, 12, 4), (2, 12, 4), (3, 13, 3), (4, 13, 3), (5, 13, 3), (6, 13, 3), (7, 15, 1))
DOWN_LAYERS = ((0, 0, 4), (1, 0, 5), (2, 0, 5), (3, 0, 3), (4, 0, 4), (5, 0, 4), (6, 0, 4), (7, 0, 1))


def spots(layers, shift):
    where, at = {}, 0
    for field, first, count in layers:
        for x in range(first, first + count):
            where[field, x + shift] = at
            at += 1
    return where, at


UP_AT, UP_COUNT = spots(UP_LAYERS, -16)
DOWN_AT, DOWN_COUNT = spots(DOWN_LAYERS, 16)
X_LAYERS = max(UP_COUNT, DOWN_COUNT)


def chebyshev_weights(lower_end, upper_end, sweep_count):
    middle = 0.5 * (upper_end + lower_end)
    radius = 0.5 * (upper_end - lower_end)
    return [
        1.0 / (middle + radius * math.cos(math.pi * (2 * number + 1) / (2 * sweep_count)))
        for number in range(sweep_count)
    ]


EM_WEIGHTS = chebyshev_weights(em_lower, em_upper, EM_SWEEPS)
HEAT_WEIGHTS = chebyshev_weights(heat_lower, heat_upper, HEAT_SWEEPS)


def on_first_core():
    return lax.rem(lax.axis_index("gz"), 2) == 0


def lanes(shape):
    return lax.broadcasted_iota(jnp.int32, shape, len(shape) - 1)


def rows(shape):
    return lax.broadcasted_iota(jnp.int32, shape, len(shape) - 2)


def roll(values, by, axis):
    size = values.shape[axis]
    by = by % size
    return values if by == 0 else pltpu.roll(values, by, axis)


def call(body, out_shapes, scratch=(), name=None, limit=8 << 20, near=False, **options):
    return pl.pallas_call(
        body,
        out_shape=[
            pltpu.VMEM(s, F32) if near else jax.ShapeDtypeStruct(s, F32) for s in out_shapes
        ],
        scratch_shapes=[pltpu.VMEM(s, F32) if isinstance(s, tuple) else s for s in scratch],
        compiler_params=pltpu.CompilerParams(vmem_limit_bytes=limit),
        name=name,
        **options,
    )


def swap_store(first, fwd, bwd, at, up, down):
    fwd[at] = jnp.where(first, up, down)
    bwd[at] = jnp.where(first, down, up)


def y_tiles(v, first, fwd, bwd, at):
    row = rows((8, 128))
    low_half = row < 4
    tops = [a[8:16] for a in v]
    ends = [a[0:8] for a in v]
    for pair in range(4):
        a, b = 2 * pair, 2 * pair + 1
        up = jnp.where(low_half, roll(tops[b], 4, 0), tops[a])
        down = jnp.where(low_half, ends[a], roll(ends[b], 4, 0))
        if pair == 3:
            down = jnp.where(row == 5, roll(ends[0], 1, 0), down)
            down = jnp.where(row == 6, roll(ends[2], 2, 0), down)
        part = pl.ds(8 * pair, 8)
        fwd[at, part] = jnp.where(first, up, down)
        bwd[at, part] = jnp.where(first, down, up)


def pack_xy(*refs):
    far, (xf, xb, yf, yb, scaled), near, arrived = refs[:5], refs[5:10], refs[10:15], refs[15]
    copies = [
        pltpu.make_async_copy(a, b, arrived.at[n]) for n, (a, b) in enumerate(zip(far, near))
    ]
    for copy in copies:
        copy.start()
    for copy in copies:
        copy.wait()
    field, sigma, warmth, _, source = near
    first = on_first_core()
    inverse = 1.0 / (4.0 + sigma[...])
    scaled[3] = inverse
    for c in range(3):
        scaled[c] = source[c] * inverse

    def layer(f, x):
        if f < 3:
            return field[f, x]
        return warmth[x] if f == 7 else scaled[f - 3, x]

    ups = [(f, x) for f, start, n in UP_LAYERS for x in range(start, start + n)]
    downs = [(f, x) for f, start, n in DOWN_LAYERS for x in range(start, start + n)]
    for at in range(X_LAYERS):
        up = layer(*ups[min(at, len(ups) - 1)])
        down = layer(*downs[min(at, len(downs) - 1)])
        swap_store(first, xf, xb, at, up, down)

    def step(x, carry):
        y_tiles([layer(f, x) for f in range(8)], first, yf, yb, x)
        return carry

    lax.fori_loop(0, 16, step, 0, unroll=4)


class Halo:
    def __init__(self, got_fwd, got_bwd):
        self.got_fwd, self.got_bwd = got_fwd, got_bwd
        self.first = on_first_core()
        gx = lax.axis_index("gx")
        self.below, self.above = gx > 0, gx < lax.axis_size("gx") - 1

    def layer(self, f, x):
        if x < 0:
            at, near, far, inside = UP_AT.get((f, x)), self.got_fwd, self.got_bwd, self.below
        else:
            at, near, far, inside = DOWN_AT.get((f, x)), self.got_bwd, self.got_fwd, self.above
        if at is None:
            return None
        return jnp.where(inside, jnp.where(self.first, near[at], far[at]), 0.0)


def pack_corners(xf, xb, fwd, bwd):
    halo = Halo(xf, xb)
    zero = jnp.zeros((16, 128), F32)
    for number, x in enumerate(HALO_X):
        v = [halo.layer(f, x) for f in range(7)]
        y_tiles([zero if a is None else a for a in v] + [zero], halo.first, fwd, bwd, number)


def y_halo(first, got, at, pair):
    gy = lax.axis_index("gy")
    part = pl.ds(8 * pair, 8)
    f, b = got[0][at, part], got[1][at, part]
    lower = jnp.where(gy > 0, jnp.where(first, f, b), 0.0)
    upper = jnp.where(gy < lax.axis_size("gy") - 1, jnp.where(first, b, f), 0.0)
    return lower, upper


HALO_X = tuple(range(-LOW, 0)) + tuple(range(16, 16 + HIGH))
X_ALL = LOW + 16 + HIGH
BLOCKS = 5
Y_LANES = LOW + 16 + HIGH
X_PAIRS = (X_ALL + 1) // 2


def y_slabs(first, got, at, v):
    low_half = rows((8, 128)) < 4
    window = lanes((24, 128)) // 16
    slabs, acc = [], None
    for pair in range(4):
        lower, upper = y_halo(first, got, at, pair)
        ends = [jnp.where(low_half, upper, lower)]
        if pair < 3:
            ends.append(roll(jnp.where(low_half, lower, upper), 4, 0))
        else:
            ends.append(roll(upper, 3, 0))
        for f, tile in zip((2 * pair, 2 * pair + 1), ends):
            slabs.append(jnp.concatenate([v[f], tile], axis=0))
            moved = roll(slabs[f], 16 * f + 8, 1)
            acc = moved if acc is None else jnp.where(window == f, moved, acc)
    return slabs, acc


def z_tiles(a, b):
    half = (lanes((24, 128)) // 8) % 2 == 0
    return jnp.where(half, a, roll(b, 8, 1)), jnp.where(half, roll(a, -8, 1), b)


def pack_inner(field, scaled, warmth, yf, yb, position, whole, packed, up, down):
    del position
    first = on_first_core()

    def step(k, carry):
        windows = []
        for x in (2 * k, 2 * k + 1):
            v = [field[f, x] for f in range(3)] + [scaled[f, x] for f in range(4)] + [warmth[x]]
            slabs, acc = y_slabs(first, (yf, yb), x, v)
            for f in range(8):
                whole[f, x] = slabs[f]
            packed[x] = acc
            windows.append(acc)
        up[k], down[k] = z_tiles(*windows)
        return carry

    lax.fori_loop(0, 8, step, 0, unroll=2)


def pack_outer(xf, xb, cf, cb, inner_up, inner_down, whole, packed, up, down):
    halo = Halo(xf, xb)
    zero = jnp.zeros((16, 128), F32)
    windows = []
    for number, x in enumerate(HALO_X):
        v = [halo.layer(f, x) for f in range(7)]
        slabs, acc = y_slabs(
            halo.first, (cf, cb), number, [zero if a is None else a for a in v] + [zero]
        )
        for f in range(8):
            whole[f, number] = slabs[f]
        packed[number] = acc
        windows.append(acc)
    windows.append(jnp.zeros((24, 128), F32))
    for pair in range(len(windows) // 2):
        k = pair if pair < LOW // 2 else pair + 8
        up[k], down[k] = z_tiles(windows[2 * pair], windows[2 * pair + 1])
    up[LOW // 2 : LOW // 2 + 8] = inner_up[...]
    down[LOW // 2 : LOW // 2 + 8] = inner_down[...]


def twist(a, b, c, d):
    return (a - b) - (c - d)


def curls(e, e_up_y, e_up_z, e_up_x):
    (ex, ey, ez), (ex_y, ez_y), (ex_z, ey_z), (ey_x, ez_x) = e, e_up_y, e_up_z, e_up_x
    return twist(ez_y, ez, ey_z, ey), twist(ex_z, ex, ez_x, ez), twist(ey_x, ey, ex_y, ex)


def relaxed(weight, e, h, g, c, c_down_x, c_down_y, c_down_z):
    (cx, cy, cz), (cy_x, cz_x), (cx_y, cz_y), (cx_z, cy_z) = c, c_down_x, c_down_y, c_down_z
    k = twist(cz, cz_y, cy, cy_z), twist(cx, cx_z, cz, cz_x), twist(cy, cy_x, cx, cx_y)
    g = g * weight
    keep = (1.0 - weight) + 4.0 * g
    return [keep * e[f] + weight * h[f] - g * k[f] for f in range(3)]


def lane_curls(get, source, at):
    row = rows((24, 128))
    e = [get(source, f, at) for f in range(3)]
    up_y = roll(e[0], -1, 0), roll(e[2], -1, 0)
    if source == 0:
        up_y = [jnp.where(row == 19, get(0, 7, at)[16 + n : 17 + n], up_y[n]) for n in range(2)]
    up_z = roll(e[0], -1, 1), roll(e[1], -1, 1)
    return e, curls(e, up_y, up_z, (get(source, 1, at + 1), get(source, 2, at + 1)))


def lane_sweep(get, source, at, carry):
    e, c = lane_curls(get, source, at)
    h, g = [get(0, 3 + f, at) for f in range(3)], get(0, 6, at)
    down_y = roll(c[0], 1, 0), roll(c[2], 1, 0)
    down_z = roll(c[0], 1, 1), roll(c[1], 1, 1)
    new = relaxed(EM_WEIGHTS[source], e, h, g, c, carry, down_y, down_z)
    return new, (c[1], c[2])


def bulk(whole, swept):
    def get(number, f, x):
        return whole[f, x] if number == 0 else swept[number - 1, f, x]

    for number in range(EM_SWEEPS):

        def step(x, carry, number=number):
            new, carry = lane_sweep(get, number, x, carry)
            for f in range(3):
                swept[number, f, x] = new[f]
            return carry

        _, c = lane_curls(get, number, number)
        lax.fori_loop(number + 1, 15 - number, step, (c[1], c[2]), unroll=4)


def swept_low(number):
    return range(number - LOW, number)


def swept_high(number):
    return range(16 - number, 21 - number)


def rest_of_bulk(inner, outer, swept, final, whole_sum, shifted, others):
    def target(number):
        return final if number == EM_SWEEPS else others.at[number - 1]

    def get(number, f, x):
        if number == 0:
            return inner[f, x] if 0 <= x < 16 else outer[f, HALO_X.index(x)]
        if number <= x <= 15 - number:
            return swept[number - 1, f, x]
        low, high = swept_low(number), swept_high(number)
        return target(number)[f, low.index(x) if x < number else len(low) + high.index(x)]

    for number in range(EM_SWEEPS):
        to = target(number + 1)
        at = 0
        for layers in (swept_low(number + 1), swept_high(number + 1)):
            _, c = lane_curls(get, number, layers[0] - 1)
            carry = c[1], c[2]
            for x in layers:
                new, carry = lane_sweep(get, number, x, carry)
                for f in range(3):
                    to[f, at] = new[f]
                at += 1

    for x in range(16):
        ex, ey, ez = (get(EM_SWEEPS, f, x) for f in range(3))
        ey_x, ez_x = (get(EM_SWEEPS, f, x + 1) for f in (1, 2))
        ex, upright = ex * ex, ez * ez + ez_x * ez_x
        flat = (ex + roll(ex, -1, 0)) + (ey * ey + ey_x * ey_x)
        upright = upright + roll(upright, -1, 0)
        whole_sum[x] = flat[0:16] + upright[0:16]
        shifted[x] = roll(flat[0:16], -1, 1)


def of_layer(at):
    return at % BLOCKS, Y_LANES * (at // BLOCKS)


def edge(
    inner, outer, below_z, above_z, whole_sum, shifted, xf, xb, yf, yb, sigma, warmth, storage, position, nodes,
    final, send, partial, beside, stack, fields, spare, last, heat,
):
    first = on_first_core()
    gx, gz = lax.axis_index("gx"), lax.axis_index("gz")
    half = (lanes((24, 128)) // 8) % 2 == 0
    has_below, has_above = gz > 0, gz < lax.axis_size("gz") - 1
    nothing = jnp.zeros((1, 128), F32)
    for block in range(BLOCKS):
        for face in range(2):
            for n in range(BLOCKS):
                stack[block, face, Y_LANES * n + 24 : Y_LANES * n + 25, :] = nothing
            stack[block, face, 125:128, :] = jnp.zeros((3, 128), F32)
    for k in range(X_PAIRS):
        lower = jnp.where(has_below, below_z[k], 0.0)
        upper = jnp.where(has_above, above_z[k], 0.0)
        for at in range(2 * k, min(2 * k + 2, X_ALL)):
            if at % 2:
                came = jnp.where(half, roll(lower, -8, 1), upper)
            else:
                came = jnp.where(half, lower, roll(upper, 8, 1))
            beside[at] = came
            block, lane_at = of_layer(at)
            x = at - LOW
            own = inner[x] if 0 <= x < 16 else outer[HALO_X.index(x)]
            for face in range(2):
                window = jnp.where(half, came, own) if face else jnp.where(half, own, came)
                stack[block, face, lane_at : lane_at + 24, :] = roll(window, 4, 0)
    for block in range(BLOCKS):
        for face in range(2):
            turned = stack[block, face].T
            for f in range(8):
                fields[block, f, 16 * face : 16 * face + 16, :] = turned[16 * f : 16 * f + 16]
    top = lanes((32, 128)) % Y_LANES == 24
    for block in range(BLOCKS):
        extra = fields[block, 7]
        for f, by in ((0, 4), (2, 3)):
            fields[block, f] = jnp.where(top, roll(extra, by, 1), fields[block, f])

    buffers = (fields, spare, final, spare, final)

    def ahead(source, block, f):
        if block < BLOCKS - 1:
            return source[block + 1, f]
        return roll(source[0, f], -Y_LANES, 1)

    def curls_at(source, block):
        e = [source[block, f] for f in range(3)]
        up_y = roll(e[0], -1, 1), roll(e[2], -1, 1)
        up_z = roll(e[0], -1, 0), roll(e[1], -1, 0)
        return e, curls(e, up_y, up_z, (ahead(source, block, 1), ahead(source, block, 2)))

    for number, weight in enumerate(EM_WEIGHTS):
        source, target = buffers[number], buffers[number + 1]
        _, c = curls_at(source, BLOCKS - 1)
        for f in range(3):
            last[f] = c[f]
        before = roll(c[1], Y_LANES, 1), roll(c[2], Y_LANES, 1)
        for block in range(BLOCKS):
            if block < BLOCKS - 1:
                e, c = curls_at(source, block)
            else:
                e, c = [source[block, f] for f in range(3)], [last[f] for f in range(3)]
            h, g = [fields[block, 3 + f] for f in range(3)], fields[block, 6]
            down_y = roll(c[0], 1, 1), roll(c[2], 1, 1)
            down_z = roll(c[0], 1, 0), roll(c[1], 1, 0)
            new = relaxed(weight, e, h, g, c, before, down_y, down_z)
            for f in range(3):
                target[block, f] = new[f]
            before = c[1], c[2]

    for block in range(BLOCKS):
        ex, ey, ez = (final[block, f] * final[block, f] for f in range(3))
        ey_x, ez_x = (ahead(final, block, f) for f in (1, 2))
        flat, upright = (ex + roll(ex, -1, 1)) + (ey + ey_x * ey_x), ez + ez_x * ez_x
        both = flat + (upright + roll(upright, -1, 1))
        stack[block, 0, 0:8, :] = both[24:32]
        stack[block, 0, 120:128, :] = both[0:8]
        stack[block, 0, 59:64, :] = flat[4:9]
        stack[block, 0, 64:67, :] = flat[25:28]
    for block in range(BLOCKS):
        stack[block, 1] = stack[block, 0].T
    lane = lanes((16, 128))
    for x in range(16):
        block, lane_at = of_layer(x + LOW)
        near = stack[block, 1, lane_at + LOW : lane_at + LOW + 16, :]
        here = jnp.where((lane < 4) | (lane >= 124), near, whole_sum[x])
        above = jnp.where((lane < 3) | (lane >= 123), roll(near, 64, 1), shifted[x])
        heat[x] = sigma[x] * (0.25 * (here + above))

    count = send.shape[0]
    spread = (rows((count, 256)) == position[...]).astype(jnp.bfloat16)
    left = heat[...].reshape(256, 128)
    total = nodes[...]
    for _ in range(3):
        piece = left.astype(jnp.bfloat16)
        left = left - piece.astype(F32)
        total = total + jnp.dot(spread, piece, preferred_element_type=F32)
    send[...] = total

    row = rows((16, 128))
    low_at, high_at = UP_AT[7, -1], DOWN_AT[7, 16]
    under = jnp.where(gx > 0, jnp.where(first, xf[low_at], xb[low_at]), 0.0)
    over = jnp.where(
        gx < lax.axis_size("gx") - 1, jnp.where(first, xb[high_at], xf[high_at]), 0.0
    )
    for x in range(16):
        t = warmth[x]
        ends = roll(beside[x + LOW, 0:16, :], 8, 1)
        lower, upper = y_halo(first, (yf, yb), x, 3)
        total = (warmth[x - 1] if x else under) + (warmth[x + 1] if x < 15 else over)
        total = total + jnp.where(row == 0, lower[3:4], roll(t, 1, 0))
        total = total + jnp.where(row == 15, upper[4:5], roll(t, -1, 0))
        total = total + roll(jnp.where(lane == 127, ends, t), 1, 1)
        total = total + roll(jnp.where(lane == 0, ends, t), -1, 1)
        partial[x] = t + HEAT_WEIGHTS[0] * (total - 6.0 * t) / (6.0 + storage[x])


def merge(swept, final, near, out, stack):
    for block in range(BLOCKS):
        for f in range(3):
            stack[block, 32 * f : 32 * f + 8, :] = near[block, f, 24:32, :]
            at = (32 * f - 8) % 128
            stack[block, at : at + 8, :] = near[block, f, 0:8, :]
    for block in range(BLOCKS):
        stack[block] = stack[block].T
    lane = lanes((16, 128))
    outer = (lane < 4) | (lane >= 124)
    for x in range(16):
        block, lane_at = of_layer(x + LOW)
        windows = stack[block, lane_at + LOW : lane_at + LOW + 16, :]
        for f in range(3):
            if EM_SWEEPS <= x <= 15 - EM_SWEEPS:
                inner = swept[EM_SWEEPS - 1, f, x, 0:16, :]
            else:
                low, high = swept_low(EM_SWEEPS), swept_high(EM_SWEEPS)
                at = low.index(x) if x in low else len(low) + high.index(x)
                inner = final[f, at, 0:16, :]
            out[f, x] = jnp.where(outer, roll(windows, -32 * f, 1), inner)


def place(owners, columns, position, nodes):
    groups = lax.axis_size("gy") * lax.axis_size("gz")
    owner, column = owners[...], columns[...]
    member = rows((groups, 256)) == owner
    earlier = (rows((256, 256)) < lanes((256, 256))).astype(jnp.bfloat16)
    before = jnp.dot(member.astype(jnp.bfloat16), earlier, preferred_element_type=F32)
    rank = jnp.sum(jnp.where(member, before, 0.0), axis=0, keepdims=True).astype(jnp.int32)
    position[...] = owner * (CAP + 1) + rank
    count = nodes.shape[0]
    spread = (rows((count, 256)) == owner * (CAP + 1) + CAP).astype(jnp.bfloat16)
    listed = jnp.where(rows((128, 256)) == rank, column + 1, 0).astype(F32).astype(jnp.bfloat16)
    nodes[...] = lax.dot_general(
        spread, listed, (((1,), (1,)), ((), ())), preferred_element_type=F32
    )


def warm(got, partial, warmth, storage, xf, xb, yf, yb, up, down, rest, heat, mid):
    first = on_first_core()
    groups = got.shape[0] // (CAP + 1)
    ids = got[pl.ds(CAP, groups, stride=CAP + 1), :]
    lane = lanes((groups, 256))
    total = None
    for r in range(CAP):
        hit = (ids[:, r : r + 1] == (lane + 1).astype(F32)).astype(jnp.bfloat16)
        left = got[pl.ds(r, groups, stride=CAP + 1), :]
        for _ in range(3):
            piece = left.astype(jnp.bfloat16)
            left = left - piece.astype(F32)
            term = lax.dot_general(
                hit, piece, (((0,), (0,)), ((), ())), preferred_element_type=F32
            )
            total = term if total is None else total + term
    heat[...] = total.reshape(16, 16, 128)
    lane = lanes((16, 128))
    row = rows((16, 128))
    for x in range(16):
        mid[x] = partial[x] + HEAT_WEIGHTS[0] * heat[x] / (6.0 + storage[x])
    xf[...] = jnp.where(first, mid[15], mid[0])
    xb[...] = jnp.where(first, mid[0], mid[15])
    ups = downs = jnp.zeros((16, 128), F32)
    for x in range(16):
        t = mid[x]
        top, end = t[15:16], t[0:1]
        yf[x : x + 1] = jnp.where(first, top, end)
        yb[x : x + 1] = jnp.where(first, end, top)
        ups = jnp.where(lane == 8 * x, roll(t, 8 * x + 1, 1), ups)
        downs = jnp.where(lane == 8 * x, roll(t, 8 * x, 1), downs)
        near = jnp.where(row == 0, 0.0, roll(t, 1, 0)) + jnp.where(row == 15, 0.0, roll(t, -1, 0))
        near = near + jnp.where(lane == 0, 0.0, roll(t, 1, 1))
        near = near + jnp.where(lane == 127, 0.0, roll(t, -1, 1))
        if x > 0:
            near = near + mid[x - 1]
        if x < 15:
            near = near + mid[x + 1]
        s = storage[x]
        push = s * warmth[x] + heat[x] - (6.0 + s) * t + near
        rest[x] = t + HEAT_WEIGHTS[1] * push / (6.0 + s)
    up[...] = ups
    down[...] = downs


def finish(rest, storage, xf, xb, yf, yb, from_below, from_above, out):
    first = on_first_core()
    gx, gy, gz = (lax.axis_index(a) for a in ("gx", "gy", "gz"))
    ends = [a > 0 for a in (gx, gy, gz)]
    tops = [a < lax.axis_size(n) - 1 for a, n in ((gx, "gx"), (gy, "gy"), (gz, "gz"))]
    f, b = xf[...], xb[...]
    x_low = jnp.where(ends[0], jnp.where(first, f, b), 0.0)
    x_high = jnp.where(tops[0], jnp.where(first, b, f), 0.0)
    f, b = yf[...], yb[...]
    y_low = jnp.where(ends[1], jnp.where(first, f, b), 0.0)
    y_high = jnp.where(tops[1], jnp.where(first, b, f), 0.0)
    z_low = jnp.where(ends[2], from_below[...], 0.0)
    z_high = jnp.where(tops[2], from_above[...], 0.0)
    lane = lanes((16, 128))
    row = rows((16, 128))
    for x in range(16):
        near = jnp.where(row == 0, y_low[x : x + 1], 0.0)
        near = near + jnp.where(row == 15, y_high[x : x + 1], 0.0)
        near = near + jnp.where(lane == 0, roll(z_low, -8 * x, 1), 0.0)
        near = near + jnp.where(lane == 127, roll(z_high, 127 - 8 * x, 1), 0.0)
        if x == 0:
            near = near + x_low
        if x == 15:
            near = near + x_high
        out[x] = rest[x] + HEAT_WEIGHTS[1] * near / (6.0 + storage[x])


def around(axis):
    n, m = lax.axis_size(axis), lax.axis_size("gz")

    def target(a, c):
        to = a + (1 if c % 2 == 0 else -1)
        return (to, c) if 0 <= to < n else (a, c ^ 1)

    forward = []
    for a in range(n):
        for c in range(m):
            to = target(a, c)
            forward.append((a * m + c, to[0] * m + to[1]))
    return forward, [(j, i) for i, j in forward]


def exchange(axis, fwd, bwd):
    forward, backward = around(axis)
    names = (axis, "gz")
    return lax.ppermute(fwd, names, forward), lax.ppermute(bwd, names, backward)


def exchange_z(up, down):
    m = lax.axis_size("gz")
    ring = [(i, (i + 1) % m) for i in range(m)]
    return lax.ppermute(up, "gz", ring), lax.ppermute(down, "gz", [(j, i) for i, j in ring])


def local(field, source, sigma, warmth, storage, partition, column):
    groups = lax.axis_size("gy") * lax.axis_size("gz")
    count = groups * (CAP + 1)
    cube = (16, 16, 128)
    face = (16, 128)
    x_message, y_message, corners = (X_LAYERS, 16, 128), (16, 32, 128), (len(HALO_X), 32, 128)
    here = (field, sigma, warmth, storage, source)
    xf, xb, yf, yb, scaled, field, sigma, warmth, storage = call(
        pack_xy,
        [x_message, x_message, y_message, y_message, (4, *cube), (3, *cube), cube, cube, cube],
        [(3, *cube), pltpu.SemaphoreType.DMA((5,))],
        name="pack_xy",
        near=True,
        in_specs=[pl.BlockSpec(memory_space=pltpu.HBM)] * 5,
    )(*(pltpu.with_memory_space_constraint(v, pltpu.HBM) for v in here))
    xf, xb = exchange("gx", xf, xb)
    yf, yb = exchange("gy", yf, yb)
    position, nodes = pl.pallas_call(
        place,
        out_shape=[
            jax.ShapeDtypeStruct((1, 256), jnp.int32),
            jax.ShapeDtypeStruct((count, 128), F32),
        ],
        compiler_params=pltpu.CompilerParams(vmem_limit_bytes=8 << 20),
        name="place",
    )(partition.reshape(1, 256), column.reshape(1, 256))
    cf, cb = call(pack_corners, [corners, corners], name="pack_corners")(xf, xb)
    cf, cb = exchange("gy", cf, cb)
    layer, halo = (24, 128), len(HALO_X)
    inner, inner_packed, inner_up, inner_down = call(
        pack_inner,
        [(8, 16, *layer), (16, *layer), (8, *layer), (8, *layer)],
        name="pack_inner",
        near=True,
    )(field, scaled, warmth, yf, yb, position)
    (swept,) = call(
        bulk,
        [(EM_SWEEPS, 3, 16, *layer)],
        name="bulk",
        near=True,
        cost_estimate=pl.CostEstimate(flops=10**9, bytes_accessed=10**7, transcendentals=0),
    )(inner)
    outer, outer_packed, up, down = call(
        pack_outer,
        [(8, halo, *layer), (halo, *layer), (X_PAIRS, *layer), (X_PAIRS, *layer)],
        name="pack_outer",
        near=True,
    )(xf, xb, cf, cb, inner_up, inner_down)
    below_z, above_z = exchange_z(up, down)
    final, whole_sum, shifted = call(
        rest_of_bulk,
        [(3, halo, *layer), cube, cube],
        [(EM_SWEEPS - 1, 3, halo, *layer)],
        name="rest_of_bulk",
        near=True,
        cost_estimate=pl.CostEstimate(flops=10**9, bytes_accessed=10**7, transcendentals=0),
    )(inner, outer, swept)
    near, send, partial = call(
        edge,
        [(BLOCKS, 3, 32, 128), (count, 128), cube],
        [
            (X_ALL, *layer),
            (BLOCKS, 2, 128, 128),
            (BLOCKS, 8, 32, 128),
            (BLOCKS, 3, 32, 128),
            (3, 32, 128),
            cube,
        ],
        name="edge",
    )(
        inner_packed, outer_packed, below_z, above_z, whole_sum, shifted, xf, xb, yf, yb, sigma,
        warmth, storage, position, nodes,
    )
    got = lax.all_to_all(
        send.reshape(count, 1, 128), ("gy", "gz"), split_axis=0, concat_axis=0, tiled=True
    ).reshape(count, 128)
    xf, xb, yf, yb, up, down, rest = call(
        warm, [face, face, face, face, face, face, cube], [cube, cube], name="warm"
    )(got, partial, warmth, storage)
    xf, xb = exchange("gx", xf, xb)
    yf, yb = exchange("gy", yf, yb)
    below_z, above_z = exchange_z(up, down)
    (updated,) = call(finish, [cube], name="finish")(
        rest, storage, xf, xb, yf, yb, below_z, above_z
    )
    (out,) = call(
        merge,
        [(3, *cube)],
        [(BLOCKS, 128, 128)],
        name="merge",
        cost_estimate=pl.CostEstimate(flops=10**9, bytes_accessed=10**6, transcendentals=0),
    )(swept, final, near)
    return out, updated


def solution(mesh):
    in_specs = (
        P(None, "gx", "gy", "gz"),
        P(None, "gx", "gy", "gz"),
        P("gx", "gy", "gz"),
        P("gx", "gy", "gz"),
        P("gx", "gy", "gz"),
        P("gx", "gy", "gz", None, None),
        P("gx", "gy", "gz", None),
    )
    out_specs = (P(None, "gx", "gy", "gz"), P("gx", "gy", "gz"))
    return jax.shard_map(local, mesh=mesh, in_specs=in_specs, out_specs=out_specs, check_vma=False)
```

```python
import functools
import math

import jax
import jax.numpy as jnp
from jax import lax
from jax.experimental import pallas as pl
from jax.experimental.pallas import tpu as pltpu
from jax.sharding import PartitionSpec as P

EM_SWEEPS = 4
HEAT_SWEEPS = 2
CAP = 8
LOW, HIGH = 4, 5
F32 = jnp.float32

em_lower = 0.02
em_upper = 3.0
heat_lower = 0.07
heat_upper = 2.0

UP_LAYERS = ((0, 12, 4), (1, 12, 4), (2, 12, 4), (3, 13, 3), (4, 13, 3), (5, 13, 3), (6, 13, 3), (7, 15, 1))
DOWN_LAYERS = ((0, 0, 4), (1, 0, 5), (2, 0, 5), (3, 0, 3), (4, 0, 4), (5, 0, 4), (6, 0, 4), (7, 0, 1))


def spots(layers, shift):
    where, at = {}, 0
    for field, first, count in layers:
        for x in range(first, first + count):
            where[field, x + shift] = at
            at += 1
    return where, at


UP_AT, UP_COUNT = spots(UP_LAYERS, -16)
DOWN_AT, DOWN_COUNT = spots(DOWN_LAYERS, 16)
X_LAYERS = max(UP_COUNT, DOWN_COUNT)


def chebyshev_weights(lower_end, upper_end, sweep_count):
    middle = 0.5 * (upper_end + lower_end)
    radius = 0.5 * (upper_end - lower_end)
    return [
        1.0 / (middle + radius * math.cos(math.pi * (2 * number + 1) / (2 * sweep_count)))
        for number in range(sweep_count)
    ]


EM_WEIGHTS = chebyshev_weights(em_lower, em_upper, EM_SWEEPS)
HEAT_WEIGHTS = chebyshev_weights(heat_lower, heat_upper, HEAT_SWEEPS)


def on_first_core():
    return lax.rem(lax.axis_index("gz"), 2) == 0


def lanes(shape):
    return lax.broadcasted_iota(jnp.int32, shape, len(shape) - 1)


def rows(shape):
    return lax.broadcasted_iota(jnp.int32, shape, len(shape) - 2)


def roll(values, by, axis):
    size = values.shape[axis]
    by = by % size
    return values if by == 0 else pltpu.roll(values, by, axis)


def call(body, out_shapes, scratch=(), name=None, limit=8 << 20, near=False, **options):
    return pl.pallas_call(
        body,
        out_shape=[
            pltpu.VMEM(s, F32) if near else jax.ShapeDtypeStruct(s, F32) for s in out_shapes
        ],
        scratch_shapes=[pltpu.VMEM(s, F32) if isinstance(s, tuple) else s for s in scratch],
        compiler_params=pltpu.CompilerParams(vmem_limit_bytes=limit),
        name=name,
        **options,
    )


def swap_store(first, fwd, bwd, at, up, down):
    fwd[at] = jnp.where(first, up, down)
    bwd[at] = jnp.where(first, down, up)


def y_tiles(v, first, fwd, bwd, at):
    row = rows((8, 128))
    low_half = row < 4
    tops = [a[8:16] for a in v]
    ends = [a[0:8] for a in v]
    for pair in range(4):
        a, b = 2 * pair, 2 * pair + 1
        up = jnp.where(low_half, roll(tops[b], 4, 0), tops[a])
        down = jnp.where(low_half, ends[a], roll(ends[b], 4, 0))
        if pair == 3:
            down = jnp.where(row == 5, roll(ends[0], 1, 0), down)
            down = jnp.where(row == 6, roll(ends[2], 2, 0), down)
        part = pl.ds(8 * pair, 8)
        fwd[at, part] = jnp.where(first, up, down)
        bwd[at, part] = jnp.where(first, down, up)


def pack_xy(*refs):
    far, (xf, xb, yf, yb, scaled), near, arrived = refs[:5], refs[5:10], refs[10:15], refs[15]
    copies = [
        pltpu.make_async_copy(a, b, arrived.at[n]) for n, (a, b) in enumerate(zip(far, near))
    ]
    for copy in copies:
        copy.start()
    for copy in copies:
        copy.wait()
    field, sigma, warmth, _, source = near
    first = on_first_core()
    inverse = 1.0 / (4.0 + sigma[...])
    scaled[3] = inverse
    for c in range(3):
        scaled[c] = source[c] * inverse

    def layer(f, x):
        if f < 3:
            return field[f, x]
        return warmth[x] if f == 7 else scaled[f - 3, x]

    ups = [(f, x) for f, start, n in UP_LAYERS for x in range(start, start + n)]
    downs = [(f, x) for f, start, n in DOWN_LAYERS for x in range(start, start + n)]
    for at in range(X_LAYERS):
        up = layer(*ups[min(at, len(ups) - 1)])
        down = layer(*downs[min(at, len(downs) - 1)])
        swap_store(first, xf, xb, at, up, down)

    def step(x, carry):
        y_tiles([layer(f, x) for f in range(8)], first, yf, yb, x)
        return carry

    lax.fori_loop(0, 16, step, 0, unroll=4)


class Halo:
    def __init__(self, got_fwd, got_bwd):
        self.got_fwd, self.got_bwd = got_fwd, got_bwd
        self.first = on_first_core()
        gx = lax.axis_index("gx")
        self.below, self.above = gx > 0, gx < lax.axis_size("gx") - 1

    def layer(self, f, x):
        if x < 0:
            at, near, far, inside = UP_AT.get((f, x)), self.got_fwd, self.got_bwd, self.below
        else:
            at, near, far, inside = DOWN_AT.get((f, x)), self.got_bwd, self.got_fwd, self.above
        if at is None:
            return None
        return jnp.where(inside, jnp.where(self.first, near[at], far[at]), 0.0)


def pack_corners(xf, xb, position, fwd, bwd):
    del position
    halo = Halo(xf, xb)
    zero = jnp.zeros((16, 128), F32)
    for number, x in enumerate(HALO_X):
        v = [halo.layer(f, x) for f in range(7)]
        y_tiles([zero if a is None else a for a in v] + [zero], halo.first, fwd, bwd, number)


def y_halo(first, got, at, pair):
    gy = lax.axis_index("gy")
    part = pl.ds(8 * pair, 8)
    f, b = got[0][at, part], got[1][at, part]
    lower = jnp.where(gy > 0, jnp.where(first, f, b), 0.0)
    upper = jnp.where(gy < lax.axis_size("gy") - 1, jnp.where(first, b, f), 0.0)
    return lower, upper


HALO_X = tuple(range(-LOW, 0)) + tuple(range(16, 16 + HIGH))
X_ALL = LOW + 16 + HIGH
BLOCKS = 5
Y_LANES = LOW + 16 + HIGH
X_PAIRS = (X_ALL + 1) // 2


def y_slabs(first, got, at, v):
    low_half = rows((8, 128)) < 4
    window = lanes((24, 128)) // 16
    slabs, acc = [], None
    for pair in range(4):
        lower, upper = y_halo(first, got, at, pair)
        ends = [jnp.where(low_half, upper, lower)]
        if pair < 3:
            ends.append(roll(jnp.where(low_half, lower, upper), 4, 0))
        else:
            ends.append(roll(upper, 3, 0))
        for f, tile in zip((2 * pair, 2 * pair + 1), ends):
            slabs.append(jnp.concatenate([v[f], tile], axis=0))
            moved = roll(slabs[f], 16 * f + 8, 1)
            acc = moved if acc is None else jnp.where(window == f, moved, acc)
    return slabs, acc


def z_tiles(a, b):
    half = (lanes((24, 128)) // 8) % 2 == 0
    return jnp.where(half, a, roll(b, 8, 1)), jnp.where(half, roll(a, -8, 1), b)


def pack_inner(field, scaled, warmth, yf, yb, whole, packed, up, down):
    first = on_first_core()

    def step(k, carry):
        windows = []
        for x in (2 * k, 2 * k + 1):
            v = [field[f, x] for f in range(3)] + [scaled[f, x] for f in range(4)] + [warmth[x]]
            slabs, acc = y_slabs(first, (yf, yb), x, v)
            for f in range(8):
                whole[f, x] = slabs[f]
            packed[x] = acc
            windows.append(acc)
        up[k], down[k] = z_tiles(*windows)
        return carry

    lax.fori_loop(0, 8, step, 0, unroll=2)


def pack_outer(xf, xb, cf, cb, inner_up, inner_down, swept, whole, packed, up, down):
    del swept
    halo = Halo(xf, xb)
    zero = jnp.zeros((16, 128), F32)
    windows = []
    for number, x in enumerate(HALO_X):
        v = [halo.layer(f, x) for f in range(7)]
        slabs, acc = y_slabs(
            halo.first, (cf, cb), number, [zero if a is None else a for a in v] + [zero]
        )
        for f in range(8):
            whole[f, number] = slabs[f]
        packed[number] = acc
        windows.append(acc)
    windows.append(jnp.zeros((24, 128), F32))
    for pair in range(len(windows) // 2):
        k = pair if pair < LOW // 2 else pair + 8
        up[k], down[k] = z_tiles(windows[2 * pair], windows[2 * pair + 1])
    up[LOW // 2 : LOW // 2 + 8] = inner_up[...]
    down[LOW // 2 : LOW // 2 + 8] = inner_down[...]


def twist(a, b, c, d):
    return (a - b) - (c - d)


def curls(e, e_up_y, e_up_z, e_up_x):
    (ex, ey, ez), (ex_y, ez_y), (ex_z, ey_z), (ey_x, ez_x) = e, e_up_y, e_up_z, e_up_x
    return twist(ez_y, ez, ey_z, ey), twist(ex_z, ex, ez_x, ez), twist(ey_x, ey, ex_y, ex)


def relaxed(weight, e, h, g, c, c_down_x, c_down_y, c_down_z):
    (cx, cy, cz), (cy_x, cz_x), (cx_y, cz_y), (cx_z, cy_z) = c, c_down_x, c_down_y, c_down_z
    k = twist(cz, cz_y, cy, cy_z), twist(cx, cx_z, cz, cz_x), twist(cy, cy_x, cx, cx_y)
    g = g * weight
    keep = (1.0 - weight) + 4.0 * g
    return [keep * e[f] + weight * h[f] - g * k[f] for f in range(3)]


def lane_curls(get, source, at):
    row = rows((24, 128))
    e = [get(source, f, at) for f in range(3)]
    up_y = roll(e[0], -1, 0), roll(e[2], -1, 0)
    if source == 0:
        up_y = [jnp.where(row == 19, get(0, 7, at)[16 + n : 17 + n], up_y[n]) for n in range(2)]
    up_z = roll(e[0], -1, 1), roll(e[1], -1, 1)
    return e, curls(e, up_y, up_z, (get(source, 1, at + 1), get(source, 2, at + 1)))


def lane_sweep(get, source, at, carry):
    e, c = lane_curls(get, source, at)
    h, g = [get(0, 3 + f, at) for f in range(3)], get(0, 6, at)
    down_y = roll(c[0], 1, 0), roll(c[2], 1, 0)
    down_z = roll(c[0], 1, 1), roll(c[1], 1, 1)
    new = relaxed(EM_WEIGHTS[source], e, h, g, c, carry, down_y, down_z)
    return new, (c[1], c[2])


def bulk(whole, swept):
    def get(number, f, x):
        return whole[f, x] if number == 0 else swept[number - 1, f, x]

    for number in range(EM_SWEEPS):

        def step(x, carry, number=number):
            new, carry = lane_sweep(get, number, x, carry)
            for f in range(3):
                swept[number, f, x] = new[f]
            return carry

        _, c = lane_curls(get, number, number)
        lax.fori_loop(number + 1, 15 - number, step, (c[1], c[2]), unroll=4)


def swept_low(number):
    return range(number - LOW, number)


def swept_high(number):
    return range(16 - number, 21 - number)


def rest_of_bulk(
    inner, outer, swept, xf, xb, yf, yb, warmth, storage, final, whole_sum, shifted, began, others
):
    def target(number):
        return final if number == EM_SWEEPS else others.at[number - 1]

    def get(number, f, x):
        if number == 0:
            return inner[f, x] if 0 <= x < 16 else outer[f, HALO_X.index(x)]
        if number <= x <= 15 - number:
            return swept[number - 1, f, x]
        low, high = swept_low(number), swept_high(number)
        return target(number)[f, low.index(x) if x < number else len(low) + high.index(x)]

    for number in range(EM_SWEEPS):
        to = target(number + 1)
        at = 0
        for layers in (swept_low(number + 1), swept_high(number + 1)):
            _, c = lane_curls(get, number, layers[0] - 1)
            carry = c[1], c[2]
            for x in layers:
                new, carry = lane_sweep(get, number, x, carry)
                for f in range(3):
                    to[f, at] = new[f]
                at += 1

    for x in range(16):
        ex, ey, ez = (get(EM_SWEEPS, f, x) for f in range(3))
        ey_x, ez_x = (get(EM_SWEEPS, f, x + 1) for f in (1, 2))
        ex, upright = ex * ex, ez * ez + ez_x * ez_x
        flat = (ex + roll(ex, -1, 0)) + (ey * ey + ey_x * ey_x)
        upright = upright + roll(upright, -1, 0)
        whole_sum[x] = flat[0:16] + upright[0:16]
        shifted[x] = roll(flat[0:16], -1, 1)

    first, gx = on_first_core(), lax.axis_index("gx")
    row, lane = rows((16, 128)), lanes((16, 128))
    low_at, high_at = UP_AT[7, -1], DOWN_AT[7, 16]
    under = jnp.where(gx > 0, jnp.where(first, xf[low_at], xb[low_at]), 0.0)
    over = jnp.where(
        gx < lax.axis_size("gx") - 1, jnp.where(first, xb[high_at], xf[high_at]), 0.0
    )
    for x in range(16):
        t = warmth[x]
        lower, upper = y_halo(first, (yf, yb), x, 3)
        total = (warmth[x - 1] if x else under) + (warmth[x + 1] if x < 15 else over)
        total = total + jnp.where(row == 0, lower[3:4], roll(t, 1, 0))
        total = total + jnp.where(row == 15, upper[4:5], roll(t, -1, 0))
        total = total + jnp.where(lane == 0, 0.0, roll(t, 1, 1))
        total = total + jnp.where(lane == 127, 0.0, roll(t, -1, 1))
        began[x] = t + HEAT_WEIGHTS[0] * (total - 6.0 * t) / (6.0 + storage[x])


def of_layer(at):
    return at % BLOCKS, Y_LANES * (at // BLOCKS)


def edge(
    inner, outer, below_z, above_z, whole_sum, shifted, sigma, began, storage, position, nodes,
    final, send, partial, beside, stack, fields, spare, last, heat,
):
    gz = lax.axis_index("gz")
    half = (lanes((24, 128)) // 8) % 2 == 0
    has_below, has_above = gz > 0, gz < lax.axis_size("gz") - 1
    nothing = jnp.zeros((1, 128), F32)
    for block in range(BLOCKS):
        for face in range(2):
            for n in range(BLOCKS):
                stack[block, face, Y_LANES * n + 24 : Y_LANES * n + 25, :] = nothing
            stack[block, face, 125:128, :] = jnp.zeros((3, 128), F32)
    for k in range(X_PAIRS):
        lower = jnp.where(has_below, below_z[k], 0.0)
        upper = jnp.where(has_above, above_z[k], 0.0)
        for at in range(2 * k, min(2 * k + 2, X_ALL)):
            if at % 2:
                came = jnp.where(half, roll(lower, -8, 1), upper)
            else:
                came = jnp.where(half, lower, roll(upper, 8, 1))
            beside[at] = came
            block, lane_at = of_layer(at)
            x = at - LOW
            own = inner[x] if 0 <= x < 16 else outer[HALO_X.index(x)]
            for face in range(2):
                window = jnp.where(half, came, own) if face else jnp.where(half, own, came)
                stack[block, face, lane_at : lane_at + 24, :] = roll(window, 4, 0)
    for block in range(BLOCKS):
        for face in range(2):
            turned = stack[block, face].T
            for f in range(8):
                fields[block, f, 16 * face : 16 * face + 16, :] = turned[16 * f : 16 * f + 16]
    top = lanes((32, 128)) % Y_LANES == 24
    for block in range(BLOCKS):
        extra = fields[block, 7]
        for f, by in ((0, 4), (2, 3)):
            fields[block, f] = jnp.where(top, roll(extra, by, 1), fields[block, f])

    buffers = (fields, spare, final, spare, final)

    def ahead(source, block, f):
        if block < BLOCKS - 1:
            return source[block + 1, f]
        return roll(source[0, f], -Y_LANES, 1)

    def curls_at(source, block):
        e = [source[block, f] for f in range(3)]
        up_y = roll(e[0], -1, 1), roll(e[2], -1, 1)
        up_z = roll(e[0], -1, 0), roll(e[1], -1, 0)
        return e, curls(e, up_y, up_z, (ahead(source, block, 1), ahead(source, block, 2)))

    for number, weight in enumerate(EM_WEIGHTS):
        source, target = buffers[number], buffers[number + 1]
        _, c = curls_at(source, BLOCKS - 1)
        for f in range(3):
            last[f] = c[f]
        before = roll(c[1], Y_LANES, 1), roll(c[2], Y_LANES, 1)
        for block in range(BLOCKS):
            if block < BLOCKS - 1:
                e, c = curls_at(source, block)
            else:
                e, c = [source[block, f] for f in range(3)], [last[f] for f in range(3)]
            h, g = [fields[block, 3 + f] for f in range(3)], fields[block, 6]
            down_y = roll(c[0], 1, 1), roll(c[2], 1, 1)
            down_z = roll(c[0], 1, 0), roll(c[1], 1, 0)
            new = relaxed(weight, e, h, g, c, before, down_y, down_z)
            for f in range(3):
                target[block, f] = new[f]
            before = c[1], c[2]

    for block in range(BLOCKS):
        ex, ey, ez = (final[block, f] * final[block, f] for f in range(3))
        ey_x, ez_x = (ahead(final, block, f) for f in (1, 2))
        flat, upright = (ex + roll(ex, -1, 1)) + (ey + ey_x * ey_x), ez + ez_x * ez_x
        both = flat + (upright + roll(upright, -1, 1))
        stack[block, 0, 0:8, :] = both[24:32]
        stack[block, 0, 120:128, :] = both[0:8]
        stack[block, 0, 59:64, :] = flat[4:9]
        stack[block, 0, 64:67, :] = flat[25:28]
    for block in range(BLOCKS):
        stack[block, 1] = stack[block, 0].T
    lane = lanes((16, 128))
    for x in range(16):
        block, lane_at = of_layer(x + LOW)
        near = stack[block, 1, lane_at + LOW : lane_at + LOW + 16, :]
        here = jnp.where((lane < 4) | (lane >= 124), near, whole_sum[x])
        above = jnp.where((lane < 3) | (lane >= 123), roll(near, 64, 1), shifted[x])
        heat[x] = sigma[x] * (0.25 * (here + above))

    count = send.shape[0]
    spread = (rows((count, 256)) == position[...]).astype(jnp.bfloat16)
    left = heat[...].reshape(256, 128)
    total = nodes[...]
    for _ in range(3):
        piece = left.astype(jnp.bfloat16)
        left = left - piece.astype(F32)
        total = total + jnp.dot(spread, piece, preferred_element_type=F32)
    send[...] = total

    for x in range(16):
        ends = beside[x + LOW, 0:16, :]
        halo = jnp.where(lane == 0, roll(ends, 9, 1), jnp.where(lane == 127, roll(ends, 7, 1), 0.0))
        partial[x] = began[x] + HEAT_WEIGHTS[0] * halo / (6.0 + storage[x])


def merge(swept, final, near, out, stack):
    for block in range(BLOCKS):
        for f in range(3):
            stack[block, 32 * f : 32 * f + 8, :] = near[block, f, 24:32, :]
            at = (32 * f - 8) % 128
            stack[block, at : at + 8, :] = near[block, f, 0:8, :]
    for block in range(BLOCKS):
        stack[block] = stack[block].T
    lane = lanes((16, 128))
    outer = (lane < 4) | (lane >= 124)
    for x in range(16):
        block, lane_at = of_layer(x + LOW)
        windows = stack[block, lane_at + LOW : lane_at + LOW + 16, :]
        for f in range(3):
            if EM_SWEEPS <= x <= 15 - EM_SWEEPS:
                inner = swept[EM_SWEEPS - 1, f, x, 0:16, :]
            else:
                low, high = swept_low(EM_SWEEPS), swept_high(EM_SWEEPS)
                at = low.index(x) if x in low else len(low) + high.index(x)
                inner = final[f, at, 0:16, :]
            out[f, x] = jnp.where(outer, roll(windows, -32 * f, 1), inner)


def place(owners, columns, position, nodes):
    groups = lax.axis_size("gy") * lax.axis_size("gz")
    owner, column = owners[...], columns[...]
    member = rows((groups, 256)) == owner
    earlier = (rows((256, 256)) < lanes((256, 256))).astype(jnp.bfloat16)
    before = jnp.dot(member.astype(jnp.bfloat16), earlier, preferred_element_type=F32)
    rank = jnp.sum(jnp.where(member, before, 0.0), axis=0, keepdims=True).astype(jnp.int32)
    position[...] = owner * (CAP + 1) + rank
    count = nodes.shape[0]
    spread = (rows((count, 256)) == owner * (CAP + 1) + CAP).astype(jnp.bfloat16)
    listed = jnp.where(rows((128, 256)) == rank, column + 1, 0).astype(F32).astype(jnp.bfloat16)
    nodes[...] = lax.dot_general(
        spread, listed, (((1,), (1,)), ((), ())), preferred_element_type=F32
    )


def warm(got, partial, warmth, storage, xf, xb, yf, yb, up, down, rest, heat, mid):
    first = on_first_core()
    groups = got.shape[0] // (CAP + 1)
    ids = got[pl.ds(CAP, groups, stride=CAP + 1), :].T
    node = rows((256, 1)) + 1
    per = max(1, 128 // groups)
    total = None
    for r in range(0, CAP, per):
        number = jnp.concatenate([ids[r + n : r + n + 1, :] for n in range(per)], axis=1)
        hit = (number == node.astype(F32)).astype(jnp.bfloat16)
        left = jnp.concatenate(
            [got[pl.ds(r + n, groups, stride=CAP + 1), :] for n in range(per)], axis=0
        )
        for _ in range(3):
            piece = left.astype(jnp.bfloat16)
            left = left - piece.astype(F32)
            term = jnp.dot(hit, piece, preferred_element_type=F32)
            total = term if total is None else total + term
    heat[...] = total.reshape(16, 16, 128)
    lane = lanes((16, 128))
    row = rows((16, 128))
    for x in range(16):
        mid[x] = partial[x] + HEAT_WEIGHTS[0] * heat[x] / (6.0 + storage[x])
    xf[...] = jnp.where(first, mid[15], mid[0])
    xb[...] = jnp.where(first, mid[0], mid[15])
    ups = downs = jnp.zeros((16, 128), F32)
    for x in range(16):
        t = mid[x]
        top, end = t[15:16], t[0:1]
        yf[x : x + 1] = jnp.where(first, top, end)
        yb[x : x + 1] = jnp.where(first, end, top)
        ups = jnp.where(lane == 8 * x, roll(t, 8 * x + 1, 1), ups)
        downs = jnp.where(lane == 8 * x, roll(t, 8 * x, 1), downs)
        near = jnp.where(row == 0, 0.0, roll(t, 1, 0)) + jnp.where(row == 15, 0.0, roll(t, -1, 0))
        near = near + jnp.where(lane == 0, 0.0, roll(t, 1, 1))
        near = near + jnp.where(lane == 127, 0.0, roll(t, -1, 1))
        if x > 0:
            near = near + mid[x - 1]
        if x < 15:
            near = near + mid[x + 1]
        s = storage[x]
        push = s * warmth[x] + heat[x] - (6.0 + s) * t + near
        rest[x] = t + HEAT_WEIGHTS[1] * push / (6.0 + s)
    up[...] = ups
    down[...] = downs


def finish(rest, storage, xf, xb, yf, yb, from_below, from_above, out):
    first = on_first_core()
    gx, gy, gz = (lax.axis_index(a) for a in ("gx", "gy", "gz"))
    ends = [a > 0 for a in (gx, gy, gz)]
    tops = [a < lax.axis_size(n) - 1 for a, n in ((gx, "gx"), (gy, "gy"), (gz, "gz"))]
    f, b = xf[...], xb[...]
    x_low = jnp.where(ends[0], jnp.where(first, f, b), 0.0)
    x_high = jnp.where(tops[0], jnp.where(first, b, f), 0.0)
    f, b = yf[...], yb[...]
    y_low = jnp.where(ends[1], jnp.where(first, f, b), 0.0)
    y_high = jnp.where(tops[1], jnp.where(first, b, f), 0.0)
    z_low = jnp.where(ends[2], from_below[...], 0.0)
    z_high = jnp.where(tops[2], from_above[...], 0.0)
    lane = lanes((16, 128))
    row = rows((16, 128))
    for x in range(16):
        near = jnp.where(row == 0, y_low[x : x + 1], 0.0)
        near = near + jnp.where(row == 15, y_high[x : x + 1], 0.0)
        near = near + jnp.where(lane == 0, roll(z_low, -8 * x, 1), 0.0)
        near = near + jnp.where(lane == 127, roll(z_high, 127 - 8 * x, 1), 0.0)
        if x == 0:
            near = near + x_low
        if x == 15:
            near = near + x_high
        out[x] = rest[x] + HEAT_WEIGHTS[1] * near / (6.0 + storage[x])


def around(axis):
    n, m = lax.axis_size(axis), lax.axis_size("gz")

    def target(a, c):
        to = a + (1 if c % 2 == 0 else -1)
        return (to, c) if 0 <= to < n else (a, c ^ 1)

    forward = []
    for a in range(n):
        for c in range(m):
            to = target(a, c)
            forward.append((a * m + c, to[0] * m + to[1]))
    return forward, [(j, i) for i, j in forward]


def exchange(axis, fwd, bwd):
    forward, backward = around(axis)
    names = (axis, "gz")
    return lax.ppermute(fwd, names, forward), lax.ppermute(bwd, names, backward)


def exchange_z(up, down):
    m = lax.axis_size("gz")
    ring = [(i, (i + 1) % m) for i in range(m)]
    return lax.ppermute(up, "gz", ring), lax.ppermute(down, "gz", [(j, i) for i, j in ring])


def local(field, source, sigma, warmth, storage, partition, column):
    groups = lax.axis_size("gy") * lax.axis_size("gz")
    count = groups * (CAP + 1)
    cube = (16, 16, 128)
    face = (16, 128)
    x_message, y_message, corners = (X_LAYERS, 16, 128), (16, 32, 128), (len(HALO_X), 32, 128)
    here = (field, sigma, warmth, storage, source)
    xf, xb, yf, yb, scaled, field, sigma, warmth, storage = call(
        pack_xy,
        [x_message, x_message, y_message, y_message, (4, *cube), (3, *cube), cube, cube, cube],
        [(3, *cube), pltpu.SemaphoreType.DMA((5,))],
        name="pack_xy",
        near=True,
        in_specs=[pl.BlockSpec(memory_space=pltpu.HBM)] * 5,
    )(*(pltpu.with_memory_space_constraint(v, pltpu.HBM) for v in here))
    xf, xb = exchange("gx", xf, xb)
    yf, yb = exchange("gy", yf, yb)
    position, nodes = pl.pallas_call(
        place,
        out_shape=[
            jax.ShapeDtypeStruct((1, 256), jnp.int32),
            jax.ShapeDtypeStruct((count, 128), F32),
        ],
        compiler_params=pltpu.CompilerParams(vmem_limit_bytes=8 << 20),
        name="place",
    )(partition.reshape(1, 256), column.reshape(1, 256))
    cf, cb = call(pack_corners, [corners, corners], name="pack_corners")(
        xf, xb, position
    )
    cf, cb = exchange("gy", cf, cb)
    layer, halo = (24, 128), len(HALO_X)
    inner, inner_packed, inner_up, inner_down = call(
        pack_inner,
        [(8, 16, *layer), (16, *layer), (8, *layer), (8, *layer)],
        name="pack_inner",
        near=True,
    )(field, scaled, warmth, yf, yb)
    (swept,) = call(
        bulk,
        [(EM_SWEEPS, 3, 16, *layer)],
        name="bulk",
        near=True,
        cost_estimate=pl.CostEstimate(flops=10**9, bytes_accessed=10**7, transcendentals=0),
    )(inner)
    outer, outer_packed, up, down = call(
        pack_outer,
        [(8, halo, *layer), (halo, *layer), (X_PAIRS, *layer), (X_PAIRS, *layer)],
        name="pack_outer",
        near=True,
    )(xf, xb, cf, cb, inner_up, inner_down, swept)
    below_z, above_z = exchange_z(up, down)
    final, whole_sum, shifted, began = call(
        rest_of_bulk,
        [(3, halo, *layer), cube, cube, cube],
        [(EM_SWEEPS - 1, 3, halo, *layer)],
        name="rest_of_bulk",
        near=True,
        cost_estimate=pl.CostEstimate(flops=10**9, bytes_accessed=10**7, transcendentals=0),
    )(inner, outer, swept, xf, xb, yf, yb, warmth, storage)
    near, send, partial = call(
        edge,
        [(BLOCKS, 3, 32, 128), (count, 128), cube],
        [
            (X_ALL, *layer),
            (BLOCKS, 2, 128, 128),
            (BLOCKS, 8, 32, 128),
            (BLOCKS, 3, 32, 128),
            (3, 32, 128),
            cube,
        ],
        name="edge",
    )(
        inner_packed, outer_packed, below_z, above_z, whole_sum, shifted, sigma, began, storage,
        position, nodes,
    )
    got = lax.all_to_all(
        send.reshape(count, 1, 128), ("gy", "gz"), split_axis=0, concat_axis=0, tiled=True
    ).reshape(count, 128)
    xf, xb, yf, yb, up, down, rest = call(
        warm, [face, face, face, face, face, face, cube], [cube, cube], name="warm"
    )(got, partial, warmth, storage)
    xf, xb = exchange("gx", xf, xb)
    yf, yb = exchange("gy", yf, yb)
    below_z, above_z = exchange_z(up, down)
    (updated,) = call(finish, [cube], name="finish")(
        rest, storage, xf, xb, yf, yb, below_z, above_z
    )
    (out,) = call(
        merge,
        [(3, *cube)],
        [(BLOCKS, 128, 128)],
        name="merge",
        cost_estimate=pl.CostEstimate(flops=10**9, bytes_accessed=10**6, transcendentals=0),
    )(swept, final, near)
    return out, updated


def solution(mesh):
    in_specs = (
        P(None, "gx", "gy", "gz"),
        P(None, "gx", "gy", "gz"),
        P("gx", "gy", "gz"),
        P("gx", "gy", "gz"),
        P("gx", "gy", "gz"),
        P("gx", "gy", "gz", None, None),
        P("gx", "gy", "gz", None),
    )
    out_specs = (P(None, "gx", "gy", "gz"), P("gx", "gy", "gz"))
    return jax.shard_map(local, mesh=mesh, in_specs=in_specs, out_specs=out_specs, check_vma=False)
```

```python
import functools
import math

import jax
import jax.numpy as jnp
from jax import lax
from jax.experimental import pallas as pl
from jax.experimental.pallas import tpu as pltpu
from jax.sharding import PartitionSpec as P

EM_SWEEPS = 4
HEAT_SWEEPS = 2
CAP = 8
LOW, HIGH = 4, 5
F32 = jnp.float32

em_lower = 0.02
em_upper = 3.0
heat_lower = 0.07
heat_upper = 2.0

UP_LAYERS = ((0, 12, 4), (1, 12, 4), (2, 12, 4), (3, 13, 3), (4, 13, 3), (5, 13, 3), (6, 13, 3), (7, 15, 1))
DOWN_LAYERS = ((0, 0, 4), (1, 0, 5), (2, 0, 5), (3, 0, 3), (4, 0, 4), (5, 0, 4), (6, 0, 4), (7, 0, 1))


def spots(layers, shift):
    where, at = {}, 0
    for field, first, count in layers:
        for x in range(first, first + count):
            where[field, x + shift] = at
            at += 1
    return where, at


UP_AT, UP_COUNT = spots(UP_LAYERS, -16)
DOWN_AT, DOWN_COUNT = spots(DOWN_LAYERS, 16)
X_LAYERS = max(UP_COUNT, DOWN_COUNT)


def chebyshev_weights(lower_end, upper_end, sweep_count):
    middle = 0.5 * (upper_end + lower_end)
    radius = 0.5 * (upper_end - lower_end)
    return [
        1.0 / (middle + radius * math.cos(math.pi * (2 * number + 1) / (2 * sweep_count)))
        for number in range(sweep_count)
    ]


EM_WEIGHTS = chebyshev_weights(em_lower, em_upper, EM_SWEEPS)
HEAT_WEIGHTS = chebyshev_weights(heat_lower, heat_upper, HEAT_SWEEPS)


def on_first_core():
    return lax.rem(lax.axis_index("gz"), 2) == 0


def lanes(shape):
    return lax.broadcasted_iota(jnp.int32, shape, len(shape) - 1)


def rows(shape):
    return lax.broadcasted_iota(jnp.int32, shape, len(shape) - 2)


def roll(values, by, axis):
    size = values.shape[axis]
    by = by % size
    return values if by == 0 else pltpu.roll(values, by, axis)


def call(body, out_shapes, scratch=(), name=None, limit=8 << 20, near=False, **options):
    return pl.pallas_call(
        body,
        out_shape=[
            pltpu.VMEM(s, F32) if near else jax.ShapeDtypeStruct(s, F32) for s in out_shapes
        ],
        scratch_shapes=[pltpu.VMEM(s, F32) if isinstance(s, tuple) else s for s in scratch],
        compiler_params=pltpu.CompilerParams(vmem_limit_bytes=limit),
        name=name,
        **options,
    )


def swap_store(first, fwd, bwd, at, up, down):
    fwd[at] = jnp.where(first, up, down)
    bwd[at] = jnp.where(first, down, up)


def y_tiles(v, first, fwd, bwd, at):
    row = rows((8, 128))
    low_half = row < 4
    tops = [a[8:16] for a in v]
    ends = [a[0:8] for a in v]
    for pair in range(4):
        a, b = 2 * pair, 2 * pair + 1
        up = jnp.where(low_half, roll(tops[b], 4, 0), tops[a])
        down = jnp.where(low_half, ends[a], roll(ends[b], 4, 0))
        if pair == 3:
            down = jnp.where(row == 5, roll(ends[0], 1, 0), down)
            down = jnp.where(row == 6, roll(ends[2], 2, 0), down)
        part = pl.ds(8 * pair, 8)
        fwd[at, part] = jnp.where(first, up, down)
        bwd[at, part] = jnp.where(first, down, up)


def pack_xy(*refs):
    far, (xf, xb, yf, yb, scaled), near, arrived = refs[:5], refs[5:10], refs[10:15], refs[15]
    copies = [
        pltpu.make_async_copy(a, b, arrived.at[n]) for n, (a, b) in enumerate(zip(far, near))
    ]
    for copy in copies:
        copy.start()
    for copy in copies:
        copy.wait()
    field, sigma, warmth, _, source = near
    first = on_first_core()
    inverse = 1.0 / (4.0 + sigma[...])
    scaled[3] = inverse
    for c in range(3):
        scaled[c] = source[c] * inverse

    def layer(f, x):
        if f < 3:
            return field[f, x]
        return warmth[x] if f == 7 else scaled[f - 3, x]

    ups = [(f, x) for f, start, n in UP_LAYERS for x in range(start, start + n)]
    downs = [(f, x) for f, start, n in DOWN_LAYERS for x in range(start, start + n)]
    for at in range(X_LAYERS):
        up = layer(*ups[min(at, len(ups) - 1)])
        down = layer(*downs[min(at, len(downs) - 1)])
        swap_store(first, xf, xb, at, up, down)

    def step(x, carry):
        y_tiles([layer(f, x) for f in range(8)], first, yf, yb, x)
        return carry

    lax.fori_loop(0, 16, step, 0, unroll=4)


class Halo:
    def __init__(self, got_fwd, got_bwd):
        self.got_fwd, self.got_bwd = got_fwd, got_bwd
        self.first = on_first_core()
        gx = lax.axis_index("gx")
        self.below, self.above = gx > 0, gx < lax.axis_size("gx") - 1

    def layer(self, f, x):
        if x < 0:
            at, near, far, inside = UP_AT.get((f, x)), self.got_fwd, self.got_bwd, self.below
        else:
            at, near, far, inside = DOWN_AT.get((f, x)), self.got_bwd, self.got_fwd, self.above
        if at is None:
            return None
        return jnp.where(inside, jnp.where(self.first, near[at], far[at]), 0.0)


def pack_corners(xf, xb, position, fwd, bwd):
    del position
    halo = Halo(xf, xb)
    zero = jnp.zeros((16, 128), F32)
    for number, x in enumerate(HALO_X):
        v = [halo.layer(f, x) for f in range(7)]
        y_tiles([zero if a is None else a for a in v] + [zero], halo.first, fwd, bwd, number)


def y_halo(first, got, at, pair):
    gy = lax.axis_index("gy")
    part = pl.ds(8 * pair, 8)
    f, b = got[0][at, part], got[1][at, part]
    lower = jnp.where(gy > 0, jnp.where(first, f, b), 0.0)
    upper = jnp.where(gy < lax.axis_size("gy") - 1, jnp.where(first, b, f), 0.0)
    return lower, upper


HALO_X = tuple(range(-LOW, 0)) + tuple(range(16, 16 + HIGH))
X_ALL = LOW + 16 + HIGH
BLOCKS = 5
Y_LANES = LOW + 16 + HIGH
X_PAIRS = (X_ALL + 1) // 2


def y_slabs(first, got, at, v):
    low_half = rows((8, 128)) < 4
    window = lanes((24, 128)) // 16
    slabs, acc = [], None
    for pair in range(4):
        lower, upper = y_halo(first, got, at, pair)
        ends = [jnp.where(low_half, upper, lower)]
        if pair < 3:
            ends.append(roll(jnp.where(low_half, lower, upper), 4, 0))
        else:
            ends.append(roll(upper, 3, 0))
        for f, tile in zip((2 * pair, 2 * pair + 1), ends):
            slabs.append(jnp.concatenate([v[f], tile], axis=0))
            moved = roll(slabs[f], 16 * f + 8, 1)
            acc = moved if acc is None else jnp.where(window == f, moved, acc)
    return slabs, acc


def z_tiles(a, b):
    half = (lanes((24, 128)) // 8) % 2 == 0
    return jnp.where(half, a, roll(b, 8, 1)), jnp.where(half, roll(a, -8, 1), b)


def pack_inner(
    field, scaled, warmth, storage, xf, xb, yf, yb, whole, packed, up, down, began, padded
):
    first, gx = on_first_core(), lax.axis_index("gx")
    low_at, high_at = UP_AT[7, -1], DOWN_AT[7, 16]
    padded[0] = jnp.where(gx > 0, jnp.where(first, xf[low_at], xb[low_at]), 0.0)
    padded[17] = jnp.where(
        gx < lax.axis_size("gx") - 1, jnp.where(first, xb[high_at], xf[high_at]), 0.0
    )
    padded[1:17] = warmth[...]
    row, lane = rows((16, 128)), lanes((16, 128))

    def step(k, carry):
        windows = []
        for x in (2 * k, 2 * k + 1):
            t = warmth[x]
            lower, upper = y_halo(first, (yf, yb), x, 3)
            total = padded[x] + padded[x + 2]
            total = total + jnp.where(row == 0, lower[3:4], roll(t, 1, 0))
            total = total + jnp.where(row == 15, upper[4:5], roll(t, -1, 0))
            total = total + jnp.where(lane == 0, 0.0, roll(t, 1, 1))
            total = total + jnp.where(lane == 127, 0.0, roll(t, -1, 1))
            weight = HEAT_WEIGHTS[0] / (6.0 + storage[x])
            start = t + weight * (total - 6.0 * t)
            began[x] = start
            t = jnp.where(lane == 126, roll(start, -1, 1), t)
            t = jnp.where(lane == 125, roll(weight, -2, 1), t)
            t = jnp.where(lane == 1, roll(start, 1, 1), t)
            t = jnp.where(lane == 2, roll(weight, 2, 1), t)
            v = [field[f, x] for f in range(3)] + [scaled[f, x] for f in range(4)] + [t]
            slabs, acc = y_slabs(first, (yf, yb), x, v)
            for f in range(8):
                whole[f, x] = slabs[f]
            packed[x] = acc
            windows.append(acc)
        up[k], down[k] = z_tiles(*windows)
        return carry

    lax.fori_loop(0, 8, step, 0, unroll=2)


def pack_outer(xf, xb, cf, cb, inner_up, inner_down, swept, whole, packed, up, down):
    del swept
    halo = Halo(xf, xb)
    zero = jnp.zeros((16, 128), F32)
    windows = []
    for number, x in enumerate(HALO_X):
        v = [halo.layer(f, x) for f in range(7)]
        slabs, acc = y_slabs(
            halo.first, (cf, cb), number, [zero if a is None else a for a in v] + [zero]
        )
        for f in range(8):
            whole[f, number] = slabs[f]
        packed[number] = acc
        windows.append(acc)
    windows.append(jnp.zeros((24, 128), F32))
    for pair in range(len(windows) // 2):
        k = pair if pair < LOW // 2 else pair + 8
        up[k], down[k] = z_tiles(windows[2 * pair], windows[2 * pair + 1])
    up[LOW // 2 : LOW // 2 + 8] = inner_up[...]
    down[LOW // 2 : LOW // 2 + 8] = inner_down[...]


def twist(a, b, c, d):
    return (a - b) - (c - d)


def curls(e, e_up_y, e_up_z, e_up_x):
    (ex, ey, ez), (ex_y, ez_y), (ex_z, ey_z), (ey_x, ez_x) = e, e_up_y, e_up_z, e_up_x
    return twist(ez_y, ez, ey_z, ey), twist(ex_z, ex, ez_x, ez), twist(ey_x, ey, ex_y, ex)


def relaxed(weight, e, h, g, c, c_down_x, c_down_y, c_down_z):
    (cx, cy, cz), (cy_x, cz_x), (cx_y, cz_y), (cx_z, cy_z) = c, c_down_x, c_down_y, c_down_z
    k = twist(cz, cz_y, cy, cy_z), twist(cx, cx_z, cz, cz_x), twist(cy, cy_x, cx, cx_y)
    g = g * weight
    keep = (1.0 - weight) + 4.0 * g
    return [keep * e[f] + weight * h[f] - g * k[f] for f in range(3)]


def lane_curls(get, source, at):
    row = rows((24, 128))
    e = [get(source, f, at) for f in range(3)]
    up_y = roll(e[0], -1, 0), roll(e[2], -1, 0)
    if source == 0:
        up_y = [jnp.where(row == 19, get(0, 7, at)[16 + n : 17 + n], up_y[n]) for n in range(2)]
    up_z = roll(e[0], -1, 1), roll(e[1], -1, 1)
    return e, curls(e, up_y, up_z, (get(source, 1, at + 1), get(source, 2, at + 1)))


def lane_sweep(get, source, at, carry):
    e, c = lane_curls(get, source, at)
    h, g = [get(0, 3 + f, at) for f in range(3)], get(0, 6, at)
    down_y = roll(c[0], 1, 0), roll(c[2], 1, 0)
    down_z = roll(c[0], 1, 1), roll(c[1], 1, 1)
    new = relaxed(EM_WEIGHTS[source], e, h, g, c, carry, down_y, down_z)
    return new, (c[1], c[2])


def bulk(whole, swept):
    def get(number, f, x):
        return whole[f, x] if number == 0 else swept[number - 1, f, x]

    for number in range(EM_SWEEPS):

        def step(x, carry, number=number):
            new, carry = lane_sweep(get, number, x, carry)
            for f in range(3):
                swept[number, f, x] = new[f]
            return carry

        _, c = lane_curls(get, number, number)
        lax.fori_loop(number + 1, 15 - number, step, (c[1], c[2]), unroll=4)


def swept_low(number):
    return range(number - LOW, number)


def swept_high(number):
    return range(16 - number, 21 - number)


def rest_of_bulk(inner, outer, swept, final, whole_sum, shifted, others):
    def target(number):
        return final if number == EM_SWEEPS else others.at[number - 1]

    def get(number, f, x):
        if number == 0:
            return inner[f, x] if 0 <= x < 16 else outer[f, HALO_X.index(x)]
        if number <= x <= 15 - number:
            return swept[number - 1, f, x]
        low, high = swept_low(number), swept_high(number)
        return target(number)[f, low.index(x) if x < number else len(low) + high.index(x)]

    for number in range(EM_SWEEPS):
        to = target(number + 1)
        at = 0
        for layers in (swept_low(number + 1), swept_high(number + 1)):
            _, c = lane_curls(get, number, layers[0] - 1)
            carry = c[1], c[2]
            for x in layers:
                new, carry = lane_sweep(get, number, x, carry)
                for f in range(3):
                    to[f, at] = new[f]
                at += 1

    for x in range(16):
        ex, ey, ez = (get(EM_SWEEPS, f, x) for f in range(3))
        ey_x, ez_x = (get(EM_SWEEPS, f, x + 1) for f in (1, 2))
        ex, upright = ex * ex, ez * ez + ez_x * ez_x
        flat = (ex + roll(ex, -1, 0)) + (ey * ey + ey_x * ey_x)
        upright = upright + roll(upright, -1, 0)
        whole_sum[x] = flat[0:16] + upright[0:16]
        shifted[x] = roll(flat[0:16], -1, 1)


def of_layer(at):
    return at % BLOCKS, Y_LANES * (at // BLOCKS)


def edge(
    inner, outer, below_z, above_z, whole_sum, shifted, sigma, began, storage, position, into, nodes,
    final, send, partial, beside, stack, fields, spare, last, heat,
):
    gz = lax.axis_index("gz")
    half = (lanes((24, 128)) // 8) % 2 == 0
    has_below, has_above = gz > 0, gz < lax.axis_size("gz") - 1
    nothing = jnp.zeros((1, 128), F32)
    for block in range(BLOCKS):
        for face in range(2):
            for n in range(BLOCKS):
                stack[block, face, Y_LANES * n + 24 : Y_LANES * n + 25, :] = nothing
            stack[block, face, 125:128, :] = jnp.zeros((3, 128), F32)
    for k in range(X_PAIRS):
        lower = jnp.where(has_below, below_z[k], 0.0)
        upper = jnp.where(has_above, above_z[k], 0.0)
        for at in range(2 * k, min(2 * k + 2, X_ALL)):
            if at % 2:
                came = jnp.where(half, roll(lower, -8, 1), upper)
            else:
                came = jnp.where(half, lower, roll(upper, 8, 1))
            block, lane_at = of_layer(at)
            x = at - LOW
            if 0 <= x < 16:
                beside[x] = came[0:16]
            own = inner[x] if 0 <= x < 16 else outer[HALO_X.index(x)]
            for face in range(2):
                window = jnp.where(half, came, own) if face else jnp.where(half, own, came)
                stack[block, face, lane_at : lane_at + 24, :] = roll(window, 4, 0)
    for block in range(BLOCKS):
        for face in range(2):
            turned = stack[block, face].T
            for f in range(8):
                fields[block, f, 16 * face : 16 * face + 16, :] = turned[16 * f : 16 * f + 16]
    top = lanes((32, 128)) % Y_LANES == 24
    for block in range(BLOCKS):
        extra = fields[block, 7]
        for f, by in ((0, 4), (2, 3)):
            fields[block, f] = jnp.where(top, roll(extra, by, 1), fields[block, f])

    buffers = (fields, spare, final, spare, final)

    def ahead(source, block, f):
        if block < BLOCKS - 1:
            return source[block + 1, f]
        return roll(source[0, f], -Y_LANES, 1)

    def curls_at(source, block):
        e = [source[block, f] for f in range(3)]
        up_y = roll(e[0], -1, 1), roll(e[2], -1, 1)
        up_z = roll(e[0], -1, 0), roll(e[1], -1, 0)
        return e, curls(e, up_y, up_z, (ahead(source, block, 1), ahead(source, block, 2)))

    for number, weight in enumerate(EM_WEIGHTS):
        source, target = buffers[number], buffers[number + 1]
        _, c = curls_at(source, BLOCKS - 1)
        for f in range(3):
            last[f] = c[f]
        before = roll(c[1], Y_LANES, 1), roll(c[2], Y_LANES, 1)
        for block in range(BLOCKS):
            if block < BLOCKS - 1:
                e, c = curls_at(source, block)
            else:
                e, c = [source[block, f] for f in range(3)], [last[f] for f in range(3)]
            h, g = [fields[block, 3 + f] for f in range(3)], fields[block, 6]
            down_y = roll(c[0], 1, 1), roll(c[2], 1, 1)
            down_z = roll(c[0], 1, 0), roll(c[1], 1, 0)
            new = relaxed(weight, e, h, g, c, before, down_y, down_z)
            for f in range(3):
                target[block, f] = new[f]
            before = c[1], c[2]

    for block in range(BLOCKS):
        ex, ey, ez = (final[block, f] * final[block, f] for f in range(3))
        ey_x, ez_x = (ahead(final, block, f) for f in (1, 2))
        flat, upright = (ex + roll(ex, -1, 1)) + (ey + ey_x * ey_x), ez + ez_x * ez_x
        both = flat + (upright + roll(upright, -1, 1))
        stack[block, 0, 0:8, :] = both[24:32]
        stack[block, 0, 120:128, :] = both[0:8]
        stack[block, 0, 59:64, :] = flat[4:9]
        stack[block, 0, 64:67, :] = flat[25:28]
    for block in range(BLOCKS):
        stack[block, 1] = stack[block, 0].T
    lane = lanes((16, 128))
    for x in range(16):
        block, lane_at = of_layer(x + LOW)
        near = stack[block, 1, lane_at + LOW : lane_at + LOW + 16, :]
        here = jnp.where((lane < 4) | (lane >= 124), near, whole_sum[x])
        above = jnp.where((lane < 3) | (lane >= 123), roll(near, 64, 1), shifted[x])
        heat[x] = sigma[x] * (0.25 * (here + above))

    count = send.shape[0]
    columns = heat[...].reshape(256, 128)
    total = nodes[...]
    for n, left in enumerate((columns, columns[:, 127:128] * into[0], columns[:, 0:1] * into[1])):
        spread = (rows((count, 256)) == position[n : n + 1, :]).astype(jnp.bfloat16)
        for _ in range(3):
            piece = left.astype(jnp.bfloat16)
            left = left - piece.astype(F32)
            total = total + jnp.dot(spread, piece, preferred_element_type=F32)
    send[...] = total

    for x in range(16):
        ends = beside[x]
        halo = jnp.where(lane == 0, roll(ends, 9, 1), jnp.where(lane == 127, roll(ends, 7, 1), 0.0))
        partial[x] = began[x] + HEAT_WEIGHTS[0] * halo / (6.0 + storage[x])


def merge(swept, final, near, out, stack):
    for block in range(BLOCKS):
        for f in range(3):
            stack[block, 32 * f : 32 * f + 8, :] = near[block, f, 24:32, :]
            at = (32 * f - 8) % 128
            stack[block, at : at + 8, :] = near[block, f, 0:8, :]
    for block in range(BLOCKS):
        stack[block] = stack[block].T
    lane = lanes((16, 128))
    outer = (lane < 4) | (lane >= 124)
    for x in range(16):
        block, lane_at = of_layer(x + LOW)
        windows = stack[block, lane_at + LOW : lane_at + LOW + 16, :]
        for f in range(3):
            if EM_SWEEPS <= x <= 15 - EM_SWEEPS:
                inner = swept[EM_SWEEPS - 1, f, x, 0:16, :]
            else:
                low, high = swept_low(EM_SWEEPS), swept_high(EM_SWEEPS)
                at = low.index(x) if x in low else len(low) + high.index(x)
                inner = final[f, at, 0:16, :]
            out[f, x] = jnp.where(outer, roll(windows, -32 * f, 1), inner)


BELOW, ABOVE = CAP, 3 * CAP


def place(owners, columns, position, into, nodes):
    planes = lax.axis_size("gz")
    groups = lax.axis_size("gy") * planes
    owner, column = owners[...], columns[...]
    member = rows((groups, 256)) == owner
    earlier = (rows((256, 256)) < lanes((256, 256))).astype(jnp.bfloat16)
    before = jnp.dot(member.astype(jnp.bfloat16), earlier, preferred_element_type=F32)
    rank = jnp.sum(jnp.where(member, before, 0.0), axis=0, keepdims=True).astype(jnp.int32)
    count = nodes.shape[0]
    depth = lax.rem(owner, planes)
    listing = owner * (CAP + 1) + CAP
    to_above = jnp.where(depth < planes - 1, listing + (CAP + 1), -1)
    to_below = jnp.where(depth > 0, listing - (CAP + 1), -1)
    position[0:1, :] = owner * (CAP + 1) + rank
    position[1:2, :] = to_above
    position[2:3, :] = to_below
    total = None
    for target, start in ((listing, 0), (to_above, BELOW), (to_below, ABOVE)):
        spread = (rows((count, 256)) == target).astype(jnp.bfloat16)
        listed = jnp.where(rows((128, 256)) == rank + start, column + 1, 0).astype(F32)
        term = lax.dot_general(
            spread,
            listed.astype(jnp.bfloat16),
            (((1,), (1,)), ((), ())),
            preferred_element_type=F32,
        )
        total = term if total is None else total + term
    nodes[...] = total
    for n, start in enumerate((BELOW + CAP, ABOVE + CAP)):
        into[n] = (rows((128, 256)) == rank + start).astype(F32).T


def warm(got, partial, warmth, storage, xf, xb, yf, yb, rest, heat, mid):
    first = on_first_core()
    groups = got.shape[0] // (CAP + 1)
    ids = got[pl.ds(CAP, groups, stride=CAP + 1), :].T
    node = rows((256, 1)) + 1
    per = max(1, 128 // groups)
    total = None
    for r in range(0, CAP, per):
        number = jnp.concatenate([ids[r + n : r + n + 1, :] for n in range(per)], axis=1)
        hit = (number == node.astype(F32)).astype(jnp.bfloat16)
        left = jnp.concatenate(
            [got[pl.ds(r + n, groups, stride=CAP + 1), :] for n in range(per)], axis=0
        )
        for _ in range(3):
            piece = left.astype(jnp.bfloat16)
            left = left - piece.astype(F32)
            term = jnp.dot(hit, piece, preferred_element_type=F32)
            total = term if total is None else total + term
    heat[...] = total.reshape(16, 16, 128)
    lane = lanes((16, 128))
    row = rows((16, 128))
    for x in range(16):
        mid[x] = partial[x] + HEAT_WEIGHTS[0] * heat[x] / (6.0 + storage[x])
    xf[...] = jnp.where(first, mid[15], mid[0])
    xb[...] = jnp.where(first, mid[0], mid[15])
    for x in range(16):
        t = mid[x]
        top, end = t[15:16], t[0:1]
        yf[x : x + 1] = jnp.where(first, top, end)
        yb[x : x + 1] = jnp.where(first, end, top)
        near = jnp.where(row == 0, 0.0, roll(t, 1, 0)) + jnp.where(row == 15, 0.0, roll(t, -1, 0))
        near = near + jnp.where(lane == 0, 0.0, roll(t, 1, 1))
        near = near + jnp.where(lane == 127, 0.0, roll(t, -1, 1))
        if x > 0:
            near = near + mid[x - 1]
        if x < 15:
            near = near + mid[x + 1]
        s = storage[x]
        push = s * warmth[x] + heat[x] - (6.0 + s) * t + near
        rest[x] = t + HEAT_WEIGHTS[1] * push / (6.0 + s)


def beyond_z(got, beside, warmth, out):
    groups = got.shape[0] // (CAP + 1)
    listing = got[pl.ds(CAP, groups, stride=CAP + 1), :].T
    node = (rows((256, 1)) + 1).astype(F32)
    per = max(1, 128 // groups)

    def beside_rows(at):
        return jnp.concatenate([listing[at + n : at + n + 1, :] for n in range(per)], axis=1)

    heat = []
    for start in (BELOW, ABOVE):
        total = None
        for r in range(0, CAP, per):
            hit = beside_rows(start + r) == node
            term = jnp.where(hit, beside_rows(start + CAP + r), 0.0)
            total = term if total is None else total + term
        heat.append(jnp.sum(total, axis=1, keepdims=True))
    lane = lanes((16, 128))
    for x in range(16):
        ends, t = beside[x], warmth[x]
        part = slice(16 * x, 16 * x + 16)
        low = ends[:, 118:119] + ends[:, 117:118] * (t[:, 0:1] + heat[0][part])
        high = ends[:, 121:122] + ends[:, 122:123] * (t[:, 127:128] + heat[1][part])
        out[x] = jnp.where(lane == 0, low, jnp.where(lane == 127, high, 0.0))


def finish(rest, storage, xf, xb, yf, yb, beyond, out):
    first = on_first_core()
    gx, gy = lax.axis_index("gx"), lax.axis_index("gy")
    f, b = xf[...], xb[...]
    x_low = jnp.where(gx > 0, jnp.where(first, f, b), 0.0)
    x_high = jnp.where(gx < lax.axis_size("gx") - 1, jnp.where(first, b, f), 0.0)
    f, b = yf[...], yb[...]
    y_low = jnp.where(gy > 0, jnp.where(first, f, b), 0.0)
    y_high = jnp.where(gy < lax.axis_size("gy") - 1, jnp.where(first, b, f), 0.0)
    row = rows((16, 128))
    for x in range(16):
        near = beyond[x] + jnp.where(row == 0, y_low[x : x + 1], 0.0)
        near = near + jnp.where(row == 15, y_high[x : x + 1], 0.0)
        if x == 0:
            near = near + x_low
        if x == 15:
            near = near + x_high
        out[x] = rest[x] + HEAT_WEIGHTS[1] * near / (6.0 + storage[x])


def around(axis):
    n, m = lax.axis_size(axis), lax.axis_size("gz")

    def target(a, c):
        to = a + (1 if c % 2 == 0 else -1)
        return (to, c) if 0 <= to < n else (a, c ^ 1)

    forward = []
    for a in range(n):
        for c in range(m):
            to = target(a, c)
            forward.append((a * m + c, to[0] * m + to[1]))
    return forward, [(j, i) for i, j in forward]


def exchange(axis, fwd, bwd):
    forward, backward = around(axis)
    names = (axis, "gz")
    return lax.ppermute(fwd, names, forward), lax.ppermute(bwd, names, backward)


def exchange_z(up, down):
    m = lax.axis_size("gz")
    ring = [(i, (i + 1) % m) for i in range(m)]
    return lax.ppermute(up, "gz", ring), lax.ppermute(down, "gz", [(j, i) for i, j in ring])


def local(field, source, sigma, warmth, storage, partition, column):
    groups = lax.axis_size("gy") * lax.axis_size("gz")
    count = groups * (CAP + 1)
    cube = (16, 16, 128)
    face = (16, 128)
    x_message, y_message, corners = (X_LAYERS, 16, 128), (16, 32, 128), (len(HALO_X), 32, 128)
    here = (field, sigma, warmth, storage, source)
    xf, xb, yf, yb, scaled, field, sigma, warmth, storage = call(
        pack_xy,
        [x_message, x_message, y_message, y_message, (4, *cube), (3, *cube), cube, cube, cube],
        [(3, *cube), pltpu.SemaphoreType.DMA((5,))],
        name="pack_xy",
        near=True,
        in_specs=[pl.BlockSpec(memory_space=pltpu.HBM)] * 5,
    )(*(pltpu.with_memory_space_constraint(v, pltpu.HBM) for v in here))
    xf, xb = exchange("gx", xf, xb)
    yf, yb = exchange("gy", yf, yb)
    position, into, nodes = pl.pallas_call(
        place,
        out_shape=[
            jax.ShapeDtypeStruct((3, 256), jnp.int32),
            jax.ShapeDtypeStruct((2, 256, 128), F32),
            jax.ShapeDtypeStruct((count, 128), F32),
        ],
        compiler_params=pltpu.CompilerParams(vmem_limit_bytes=8 << 20),
        name="place",
    )(partition.reshape(1, 256), column.reshape(1, 256))
    cf, cb = call(pack_corners, [corners, corners], name="pack_corners")(
        xf, xb, position
    )
    cf, cb = exchange("gy", cf, cb)
    layer, halo = (24, 128), len(HALO_X)
    inner, inner_packed, inner_up, inner_down, began = call(
        pack_inner,
        [(8, 16, *layer), (16, *layer), (8, *layer), (8, *layer), cube],
        [(18, 16, 128)],
        name="pack_inner",
        near=True,
    )(field, scaled, warmth, storage, xf, xb, yf, yb)
    (swept,) = call(
        bulk,
        [(EM_SWEEPS, 3, 16, *layer)],
        name="bulk",
        near=True,
        cost_estimate=pl.CostEstimate(flops=10**9, bytes_accessed=10**7, transcendentals=0),
    )(inner)
    outer, outer_packed, up, down = call(
        pack_outer,
        [(8, halo, *layer), (halo, *layer), (X_PAIRS, *layer), (X_PAIRS, *layer)],
        name="pack_outer",
        near=True,
    )(xf, xb, cf, cb, inner_up, inner_down, swept)
    below_z, above_z = exchange_z(up, down)
    final, whole_sum, shifted = call(
        rest_of_bulk,
        [(3, halo, *layer), cube, cube],
        [(EM_SWEEPS - 1, 3, halo, *layer)],
        name="rest_of_bulk",
        near=True,
        cost_estimate=pl.CostEstimate(flops=10**9, bytes_accessed=10**7, transcendentals=0),
    )(inner, outer, swept)
    near, send, partial, beside = call(
        edge,
        [(BLOCKS, 3, 32, 128), (count, 128), cube, cube],
        [
            (BLOCKS, 2, 128, 128),
            (BLOCKS, 8, 32, 128),
            (BLOCKS, 3, 32, 128),
            (3, 32, 128),
            cube,
        ],
        name="edge",
    )(
        inner_packed, outer_packed, below_z, above_z, whole_sum, shifted, sigma, began, storage,
        position, into, nodes,
    )
    got = lax.all_to_all(
        send.reshape(count, 1, 128), ("gy", "gz"), split_axis=0, concat_axis=0, tiled=True
    ).reshape(count, 128)
    xf, xb, yf, yb, rest = call(
        warm, [face, face, face, face, cube], [cube, cube], name="warm"
    )(got, partial, warmth, storage)
    xf, xb = exchange("gx", xf, xb)
    yf, yb = exchange("gy", yf, yb)
    (beyond,) = call(
        beyond_z,
        [cube],
        name="beyond_z",
        near=True,
        cost_estimate=pl.CostEstimate(flops=10**9, bytes_accessed=10**6, transcendentals=0),
    )(got, beside, warmth)
    (updated,) = call(finish, [cube], name="finish")(rest, storage, xf, xb, yf, yb, beyond)
    (out,) = call(
        merge,
        [(3, *cube)],
        [(BLOCKS, 128, 128)],
        name="merge",
        cost_estimate=pl.CostEstimate(flops=10**9, bytes_accessed=10**6, transcendentals=0),
    )(swept, final, near)
    return out, updated


def solution(mesh):
    in_specs = (
        P(None, "gx", "gy", "gz"),
        P(None, "gx", "gy", "gz"),
        P("gx", "gy", "gz"),
        P("gx", "gy", "gz"),
        P("gx", "gy", "gz"),
        P("gx", "gy", "gz", None, None),
        P("gx", "gy", "gz", None),
    )
    out_specs = (P(None, "gx", "gy", "gz"), P("gx", "gy", "gz"))
    return jax.shard_map(local, mesh=mesh, in_specs=in_specs, out_specs=out_specs, check_vma=False)
```

```python
import functools
import math

import jax
import jax.numpy as jnp
from jax import lax
from jax.experimental import pallas as pl
from jax.experimental.pallas import tpu as pltpu
from jax.sharding import PartitionSpec as P

EM_SWEEPS = 4
HEAT_SWEEPS = 2
CAP = 8
LOW, HIGH = 4, 5
F32 = jnp.float32

em_lower = 0.02
em_upper = 3.0
heat_lower = 0.07
heat_upper = 2.0

UP_LAYERS = ((0, 12, 4), (1, 12, 4), (2, 12, 4), (3, 13, 3), (4, 13, 3), (5, 13, 3), (6, 13, 3), (7, 15, 1))
DOWN_LAYERS = ((0, 0, 4), (1, 0, 5), (2, 0, 5), (3, 0, 3), (4, 0, 4), (5, 0, 4), (6, 0, 4), (7, 0, 1))


def spots(layers, shift):
    where, at = {}, 0
    for field, first, count in layers:
        for x in range(first, first + count):
            where[field, x + shift] = at
            at += 1
    return where, at


UP_AT, UP_COUNT = spots(UP_LAYERS, -16)
DOWN_AT, DOWN_COUNT = spots(DOWN_LAYERS, 16)
X_LAYERS = max(UP_COUNT, DOWN_COUNT)


def chebyshev_weights(lower_end, upper_end, sweep_count):
    middle = 0.5 * (upper_end + lower_end)
    radius = 0.5 * (upper_end - lower_end)
    return [
        1.0 / (middle + radius * math.cos(math.pi * (2 * number + 1) / (2 * sweep_count)))
        for number in range(sweep_count)
    ]


EM_WEIGHTS = chebyshev_weights(em_lower, em_upper, EM_SWEEPS)
HEAT_WEIGHTS = chebyshev_weights(heat_lower, heat_upper, HEAT_SWEEPS)


def on_first_core():
    return lax.rem(lax.axis_index("gz"), 2) == 0


def lanes(shape):
    return lax.broadcasted_iota(jnp.int32, shape, len(shape) - 1)


def rows(shape):
    return lax.broadcasted_iota(jnp.int32, shape, len(shape) - 2)


def roll(values, by, axis):
    size = values.shape[axis]
    by = by % size
    return values if by == 0 else pltpu.roll(values, by, axis)


def call(body, out_shapes, scratch=(), name=None, limit=8 << 20, near=False, **options):
    return pl.pallas_call(
        body,
        out_shape=[
            pltpu.VMEM(s, F32) if near else jax.ShapeDtypeStruct(s, F32) for s in out_shapes
        ],
        scratch_shapes=[pltpu.VMEM(s, F32) if isinstance(s, tuple) else s for s in scratch],
        compiler_params=pltpu.CompilerParams(vmem_limit_bytes=limit),
        name=name,
        **options,
    )


def swap_store(first, fwd, bwd, at, up, down):
    fwd[at] = jnp.where(first, up, down)
    bwd[at] = jnp.where(first, down, up)


def y_tiles(v, first, fwd, bwd, at):
    row = rows((8, 128))
    low_half = row < 4
    tops = [a[8:16] for a in v]
    ends = [a[0:8] for a in v]
    for pair in range(4):
        a, b = 2 * pair, 2 * pair + 1
        up = jnp.where(low_half, roll(tops[b], 4, 0), tops[a])
        down = jnp.where(low_half, ends[a], roll(ends[b], 4, 0))
        if pair == 3:
            down = jnp.where(row == 5, roll(ends[0], 1, 0), down)
            down = jnp.where(row == 6, roll(ends[2], 2, 0), down)
        part = pl.ds(8 * pair, 8)
        fwd[at, part] = jnp.where(first, up, down)
        bwd[at, part] = jnp.where(first, down, up)


def pack_xy(*refs):
    far, (xf, xb, yf, yb, scaled), near, arrived = refs[:5], refs[5:10], refs[10:15], refs[15]
    copies = [
        pltpu.make_async_copy(a, b, arrived.at[n]) for n, (a, b) in enumerate(zip(far, near))
    ]
    for copy in copies:
        copy.start()
    for copy in copies:
        copy.wait()
    field, sigma, warmth, _, source = near
    first = on_first_core()
    inverse = 1.0 / (4.0 + sigma[...])
    scaled[3] = inverse
    for c in range(3):
        scaled[c] = source[c] * inverse

    def layer(f, x):
        if f < 3:
            return field[f, x]
        return warmth[x] if f == 7 else scaled[f - 3, x]

    ups = [(f, x) for f, start, n in UP_LAYERS for x in range(start, start + n)]
    downs = [(f, x) for f, start, n in DOWN_LAYERS for x in range(start, start + n)]
    for at in range(X_LAYERS):
        up = layer(*ups[min(at, len(ups) - 1)])
        down = layer(*downs[min(at, len(downs) - 1)])
        swap_store(first, xf, xb, at, up, down)

    def step(x, carry):
        y_tiles([layer(f, x) for f in range(8)], first, yf, yb, x)
        return carry

    lax.fori_loop(0, 16, step, 0, unroll=4)


class Halo:
    def __init__(self, got_fwd, got_bwd):
        self.got_fwd, self.got_bwd = got_fwd, got_bwd
        self.first = on_first_core()
        gx = lax.axis_index("gx")
        self.below, self.above = gx > 0, gx < lax.axis_size("gx") - 1

    def layer(self, f, x):
        if x < 0:
            at, near, far, inside = UP_AT.get((f, x)), self.got_fwd, self.got_bwd, self.below
        else:
            at, near, far, inside = DOWN_AT.get((f, x)), self.got_bwd, self.got_fwd, self.above
        if at is None:
            return None
        return jnp.where(inside, jnp.where(self.first, near[at], far[at]), 0.0)


def pack_corners(xf, xb, position, fwd, bwd):
    del position
    halo = Halo(xf, xb)
    zero = jnp.zeros((16, 128), F32)
    for number, x in enumerate(HALO_X):
        v = [halo.layer(f, x) for f in range(7)]
        y_tiles([zero if a is None else a for a in v] + [zero], halo.first, fwd, bwd, number)


def y_halo(first, got, at, pair):
    gy = lax.axis_index("gy")
    part = pl.ds(8 * pair, 8)
    f, b = got[0][at, part], got[1][at, part]
    lower = jnp.where(gy > 0, jnp.where(first, f, b), 0.0)
    upper = jnp.where(gy < lax.axis_size("gy") - 1, jnp.where(first, b, f), 0.0)
    return lower, upper


HALO_X = tuple(range(-LOW, 0)) + tuple(range(16, 16 + HIGH))
X_ALL = LOW + 16 + HIGH
BLOCKS = 5
Y_LANES = LOW + 16 + HIGH
X_PAIRS = (X_ALL + 1) // 2


def y_slabs(first, got, at, v):
    low_half = rows((8, 128)) < 4
    window = lanes((24, 128)) // 16
    slabs, acc = [], None
    for pair in range(4):
        lower, upper = y_halo(first, got, at, pair)
        ends = [jnp.where(low_half, upper, lower)]
        if pair < 3:
            ends.append(roll(jnp.where(low_half, lower, upper), 4, 0))
        else:
            ends.append(roll(upper, 3, 0))
        for f, tile in zip((2 * pair, 2 * pair + 1), ends):
            slabs.append(jnp.concatenate([v[f], tile], axis=0))
            moved = roll(slabs[f], 16 * f + 8, 1)
            acc = moved if acc is None else jnp.where(window == f, moved, acc)
    return slabs, acc


def z_tiles(a, b):
    half = (lanes((24, 128)) // 8) % 2 == 0
    return jnp.where(half, a, roll(b, 8, 1)), jnp.where(half, roll(a, -8, 1), b)


def pack_inner(
    field, scaled, warmth, storage, xf, xb, yf, yb, whole, packed, up, down, began, padded
):
    first, gx = on_first_core(), lax.axis_index("gx")
    low_at, high_at = UP_AT[7, -1], DOWN_AT[7, 16]
    padded[0] = jnp.where(gx > 0, jnp.where(first, xf[low_at], xb[low_at]), 0.0)
    padded[17] = jnp.where(
        gx < lax.axis_size("gx") - 1, jnp.where(first, xb[high_at], xf[high_at]), 0.0
    )
    padded[1:17] = warmth[...]
    row, lane = rows((16, 128)), lanes((16, 128))

    def step(k, carry):
        windows = []
        for x in (2 * k, 2 * k + 1):
            t = warmth[x]
            lower, upper = y_halo(first, (yf, yb), x, 3)
            total = padded[x] + padded[x + 2]
            total = total + jnp.where(row == 0, lower[3:4], roll(t, 1, 0))
            total = total + jnp.where(row == 15, upper[4:5], roll(t, -1, 0))
            total = total + jnp.where(lane == 0, 0.0, roll(t, 1, 1))
            total = total + jnp.where(lane == 127, 0.0, roll(t, -1, 1))
            weight = HEAT_WEIGHTS[0] / (6.0 + storage[x])
            start = t + weight * (total - 6.0 * t)
            began[x] = start
            t = jnp.where(lane == 126, roll(start, -1, 1), t)
            t = jnp.where(lane == 125, roll(weight, -2, 1), t)
            t = jnp.where(lane == 1, roll(start, 1, 1), t)
            t = jnp.where(lane == 2, roll(weight, 2, 1), t)
            v = [field[f, x] for f in range(3)] + [scaled[f, x] for f in range(4)] + [t]
            slabs, acc = y_slabs(first, (yf, yb), x, v)
            for f in range(8):
                whole[f, x] = slabs[f]
            packed[x] = acc
            windows.append(acc)
        up[k], down[k] = z_tiles(*windows)
        return carry

    lax.fori_loop(0, 8, step, 0, unroll=2)


def pack_outer(xf, xb, cf, cb, inner_up, inner_down, swept, whole, packed, up, down):
    del swept
    halo = Halo(xf, xb)
    zero = jnp.zeros((16, 128), F32)
    windows = []
    for number, x in enumerate(HALO_X):
        v = [halo.layer(f, x) for f in range(7)]
        slabs, acc = y_slabs(
            halo.first, (cf, cb), number, [zero if a is None else a for a in v] + [zero]
        )
        for f in range(8):
            whole[f, number] = slabs[f]
        packed[number] = acc
        windows.append(acc)
    windows.append(jnp.zeros((24, 128), F32))
    for pair in range(len(windows) // 2):
        k = pair if pair < LOW // 2 else pair + 8
        up[k], down[k] = z_tiles(windows[2 * pair], windows[2 * pair + 1])
    up[LOW // 2 : LOW // 2 + 8] = inner_up[...]
    down[LOW // 2 : LOW // 2 + 8] = inner_down[...]


def twist(a, b, c, d):
    return (a - b) - (c - d)


def curls(e, e_up_y, e_up_z, e_up_x):
    (ex, ey, ez), (ex_y, ez_y), (ex_z, ey_z), (ey_x, ez_x) = e, e_up_y, e_up_z, e_up_x
    return twist(ez_y, ez, ey_z, ey), twist(ex_z, ex, ez_x, ez), twist(ey_x, ey, ex_y, ex)


def relaxed(weight, e, h, g, c, c_down_x, c_down_y, c_down_z):
    (cx, cy, cz), (cy_x, cz_x), (cx_y, cz_y), (cx_z, cy_z) = c, c_down_x, c_down_y, c_down_z
    k = twist(cz, cz_y, cy, cy_z), twist(cx, cx_z, cz, cz_x), twist(cy, cy_x, cx, cx_y)
    g = g * weight
    keep = (1.0 - weight) + 4.0 * g
    return [keep * e[f] + weight * h[f] - g * k[f] for f in range(3)]


def lane_curls(get, source, at):
    row = rows((24, 128))
    e = [get(source, f, at) for f in range(3)]
    up_y = roll(e[0], -1, 0), roll(e[2], -1, 0)
    if source == 0:
        up_y = [jnp.where(row == 19, get(0, 7, at)[16 + n : 17 + n], up_y[n]) for n in range(2)]
    up_z = roll(e[0], -1, 1), roll(e[1], -1, 1)
    return e, curls(e, up_y, up_z, (get(source, 1, at + 1), get(source, 2, at + 1)))


def lane_sweep(get, source, at, carry):
    e, c = lane_curls(get, source, at)
    h, g = [get(0, 3 + f, at) for f in range(3)], get(0, 6, at)
    down_y = roll(c[0], 1, 0), roll(c[2], 1, 0)
    down_z = roll(c[0], 1, 1), roll(c[1], 1, 1)
    new = relaxed(EM_WEIGHTS[source], e, h, g, c, carry, down_y, down_z)
    return new, (c[1], c[2])


def bulk(whole, swept):
    def get(number, f, x):
        return whole[f, x] if number == 0 else swept[number - 1, f, x]

    for number in range(EM_SWEEPS):

        def step(x, carry, number=number):
            new, carry = lane_sweep(get, number, x, carry)
            for f in range(3):
                swept[number, f, x] = new[f]
            return carry

        _, c = lane_curls(get, number, number)
        lax.fori_loop(number + 1, 15 - number, step, (c[1], c[2]), unroll=4)


def swept_low(number):
    return range(number - LOW, number)


def swept_high(number):
    return range(16 - number, 21 - number)


def rest_of_bulk(inner, outer, swept, final, whole_sum, shifted, others):
    def target(number):
        return final if number == EM_SWEEPS else others.at[number - 1]

    def get(number, f, x):
        if number == 0:
            return inner[f, x] if 0 <= x < 16 else outer[f, HALO_X.index(x)]
        if number <= x <= 15 - number:
            return swept[number - 1, f, x]
        low, high = swept_low(number), swept_high(number)
        return target(number)[f, low.index(x) if x < number else len(low) + high.index(x)]

    for number in range(EM_SWEEPS):
        to = target(number + 1)
        at = 0
        for layers in (swept_low(number + 1), swept_high(number + 1)):
            _, c = lane_curls(get, number, layers[0] - 1)
            carry = c[1], c[2]
            for x in layers:
                new, carry = lane_sweep(get, number, x, carry)
                for f in range(3):
                    to[f, at] = new[f]
                at += 1

    for x in range(16):
        ex, ey, ez = (get(EM_SWEEPS, f, x) for f in range(3))
        ey_x, ez_x = (get(EM_SWEEPS, f, x + 1) for f in (1, 2))
        ex, upright = ex * ex, ez * ez + ez_x * ez_x
        flat = (ex + roll(ex, -1, 0)) + (ey * ey + ey_x * ey_x)
        upright = upright + roll(upright, -1, 0)
        whole_sum[x] = flat[0:16] + upright[0:16]
        shifted[x] = roll(flat[0:16], -1, 1)


def of_layer(at):
    return at % BLOCKS, Y_LANES * (at // BLOCKS)


def clear_gaps(stack):
    for block in range(BLOCKS):
        for n in range(BLOCKS):
            at = Y_LANES * n + 24
            stack[block, at : at + 1, :] = jnp.zeros((1, 128), F32)
        stack[block, 125:128, :] = jnp.zeros((3, 128), F32)


def put_layer(stack, at, windows):
    block, lane_at = of_layer(at)
    stack[block, lane_at : lane_at + 24, :] = roll(windows, 4, 0)


def turn(inner, outer, turned, stack):
    clear_gaps(stack)
    for at in range(X_ALL):
        x = at - LOW
        put_layer(stack, at, inner[x] if 0 <= x < 16 else outer[HALO_X.index(x)])
    for block in range(BLOCKS):
        turned[block] = stack[block].T


def edge(
    own, below_z, above_z, whole_sum, shifted, sigma, position, into, nodes,
    final, send, beside, stack, fields, spare, last, heat,
):
    gz = lax.axis_index("gz")
    half = (lanes((24, 128)) // 8) % 2 == 0
    has_below, has_above = gz > 0, gz < lax.axis_size("gz") - 1
    clear_gaps(stack)
    for k in range(X_PAIRS):
        lower = jnp.where(has_below, below_z[k], 0.0)
        upper = jnp.where(has_above, above_z[k], 0.0)
        for at in range(2 * k, min(2 * k + 2, X_ALL)):
            if at % 2:
                came = jnp.where(half, roll(lower, -8, 1), upper)
            else:
                came = jnp.where(half, lower, roll(upper, 8, 1))
            if 0 <= at - LOW < 16:
                beside[at - LOW] = came[0:16]
            put_layer(stack, at, came)
    for block in range(BLOCKS):
        came = stack[block].T
        for f in range(8):
            for n, part in enumerate((own, came, came, own)):
                at = 16 * f + 8 * (n % 2)
                values = part[block, at : at + 8, :] if part is own else part[at : at + 8]
                fields[block, f, 8 * n : 8 * n + 8, :] = values
    top = lanes((32, 128)) % Y_LANES == 24
    for block in range(BLOCKS):
        extra = fields[block, 7]
        for f, by in ((0, 4), (2, 3)):
            fields[block, f] = jnp.where(top, roll(extra, by, 1), fields[block, f])

    buffers = (fields, spare, final, spare, final)

    def ahead(source, block, f):
        if block < BLOCKS - 1:
            return source[block + 1, f]
        return roll(source[0, f], -Y_LANES, 1)

    def curls_at(source, block):
        e = [source[block, f] for f in range(3)]
        up_y = roll(e[0], -1, 1), roll(e[2], -1, 1)
        up_z = roll(e[0], -1, 0), roll(e[1], -1, 0)
        return e, curls(e, up_y, up_z, (ahead(source, block, 1), ahead(source, block, 2)))

    for number, weight in enumerate(EM_WEIGHTS):
        source, target = buffers[number], buffers[number + 1]
        _, c = curls_at(source, BLOCKS - 1)
        for f in range(3):
            last[f] = c[f]
        before = roll(c[1], Y_LANES, 1), roll(c[2], Y_LANES, 1)
        for block in range(BLOCKS):
            if block < BLOCKS - 1:
                e, c = curls_at(source, block)
            else:
                e, c = [source[block, f] for f in range(3)], [last[f] for f in range(3)]
            h, g = [fields[block, 3 + f] for f in range(3)], fields[block, 6]
            down_y = roll(c[0], 1, 1), roll(c[2], 1, 1)
            down_z = roll(c[0], 1, 0), roll(c[1], 1, 0)
            new = relaxed(weight, e, h, g, c, before, down_y, down_z)
            for f in range(3):
                target[block, f] = new[f]
            before = c[1], c[2]

    for block in range(BLOCKS):
        ex, ey, ez = (final[block, f] * final[block, f] for f in range(3))
        ey_x, ez_x = (ahead(final, block, f) for f in (1, 2))
        flat, upright = (ex + roll(ex, -1, 1)) + (ey + ey_x * ey_x), ez + ez_x * ez_x
        both = flat + (upright + roll(upright, -1, 1))
        stack[block, 0:8, :] = both[24:32]
        stack[block, 120:128, :] = both[0:8]
        stack[block, 59:64, :] = flat[4:9]
        stack[block, 64:67, :] = flat[25:28]
    for block in range(BLOCKS):
        stack[block] = stack[block].T
    lane = lanes((16, 128))
    for x in range(16):
        block, lane_at = of_layer(x + LOW)
        near = stack[block, lane_at + LOW : lane_at + LOW + 16, :]
        here = jnp.where((lane < 4) | (lane >= 124), near, whole_sum[x])
        above = jnp.where((lane < 3) | (lane >= 123), roll(near, 64, 1), shifted[x])
        heat[x] = sigma[x] * (0.25 * (here + above))

    def spread_out(target, columns, total):
        hit = (rows((total.shape[0], columns.shape[0])) == target).astype(jnp.bfloat16)
        for _ in range(3):
            piece = columns.astype(jnp.bfloat16)
            columns = columns - piece.astype(F32)
            total = total + jnp.dot(hit, piece, preferred_element_type=F32)
        return total

    columns = heat[...].reshape(256, 128)
    send[...] = spread_out(position[0:1, :], columns, jnp.zeros(send.shape, F32))
    ends = jnp.concatenate([columns[:, 127:128] * into[0], columns[:, 0:1] * into[1]], axis=0)
    target = jnp.concatenate([position[1:2, :], position[2:3, :]], axis=1)
    groups = nodes.shape[0]
    send[pl.ds(CAP, groups, stride=CAP + 1), :] = spread_out(target, ends, nodes[...])


def join_z(beside, began, storage, partial):
    lane = lanes((16, 128))
    for x in range(16):
        ends = beside[x]
        halo = jnp.where(lane == 0, roll(ends, 9, 1), jnp.where(lane == 127, roll(ends, 7, 1), 0.0))
        partial[x] = began[x] + HEAT_WEIGHTS[0] * halo / (6.0 + storage[x])


def merge(swept, final, near, out, stack):
    for block in range(BLOCKS):
        for f in range(3):
            stack[block, 32 * f : 32 * f + 8, :] = near[block, f, 24:32, :]
            at = (32 * f - 8) % 128
            stack[block, at : at + 8, :] = near[block, f, 0:8, :]
    for block in range(BLOCKS):
        stack[block] = stack[block].T
    lane = lanes((16, 128))
    outer = (lane < 4) | (lane >= 124)
    for x in range(16):
        block, lane_at = of_layer(x + LOW)
        windows = stack[block, lane_at + LOW : lane_at + LOW + 16, :]
        for f in range(3):
            if EM_SWEEPS <= x <= 15 - EM_SWEEPS:
                inner = swept[EM_SWEEPS - 1, f, x, 0:16, :]
            else:
                low, high = swept_low(EM_SWEEPS), swept_high(EM_SWEEPS)
                at = low.index(x) if x in low else len(low) + high.index(x)
                inner = final[f, at, 0:16, :]
            out[f, x] = jnp.where(outer, roll(windows, -32 * f, 1), inner)


BELOW, ABOVE = CAP, 3 * CAP


def place(owners, columns, position, into, nodes):
    planes = lax.axis_size("gz")
    groups = lax.axis_size("gy") * planes
    owner, column = owners[...], columns[...]
    member = rows((groups, 256)) == owner
    earlier = (rows((256, 256)) < lanes((256, 256))).astype(jnp.bfloat16)
    before = jnp.dot(member.astype(jnp.bfloat16), earlier, preferred_element_type=F32)
    rank = jnp.sum(jnp.where(member, before, 0.0), axis=0, keepdims=True).astype(jnp.int32)
    depth = lax.rem(owner, planes)
    to_above = jnp.where(depth < planes - 1, owner + 1, -1)
    to_below = jnp.where(depth > 0, owner - 1, -1)
    position[0:1, :] = owner * (CAP + 1) + rank
    position[1:2, :] = to_above
    position[2:3, :] = to_below
    total = None
    for target, start in ((owner, 0), (to_above, BELOW), (to_below, ABOVE)):
        spread = (rows((groups, 256)) == target).astype(jnp.bfloat16)
        listed = jnp.where(rows((128, 256)) == rank + start, column + 1, 0).astype(F32)
        term = lax.dot_general(
            spread,
            listed.astype(jnp.bfloat16),
            (((1,), (1,)), ((), ())),
            preferred_element_type=F32,
        )
        total = term if total is None else total + term
    nodes[...] = total
    for n, start in enumerate((BELOW + CAP, ABOVE + CAP)):
        into[n] = (rows((128, 256)) == rank + start).astype(F32).T


def warm(got, partial, warmth, storage, xf, xb, yf, yb, rest, heat, mid):
    first = on_first_core()
    groups = got.shape[0] // (CAP + 1)
    ids = got[pl.ds(CAP, groups, stride=CAP + 1), :].T
    node = rows((256, 1)) + 1
    per = max(1, 128 // groups)
    total = None
    for r in range(0, CAP, per):
        number = jnp.concatenate([ids[r + n : r + n + 1, :] for n in range(per)], axis=1)
        hit = (number == node.astype(F32)).astype(jnp.bfloat16)
        left = jnp.concatenate(
            [got[pl.ds(r + n, groups, stride=CAP + 1), :] for n in range(per)], axis=0
        )
        for _ in range(3):
            piece = left.astype(jnp.bfloat16)
            left = left - piece.astype(F32)
            term = jnp.dot(hit, piece, preferred_element_type=F32)
            total = term if total is None else total + term
    heat[...] = total.reshape(16, 16, 128)
    lane = lanes((16, 128))
    row = rows((16, 128))
    for x in range(16):
        mid[x] = partial[x] + HEAT_WEIGHTS[0] * heat[x] / (6.0 + storage[x])
    xf[...] = jnp.where(first, mid[15], mid[0])
    xb[...] = jnp.where(first, mid[0], mid[15])
    for x in range(16):
        t = mid[x]
        top, end = t[15:16], t[0:1]
        yf[x : x + 1] = jnp.where(first, top, end)
        yb[x : x + 1] = jnp.where(first, end, top)
        near = jnp.where(row == 0, 0.0, roll(t, 1, 0)) + jnp.where(row == 15, 0.0, roll(t, -1, 0))
        near = near + jnp.where(lane == 0, 0.0, roll(t, 1, 1))
        near = near + jnp.where(lane == 127, 0.0, roll(t, -1, 1))
        if x > 0:
            near = near + mid[x - 1]
        if x < 15:
            near = near + mid[x + 1]
        s = storage[x]
        push = s * warmth[x] + heat[x] - (6.0 + s) * t + near
        rest[x] = t + HEAT_WEIGHTS[1] * push / (6.0 + s)


def beyond_z(got, beside, warmth, out):
    groups = got.shape[0] // (CAP + 1)
    listing = got[pl.ds(CAP, groups, stride=CAP + 1), :].T
    node = (rows((256, 1)) + 1).astype(F32)
    per = max(1, 128 // groups)

    def beside_rows(at):
        return jnp.concatenate([listing[at + n : at + n + 1, :] for n in range(per)], axis=1)

    heat = []
    for start in (BELOW, ABOVE):
        total = None
        for r in range(0, CAP, per):
            hit = beside_rows(start + r) == node
            term = jnp.where(hit, beside_rows(start + CAP + r), 0.0)
            total = term if total is None else total + term
        heat.append(jnp.sum(total, axis=1, keepdims=True))
    lane = lanes((16, 128))
    for x in range(16):
        ends, t = beside[x], warmth[x]
        part = slice(16 * x, 16 * x + 16)
        low = ends[:, 118:119] + ends[:, 117:118] * (t[:, 0:1] + heat[0][part])
        high = ends[:, 121:122] + ends[:, 122:123] * (t[:, 127:128] + heat[1][part])
        out[x] = jnp.where(lane == 0, low, jnp.where(lane == 127, high, 0.0))


def finish(rest, storage, xf, xb, yf, yb, beyond, out):
    first = on_first_core()
    gx, gy = lax.axis_index("gx"), lax.axis_index("gy")
    f, b = xf[...], xb[...]
    x_low = jnp.where(gx > 0, jnp.where(first, f, b), 0.0)
    x_high = jnp.where(gx < lax.axis_size("gx") - 1, jnp.where(first, b, f), 0.0)
    f, b = yf[...], yb[...]
    y_low = jnp.where(gy > 0, jnp.where(first, f, b), 0.0)
    y_high = jnp.where(gy < lax.axis_size("gy") - 1, jnp.where(first, b, f), 0.0)
    row = rows((16, 128))
    for x in range(16):
        near = beyond[x] + jnp.where(row == 0, y_low[x : x + 1], 0.0)
        near = near + jnp.where(row == 15, y_high[x : x + 1], 0.0)
        if x == 0:
            near = near + x_low
        if x == 15:
            near = near + x_high
        out[x] = rest[x] + HEAT_WEIGHTS[1] * near / (6.0 + storage[x])


def around(axis):
    n, m = lax.axis_size(axis), lax.axis_size("gz")

    def target(a, c):
        to = a + (1 if c % 2 == 0 else -1)
        return (to, c) if 0 <= to < n else (a, c ^ 1)

    forward = []
    for a in range(n):
        for c in range(m):
            to = target(a, c)
            forward.append((a * m + c, to[0] * m + to[1]))
    return forward, [(j, i) for i, j in forward]


def exchange(axis, fwd, bwd):
    forward, backward = around(axis)
    names = (axis, "gz")
    return lax.ppermute(fwd, names, forward), lax.ppermute(bwd, names, backward)


def exchange_z(up, down):
    m = lax.axis_size("gz")
    ring = [(i, (i + 1) % m) for i in range(m)]
    return lax.ppermute(up, "gz", ring), lax.ppermute(down, "gz", [(j, i) for i, j in ring])


def local(field, source, sigma, warmth, storage, partition, column):
    groups = lax.axis_size("gy") * lax.axis_size("gz")
    count = groups * (CAP + 1)
    cube = (16, 16, 128)
    face = (16, 128)
    x_message, y_message, corners = (X_LAYERS, 16, 128), (16, 32, 128), (len(HALO_X), 32, 128)
    here = (field, sigma, warmth, storage, source)
    xf, xb, yf, yb, scaled, field, sigma, warmth, storage = call(
        pack_xy,
        [x_message, x_message, y_message, y_message, (4, *cube), (3, *cube), cube, cube, cube],
        [(3, *cube), pltpu.SemaphoreType.DMA((5,))],
        name="pack_xy",
        near=True,
        in_specs=[pl.BlockSpec(memory_space=pltpu.HBM)] * 5,
    )(*(pltpu.with_memory_space_constraint(v, pltpu.HBM) for v in here))
    xf, xb = exchange("gx", xf, xb)
    yf, yb = exchange("gy", yf, yb)
    position, into, nodes = pl.pallas_call(
        place,
        out_shape=[
            jax.ShapeDtypeStruct((3, 256), jnp.int32),
            jax.ShapeDtypeStruct((2, 256, 128), F32),
            jax.ShapeDtypeStruct((groups, 128), F32),
        ],
        compiler_params=pltpu.CompilerParams(vmem_limit_bytes=8 << 20),
        name="place",
    )(partition.reshape(1, 256), column.reshape(1, 256))
    cf, cb = call(pack_corners, [corners, corners], name="pack_corners")(
        xf, xb, position
    )
    cf, cb = exchange("gy", cf, cb)
    layer, halo = (24, 128), len(HALO_X)
    inner, inner_packed, inner_up, inner_down, began = call(
        pack_inner,
        [(8, 16, *layer), (16, *layer), (8, *layer), (8, *layer), cube],
        [(18, 16, 128)],
        name="pack_inner",
        near=True,
    )(field, scaled, warmth, storage, xf, xb, yf, yb)
    (swept,) = call(
        bulk,
        [(EM_SWEEPS, 3, 16, *layer)],
        name="bulk",
        near=True,
        cost_estimate=pl.CostEstimate(flops=10**9, bytes_accessed=10**7, transcendentals=0),
    )(inner)
    outer, outer_packed, up, down = call(
        pack_outer,
        [(8, halo, *layer), (halo, *layer), (X_PAIRS, *layer), (X_PAIRS, *layer)],
        name="pack_outer",
        near=True,
    )(xf, xb, cf, cb, inner_up, inner_down, swept)
    below_z, above_z = exchange_z(up, down)
    final, whole_sum, shifted = call(
        rest_of_bulk,
        [(3, halo, *layer), cube, cube],
        [(EM_SWEEPS - 1, 3, halo, *layer)],
        name="rest_of_bulk",
        near=True,
        cost_estimate=pl.CostEstimate(flops=10**9, bytes_accessed=10**7, transcendentals=0),
    )(inner, outer, swept)
    (own,) = call(
        turn,
        [(BLOCKS, 128, 128)],
        [(BLOCKS, 128, 128)],
        name="turn",
        near=True,
        cost_estimate=pl.CostEstimate(flops=10**8, bytes_accessed=10**6, transcendentals=0),
    )(inner_packed, outer_packed)
    near, send, beside = call(
        edge,
        [(BLOCKS, 3, 32, 128), (count, 128), cube],
        [
            (BLOCKS, 128, 128),
            (BLOCKS, 8, 32, 128),
            (BLOCKS, 3, 32, 128),
            (3, 32, 128),
            cube,
        ],
        name="edge",
        near=True,
    )(own, below_z, above_z, whole_sum, shifted, sigma, position, into, nodes)
    (partial,) = call(
        join_z,
        [cube],
        name="join_z",
        near=True,
        cost_estimate=pl.CostEstimate(flops=10**8, bytes_accessed=10**6, transcendentals=0),
    )(beside, began, storage)
    got = lax.all_to_all(
        send.reshape(count, 1, 128), ("gy", "gz"), split_axis=0, concat_axis=0, tiled=True
    ).reshape(count, 128)
    xf, xb, yf, yb, rest = call(
        warm, [face, face, face, face, cube], [cube, cube], name="warm"
    )(got, partial, warmth, storage)
    xf, xb = exchange("gx", xf, xb)
    yf, yb = exchange("gy", yf, yb)
    (beyond,) = call(
        beyond_z,
        [cube],
        name="beyond_z",
        near=True,
        cost_estimate=pl.CostEstimate(flops=10**9, bytes_accessed=10**6, transcendentals=0),
    )(got, beside, warmth)
    (updated,) = call(finish, [cube], name="finish")(rest, storage, xf, xb, yf, yb, beyond)
    (out,) = call(
        merge,
        [(3, *cube)],
        [(BLOCKS, 128, 128)],
        name="merge",
        cost_estimate=pl.CostEstimate(flops=10**9, bytes_accessed=10**6, transcendentals=0),
    )(swept, final, near)
    return out, updated


def solution(mesh):
    in_specs = (
        P(None, "gx", "gy", "gz"),
        P(None, "gx", "gy", "gz"),
        P("gx", "gy", "gz"),
        P("gx", "gy", "gz"),
        P("gx", "gy", "gz"),
        P("gx", "gy", "gz", None, None),
        P("gx", "gy", "gz", None),
    )
    out_specs = (P(None, "gx", "gy", "gz"), P("gx", "gy", "gz"))
    return jax.shard_map(local, mesh=mesh, in_specs=in_specs, out_specs=out_specs, check_vma=False)
```

```python
import functools
import math

import jax
import jax.numpy as jnp
from jax import lax
from jax.experimental import pallas as pl
from jax.experimental.pallas import tpu as pltpu
from jax.sharding import PartitionSpec as P

EM_SWEEPS = 4
HEAT_SWEEPS = 2
CAP = 8
LOW, HIGH = 4, 5
F32 = jnp.float32

em_lower = 0.02
em_upper = 3.0
heat_lower = 0.07
heat_upper = 2.0

UP_LAYERS = ((0, 12, 4), (1, 12, 4), (2, 12, 4), (3, 13, 3), (4, 13, 3), (5, 13, 3), (6, 13, 3), (7, 15, 1))
DOWN_LAYERS = ((0, 0, 4), (1, 0, 5), (2, 0, 5), (3, 0, 3), (4, 0, 4), (5, 0, 4), (6, 0, 4), (7, 0, 1))


def spots(layers, shift):
    where, at = {}, 0
    for field, first, count in layers:
        for x in range(first, first + count):
            where[field, x + shift] = at
            at += 1
    return where, at


UP_AT, UP_COUNT = spots(UP_LAYERS, -16)
DOWN_AT, DOWN_COUNT = spots(DOWN_LAYERS, 16)
X_LAYERS = max(UP_COUNT, DOWN_COUNT)


def chebyshev_weights(lower_end, upper_end, sweep_count):
    middle = 0.5 * (upper_end + lower_end)
    radius = 0.5 * (upper_end - lower_end)
    return [
        1.0 / (middle + radius * math.cos(math.pi * (2 * number + 1) / (2 * sweep_count)))
        for number in range(sweep_count)
    ]


EM_WEIGHTS = chebyshev_weights(em_lower, em_upper, EM_SWEEPS)
HEAT_WEIGHTS = chebyshev_weights(heat_lower, heat_upper, HEAT_SWEEPS)


def on_first_core():
    return lax.rem(lax.axis_index("gz"), 2) == 0


def lanes(shape):
    return lax.broadcasted_iota(jnp.int32, shape, len(shape) - 1)


def rows(shape):
    return lax.broadcasted_iota(jnp.int32, shape, len(shape) - 2)


def roll(values, by, axis):
    size = values.shape[axis]
    by = by % size
    return values if by == 0 else pltpu.roll(values, by, axis)


def call(body, out_shapes, scratch=(), name=None, limit=8 << 20, near=False, **options):
    return pl.pallas_call(
        body,
        out_shape=[
            pltpu.VMEM(s, F32) if near else jax.ShapeDtypeStruct(s, F32) for s in out_shapes
        ],
        scratch_shapes=[pltpu.VMEM(s, F32) if isinstance(s, tuple) else s for s in scratch],
        compiler_params=pltpu.CompilerParams(vmem_limit_bytes=limit),
        name=name,
        **options,
    )


def swap_store(first, fwd, bwd, at, up, down):
    fwd[at] = jnp.where(first, up, down)
    bwd[at] = jnp.where(first, down, up)


def y_tiles(v, first, fwd, bwd, at):
    row = rows((8, 128))
    low_half = row < 4
    tops = [a[8:16] for a in v]
    ends = [a[0:8] for a in v]
    for pair in range(4):
        a, b = 2 * pair, 2 * pair + 1
        up = jnp.where(low_half, roll(tops[b], 4, 0), tops[a])
        down = jnp.where(low_half, ends[a], roll(ends[b], 4, 0))
        if pair == 3:
            down = jnp.where(row == 5, roll(ends[0], 1, 0), down)
            down = jnp.where(row == 6, roll(ends[2], 2, 0), down)
        part = pl.ds(8 * pair, 8)
        fwd[at, part] = jnp.where(first, up, down)
        bwd[at, part] = jnp.where(first, down, up)


def pack_x(*refs):
    far, (xf, xb, scaled), near, arrived = refs[:5], refs[5:8], refs[8:13], refs[13]
    copies = [
        pltpu.make_async_copy(a, b, arrived.at[n]) for n, (a, b) in enumerate(zip(far, near))
    ]
    for copy in copies:
        copy.start()
    field, sigma, warmth, storage, source = near
    del storage
    first = on_first_core()
    for at in (0, 1, 2, 4):
        copies[at].wait()
    inverse = 1.0 / (4.0 + sigma[...])
    scaled[3] = inverse
    for c in range(3):
        scaled[c] = source[c] * inverse

    def layer(f, x):
        if f < 3:
            return field[f, x]
        return warmth[x] if f == 7 else scaled[f - 3, x]

    ups = [(f, x) for f, start, n in UP_LAYERS for x in range(start, start + n)]
    downs = [(f, x) for f, start, n in DOWN_LAYERS for x in range(start, start + n)]
    for at in range(X_LAYERS):
        up = layer(*ups[min(at, len(ups) - 1)])
        down = layer(*downs[min(at, len(downs) - 1)])
        swap_store(first, xf, xb, at, up, down)
    copies[3].wait()


def pack_y(field, scaled, warmth, yf, yb):
    first = on_first_core()

    def step(x, carry):
        v = [field[f, x] for f in range(3)] + [scaled[f, x] for f in range(4)] + [warmth[x]]
        y_tiles(v, first, yf, yb, x)
        return carry

    lax.fori_loop(0, 16, step, 0, unroll=4)


class Halo:
    def __init__(self, got_fwd, got_bwd):
        self.got_fwd, self.got_bwd = got_fwd, got_bwd
        self.first = on_first_core()
        gx = lax.axis_index("gx")
        self.below, self.above = gx > 0, gx < lax.axis_size("gx") - 1

    def layer(self, f, x):
        if x < 0:
            at, near, far, inside = UP_AT.get((f, x)), self.got_fwd, self.got_bwd, self.below
        else:
            at, near, far, inside = DOWN_AT.get((f, x)), self.got_bwd, self.got_fwd, self.above
        if at is None:
            return None
        return jnp.where(inside, jnp.where(self.first, near[at], far[at]), 0.0)


def pack_corners(xf, xb, targets, fwd, bwd):
    del targets
    halo = Halo(xf, xb)
    zero = jnp.zeros((16, 128), F32)
    for number, x in enumerate(HALO_X):
        v = [halo.layer(f, x) for f in range(7)]
        y_tiles([zero if a is None else a for a in v] + [zero], halo.first, fwd, bwd, number)


def y_halo(first, got, at, pair):
    gy = lax.axis_index("gy")
    part = pl.ds(8 * pair, 8)
    f, b = got[0][at, part], got[1][at, part]
    lower = jnp.where(gy > 0, jnp.where(first, f, b), 0.0)
    upper = jnp.where(gy < lax.axis_size("gy") - 1, jnp.where(first, b, f), 0.0)
    return lower, upper


HALO_X = tuple(range(-LOW, 0)) + tuple(range(16, 16 + HIGH))
X_ALL = LOW + 16 + HIGH
BLOCKS = 5
Y_LANES = LOW + 16 + HIGH
X_PAIRS = (X_ALL + 1) // 2


def y_slabs(first, got, at, v):
    low_half = rows((8, 128)) < 4
    window = lanes((24, 128)) // 16
    slabs, acc = [], None
    for pair in range(4):
        lower, upper = y_halo(first, got, at, pair)
        ends = [jnp.where(low_half, upper, lower)]
        if pair < 3:
            ends.append(roll(jnp.where(low_half, lower, upper), 4, 0))
        else:
            ends.append(roll(upper, 3, 0))
        for f, tile in zip((2 * pair, 2 * pair + 1), ends):
            slabs.append(jnp.concatenate([v[f], tile], axis=0))
            moved = roll(slabs[f], 16 * f + 8, 1)
            acc = moved if acc is None else jnp.where(window == f, moved, acc)
    return slabs, acc


def z_tiles(a, b):
    half = (lanes((24, 128)) // 8) % 2 == 0
    return jnp.where(half, a, roll(b, 8, 1)), jnp.where(half, roll(a, -8, 1), b)


def pack_inner(
    field, scaled, warmth, storage, xf, xb, yf, yb, whole, packed, up, down, began, padded
):
    first, gx = on_first_core(), lax.axis_index("gx")
    low_at, high_at = UP_AT[7, -1], DOWN_AT[7, 16]
    padded[0] = jnp.where(gx > 0, jnp.where(first, xf[low_at], xb[low_at]), 0.0)
    padded[17] = jnp.where(
        gx < lax.axis_size("gx") - 1, jnp.where(first, xb[high_at], xf[high_at]), 0.0
    )
    padded[1:17] = warmth[...]
    row, lane = rows((16, 128)), lanes((16, 128))

    def step(k, carry):
        windows = []
        for x in (2 * k, 2 * k + 1):
            t = warmth[x]
            lower, upper = y_halo(first, (yf, yb), x, 3)
            total = padded[x] + padded[x + 2]
            total = total + jnp.where(row == 0, lower[3:4], roll(t, 1, 0))
            total = total + jnp.where(row == 15, upper[4:5], roll(t, -1, 0))
            total = total + jnp.where(lane == 0, 0.0, roll(t, 1, 1))
            total = total + jnp.where(lane == 127, 0.0, roll(t, -1, 1))
            weight = HEAT_WEIGHTS[0] / (6.0 + storage[x])
            start = t + weight * (total - 6.0 * t)
            began[x] = start
            t = jnp.where(lane == 126, roll(start, -1, 1), t)
            t = jnp.where(lane == 125, roll(weight, -2, 1), t)
            t = jnp.where(lane == 1, roll(start, 1, 1), t)
            t = jnp.where(lane == 2, roll(weight, 2, 1), t)
            v = [field[f, x] for f in range(3)] + [scaled[f, x] for f in range(4)] + [t]
            slabs, acc = y_slabs(first, (yf, yb), x, v)
            for f in range(8):
                whole[f, x] = slabs[f]
            packed[x] = acc
            windows.append(acc)
        up[k], down[k] = z_tiles(*windows)
        return carry

    lax.fori_loop(0, 8, step, 0, unroll=2)


def pack_outer(xf, xb, cf, cb, inner_up, inner_down, swept, whole, packed, up, down):
    del swept
    halo = Halo(xf, xb)
    zero = jnp.zeros((16, 128), F32)
    windows = []
    for number, x in enumerate(HALO_X):
        v = [halo.layer(f, x) for f in range(7)]
        slabs, acc = y_slabs(
            halo.first, (cf, cb), number, [zero if a is None else a for a in v] + [zero]
        )
        for f in range(8):
            whole[f, number] = slabs[f]
        packed[number] = acc
        windows.append(acc)
    windows.append(jnp.zeros((24, 128), F32))
    for pair in range(len(windows) // 2):
        k = pair if pair < LOW // 2 else pair + 8
        up[k], down[k] = z_tiles(windows[2 * pair], windows[2 * pair + 1])
    up[LOW // 2 : LOW // 2 + 8] = inner_up[...]
    down[LOW // 2 : LOW // 2 + 8] = inner_down[...]


def twist(a, b, c, d):
    return (a - b) - (c - d)


def curls(e, e_up_y, e_up_z, e_up_x):
    (ex, ey, ez), (ex_y, ez_y), (ex_z, ey_z), (ey_x, ez_x) = e, e_up_y, e_up_z, e_up_x
    return twist(ez_y, ez, ey_z, ey), twist(ex_z, ex, ez_x, ez), twist(ey_x, ey, ex_y, ex)


def relaxed(weight, e, h, g, c, c_down_x, c_down_y, c_down_z):
    (cx, cy, cz), (cy_x, cz_x), (cx_y, cz_y), (cx_z, cy_z) = c, c_down_x, c_down_y, c_down_z
    k = twist(cz, cz_y, cy, cy_z), twist(cx, cx_z, cz, cz_x), twist(cy, cy_x, cx, cx_y)
    g = g * weight
    keep = (1.0 - weight) + 4.0 * g
    return [keep * e[f] + weight * h[f] - g * k[f] for f in range(3)]


def lane_curls(get, source, at):
    row = rows((24, 128))
    e = [get(source, f, at) for f in range(3)]
    up_y = roll(e[0], -1, 0), roll(e[2], -1, 0)
    if source == 0:
        up_y = [jnp.where(row == 19, get(0, 7, at)[16 + n : 17 + n], up_y[n]) for n in range(2)]
    up_z = roll(e[0], -1, 1), roll(e[1], -1, 1)
    return e, curls(e, up_y, up_z, (get(source, 1, at + 1), get(source, 2, at + 1)))


def lane_sweep(get, source, at, carry):
    e, c = lane_curls(get, source, at)
    h, g = [get(0, 3 + f, at) for f in range(3)], get(0, 6, at)
    down_y = roll(c[0], 1, 0), roll(c[2], 1, 0)
    down_z = roll(c[0], 1, 1), roll(c[1], 1, 1)
    new = relaxed(EM_WEIGHTS[source], e, h, g, c, carry, down_y, down_z)
    return new, (c[1], c[2])


def bulk(whole, swept):
    def get(number, f, x):
        return whole[f, x] if number == 0 else swept[number - 1, f, x]

    for number in range(EM_SWEEPS):

        def step(x, carry, number=number):
            new, carry = lane_sweep(get, number, x, carry)
            for f in range(3):
                swept[number, f, x] = new[f]
            return carry

        _, c = lane_curls(get, number, number)
        lax.fori_loop(number + 1, 15 - number, step, (c[1], c[2]), unroll=4)


def swept_low(number):
    return range(number - LOW, number)


def swept_high(number):
    return range(16 - number, 21 - number)


def rest_of_bulk(inner, outer, swept, final, whole_sum, shifted, others):
    def target(number):
        return final if number == EM_SWEEPS else others.at[number - 1]

    def get(number, f, x):
        if number == 0:
            return inner[f, x] if 0 <= x < 16 else outer[f, HALO_X.index(x)]
        if number <= x <= 15 - number:
            return swept[number - 1, f, x]
        low, high = swept_low(number), swept_high(number)
        return target(number)[f, low.index(x) if x < number else len(low) + high.index(x)]

    for number in range(EM_SWEEPS):
        to = target(number + 1)
        at = 0
        for layers in (swept_low(number + 1), swept_high(number + 1)):
            _, c = lane_curls(get, number, layers[0] - 1)
            carry = c[1], c[2]
            for x in layers:
                new, carry = lane_sweep(get, number, x, carry)
                for f in range(3):
                    to[f, at] = new[f]
                at += 1

    for x in range(16):
        ex, ey, ez = (get(EM_SWEEPS, f, x) for f in range(3))
        ey_x, ez_x = (get(EM_SWEEPS, f, x + 1) for f in (1, 2))
        ex, upright = ex * ex, ez * ez + ez_x * ez_x
        flat = (ex + roll(ex, -1, 0)) + (ey * ey + ey_x * ey_x)
        upright = upright + roll(upright, -1, 0)
        whole_sum[x] = flat[0:16] + upright[0:16]
        shifted[x] = roll(flat[0:16], -1, 1)


def of_layer(at):
    return at % BLOCKS, Y_LANES * (at // BLOCKS)


def clear_gaps(stack):
    for block in range(BLOCKS):
        for n in range(BLOCKS):
            at = Y_LANES * n + 24
            stack[block, at : at + 1, :] = jnp.zeros((1, 128), F32)
        stack[block, 125:128, :] = jnp.zeros((3, 128), F32)


def put_layer(stack, at, windows):
    block, lane_at = of_layer(at)
    stack[block, lane_at : lane_at + 24, :] = roll(windows, 4, 0)


def turn(inner, outer, turned, stack):
    clear_gaps(stack)
    for at in range(X_ALL):
        x = at - LOW
        put_layer(stack, at, inner[x] if 0 <= x < 16 else outer[HALO_X.index(x)])
    for block in range(BLOCKS):
        turned[block] = stack[block].T


def edge(
    own, below_z, above_z, whole_sum, shifted, sigma, targets, spread_rows, into, nodes,
    final, send, beside, stack, fields, spare, last, heat,
):
    gz = lax.axis_index("gz")
    half = (lanes((24, 128)) // 8) % 2 == 0
    has_below, has_above = gz > 0, gz < lax.axis_size("gz") - 1
    clear_gaps(stack)
    for k in range(X_PAIRS):
        lower = jnp.where(has_below, below_z[k], 0.0)
        upper = jnp.where(has_above, above_z[k], 0.0)
        for at in range(2 * k, min(2 * k + 2, X_ALL)):
            if at % 2:
                came = jnp.where(half, roll(lower, -8, 1), upper)
            else:
                came = jnp.where(half, lower, roll(upper, 8, 1))
            if 0 <= at - LOW < 16:
                beside[at - LOW] = came[0:16]
            put_layer(stack, at, came)
    for block in range(BLOCKS):
        came = stack[block].T
        for f in range(8):
            for n, part in enumerate((own, came, came, own)):
                at = 16 * f + 8 * (n % 2)
                values = part[block, at : at + 8, :] if part is own else part[at : at + 8]
                fields[block, f, 8 * n : 8 * n + 8, :] = values
    top = lanes((32, 128)) % Y_LANES == 24
    for block in range(BLOCKS):
        extra = fields[block, 7]
        for f, by in ((0, 4), (2, 3)):
            fields[block, f] = jnp.where(top, roll(extra, by, 1), fields[block, f])

    buffers = (fields, spare, final, spare, final)

    def ahead(source, block, f):
        if block < BLOCKS - 1:
            return source[block + 1, f]
        return roll(source[0, f], -Y_LANES, 1)

    def curls_at(source, block):
        e = [source[block, f] for f in range(3)]
        up_y = roll(e[0], -1, 1), roll(e[2], -1, 1)
        up_z = roll(e[0], -1, 0), roll(e[1], -1, 0)
        return e, curls(e, up_y, up_z, (ahead(source, block, 1), ahead(source, block, 2)))

    for number, weight in enumerate(EM_WEIGHTS):
        source, target = buffers[number], buffers[number + 1]
        _, c = curls_at(source, BLOCKS - 1)
        for f in range(3):
            last[f] = c[f]
        before = roll(c[1], Y_LANES, 1), roll(c[2], Y_LANES, 1)
        for block in range(BLOCKS):
            if block < BLOCKS - 1:
                e, c = curls_at(source, block)
            else:
                e, c = [source[block, f] for f in range(3)], [last[f] for f in range(3)]
            h, g = [fields[block, 3 + f] for f in range(3)], fields[block, 6]
            down_y = roll(c[0], 1, 1), roll(c[2], 1, 1)
            down_z = roll(c[0], 1, 0), roll(c[1], 1, 0)
            new = relaxed(weight, e, h, g, c, before, down_y, down_z)
            for f in range(3):
                target[block, f] = new[f]
            before = c[1], c[2]

    for block in range(BLOCKS):
        ex, ey, ez = (final[block, f] * final[block, f] for f in range(3))
        ey_x, ez_x = (ahead(final, block, f) for f in (1, 2))
        flat, upright = (ex + roll(ex, -1, 1)) + (ey + ey_x * ey_x), ez + ez_x * ez_x
        both = flat + (upright + roll(upright, -1, 1))
        stack[block, 0:8, :] = both[24:32]
        stack[block, 120:128, :] = both[0:8]
        stack[block, 59:64, :] = flat[4:9]
        stack[block, 64:67, :] = flat[25:28]
    for block in range(BLOCKS):
        stack[block] = stack[block].T
    lane = lanes((16, 128))
    for x in range(16):
        block, lane_at = of_layer(x + LOW)
        near = stack[block, lane_at + LOW : lane_at + LOW + 16, :]
        here = jnp.where((lane < 4) | (lane >= 124), near, whole_sum[x])
        above = jnp.where((lane < 3) | (lane >= 123), roll(near, 64, 1), shifted[x])
        heat[x] = sigma[x] * (0.25 * (here + above))

    def spread_out(hit, columns, total):
        for _ in range(3):
            piece = columns.astype(jnp.bfloat16)
            columns = columns - piece.astype(F32)
            term = jnp.dot(hit, piece, preferred_element_type=F32)
            total = term if total is None else total + term
        return total

    columns = heat[...].reshape(256, 128)
    send[...] = spread_out(spread_rows[...], columns, None)
    ends = jnp.concatenate([columns[:, 127:128] * into[0], columns[:, 0:1] * into[1]], axis=0)
    target = jnp.concatenate([targets[0:1, :], targets[1:2, :]], axis=1)
    groups = nodes.shape[0]
    hit = (rows((groups, 512)) == target).astype(jnp.bfloat16)
    send[pl.ds(CAP, groups, stride=CAP + 1), :] = spread_out(hit, ends, nodes[...])


def merge(swept, final, near, got, beside, warmth, out, beyond, stack):
    beyond_z(got, beside, warmth, beyond)
    for block in range(BLOCKS):
        for f in range(3):
            stack[block, 32 * f : 32 * f + 8, :] = near[block, f, 24:32, :]
            at = (32 * f - 8) % 128
            stack[block, at : at + 8, :] = near[block, f, 0:8, :]
    for block in range(BLOCKS):
        stack[block] = stack[block].T
    lane = lanes((16, 128))
    outer = (lane < 4) | (lane >= 124)
    for x in range(16):
        block, lane_at = of_layer(x + LOW)
        windows = stack[block, lane_at + LOW : lane_at + LOW + 16, :]
        for f in range(3):
            if EM_SWEEPS <= x <= 15 - EM_SWEEPS:
                inner = swept[EM_SWEEPS - 1, f, x, 0:16, :]
            else:
                low, high = swept_low(EM_SWEEPS), swept_high(EM_SWEEPS)
                at = low.index(x) if x in low else len(low) + high.index(x)
                inner = final[f, at, 0:16, :]
            out[f, x] = jnp.where(outer, roll(windows, -32 * f, 1), inner)


BELOW, ABOVE = CAP, 3 * CAP


def place(owners, columns, targets, spread_rows, into, nodes):
    planes = lax.axis_size("gz")
    groups = lax.axis_size("gy") * planes
    owner, column = owners[...], columns[...]
    member = rows((groups, 256)) == owner
    earlier = (rows((256, 256)) < lanes((256, 256))).astype(jnp.bfloat16)
    before = jnp.dot(member.astype(jnp.bfloat16), earlier, preferred_element_type=F32)
    rank = jnp.sum(jnp.where(member, before, 0.0), axis=0, keepdims=True).astype(jnp.int32)
    depth = lax.rem(owner, planes)
    to_above = jnp.where(depth < planes - 1, owner + 1, -1)
    to_below = jnp.where(depth > 0, owner - 1, -1)
    count = spread_rows.shape[0]
    spread_rows[...] = (rows((count, 256)) == owner * (CAP + 1) + rank).astype(jnp.bfloat16)
    targets[0:1, :] = to_above
    targets[1:2, :] = to_below
    total = None
    for target, start in ((owner, 0), (to_above, BELOW), (to_below, ABOVE)):
        spread = (rows((groups, 256)) == target).astype(jnp.bfloat16)
        listed = jnp.where(rows((128, 256)) == rank + start, column + 1, 0).astype(F32)
        term = lax.dot_general(
            spread,
            listed.astype(jnp.bfloat16),
            (((1,), (1,)), ((), ())),
            preferred_element_type=F32,
        )
        total = term if total is None else total + term
    nodes[...] = total
    for n, start in enumerate((BELOW + CAP, ABOVE + CAP)):
        into[n] = (rows((128, 256)) == rank + start).astype(F32).T


def warm(got, beside, began, warmth, storage, xf, xb, yf, yb, rest, heat, mid):
    first = on_first_core()
    groups = got.shape[0] // (CAP + 1)
    ids = got[pl.ds(CAP, groups, stride=CAP + 1), :].T
    node = rows((256, 1)) + 1
    per = max(1, 128 // groups)
    total = None
    for r in range(0, CAP, per):
        number = jnp.concatenate([ids[r + n : r + n + 1, :] for n in range(per)], axis=1)
        hit = (number == node.astype(F32)).astype(jnp.bfloat16)
        left = jnp.concatenate(
            [got[pl.ds(r + n, groups, stride=CAP + 1), :] for n in range(per)], axis=0
        )
        for _ in range(3):
            piece = left.astype(jnp.bfloat16)
            left = left - piece.astype(F32)
            term = jnp.dot(hit, piece, preferred_element_type=F32)
            total = term if total is None else total + term
    heat[...] = total.reshape(16, 16, 128)
    lane = lanes((16, 128))
    row = rows((16, 128))
    for x in range(16):
        ends = beside[x]
        halo = jnp.where(lane == 0, roll(ends, 9, 1), jnp.where(lane == 127, roll(ends, 7, 1), 0.0))
        mid[x] = began[x] + HEAT_WEIGHTS[0] * (heat[x] + halo) / (6.0 + storage[x])
    xf[...] = jnp.where(first, mid[15], mid[0])
    xb[...] = jnp.where(first, mid[0], mid[15])
    for x in range(16):
        t = mid[x]
        top, end = t[15:16], t[0:1]
        yf[x : x + 1] = jnp.where(first, top, end)
        yb[x : x + 1] = jnp.where(first, end, top)
        near = jnp.where(row == 0, 0.0, roll(t, 1, 0)) + jnp.where(row == 15, 0.0, roll(t, -1, 0))
        near = near + jnp.where(lane == 0, 0.0, roll(t, 1, 1))
        near = near + jnp.where(lane == 127, 0.0, roll(t, -1, 1))
        if x > 0:
            near = near + mid[x - 1]
        if x < 15:
            near = near + mid[x + 1]
        s = storage[x]
        push = s * warmth[x] + heat[x] - (6.0 + s) * t + near
        rest[x] = t + HEAT_WEIGHTS[1] * push / (6.0 + s)


def beyond_z(got, beside, warmth, out):
    groups = got.shape[0] // (CAP + 1)
    listing = got[pl.ds(CAP, groups, stride=CAP + 1), :].T
    node = (rows((256, 1)) + 1).astype(F32)
    per = max(1, 128 // groups)

    def beside_rows(at):
        return jnp.concatenate([listing[at + n : at + n + 1, :] for n in range(per)], axis=1)

    heat = []
    for start in (BELOW, ABOVE):
        total = None
        for r in range(0, CAP, per):
            hit = beside_rows(start + r) == node
            term = jnp.where(hit, beside_rows(start + CAP + r), 0.0)
            total = term if total is None else total + term
        heat.append(jnp.sum(total, axis=1, keepdims=True))
    lane = lanes((16, 128))
    for x in range(16):
        ends, t = beside[x], warmth[x]
        part = slice(16 * x, 16 * x + 16)
        low = ends[:, 118:119] + ends[:, 117:118] * (t[:, 0:1] + heat[0][part])
        high = ends[:, 121:122] + ends[:, 122:123] * (t[:, 127:128] + heat[1][part])
        out[x] = jnp.where(lane == 0, low, jnp.where(lane == 127, high, 0.0))


def finish(rest, storage, xf, xb, yf, yb, beyond, out):
    first = on_first_core()
    gx, gy = lax.axis_index("gx"), lax.axis_index("gy")
    f, b = xf[...], xb[...]
    x_low = jnp.where(gx > 0, jnp.where(first, f, b), 0.0)
    x_high = jnp.where(gx < lax.axis_size("gx") - 1, jnp.where(first, b, f), 0.0)
    f, b = yf[...], yb[...]
    y_low = jnp.where(gy > 0, jnp.where(first, f, b), 0.0)
    y_high = jnp.where(gy < lax.axis_size("gy") - 1, jnp.where(first, b, f), 0.0)
    row = rows((16, 128))
    for x in range(16):
        near = beyond[x] + jnp.where(row == 0, y_low[x : x + 1], 0.0)
        near = near + jnp.where(row == 15, y_high[x : x + 1], 0.0)
        if x == 0:
            near = near + x_low
        if x == 15:
            near = near + x_high
        out[x] = rest[x] + HEAT_WEIGHTS[1] * near / (6.0 + storage[x])


def around(axis):
    n, m = lax.axis_size(axis), lax.axis_size("gz")

    def target(a, c):
        to = a + (1 if c % 2 == 0 else -1)
        return (to, c) if 0 <= to < n else (a, c ^ 1)

    forward = []
    for a in range(n):
        for c in range(m):
            to = target(a, c)
            forward.append((a * m + c, to[0] * m + to[1]))
    return forward, [(j, i) for i, j in forward]


def exchange(axis, fwd, bwd):
    forward, backward = around(axis)
    names = (axis, "gz")
    return lax.ppermute(fwd, names, forward), lax.ppermute(bwd, names, backward)


def exchange_z(up, down):
    m = lax.axis_size("gz")
    ring = [(i, (i + 1) % m) for i in range(m)]
    return lax.ppermute(up, "gz", ring), lax.ppermute(down, "gz", [(j, i) for i, j in ring])


def local(field, source, sigma, warmth, storage, partition, column):
    groups = lax.axis_size("gy") * lax.axis_size("gz")
    count = groups * (CAP + 1)
    cube = (16, 16, 128)
    face = (16, 128)
    x_message, y_message, corners = (X_LAYERS, 16, 128), (16, 32, 128), (len(HALO_X), 32, 128)
    here = (field, sigma, warmth, storage, source)
    xf, xb, scaled, field, sigma, warmth, storage = call(
        pack_x,
        [x_message, x_message, (4, *cube), (3, *cube), cube, cube, cube],
        [(3, *cube), pltpu.SemaphoreType.DMA((5,))],
        name="pack_x",
        near=True,
        in_specs=[pl.BlockSpec(memory_space=pltpu.HBM)] * 5,
    )(*(pltpu.with_memory_space_constraint(v, pltpu.HBM) for v in here))
    xf, xb = exchange("gx", xf, xb)
    yf, yb = call(pack_y, [y_message, y_message], name="pack_y", near=True)(field, scaled, warmth)
    yf, yb = exchange("gy", yf, yb)
    targets, spread_rows, into, nodes = pl.pallas_call(
        place,
        out_shape=[
            jax.ShapeDtypeStruct((2, 256), jnp.int32),
            jax.ShapeDtypeStruct((count, 256), jnp.bfloat16),
            jax.ShapeDtypeStruct((2, 256, 128), F32),
            jax.ShapeDtypeStruct((groups, 128), F32),
        ],
        compiler_params=pltpu.CompilerParams(vmem_limit_bytes=8 << 20),
        name="place",
    )(partition.reshape(1, 256), column.reshape(1, 256))
    cf, cb = call(pack_corners, [corners, corners], name="pack_corners")(
        xf, xb, targets
    )
    cf, cb = exchange("gy", cf, cb)
    layer, halo = (24, 128), len(HALO_X)
    inner, inner_packed, inner_up, inner_down, began = call(
        pack_inner,
        [(8, 16, *layer), (16, *layer), (8, *layer), (8, *layer), cube],
        [(18, 16, 128)],
        name="pack_inner",
        near=True,
    )(field, scaled, warmth, storage, xf, xb, yf, yb)
    (swept,) = call(
        bulk,
        [(EM_SWEEPS, 3, 16, *layer)],
        name="bulk",
        near=True,
        cost_estimate=pl.CostEstimate(flops=10**9, bytes_accessed=10**7, transcendentals=0),
    )(inner)
    outer, outer_packed, up, down = call(
        pack_outer,
        [(8, halo, *layer), (halo, *layer), (X_PAIRS, *layer), (X_PAIRS, *layer)],
        name="pack_outer",
        near=True,
    )(xf, xb, cf, cb, inner_up, inner_down, swept)
    below_z, above_z = exchange_z(up, down)
    final, whole_sum, shifted = call(
        rest_of_bulk,
        [(3, halo, *layer), cube, cube],
        [(EM_SWEEPS - 1, 3, halo, *layer)],
        name="rest_of_bulk",
        near=True,
        cost_estimate=pl.CostEstimate(flops=10**9, bytes_accessed=10**7, transcendentals=0),
    )(inner, outer, swept)
    (own,) = call(
        turn,
        [(BLOCKS, 128, 128)],
        [(BLOCKS, 128, 128)],
        name="turn",
        near=True,
        cost_estimate=pl.CostEstimate(flops=10**8, bytes_accessed=10**6, transcendentals=0),
    )(inner_packed, outer_packed)
    near, send, beside = call(
        edge,
        [(BLOCKS, 3, 32, 128), (count, 128), cube],
        [
            (BLOCKS, 128, 128),
            (BLOCKS, 8, 32, 128),
            (BLOCKS, 3, 32, 128),
            (3, 32, 128),
            cube,
        ],
        name="edge",
        near=True,
    )(
        own, below_z, above_z, whole_sum, shifted, sigma, targets, spread_rows, into, nodes
    )
    got = lax.all_to_all(
        send.reshape(count, 1, 128), ("gy", "gz"), split_axis=0, concat_axis=0, tiled=True
    ).reshape(count, 128)
    xf, xb, yf, yb, rest = call(
        warm, [face, face, face, face, cube], [cube, cube], name="warm"
    )(got, beside, began, warmth, storage)
    xf, xb = exchange("gx", xf, xb)
    yf, yb = exchange("gy", yf, yb)
    out, beyond = call(
        merge,
        [(3, *cube), cube],
        [(BLOCKS, 128, 128)],
        name="merge",
        cost_estimate=pl.CostEstimate(flops=10**9, bytes_accessed=10**6, transcendentals=0),
    )(swept, final, near, got, beside, warmth)
    (updated,) = call(finish, [cube], name="finish")(rest, storage, xf, xb, yf, yb, beyond)
    return out, updated


def solution(mesh):
    in_specs = (
        P(None, "gx", "gy", "gz"),
        P(None, "gx", "gy", "gz"),
        P("gx", "gy", "gz"),
        P("gx", "gy", "gz"),
        P("gx", "gy", "gz"),
        P("gx", "gy", "gz", None, None),
        P("gx", "gy", "gz", None),
    )
    out_specs = (P(None, "gx", "gy", "gz"), P("gx", "gy", "gz"))
    return jax.shard_map(local, mesh=mesh, in_specs=in_specs, out_specs=out_specs, check_vma=False)
```

```python
import functools
import math

import jax
import jax.numpy as jnp
from jax import lax
from jax.experimental import pallas as pl
from jax.experimental.pallas import tpu as pltpu
from jax.sharding import PartitionSpec as P

EM_SWEEPS = 4
HEAT_SWEEPS = 2
CAP = 8
LOW, HIGH = 4, 5
F32 = jnp.float32

em_lower = 0.02
em_upper = 3.0
heat_lower = 0.07
heat_upper = 2.0

UP_LAYERS = ((0, 12, 4), (1, 12, 4), (2, 12, 4), (3, 13, 3), (4, 13, 3), (5, 13, 3), (6, 13, 3), (7, 15, 1))
DOWN_LAYERS = ((0, 0, 4), (1, 0, 5), (2, 0, 5), (3, 0, 3), (4, 0, 4), (5, 0, 4), (6, 0, 4), (7, 0, 1))


def spots(layers, shift):
    where, at = {}, 0
    for field, first, count in layers:
        for x in range(first, first + count):
            where[field, x + shift] = at
            at += 1
    return where, at


UP_AT, UP_COUNT = spots(UP_LAYERS, -16)
DOWN_AT, DOWN_COUNT = spots(DOWN_LAYERS, 16)
X_LAYERS = max(UP_COUNT, DOWN_COUNT)


def chebyshev_weights(lower_end, upper_end, sweep_count):
    middle = 0.5 * (upper_end + lower_end)
    radius = 0.5 * (upper_end - lower_end)
    return [
        1.0 / (middle + radius * math.cos(math.pi * (2 * number + 1) / (2 * sweep_count)))
        for number in range(sweep_count)
    ]


EM_WEIGHTS = chebyshev_weights(em_lower, em_upper, EM_SWEEPS)
HEAT_WEIGHTS = chebyshev_weights(heat_lower, heat_upper, HEAT_SWEEPS)


def on_first_core():
    return lax.rem(lax.axis_index("gz"), 2) == 0


def lanes(shape):
    return lax.broadcasted_iota(jnp.int32, shape, len(shape) - 1)


def rows(shape):
    return lax.broadcasted_iota(jnp.int32, shape, len(shape) - 2)


def roll(values, by, axis):
    size = values.shape[axis]
    by = by % size
    return values if by == 0 else pltpu.roll(values, by, axis)


def call(body, out_shapes, scratch=(), name=None, limit=8 << 20, near=False, **options):
    return pl.pallas_call(
        body,
        out_shape=[
            pltpu.VMEM(s, F32) if near else jax.ShapeDtypeStruct(s, F32) for s in out_shapes
        ],
        scratch_shapes=[pltpu.VMEM(s, F32) if isinstance(s, tuple) else s for s in scratch],
        compiler_params=pltpu.CompilerParams(vmem_limit_bytes=limit),
        name=name,
        **options,
    )


def swap_store(first, fwd, bwd, at, up, down):
    fwd[at] = jnp.where(first, up, down)
    bwd[at] = jnp.where(first, down, up)


def y_tiles(v):
    row = rows((8, 128))
    low_half = row < 4
    tops = [a[8:16] for a in v]
    ends = [a[0:8] for a in v]
    ups, downs = [], []
    for pair in range(4):
        a, b = 2 * pair, 2 * pair + 1
        ups.append(jnp.where(low_half, roll(tops[b], 4, 0), tops[a]))
        down = jnp.where(low_half, ends[a], roll(ends[b], 4, 0))
        if pair == 3:
            down = jnp.where(row == 5, roll(ends[0], 1, 0), down)
            down = jnp.where(row == 6, roll(ends[2], 2, 0), down)
        downs.append(down)
    return ups, downs


def put_y_tiles(tiles, first, fwd, bwd, at):
    for pair, (up, down) in enumerate(zip(*tiles)):
        part = pl.ds(8 * pair, 8)
        fwd[at, part] = jnp.where(first, up, down)
        bwd[at, part] = jnp.where(first, down, up)


def pack_x(*refs):
    far, (xf, xb, scaled), near, arrived = refs[:5], refs[5:8], refs[8:13], refs[13]
    copies = [
        pltpu.make_async_copy(a, b, arrived.at[n]) for n, (a, b) in enumerate(zip(far, near))
    ]
    for copy in copies:
        copy.start()
    field, sigma, warmth, storage, source = near
    del storage
    first = on_first_core()
    for at in (0, 1, 2, 4):
        copies[at].wait()
    inverse = 1.0 / (4.0 + sigma[...])
    scaled[3] = inverse
    for c in range(3):
        scaled[c] = source[c] * inverse

    def layer(f, x):
        if f < 3:
            return field[f, x]
        return warmth[x] if f == 7 else scaled[f - 3, x]

    ups = [(f, x) for f, start, n in UP_LAYERS for x in range(start, start + n)]
    downs = [(f, x) for f, start, n in DOWN_LAYERS for x in range(start, start + n)]
    for at in range(X_LAYERS):
        up = layer(*ups[min(at, len(ups) - 1)])
        down = layer(*downs[min(at, len(downs) - 1)])
        swap_store(first, xf, xb, at, up, down)
    copies[3].wait()


def pack_y(field, scaled, warmth, yf, yb):
    first = on_first_core()

    def step(x, carry):
        v = [field[f, x] for f in range(3)] + [scaled[f, x] for f in range(4)] + [warmth[x]]
        put_y_tiles(y_tiles(v), first, yf, yb, x)
        return carry

    lax.fori_loop(0, 16, step, 0, unroll=4)


class Halo:
    def __init__(self, got_fwd, got_bwd):
        self.got_fwd, self.got_bwd = got_fwd, got_bwd
        self.first = on_first_core()
        gx = lax.axis_index("gx")
        self.below, self.above = gx > 0, gx < lax.axis_size("gx") - 1

    def layer(self, f, x):
        if x < 0:
            at, near, far, inside = UP_AT.get((f, x)), self.got_fwd, self.got_bwd, self.below
        else:
            at, near, far, inside = DOWN_AT.get((f, x)), self.got_bwd, self.got_fwd, self.above
        if at is None:
            return None
        return jnp.where(inside, jnp.where(self.first, near[at], far[at]), 0.0)


def pack_corners(xf, xb, targets, fwd, bwd):
    del targets
    halo = Halo(xf, xb)
    zero = jnp.zeros((16, 128), F32)
    row = rows((8, 128)) % 4
    tiles = {}
    for x in HALO_X:
        v = [halo.layer(f, x) for f in range(7)]
        tiles[x] = y_tiles([zero if a is None else a for a in v] + [zero])
    for at, (x, sharer, shift) in enumerate(CORNERS):
        ups, downs = tiles[x]
        if sharer is not None:
            other_ups, other_downs = tiles[sharer]
            ups = [jnp.where(row >= 4 - shift, a, roll(b, -shift, 0)) for a, b in zip(ups, other_ups)]
            downs = [jnp.where(row < shift, a, roll(b, shift, 0)) for a, b in zip(downs, other_downs)]
        put_y_tiles((ups, downs), halo.first, fwd, bwd, at)


def y_halo(first, got, at, pair):
    gy = lax.axis_index("gy")
    part = pl.ds(8 * pair, 8)
    f, b = got[0][at, part], got[1][at, part]
    lower = jnp.where(gy > 0, jnp.where(first, f, b), 0.0)
    upper = jnp.where(gy < lax.axis_size("gy") - 1, jnp.where(first, b, f), 0.0)
    return lower, upper


CORNERS = (
    (-3, None, 0), (-2, None, 0), (-1, None, 0), (16, None, 0), (17, None, 0), (19, -4, 2), (18, 20, 3),
)
HALO_X = tuple(range(-LOW, 0)) + tuple(range(16, 16 + HIGH))
X_ALL = LOW + 16 + HIGH
BLOCKS = 5
Y_LANES = LOW + 16 + HIGH
X_PAIRS = (X_ALL + 1) // 2


def y_slabs(first, got, at, v, shift=0):
    low_half = rows((8, 128)) < 4
    window = lanes((24, 128)) // 16
    slabs, acc = [], None
    for pair in range(4):
        lower, upper = y_halo(first, got, at, pair)
        lower, upper = roll(lower, shift, 0), roll(upper, -shift, 0)
        ends = [jnp.where(low_half, upper, lower)]
        if pair < 3:
            ends.append(roll(jnp.where(low_half, lower, upper), 4, 0))
        else:
            ends.append(roll(upper, 3, 0))
        for f, tile in zip((2 * pair, 2 * pair + 1), ends):
            slabs.append(jnp.concatenate([v[f], tile], axis=0))
            moved = roll(slabs[f], 16 * f + 8, 1)
            acc = moved if acc is None else jnp.where(window == f, moved, acc)
    return slabs, acc


def z_tiles(a, b):
    half = (lanes((24, 128)) // 8) % 2 == 0
    return jnp.where(half, a, roll(b, 8, 1)), jnp.where(half, roll(a, -8, 1), b)


def pack_inner(
    field, scaled, warmth, storage, xf, xb, yf, yb, whole, packed, up, down, began, padded
):
    first, gx = on_first_core(), lax.axis_index("gx")
    low_at, high_at = UP_AT[7, -1], DOWN_AT[7, 16]
    padded[0] = jnp.where(gx > 0, jnp.where(first, xf[low_at], xb[low_at]), 0.0)
    padded[17] = jnp.where(
        gx < lax.axis_size("gx") - 1, jnp.where(first, xb[high_at], xf[high_at]), 0.0
    )
    padded[1:17] = warmth[...]
    row, lane = rows((16, 128)), lanes((16, 128))

    def step(k, carry):
        windows = []
        for x in (2 * k, 2 * k + 1):
            t = warmth[x]
            lower, upper = y_halo(first, (yf, yb), x, 3)
            total = padded[x] + padded[x + 2]
            total = total + jnp.where(row == 0, lower[3:4], roll(t, 1, 0))
            total = total + jnp.where(row == 15, upper[4:5], roll(t, -1, 0))
            total = total + jnp.where(lane == 0, 0.0, roll(t, 1, 1))
            total = total + jnp.where(lane == 127, 0.0, roll(t, -1, 1))
            weight = HEAT_WEIGHTS[0] / (6.0 + storage[x])
            start = t + weight * (total - 6.0 * t)
            began[x] = start
            t = jnp.where(lane == 126, roll(start, -1, 1), t)
            t = jnp.where(lane == 125, roll(weight, -2, 1), t)
            t = jnp.where(lane == 1, roll(start, 1, 1), t)
            t = jnp.where(lane == 2, roll(weight, 2, 1), t)
            v = [field[f, x] for f in range(3)] + [scaled[f, x] for f in range(4)] + [t]
            slabs, acc = y_slabs(first, (yf, yb), x, v)
            for f in range(8):
                whole[f, x] = slabs[f]
            packed[x] = acc
            windows.append(acc)
        up[k], down[k] = z_tiles(*windows)
        return carry

    lax.fori_loop(0, 8, step, 0, unroll=2)


def pack_outer(xf, xb, cf, cb, inner_up, inner_down, swept, whole, packed, up, down):
    del swept
    halo = Halo(xf, xb)
    zero = jnp.zeros((16, 128), F32)
    windows = []
    place_of = {}
    for at, (x, sharer, shift) in enumerate(CORNERS):
        place_of[x], place_of[sharer] = (at, 0), (at, shift)
    for number, x in enumerate(HALO_X):
        v = [halo.layer(f, x) for f in range(7)]
        at, shift = place_of[x]
        slabs, acc = y_slabs(
            halo.first, (cf, cb), at, [zero if a is None else a for a in v] + [zero], shift
        )
        for f in range(8):
            whole[f, number] = slabs[f]
        packed[number] = acc
        windows.append(acc)
    windows.append(jnp.zeros((24, 128), F32))
    for pair in range(len(windows) // 2):
        k = pair if pair < LOW // 2 else pair + 8
        up[k], down[k] = z_tiles(windows[2 * pair], windows[2 * pair + 1])
    up[LOW // 2 : LOW // 2 + 8] = inner_up[...]
    down[LOW // 2 : LOW // 2 + 8] = inner_down[...]


def twist(a, b, c, d):
    return (a - b) - (c - d)


def curls(e, e_up_y, e_up_z, e_up_x):
    (ex, ey, ez), (ex_y, ez_y), (ex_z, ey_z), (ey_x, ez_x) = e, e_up_y, e_up_z, e_up_x
    return twist(ez_y, ez, ey_z, ey), twist(ex_z, ex, ez_x, ez), twist(ey_x, ey, ex_y, ex)


def relaxed(weight, e, h, g, c, c_down_x, c_down_y, c_down_z):
    (cx, cy, cz), (cy_x, cz_x), (cx_y, cz_y), (cx_z, cy_z) = c, c_down_x, c_down_y, c_down_z
    k = twist(cz, cz_y, cy, cy_z), twist(cx, cx_z, cz, cz_x), twist(cy, cy_x, cx, cx_y)
    g = g * weight
    keep = (1.0 - weight) + 4.0 * g
    return [keep * e[f] + weight * h[f] - g * k[f] for f in range(3)]


def lane_curls(get, source, at):
    row = rows((24, 128))
    e = [get(source, f, at) for f in range(3)]
    up_y = roll(e[0], -1, 0), roll(e[2], -1, 0)
    if source == 0:
        up_y = [jnp.where(row == 19, get(0, 7, at)[16 + n : 17 + n], up_y[n]) for n in range(2)]
    up_z = roll(e[0], -1, 1), roll(e[1], -1, 1)
    return e, curls(e, up_y, up_z, (get(source, 1, at + 1), get(source, 2, at + 1)))


def lane_sweep(get, source, at, carry):
    e, c = lane_curls(get, source, at)
    h, g = [get(0, 3 + f, at) for f in range(3)], get(0, 6, at)
    down_y = roll(c[0], 1, 0), roll(c[2], 1, 0)
    down_z = roll(c[0], 1, 1), roll(c[1], 1, 1)
    new = relaxed(EM_WEIGHTS[source], e, h, g, c, carry, down_y, down_z)
    return new, (c[1], c[2])


def bulk(whole, swept):
    def get(number, f, x):
        return whole[f, x] if number == 0 else swept[number - 1, f, x]

    for number in range(EM_SWEEPS - 1):

        def step(x, carry, number=number):
            new, carry = lane_sweep(get, number, x, carry)
            for f in range(3):
                swept[number, f, x] = new[f]
            return carry

        _, c = lane_curls(get, number, number)
        lax.fori_loop(number + 1, 15 - number, step, (c[1], c[2]), unroll=4)


def swept_low(number):
    return range(number - LOW, number)


def swept_high(number):
    return range(16 - number, 21 - number)


def rest_of_bulk(inner, outer, swept, final, whole_sum, shifted, others):
    def get(number, f, x):
        if number == 0:
            return inner[f, x] if 0 <= x < 16 else outer[f, HALO_X.index(x)]
        if number == EM_SWEEPS:
            return final[f, x]
        if number <= x <= 15 - number:
            return swept[number - 1, f, x]
        low, high = swept_low(number), swept_high(number)
        return others[number - 1, f, low.index(x) if x < number else len(low) + high.index(x)]

    for number in range(EM_SWEEPS):
        at = 0
        ranges = (swept_low(number + 1), swept_high(number + 1))
        if number == EM_SWEEPS - 1:
            ranges = (range(17),)
        for layers in ranges:
            _, c = lane_curls(get, number, layers[0] - 1)
            carry = c[1], c[2]
            for x in layers:
                new, carry = lane_sweep(get, number, x, carry)
                for f in range(3):
                    if number == EM_SWEEPS - 1:
                        final[f, x] = new[f]
                    else:
                        others[number, f, at] = new[f]
                at += 1

    for x in range(16):
        ex, ey, ez = (get(EM_SWEEPS, f, x) for f in range(3))
        ey_x, ez_x = (get(EM_SWEEPS, f, x + 1) for f in (1, 2))
        ex, upright = ex * ex, ez * ez + ez_x * ez_x
        flat = (ex + roll(ex, -1, 0)) + (ey * ey + ey_x * ey_x)
        upright = upright + roll(upright, -1, 0)
        whole_sum[x] = flat[0:16] + upright[0:16]
        shifted[x] = roll(flat[0:16], -1, 1)


def of_layer(at):
    return at % BLOCKS, Y_LANES * (at // BLOCKS)


def clear_gaps(stack):
    for block in range(BLOCKS):
        for n in range(BLOCKS):
            at = Y_LANES * n + 24
            stack[block, at : at + 1, :] = jnp.zeros((1, 128), F32)
        stack[block, 125:128, :] = jnp.zeros((3, 128), F32)


def put_layer(stack, at, windows):
    block, lane_at = of_layer(at)
    stack[block, lane_at : lane_at + 24, :] = roll(windows, 4, 0)


def turn(inner, outer, turned, stack):
    clear_gaps(stack)
    for at in range(X_ALL):
        x = at - LOW
        put_layer(stack, at, inner[x] if 0 <= x < 16 else outer[HALO_X.index(x)])
    for block in range(BLOCKS):
        turned[block] = stack[block].T


def edge(
    own, below_z, above_z, whole_sum, shifted, sigma, targets, spread_rows, into, nodes,
    final, send, beside, stack, fields, spare, last, heat,
):
    gz = lax.axis_index("gz")
    half = (lanes((24, 128)) // 8) % 2 == 0
    has_below, has_above = gz > 0, gz < lax.axis_size("gz") - 1
    clear_gaps(stack)
    for k in range(X_PAIRS):
        lower = jnp.where(has_below, below_z[k], 0.0)
        upper = jnp.where(has_above, above_z[k], 0.0)
        for at in range(2 * k, min(2 * k + 2, X_ALL)):
            if at % 2:
                came = jnp.where(half, roll(lower, -8, 1), upper)
            else:
                came = jnp.where(half, lower, roll(upper, 8, 1))
            if 0 <= at - LOW < 16:
                beside[at - LOW] = came[0:16]
            put_layer(stack, at, came)
    for block in range(BLOCKS):
        came = stack[block].T
        for f in range(8):
            for n, part in enumerate((own, came, came, own)):
                at = 16 * f + 8 * (n % 2)
                values = part[block, at : at + 8, :] if part is own else part[at : at + 8]
                fields[block, f, 8 * n : 8 * n + 8, :] = values
    top = lanes((32, 128)) % Y_LANES == 24
    for block in range(BLOCKS):
        extra = fields[block, 7]
        for f, by in ((0, 4), (2, 3)):
            fields[block, f] = jnp.where(top, roll(extra, by, 1), fields[block, f])

    buffers = (fields, spare, final, spare, final)

    def ahead(source, block, f):
        if block < BLOCKS - 1:
            return source[block + 1, f]
        return roll(source[0, f], -Y_LANES, 1)

    def curls_at(source, block):
        e = [source[block, f] for f in range(3)]
        up_y = roll(e[0], -1, 1), roll(e[2], -1, 1)
        up_z = roll(e[0], -1, 0), roll(e[1], -1, 0)
        return e, curls(e, up_y, up_z, (ahead(source, block, 1), ahead(source, block, 2)))

    for number, weight in enumerate(EM_WEIGHTS):
        source, target = buffers[number], buffers[number + 1]
        _, c = curls_at(source, BLOCKS - 1)
        for f in range(3):
            last[f] = c[f]
        before = roll(c[1], Y_LANES, 1), roll(c[2], Y_LANES, 1)
        for block in range(BLOCKS):
            if block < BLOCKS - 1:
                e, c = curls_at(source, block)
            else:
                e, c = [source[block, f] for f in range(3)], [last[f] for f in range(3)]
            h, g = [fields[block, 3 + f] for f in range(3)], fields[block, 6]
            down_y = roll(c[0], 1, 1), roll(c[2], 1, 1)
            down_z = roll(c[0], 1, 0), roll(c[1], 1, 0)
            new = relaxed(weight, e, h, g, c, before, down_y, down_z)
            for f in range(3):
                target[block, f] = new[f]
            before = c[1], c[2]

    for block in range(BLOCKS):
        ex, ey, ez = (final[block, f] * final[block, f] for f in range(3))
        ey_x, ez_x = (ahead(final, block, f) for f in (1, 2))
        flat, upright = (ex + roll(ex, -1, 1)) + (ey + ey_x * ey_x), ez + ez_x * ez_x
        both = flat + (upright + roll(upright, -1, 1))
        stack[block, 0:8, :] = both[24:32]
        stack[block, 120:128, :] = both[0:8]
        stack[block, 59:64, :] = flat[4:9]
        stack[block, 64:67, :] = flat[25:28]
    for block in range(BLOCKS):
        stack[block] = stack[block].T
    lane = lanes((16, 128))
    for x in range(16):
        block, lane_at = of_layer(x + LOW)
        near = stack[block, lane_at + LOW : lane_at + LOW + 16, :]
        here = jnp.where((lane < 4) | (lane >= 124), near, whole_sum[x])
        above = jnp.where((lane < 3) | (lane >= 123), roll(near, 64, 1), shifted[x])
        heat[x] = sigma[x] * (0.25 * (here + above))

    def spread_out(hit, columns, total):
        for _ in range(3):
            piece = columns.astype(jnp.bfloat16)
            columns = columns - piece.astype(F32)
            term = jnp.dot(hit, piece, preferred_element_type=F32)
            total = term if total is None else total + term
        return total

    columns = heat[...].reshape(256, 128)
    send[...] = spread_out(spread_rows[...], columns, None)
    ends = jnp.concatenate([columns[:, 127:128] * into[0], columns[:, 0:1] * into[1]], axis=0)
    target = jnp.concatenate([targets[0:1, :], targets[1:2, :]], axis=1)
    groups = nodes.shape[0]
    hit = (rows((groups, 512)) == target).astype(jnp.bfloat16)
    send[pl.ds(CAP, groups, stride=CAP + 1), :] = spread_out(hit, ends, nodes[...])


def merge(final, near, got, beside, warmth, out, beyond, stack):
    beyond_z(got, beside, warmth, beyond)
    for block in range(BLOCKS):
        for f in range(3):
            stack[block, 32 * f : 32 * f + 8, :] = near[block, f, 24:32, :]
            at = (32 * f - 8) % 128
            stack[block, at : at + 8, :] = near[block, f, 0:8, :]
    for block in range(BLOCKS):
        stack[block] = stack[block].T
    lane = lanes((16, 128))
    outer = (lane < 4) | (lane >= 124)
    for x in range(16):
        block, lane_at = of_layer(x + LOW)
        windows = stack[block, lane_at + LOW : lane_at + LOW + 16, :]
        for f in range(3):
            inner = final[f, x, 0:16, :]
            out[f, x] = jnp.where(outer, roll(windows, -32 * f, 1), inner)


BELOW, ABOVE = CAP, 3 * CAP


def place(owners, columns, targets, spread_rows, into, nodes):
    planes = lax.axis_size("gz")
    groups = lax.axis_size("gy") * planes
    owner, column = owners[...], columns[...]
    member = rows((groups, 256)) == owner
    earlier = (rows((256, 256)) < lanes((256, 256))).astype(jnp.bfloat16)
    before = jnp.dot(member.astype(jnp.bfloat16), earlier, preferred_element_type=F32)
    rank = jnp.sum(jnp.where(member, before, 0.0), axis=0, keepdims=True).astype(jnp.int32)
    depth = lax.rem(owner, planes)
    to_above = jnp.where(depth < planes - 1, owner + 1, -1)
    to_below = jnp.where(depth > 0, owner - 1, -1)
    count = spread_rows.shape[0]
    spread_rows[...] = (rows((count, 256)) == owner * (CAP + 1) + rank).astype(jnp.bfloat16)
    targets[0:1, :] = to_above
    targets[1:2, :] = to_below
    total = None
    for target, start in ((owner, 0), (to_above, BELOW), (to_below, ABOVE)):
        spread = (rows((groups, 256)) == target).astype(jnp.bfloat16)
        listed = jnp.where(rows((128, 256)) == rank + start, column + 1, 0).astype(F32)
        term = lax.dot_general(
            spread,
            listed.astype(jnp.bfloat16),
            (((1,), (1,)), ((), ())),
            preferred_element_type=F32,
        )
        total = term if total is None else total + term
    nodes[...] = total
    for n, start in enumerate((BELOW + CAP, ABOVE + CAP)):
        into[n] = (rows((128, 256)) == rank + start).astype(F32).T


def warm(got, beside, began, warmth, storage, xf, xb, yf, yb, rest, heat, mid):
    first = on_first_core()
    groups = got.shape[0] // (CAP + 1)
    ids = got[pl.ds(CAP, groups, stride=CAP + 1), :].T
    node = rows((256, 1)) + 1
    per = max(1, 128 // groups)
    total = None
    for r in range(0, CAP, per):
        number = jnp.concatenate([ids[r + n : r + n + 1, :] for n in range(per)], axis=1)
        hit = (number == node.astype(F32)).astype(jnp.bfloat16)
        left = jnp.concatenate(
            [got[pl.ds(r + n, groups, stride=CAP + 1), :] for n in range(per)], axis=0
        )
        for _ in range(3):
            piece = left.astype(jnp.bfloat16)
            left = left - piece.astype(F32)
            term = jnp.dot(hit, piece, preferred_element_type=F32)
            total = term if total is None else total + term
    heat[...] = total.reshape(16, 16, 128)
    lane = lanes((16, 128))
    row = rows((16, 128))
    for x in range(16):
        ends = beside[x]
        halo = jnp.where(lane == 0, roll(ends, 9, 1), jnp.where(lane == 127, roll(ends, 7, 1), 0.0))
        mid[x] = began[x] + HEAT_WEIGHTS[0] * (heat[x] + halo) / (6.0 + storage[x])
    xf[...] = jnp.where(first, mid[15], mid[0])
    xb[...] = jnp.where(first, mid[0], mid[15])
    for x in range(16):
        t = mid[x]
        top, end = t[15:16], t[0:1]
        yf[x : x + 1] = jnp.where(first, top, end)
        yb[x : x + 1] = jnp.where(first, end, top)
        near = jnp.where(row == 0, 0.0, roll(t, 1, 0)) + jnp.where(row == 15, 0.0, roll(t, -1, 0))
        near = near + jnp.where(lane == 0, 0.0, roll(t, 1, 1))
        near = near + jnp.where(lane == 127, 0.0, roll(t, -1, 1))
        if x > 0:
            near = near + mid[x - 1]
        if x < 15:
            near = near + mid[x + 1]
        s = storage[x]
        push = s * warmth[x] + heat[x] - (6.0 + s) * t + near
        rest[x] = t + HEAT_WEIGHTS[1] * push / (6.0 + s)


def beyond_z(got, beside, warmth, out):
    groups = got.shape[0] // (CAP + 1)
    listing = got[pl.ds(CAP, groups, stride=CAP + 1), :].T
    node = (rows((256, 1)) + 1).astype(F32)
    per = max(1, 128 // groups)

    def beside_rows(at):
        return jnp.concatenate([listing[at + n : at + n + 1, :] for n in range(per)], axis=1)

    heat = []
    for start in (BELOW, ABOVE):
        total = None
        for r in range(0, CAP, per):
            hit = beside_rows(start + r) == node
            term = jnp.where(hit, beside_rows(start + CAP + r), 0.0)
            total = term if total is None else total + term
        heat.append(jnp.sum(total, axis=1, keepdims=True))
    lane = lanes((16, 128))
    for x in range(16):
        ends, t = beside[x], warmth[x]
        part = slice(16 * x, 16 * x + 16)
        low = ends[:, 118:119] + ends[:, 117:118] * (t[:, 0:1] + heat[0][part])
        high = ends[:, 121:122] + ends[:, 122:123] * (t[:, 127:128] + heat[1][part])
        out[x] = jnp.where(lane == 0, low, jnp.where(lane == 127, high, 0.0))


def finish(rest, storage, xf, xb, yf, yb, beyond, out):
    first = on_first_core()
    gx, gy = lax.axis_index("gx"), lax.axis_index("gy")
    f, b = xf[...], xb[...]
    x_low = jnp.where(gx > 0, jnp.where(first, f, b), 0.0)
    x_high = jnp.where(gx < lax.axis_size("gx") - 1, jnp.where(first, b, f), 0.0)
    f, b = yf[...], yb[...]
    y_low = jnp.where(gy > 0, jnp.where(first, f, b), 0.0)
    y_high = jnp.where(gy < lax.axis_size("gy") - 1, jnp.where(first, b, f), 0.0)
    row = rows((16, 128))
    for x in range(16):
        near = beyond[x] + jnp.where(row == 0, y_low[x : x + 1], 0.0)
        near = near + jnp.where(row == 15, y_high[x : x + 1], 0.0)
        if x == 0:
            near = near + x_low
        if x == 15:
            near = near + x_high
        out[x] = rest[x] + HEAT_WEIGHTS[1] * near / (6.0 + storage[x])


def around(axis):
    n, m = lax.axis_size(axis), lax.axis_size("gz")

    def target(a, c):
        to = a + (1 if c % 2 == 0 else -1)
        return (to, c) if 0 <= to < n else (a, c ^ 1)

    forward = []
    for a in range(n):
        for c in range(m):
            to = target(a, c)
            forward.append((a * m + c, to[0] * m + to[1]))
    return forward, [(j, i) for i, j in forward]


def exchange(axis, fwd, bwd):
    forward, backward = around(axis)
    names = (axis, "gz")
    return lax.ppermute(fwd, names, forward), lax.ppermute(bwd, names, backward)


def exchange_z(up, down):
    m = lax.axis_size("gz")
    ring = [(i, (i + 1) % m) for i in range(m)]
    return lax.ppermute(up, "gz", ring), lax.ppermute(down, "gz", [(j, i) for i, j in ring])


def local(field, source, sigma, warmth, storage, partition, column):
    groups = lax.axis_size("gy") * lax.axis_size("gz")
    count = groups * (CAP + 1)
    cube = (16, 16, 128)
    face = (16, 128)
    x_message, y_message, corners = (X_LAYERS, 16, 128), (16, 32, 128), (len(CORNERS), 32, 128)
    here = (field, sigma, warmth, storage, source)
    xf, xb, scaled, field, sigma, warmth, storage = call(
        pack_x,
        [x_message, x_message, (4, *cube), (3, *cube), cube, cube, cube],
        [(3, *cube), pltpu.SemaphoreType.DMA((5,))],
        name="pack_x",
        near=True,
        in_specs=[pl.BlockSpec(memory_space=pltpu.HBM)] * 5,
    )(*(pltpu.with_memory_space_constraint(v, pltpu.HBM) for v in here))
    xf, xb = exchange("gx", xf, xb)
    yf, yb = call(pack_y, [y_message, y_message], name="pack_y", near=True)(field, scaled, warmth)
    yf, yb = exchange("gy", yf, yb)
    targets, spread_rows, into, nodes = pl.pallas_call(
        place,
        out_shape=[
            jax.ShapeDtypeStruct((2, 256), jnp.int32),
            jax.ShapeDtypeStruct((count, 256), jnp.bfloat16),
            jax.ShapeDtypeStruct((2, 256, 128), F32),
            jax.ShapeDtypeStruct((groups, 128), F32),
        ],
        compiler_params=pltpu.CompilerParams(vmem_limit_bytes=8 << 20),
        name="place",
    )(partition.reshape(1, 256), column.reshape(1, 256))
    cf, cb = call(pack_corners, [corners, corners], name="pack_corners")(
        xf, xb, targets
    )
    cf, cb = exchange("gy", cf, cb)
    layer, halo = (24, 128), len(HALO_X)
    inner, inner_packed, inner_up, inner_down, began = call(
        pack_inner,
        [(8, 16, *layer), (16, *layer), (8, *layer), (8, *layer), cube],
        [(18, 16, 128)],
        name="pack_inner",
        near=True,
    )(field, scaled, warmth, storage, xf, xb, yf, yb)
    (swept,) = call(
        bulk,
        [(EM_SWEEPS - 1, 3, 16, *layer)],
        name="bulk",
        near=True,
        cost_estimate=pl.CostEstimate(flops=10**9, bytes_accessed=10**7, transcendentals=0),
    )(inner)
    outer, outer_packed, up, down = call(
        pack_outer,
        [(8, halo, *layer), (halo, *layer), (X_PAIRS, *layer), (X_PAIRS, *layer)],
        name="pack_outer",
        near=True,
    )(xf, xb, cf, cb, inner_up, inner_down, swept)
    below_z, above_z = exchange_z(up, down)
    final, whole_sum, shifted = call(
        rest_of_bulk,
        [(3, 17, *layer), cube, cube],
        [(EM_SWEEPS - 1, 3, halo, *layer)],
        name="rest_of_bulk",
        near=True,
        cost_estimate=pl.CostEstimate(flops=10**9, bytes_accessed=10**7, transcendentals=0),
    )(inner, outer, swept)
    (own,) = call(
        turn,
        [(BLOCKS, 128, 128)],
        [(BLOCKS, 128, 128)],
        name="turn",
        near=True,
        cost_estimate=pl.CostEstimate(flops=10**8, bytes_accessed=10**6, transcendentals=0),
    )(inner_packed, outer_packed)
    near, send, beside = call(
        edge,
        [(BLOCKS, 3, 32, 128), (count, 128), cube],
        [
            (BLOCKS, 128, 128),
            (BLOCKS, 8, 32, 128),
            (BLOCKS, 3, 32, 128),
            (3, 32, 128),
            cube,
        ],
        name="edge",
        near=True,
    )(
        own, below_z, above_z, whole_sum, shifted, sigma, targets, spread_rows, into, nodes
    )
    got = lax.all_to_all(
        send.reshape(count, 1, 128), ("gy", "gz"), split_axis=0, concat_axis=0, tiled=True
    ).reshape(count, 128)
    xf, xb, yf, yb, rest = call(
        warm, [face, face, face, face, cube], [cube, cube], name="warm"
    )(got, beside, began, warmth, storage)
    xf, xb = exchange("gx", xf, xb)
    yf, yb = exchange("gy", yf, yb)
    out, beyond = call(
        merge,
        [(3, *cube), cube],
        [(BLOCKS, 128, 128)],
        name="merge",
        cost_estimate=pl.CostEstimate(flops=10**9, bytes_accessed=10**6, transcendentals=0),
    )(final, near, got, beside, warmth)
    (updated,) = call(finish, [cube], name="finish")(rest, storage, xf, xb, yf, yb, beyond)
    return out, updated


def solution(mesh):
    in_specs = (
        P(None, "gx", "gy", "gz"),
        P(None, "gx", "gy", "gz"),
        P("gx", "gy", "gz"),
        P("gx", "gy", "gz"),
        P("gx", "gy", "gz"),
        P("gx", "gy", "gz", None, None),
        P("gx", "gy", "gz", None),
    )
    out_specs = (P(None, "gx", "gy", "gz"), P("gx", "gy", "gz"))
    return jax.shard_map(local, mesh=mesh, in_specs=in_specs, out_specs=out_specs, check_vma=False)
```

```python
import functools
import math

import jax
import jax.numpy as jnp
from jax import lax
from jax.experimental import pallas as pl
from jax.experimental.pallas import tpu as pltpu
from jax.sharding import PartitionSpec as P

EM_SWEEPS = 4
HEAT_SWEEPS = 2
CAP = 8
LOW, HIGH = 4, 5
F32 = jnp.float32

em_lower = 0.02
em_upper = 3.0
heat_lower = 0.07
heat_upper = 2.0

UP_LAYERS = ((0, 12, 4), (1, 12, 4), (2, 12, 4), (3, 13, 3), (4, 13, 3), (5, 13, 3), (6, 13, 3), (7, 15, 1))
DOWN_LAYERS = ((0, 0, 4), (1, 0, 5), (2, 0, 5), (3, 0, 3), (4, 0, 4), (5, 0, 4), (6, 0, 4), (7, 0, 1))


def spots(layers, shift):
    where, at = {}, 0
    for field, first, count in layers:
        for x in range(first, first + count):
            where[field, x + shift] = at
            at += 1
    return where, at


UP_AT, UP_COUNT = spots(UP_LAYERS, -16)
DOWN_AT, DOWN_COUNT = spots(DOWN_LAYERS, 16)
X_LAYERS = max(UP_COUNT, DOWN_COUNT)


def chebyshev_weights(lower_end, upper_end, sweep_count):
    middle = 0.5 * (upper_end + lower_end)
    radius = 0.5 * (upper_end - lower_end)
    return [
        1.0 / (middle + radius * math.cos(math.pi * (2 * number + 1) / (2 * sweep_count)))
        for number in range(sweep_count)
    ]


EM_WEIGHTS = chebyshev_weights(em_lower, em_upper, EM_SWEEPS)
HEAT_WEIGHTS = chebyshev_weights(heat_lower, heat_upper, HEAT_SWEEPS)


def on_first_core():
    return lax.rem(lax.axis_index("gz"), 2) == 0


def lanes(shape):
    return lax.broadcasted_iota(jnp.int32, shape, len(shape) - 1)


def rows(shape):
    return lax.broadcasted_iota(jnp.int32, shape, len(shape) - 2)


def roll(values, by, axis):
    size = values.shape[axis]
    by = by % size
    return values if by == 0 else pltpu.roll(values, by, axis)


def call(body, out_shapes, scratch=(), name=None, limit=8 << 20, near=False, **options):
    return pl.pallas_call(
        body,
        out_shape=[
            pltpu.VMEM(s, F32) if near else jax.ShapeDtypeStruct(s, F32) for s in out_shapes
        ],
        scratch_shapes=[pltpu.VMEM(s, F32) if isinstance(s, tuple) else s for s in scratch],
        compiler_params=pltpu.CompilerParams(vmem_limit_bytes=limit),
        name=name,
        **options,
    )


def swap_store(first, fwd, bwd, at, up, down):
    fwd[at] = jnp.where(first, up, down)
    bwd[at] = jnp.where(first, down, up)


def y_tiles(v):
    row = rows((8, 128))
    low_half = row < 4
    tops = [a[8:16] for a in v]
    ends = [a[0:8] for a in v]
    ups, downs = [], []
    for pair in range(4):
        a, b = 2 * pair, 2 * pair + 1
        ups.append(jnp.where(low_half, roll(tops[b], 4, 0), tops[a]))
        down = jnp.where(low_half, ends[a], roll(ends[b], 4, 0))
        if pair == 3:
            down = jnp.where(row == 5, roll(ends[0], 1, 0), down)
            down = jnp.where(row == 6, roll(ends[2], 2, 0), down)
        downs.append(down)
    return ups, downs


def put_y_tiles(tiles, first, fwd, bwd, at):
    for pair, (up, down) in enumerate(zip(*tiles)):
        part = pl.ds(8 * pair, 8)
        fwd[at, part] = jnp.where(first, up, down)
        bwd[at, part] = jnp.where(first, down, up)


def pack_x(*refs):
    far, (xf, xb, scaled), near, arrived = refs[:5], refs[5:8], refs[8:13], refs[13]
    copies = [
        pltpu.make_async_copy(a, b, arrived.at[n]) for n, (a, b) in enumerate(zip(far, near))
    ]
    for copy in copies:
        copy.start()
    field, sigma, warmth, storage, source = near
    del storage
    first = on_first_core()
    for at in (0, 1, 2, 4):
        copies[at].wait()
    inverse = 1.0 / (4.0 + sigma[...])
    scaled[3] = inverse
    for c in range(3):
        scaled[c] = source[c] * inverse

    def layer(f, x):
        if f < 3:
            return field[f, x]
        return warmth[x] if f == 7 else scaled[f - 3, x]

    ups = [(f, x) for f, start, n in UP_LAYERS for x in range(start, start + n)]
    downs = [(f, x) for f, start, n in DOWN_LAYERS for x in range(start, start + n)]
    for at in range(X_LAYERS):
        up = layer(*ups[min(at, len(ups) - 1)])
        down = layer(*downs[min(at, len(downs) - 1)])
        swap_store(first, xf, xb, at, up, down)
    copies[3].wait()


def pack_y(field, scaled, warmth, yf, yb):
    first = on_first_core()

    def step(x, carry):
        v = [field[f, x] for f in range(3)] + [scaled[f, x] for f in range(4)] + [warmth[x]]
        put_y_tiles(y_tiles(v), first, yf, yb, x)
        return carry

    lax.fori_loop(0, 16, step, 0, unroll=4)


class Halo:
    def __init__(self, got_fwd, got_bwd):
        self.got_fwd, self.got_bwd = got_fwd, got_bwd
        self.first = on_first_core()
        gx = lax.axis_index("gx")
        self.below, self.above = gx > 0, gx < lax.axis_size("gx") - 1

    def layer(self, f, x):
        if x < 0:
            at, near, far, inside = UP_AT.get((f, x)), self.got_fwd, self.got_bwd, self.below
        else:
            at, near, far, inside = DOWN_AT.get((f, x)), self.got_bwd, self.got_fwd, self.above
        if at is None:
            return None
        return jnp.where(inside, jnp.where(self.first, near[at], far[at]), 0.0)


def pack_corners(xf, xb, targets, fwd, bwd):
    del targets
    halo = Halo(xf, xb)
    zero = jnp.zeros((16, 128), F32)
    row = rows((8, 128)) % 4
    tiles = {}
    for x in HALO_X:
        v = [halo.layer(f, x) for f in range(7)]
        tiles[x] = y_tiles([zero if a is None else a for a in v] + [zero])
    for at, (x, sharer, shift) in enumerate(CORNERS):
        ups, downs = tiles[x]
        if sharer is not None:
            other_ups, other_downs = tiles[sharer]
            ups = [jnp.where(row >= 4 - shift, a, roll(b, -shift, 0)) for a, b in zip(ups, other_ups)]
            downs = [jnp.where(row < shift, a, roll(b, shift, 0)) for a, b in zip(downs, other_downs)]
        put_y_tiles((ups, downs), halo.first, fwd, bwd, at)


def y_halo(first, got, at, pair):
    gy = lax.axis_index("gy")
    part = pl.ds(8 * pair, 8)
    f, b = got[0][at, part], got[1][at, part]
    lower = jnp.where(gy > 0, jnp.where(first, f, b), 0.0)
    upper = jnp.where(gy < lax.axis_size("gy") - 1, jnp.where(first, b, f), 0.0)
    return lower, upper


CORNERS = (
    (-3, None, 0), (-2, None, 0), (-1, None, 0), (16, None, 0), (17, None, 0), (19, -4, 2), (18, 20, 3),
)
HALO_X = tuple(range(-LOW, 0)) + tuple(range(16, 16 + HIGH))
X_ALL = LOW + 16 + HIGH
BLOCKS = 5
Y_LANES = LOW + 16 + HIGH
X_PAIRS = (X_ALL + 1) // 2


def y_slabs(first, got, at, v, shift=0):
    low_half = rows((8, 128)) < 4
    window = lanes((24, 128)) // 16
    slabs, acc = [], None
    for pair in range(4):
        lower, upper = y_halo(first, got, at, pair)
        lower, upper = roll(lower, shift, 0), roll(upper, -shift, 0)
        ends = [jnp.where(low_half, upper, lower)]
        if pair < 3:
            ends.append(roll(jnp.where(low_half, lower, upper), 4, 0))
        else:
            ends.append(roll(upper, 3, 0))
        for f, tile in zip((2 * pair, 2 * pair + 1), ends):
            slabs.append(jnp.concatenate([v[f], tile], axis=0))
            moved = roll(slabs[f], 16 * f + 8, 1)
            acc = moved if acc is None else jnp.where(window == f, moved, acc)
    return slabs, acc


def z_tiles(a, b):
    half = (lanes((24, 128)) // 8) % 2 == 0
    return jnp.where(half, a, roll(b, 8, 1)), jnp.where(half, roll(a, -8, 1), b)


def pack_inner(
    field, scaled, warmth, storage, xf, xb, yf, yb, whole, packed, up, down, began, padded
):
    first, gx = on_first_core(), lax.axis_index("gx")
    low_at, high_at = UP_AT[7, -1], DOWN_AT[7, 16]
    padded[0] = jnp.where(gx > 0, jnp.where(first, xf[low_at], xb[low_at]), 0.0)
    padded[17] = jnp.where(
        gx < lax.axis_size("gx") - 1, jnp.where(first, xb[high_at], xf[high_at]), 0.0
    )
    padded[1:17] = warmth[...]
    row, lane = rows((16, 128)), lanes((16, 128))

    def step(k, carry):
        windows = []
        for x in (2 * k, 2 * k + 1):
            t = warmth[x]
            lower, upper = y_halo(first, (yf, yb), x, 3)
            total = padded[x] + padded[x + 2]
            total = total + jnp.where(row == 0, lower[3:4], roll(t, 1, 0))
            total = total + jnp.where(row == 15, upper[4:5], roll(t, -1, 0))
            total = total + jnp.where(lane == 0, 0.0, roll(t, 1, 1))
            total = total + jnp.where(lane == 127, 0.0, roll(t, -1, 1))
            weight = HEAT_WEIGHTS[0] / (6.0 + storage[x])
            start = t + weight * (total - 6.0 * t)
            began[x] = start
            t = jnp.where(lane == 126, roll(start, -1, 1), t)
            t = jnp.where(lane == 125, roll(weight, -2, 1), t)
            t = jnp.where(lane == 1, roll(start, 1, 1), t)
            t = jnp.where(lane == 2, roll(weight, 2, 1), t)
            v = [field[f, x] for f in range(3)] + [scaled[f, x] for f in range(4)] + [t]
            slabs, acc = y_slabs(first, (yf, yb), x, v)
            for f in range(8):
                whole[f, x] = slabs[f]
            packed[x] = acc
            windows.append(acc)
        up[k], down[k] = z_tiles(*windows)
        return carry

    lax.fori_loop(0, 8, step, 0, unroll=2)


def pack_outer(xf, xb, cf, cb, inner_up, inner_down, swept, whole, packed, up, down):
    del swept
    halo = Halo(xf, xb)
    zero = jnp.zeros((16, 128), F32)
    windows = []
    place_of = {}
    for at, (x, sharer, shift) in enumerate(CORNERS):
        place_of[x], place_of[sharer] = (at, 0), (at, shift)
    for number, x in enumerate(HALO_X):
        v = [halo.layer(f, x) for f in range(7)]
        at, shift = place_of[x]
        slabs, acc = y_slabs(
            halo.first, (cf, cb), at, [zero if a is None else a for a in v] + [zero], shift
        )
        for f in range(8):
            whole[f, number] = slabs[f]
        packed[number] = acc
        windows.append(acc)
    windows.append(jnp.zeros((24, 128), F32))
    for pair in range(len(windows) // 2):
        k = pair if pair < LOW // 2 else pair + 8
        up[k], down[k] = z_tiles(windows[2 * pair], windows[2 * pair + 1])
    up[LOW // 2 : LOW // 2 + 8] = inner_up[...]
    down[LOW // 2 : LOW // 2 + 8] = inner_down[...]


def twist(a, b, c, d):
    return (a - b) - (c - d)


def curls(e, e_up_y, e_up_z, e_up_x):
    (ex, ey, ez), (ex_y, ez_y), (ex_z, ey_z), (ey_x, ez_x) = e, e_up_y, e_up_z, e_up_x
    return twist(ez_y, ez, ey_z, ey), twist(ex_z, ex, ez_x, ez), twist(ey_x, ey, ex_y, ex)


def relaxed(weight, e, h, g, c, c_down_x, c_down_y, c_down_z):
    (cx, cy, cz), (cy_x, cz_x), (cx_y, cz_y), (cx_z, cy_z) = c, c_down_x, c_down_y, c_down_z
    k = twist(cz, cz_y, cy, cy_z), twist(cx, cx_z, cz, cz_x), twist(cy, cy_x, cx, cx_y)
    g = g * weight
    keep = (1.0 - weight) + 4.0 * g
    return [keep * e[f] + weight * h[f] - g * k[f] for f in range(3)]


def lane_curls(get, source, at):
    row = rows((24, 128))
    e = [get(source, f, at) for f in range(3)]
    up_y = roll(e[0], -1, 0), roll(e[2], -1, 0)
    if source == 0:
        up_y = [jnp.where(row == 19, get(0, 7, at)[16 + n : 17 + n], up_y[n]) for n in range(2)]
    up_z = roll(e[0], -1, 1), roll(e[1], -1, 1)
    return e, curls(e, up_y, up_z, (get(source, 1, at + 1), get(source, 2, at + 1)))


def lane_sweep(get, source, at, carry):
    e, c = lane_curls(get, source, at)
    h, g = [get(0, 3 + f, at) for f in range(3)], get(0, 6, at)
    down_y = roll(c[0], 1, 0), roll(c[2], 1, 0)
    down_z = roll(c[0], 1, 1), roll(c[1], 1, 1)
    new = relaxed(EM_WEIGHTS[source], e, h, g, c, carry, down_y, down_z)
    return new, (c[1], c[2])


def bulk(whole, swept):
    def get(number, f, x):
        return whole[f, x] if number == 0 else swept[number - 1, f, x]

    for number in range(EM_SWEEPS - 1):

        def step(x, carry, number=number):
            new, carry = lane_sweep(get, number, x, carry)
            for f in range(3):
                swept[number, f, x] = new[f]
            return carry

        _, c = lane_curls(get, number, number)
        lax.fori_loop(number + 1, 15 - number, step, (c[1], c[2]), unroll=4)


def swept_low(number):
    return range(number - LOW, number)


def swept_high(number):
    return range(16 - number, 21 - number)


def rest_of_bulk(inner, outer, swept, final, whole_sum, shifted, others):
    def get(number, f, x):
        if number == 0:
            return inner[f, x] if 0 <= x < 16 else outer[f, HALO_X.index(x)]
        if number == EM_SWEEPS:
            return final[f, x]
        if number <= x <= 15 - number:
            return swept[number - 1, f, x]
        low, high = swept_low(number), swept_high(number)
        return others[number - 1, f, low.index(x) if x < number else len(low) + high.index(x)]

    for number in range(EM_SWEEPS):
        at = 0
        ranges = (swept_low(number + 1), swept_high(number + 1))
        if number == EM_SWEEPS - 1:
            ranges = (range(17),)
        for layers in ranges:
            _, c = lane_curls(get, number, layers[0] - 1)
            carry = c[1], c[2]
            for x in layers:
                new, carry = lane_sweep(get, number, x, carry)
                for f in range(3):
                    if number == EM_SWEEPS - 1:
                        final[f, x] = new[f]
                    else:
                        others[number, f, at] = new[f]
                at += 1

    for x in range(16):
        ex, ey, ez = (get(EM_SWEEPS, f, x) for f in range(3))
        ey_x, ez_x = (get(EM_SWEEPS, f, x + 1) for f in (1, 2))
        ex, upright = ex * ex, ez * ez + ez_x * ez_x
        flat = (ex + roll(ex, -1, 0)) + (ey * ey + ey_x * ey_x)
        upright = upright + roll(upright, -1, 0)
        whole_sum[x] = flat[0:16] + upright[0:16]
        shifted[x] = roll(flat[0:16], -1, 1)


def of_layer(at):
    return at % BLOCKS, Y_LANES * (at // BLOCKS)


def clear_gaps(stack):
    for block in range(BLOCKS):
        for n in range(BLOCKS):
            at = Y_LANES * n + 24
            stack[block, at : at + 1, :] = jnp.zeros((1, 128), F32)
        stack[block, 125:128, :] = jnp.zeros((3, 128), F32)


def put_layer(stack, at, windows):
    block, lane_at = of_layer(at)
    stack[block, lane_at : lane_at + 24, :] = roll(windows, 4, 0)


def turn(inner, outer, turned, stack):
    clear_gaps(stack)
    for at in range(X_ALL):
        x = at - LOW
        put_layer(stack, at, inner[x] if 0 <= x < 16 else outer[HALO_X.index(x)])
    for block in range(BLOCKS):
        turned[block] = stack[block].T


def edge(
    own, below_z, above_z, whole_sum, shifted, sigma, targets, spread_rows, into, nodes,
    final, send, beside, stack, fields, spare, last, heat,
):
    gz = lax.axis_index("gz")
    half = (lanes((24, 128)) // 8) % 2 == 0
    has_below, has_above = gz > 0, gz < lax.axis_size("gz") - 1
    clear_gaps(stack)
    for k in range(X_PAIRS):
        lower = jnp.where(has_below, below_z[k], 0.0)
        upper = jnp.where(has_above, above_z[k], 0.0)
        for at in range(2 * k, min(2 * k + 2, X_ALL)):
            if at % 2:
                came = jnp.where(half, roll(lower, -8, 1), upper)
            else:
                came = jnp.where(half, lower, roll(upper, 8, 1))
            if 0 <= at - LOW < 16:
                beside[at - LOW] = came[0:16]
            put_layer(stack, at, came)
    for block in range(BLOCKS):
        came = stack[block].T
        for f in range(8):
            for n, part in enumerate((own, came, came, own)):
                at = 16 * f + 8 * (n % 2)
                values = part[block, at : at + 8, :] if part is own else part[at : at + 8]
                fields[block, f, 8 * n : 8 * n + 8, :] = values
    top = lanes((32, 128)) % Y_LANES == 24
    for block in range(BLOCKS):
        extra = fields[block, 7]
        for f, by in ((0, 4), (2, 3)):
            fields[block, f] = jnp.where(top, roll(extra, by, 1), fields[block, f])

    buffers = (fields, spare, final, spare, final)

    def ahead(source, block, f):
        if block < BLOCKS - 1:
            return source[block + 1, f]
        return roll(source[0, f], -Y_LANES, 1)

    def curls_at(source, block):
        e = [source[block, f] for f in range(3)]
        up_y = roll(e[0], -1, 1), roll(e[2], -1, 1)
        up_z = roll(e[0], -1, 0), roll(e[1], -1, 0)
        return e, curls(e, up_y, up_z, (ahead(source, block, 1), ahead(source, block, 2)))

    for number, weight in enumerate(EM_WEIGHTS):
        source, target = buffers[number], buffers[number + 1]
        _, c = curls_at(source, BLOCKS - 1)
        for f in range(3):
            last[f] = c[f]
        before = roll(c[1], Y_LANES, 1), roll(c[2], Y_LANES, 1)
        for block in range(BLOCKS):
            if block < BLOCKS - 1:
                e, c = curls_at(source, block)
            else:
                e, c = [source[block, f] for f in range(3)], [last[f] for f in range(3)]
            h, g = [fields[block, 3 + f] for f in range(3)], fields[block, 6]
            down_y = roll(c[0], 1, 1), roll(c[2], 1, 1)
            down_z = roll(c[0], 1, 0), roll(c[1], 1, 0)
            new = relaxed(weight, e, h, g, c, before, down_y, down_z)
            for f in range(3):
                target[block, f] = new[f]
            before = c[1], c[2]

    for block in range(BLOCKS):
        ex, ey, ez = (final[block, f] * final[block, f] for f in range(3))
        ey_x, ez_x = (ahead(final, block, f) for f in (1, 2))
        flat, upright = (ex + roll(ex, -1, 1)) + (ey + ey_x * ey_x), ez + ez_x * ez_x
        both = flat + (upright + roll(upright, -1, 1))
        stack[block, 0:8, :] = both[24:32]
        stack[block, 120:128, :] = both[0:8]
        stack[block, 59:64, :] = flat[4:9]
        stack[block, 64:67, :] = flat[25:28]
    for block in range(BLOCKS):
        stack[block] = stack[block].T
    lane = lanes((16, 128))
    for x in range(16):
        block, lane_at = of_layer(x + LOW)
        near = stack[block, lane_at + LOW : lane_at + LOW + 16, :]
        here = jnp.where((lane < 4) | (lane >= 124), near, whole_sum[x])
        above = jnp.where((lane < 3) | (lane >= 123), roll(near, 64, 1), shifted[x])
        heat[x] = sigma[x] * (0.25 * (here + above))

    def spread_out(hit, columns, total):
        for _ in range(3):
            piece = columns.astype(jnp.bfloat16)
            columns = columns - piece.astype(F32)
            term = jnp.dot(hit, piece, preferred_element_type=F32)
            total = term if total is None else total + term
        return total

    columns = heat[...].reshape(256, 128)
    send[...] = spread_out(spread_rows[...], columns, None)
    ends = jnp.concatenate([columns[:, 127:128] * into[0], columns[:, 0:1] * into[1]], axis=0)
    target = jnp.concatenate([targets[0:1, :], targets[1:2, :]], axis=1)
    groups = nodes.shape[0]
    hit = (rows((groups, 512)) == target).astype(jnp.bfloat16)
    send[pl.ds(CAP, groups, stride=CAP + 1), :] = spread_out(hit, ends, nodes[...])


def merge(final, near, got, beside, warmth, storage, heat, mid, out, beyond, rest, stack):
    beyond_z(got, beside, warmth, beyond)
    own_part(mid, heat, warmth, storage, rest)
    for block in range(BLOCKS):
        for f in range(3):
            stack[block, 32 * f : 32 * f + 8, :] = near[block, f, 24:32, :]
            at = (32 * f - 8) % 128
            stack[block, at : at + 8, :] = near[block, f, 0:8, :]
    for block in range(BLOCKS):
        stack[block] = stack[block].T
    lane = lanes((16, 128))
    outer = (lane < 4) | (lane >= 124)
    for x in range(16):
        block, lane_at = of_layer(x + LOW)
        windows = stack[block, lane_at + LOW : lane_at + LOW + 16, :]
        for f in range(3):
            inner = final[f, x, 0:16, :]
            out[f, x] = jnp.where(outer, roll(windows, -32 * f, 1), inner)


BELOW, ABOVE = CAP, 3 * CAP


def place(owners, columns, targets, spread_rows, into, nodes):
    planes = lax.axis_size("gz")
    groups = lax.axis_size("gy") * planes
    owner, column = owners[...], columns[...]
    member = rows((groups, 256)) == owner
    earlier = (rows((256, 256)) < lanes((256, 256))).astype(jnp.bfloat16)
    before = jnp.dot(member.astype(jnp.bfloat16), earlier, preferred_element_type=F32)
    rank = jnp.sum(jnp.where(member, before, 0.0), axis=0, keepdims=True).astype(jnp.int32)
    depth = lax.rem(owner, planes)
    to_above = jnp.where(depth < planes - 1, owner + 1, -1)
    to_below = jnp.where(depth > 0, owner - 1, -1)
    count = spread_rows.shape[0]
    spread_rows[...] = (rows((count, 256)) == owner * (CAP + 1) + rank).astype(jnp.bfloat16)
    targets[0:1, :] = to_above
    targets[1:2, :] = to_below
    total = None
    for target, start in ((owner, 0), (to_above, BELOW), (to_below, ABOVE)):
        spread = (rows((groups, 256)) == target).astype(jnp.bfloat16)
        listed = jnp.where(rows((128, 256)) == rank + start, column + 1, 0).astype(F32)
        term = lax.dot_general(
            spread,
            listed.astype(jnp.bfloat16),
            (((1,), (1,)), ((), ())),
            preferred_element_type=F32,
        )
        total = term if total is None else total + term
    nodes[...] = total
    for n, start in enumerate((BELOW + CAP, ABOVE + CAP)):
        into[n] = (rows((128, 256)) == rank + start).astype(F32).T


def warm(got, beside, began, storage, xf, xb, yf, yb, heat, mid):
    first = on_first_core()
    groups = got.shape[0] // (CAP + 1)
    ids = got[pl.ds(CAP, groups, stride=CAP + 1), :].T
    node = rows((256, 1)) + 1
    per = max(1, 128 // groups)
    total = None
    for r in range(0, CAP, per):
        number = jnp.concatenate([ids[r + n : r + n + 1, :] for n in range(per)], axis=1)
        hit = (number == node.astype(F32)).astype(jnp.bfloat16)
        left = jnp.concatenate(
            [got[pl.ds(r + n, groups, stride=CAP + 1), :] for n in range(per)], axis=0
        )
        for _ in range(3):
            piece = left.astype(jnp.bfloat16)
            left = left - piece.astype(F32)
            term = jnp.dot(hit, piece, preferred_element_type=F32)
            total = term if total is None else total + term
    heat[...] = total.reshape(16, 16, 128)
    lane = lanes((16, 128))
    for x in range(16):
        ends = beside[x]
        halo = jnp.where(lane == 0, roll(ends, 9, 1), jnp.where(lane == 127, roll(ends, 7, 1), 0.0))
        mid[x] = began[x] + HEAT_WEIGHTS[0] * (heat[x] + halo) / (6.0 + storage[x])
    xf[...] = jnp.where(first, mid[15], mid[0])
    xb[...] = jnp.where(first, mid[0], mid[15])
    for x in range(16):
        t = mid[x]
        top, end = t[15:16], t[0:1]
        yf[x : x + 1] = jnp.where(first, top, end)
        yb[x : x + 1] = jnp.where(first, end, top)


def own_part(mid, heat, warmth, storage, rest):
    lane, row = lanes((16, 128)), rows((16, 128))
    for x in range(16):
        t = mid[x]
        near = jnp.where(row == 0, 0.0, roll(t, 1, 0)) + jnp.where(row == 15, 0.0, roll(t, -1, 0))
        near = near + jnp.where(lane == 0, 0.0, roll(t, 1, 1))
        near = near + jnp.where(lane == 127, 0.0, roll(t, -1, 1))
        if x > 0:
            near = near + mid[x - 1]
        if x < 15:
            near = near + mid[x + 1]
        s = storage[x]
        push = s * warmth[x] + heat[x] - (6.0 + s) * t + near
        rest[x] = t + HEAT_WEIGHTS[1] * push / (6.0 + s)


def beyond_z(got, beside, warmth, out):
    groups = got.shape[0] // (CAP + 1)
    listing = got[pl.ds(CAP, groups, stride=CAP + 1), :].T
    node = (rows((256, 1)) + 1).astype(F32)
    per = max(1, 128 // groups)

    def beside_rows(at):
        return jnp.concatenate([listing[at + n : at + n + 1, :] for n in range(per)], axis=1)

    heat = []
    for start in (BELOW, ABOVE):
        total = None
        for r in range(0, CAP, per):
            hit = beside_rows(start + r) == node
            term = jnp.where(hit, beside_rows(start + CAP + r), 0.0)
            total = term if total is None else total + term
        heat.append(jnp.sum(total, axis=1, keepdims=True))
    lane = lanes((16, 128))
    for x in range(16):
        ends, t = beside[x], warmth[x]
        part = slice(16 * x, 16 * x + 16)
        low = ends[:, 118:119] + ends[:, 117:118] * (t[:, 0:1] + heat[0][part])
        high = ends[:, 121:122] + ends[:, 122:123] * (t[:, 127:128] + heat[1][part])
        out[x] = jnp.where(lane == 0, low, jnp.where(lane == 127, high, 0.0))


def finish(rest, storage, xf, xb, yf, yb, beyond, out):
    first = on_first_core()
    gx, gy = lax.axis_index("gx"), lax.axis_index("gy")
    f, b = xf[...], xb[...]
    x_low = jnp.where(gx > 0, jnp.where(first, f, b), 0.0)
    x_high = jnp.where(gx < lax.axis_size("gx") - 1, jnp.where(first, b, f), 0.0)
    f, b = yf[...], yb[...]
    y_low = jnp.where(gy > 0, jnp.where(first, f, b), 0.0)
    y_high = jnp.where(gy < lax.axis_size("gy") - 1, jnp.where(first, b, f), 0.0)
    row = rows((16, 128))
    for x in range(16):
        near = beyond[x] + jnp.where(row == 0, y_low[x : x + 1], 0.0)
        near = near + jnp.where(row == 15, y_high[x : x + 1], 0.0)
        if x == 0:
            near = near + x_low
        if x == 15:
            near = near + x_high
        out[x] = rest[x] + HEAT_WEIGHTS[1] * near / (6.0 + storage[x])


def around(axis):
    n, m = lax.axis_size(axis), lax.axis_size("gz")

    def target(a, c):
        to = a + (1 if c % 2 == 0 else -1)
        return (to, c) if 0 <= to < n else (a, c ^ 1)

    forward = []
    for a in range(n):
        for c in range(m):
            to = target(a, c)
            forward.append((a * m + c, to[0] * m + to[1]))
    return forward, [(j, i) for i, j in forward]


def exchange(axis, fwd, bwd):
    forward, backward = around(axis)
    names = (axis, "gz")
    return lax.ppermute(fwd, names, forward), lax.ppermute(bwd, names, backward)


def exchange_z(up, down):
    m = lax.axis_size("gz")
    ring = [(i, (i + 1) % m) for i in range(m)]
    return lax.ppermute(up, "gz", ring), lax.ppermute(down, "gz", [(j, i) for i, j in ring])


def local(field, source, sigma, warmth, storage, partition, column):
    groups = lax.axis_size("gy") * lax.axis_size("gz")
    count = groups * (CAP + 1)
    cube = (16, 16, 128)
    face = (16, 128)
    x_message, y_message, corners = (X_LAYERS, 16, 128), (16, 32, 128), (len(CORNERS), 32, 128)
    here = (field, sigma, warmth, storage, source)
    xf, xb, scaled, field, sigma, warmth, storage = call(
        pack_x,
        [x_message, x_message, (4, *cube), (3, *cube), cube, cube, cube],
        [(3, *cube), pltpu.SemaphoreType.DMA((5,))],
        name="pack_x",
        near=True,
        in_specs=[pl.BlockSpec(memory_space=pltpu.HBM)] * 5,
    )(*(pltpu.with_memory_space_constraint(v, pltpu.HBM) for v in here))
    xf, xb = exchange("gx", xf, xb)
    yf, yb = call(pack_y, [y_message, y_message], name="pack_y", near=True)(field, scaled, warmth)
    yf, yb = exchange("gy", yf, yb)
    targets, spread_rows, into, nodes = pl.pallas_call(
        place,
        out_shape=[
            jax.ShapeDtypeStruct((2, 256), jnp.int32),
            jax.ShapeDtypeStruct((count, 256), jnp.bfloat16),
            jax.ShapeDtypeStruct((2, 256, 128), F32),
            jax.ShapeDtypeStruct((groups, 128), F32),
        ],
        compiler_params=pltpu.CompilerParams(vmem_limit_bytes=8 << 20),
        name="place",
    )(partition.reshape(1, 256), column.reshape(1, 256))
    cf, cb = call(pack_corners, [corners, corners], name="pack_corners")(
        xf, xb, targets
    )
    cf, cb = exchange("gy", cf, cb)
    layer, halo = (24, 128), len(HALO_X)
    inner, inner_packed, inner_up, inner_down, began = call(
        pack_inner,
        [(8, 16, *layer), (16, *layer), (8, *layer), (8, *layer), cube],
        [(18, 16, 128)],
        name="pack_inner",
        near=True,
    )(field, scaled, warmth, storage, xf, xb, yf, yb)
    (swept,) = call(
        bulk,
        [(EM_SWEEPS - 1, 3, 16, *layer)],
        name="bulk",
        near=True,
        cost_estimate=pl.CostEstimate(flops=10**9, bytes_accessed=10**7, transcendentals=0),
    )(inner)
    outer, outer_packed, up, down = call(
        pack_outer,
        [(8, halo, *layer), (halo, *layer), (X_PAIRS, *layer), (X_PAIRS, *layer)],
        name="pack_outer",
        near=True,
    )(xf, xb, cf, cb, inner_up, inner_down, swept)
    below_z, above_z = exchange_z(up, down)
    final, whole_sum, shifted = call(
        rest_of_bulk,
        [(3, 17, *layer), cube, cube],
        [(EM_SWEEPS - 1, 3, halo, *layer)],
        name="rest_of_bulk",
        near=True,
        cost_estimate=pl.CostEstimate(flops=10**9, bytes_accessed=10**7, transcendentals=0),
    )(inner, outer, swept)
    (own,) = call(
        turn,
        [(BLOCKS, 128, 128)],
        [(BLOCKS, 128, 128)],
        name="turn",
        near=True,
        cost_estimate=pl.CostEstimate(flops=10**8, bytes_accessed=10**6, transcendentals=0),
    )(inner_packed, outer_packed)
    near, send, beside = call(
        edge,
        [(BLOCKS, 3, 32, 128), (count, 128), cube],
        [
            (BLOCKS, 128, 128),
            (BLOCKS, 8, 32, 128),
            (BLOCKS, 3, 32, 128),
            (3, 32, 128),
            cube,
        ],
        name="edge",
        near=True,
    )(
        own, below_z, above_z, whole_sum, shifted, sigma, targets, spread_rows, into, nodes
    )
    got = lax.all_to_all(
        send.reshape(count, 1, 128), ("gy", "gz"), split_axis=0, concat_axis=0, tiled=True
    ).reshape(count, 128)
    xf, xb, yf, yb, heat, mid = call(
        warm, [face, face, face, face, cube, cube], name="warm", near=True
    )(got, beside, began, storage)
    xf, xb = exchange("gx", xf, xb)
    yf, yb = exchange("gy", yf, yb)
    out, beyond, rest = call(
        merge,
        [(3, *cube), cube, cube],
        [(BLOCKS, 128, 128)],
        name="merge",
        cost_estimate=pl.CostEstimate(flops=10**9, bytes_accessed=10**6, transcendentals=0),
    )(final, near, got, beside, warmth, storage, heat, mid)
    (updated,) = call(finish, [cube], name="finish")(rest, storage, xf, xb, yf, yb, beyond)
    return out, updated


def solution(mesh):
    in_specs = (
        P(None, "gx", "gy", "gz"),
        P(None, "gx", "gy", "gz"),
        P("gx", "gy", "gz"),
        P("gx", "gy", "gz"),
        P("gx", "gy", "gz"),
        P("gx", "gy", "gz", None, None),
        P("gx", "gy", "gz", None),
    )
    out_specs = (P(None, "gx", "gy", "gz"), P("gx", "gy", "gz"))
    return jax.shard_map(local, mesh=mesh, in_specs=in_specs, out_specs=out_specs, check_vma=False)
```

```python
import functools
import math

import jax
import jax.numpy as jnp
from jax import lax
from jax.experimental import pallas as pl
from jax.experimental.pallas import tpu as pltpu
from jax.sharding import PartitionSpec as P

EM_SWEEPS = 4
HEAT_SWEEPS = 2
CAP = 8
LOW, HIGH = 4, 5
F32 = jnp.float32

em_lower = 0.02
em_upper = 3.0
heat_lower = 0.07
heat_upper = 2.0

UP_LAYERS = ((0, 12, 4), (1, 12, 4), (2, 12, 4), (3, 13, 3), (4, 13, 3), (5, 13, 3), (6, 13, 3), (7, 15, 1))
DOWN_LAYERS = ((0, 0, 4), (1, 0, 5), (2, 0, 5), (3, 0, 3), (4, 0, 4), (5, 0, 4), (6, 0, 4), (7, 0, 1))


def spots(layers, shift):
    where, at = {}, 0
    for field, first, count in layers:
        for x in range(first, first + count):
            where[field, x + shift] = at
            at += 1
    return where, at


UP_AT, UP_COUNT = spots(UP_LAYERS, -16)
DOWN_AT, DOWN_COUNT = spots(DOWN_LAYERS, 16)
X_LAYERS = max(UP_COUNT, DOWN_COUNT)


def chebyshev_weights(lower_end, upper_end, sweep_count):
    middle = 0.5 * (upper_end + lower_end)
    radius = 0.5 * (upper_end - lower_end)
    return [
        1.0 / (middle + radius * math.cos(math.pi * (2 * number + 1) / (2 * sweep_count)))
        for number in range(sweep_count)
    ]


EM_WEIGHTS = chebyshev_weights(em_lower, em_upper, EM_SWEEPS)
HEAT_WEIGHTS = chebyshev_weights(heat_lower, heat_upper, HEAT_SWEEPS)


def on_first_core():
    return lax.rem(lax.axis_index("gz"), 2) == 0


def lanes(shape):
    return lax.broadcasted_iota(jnp.int32, shape, len(shape) - 1)


def rows(shape):
    return lax.broadcasted_iota(jnp.int32, shape, len(shape) - 2)


def roll(values, by, axis):
    size = values.shape[axis]
    by = by % size
    return values if by == 0 else pltpu.roll(values, by, axis)


def call(body, out_shapes, scratch=(), name=None, limit=8 << 20, near=False, **options):
    return pl.pallas_call(
        body,
        out_shape=[
            pltpu.VMEM(s, F32) if near else jax.ShapeDtypeStruct(s, F32) for s in out_shapes
        ],
        scratch_shapes=[pltpu.VMEM(s, F32) if isinstance(s, tuple) else s for s in scratch],
        compiler_params=pltpu.CompilerParams(vmem_limit_bytes=limit),
        name=name,
        **options,
    )


def swap_store(first, fwd, bwd, at, up, down):
    fwd[at] = jnp.where(first, up, down)
    bwd[at] = jnp.where(first, down, up)


def y_tiles(v):
    row = rows((8, 128))
    low_half = row < 4
    tops = [a[8:16] for a in v]
    ends = [a[0:8] for a in v]
    ups, downs = [], []
    for pair in range(4):
        a, b = 2 * pair, 2 * pair + 1
        ups.append(jnp.where(low_half, roll(tops[b], 4, 0), tops[a]))
        down = jnp.where(low_half, ends[a], roll(ends[b], 4, 0))
        if pair == 3:
            down = jnp.where(row == 5, roll(ends[0], 1, 0), down)
            down = jnp.where(row == 6, roll(ends[2], 2, 0), down)
        downs.append(down)
    return ups, downs


def put_y_tiles(tiles, first, fwd, bwd, at):
    for pair, (up, down) in enumerate(zip(*tiles)):
        part = pl.ds(8 * pair, 8)
        fwd[at, part] = jnp.where(first, up, down)
        bwd[at, part] = jnp.where(first, down, up)


def pack_x(*refs):
    far, (xf, xb, scaled), near, arrived = refs[:5], refs[5:8], refs[8:13], refs[13]
    copies = [
        pltpu.make_async_copy(a, b, arrived.at[n]) for n, (a, b) in enumerate(zip(far, near))
    ]
    for copy in copies:
        copy.start()
    field, sigma, warmth, storage, source = near
    del storage
    first = on_first_core()
    for at in (0, 1, 2, 4):
        copies[at].wait()
    inverse = 1.0 / (4.0 + sigma[...])
    scaled[3] = inverse
    for c in range(3):
        scaled[c] = source[c] * inverse

    def layer(f, x):
        if f < 3:
            return field[f, x]
        return warmth[x] if f == 7 else scaled[f - 3, x]

    ups = [(f, x) for f, start, n in UP_LAYERS for x in range(start, start + n)]
    downs = [(f, x) for f, start, n in DOWN_LAYERS for x in range(start, start + n)]
    for at in range(X_LAYERS):
        up = layer(*ups[min(at, len(ups) - 1)])
        down = layer(*downs[min(at, len(downs) - 1)])
        swap_store(first, xf, xb, at, up, down)
    copies[3].wait()


def pack_y(field, scaled, warmth, yf, yb):
    first = on_first_core()

    def step(x, carry):
        v = [field[f, x] for f in range(3)] + [scaled[f, x] for f in range(4)] + [warmth[x]]
        put_y_tiles(y_tiles(v), first, yf, yb, x)
        return carry

    lax.fori_loop(0, 16, step, 0, unroll=4)


class Halo:
    def __init__(self, got_fwd, got_bwd):
        self.got_fwd, self.got_bwd = got_fwd, got_bwd
        self.first = on_first_core()
        gx = lax.axis_index("gx")
        self.below, self.above = gx > 0, gx < lax.axis_size("gx") - 1

    def layer(self, f, x):
        if x < 0:
            at, near, far, inside = UP_AT.get((f, x)), self.got_fwd, self.got_bwd, self.below
        else:
            at, near, far, inside = DOWN_AT.get((f, x)), self.got_bwd, self.got_fwd, self.above
        if at is None:
            return None
        return jnp.where(inside, jnp.where(self.first, near[at], far[at]), 0.0)


def pack_corners(xf, xb, targets, fwd, bwd):
    del targets
    halo = Halo(xf, xb)
    zero = jnp.zeros((16, 128), F32)
    row = rows((8, 128)) % 4
    tiles = {}
    for x in HALO_X:
        v = [halo.layer(f, x) for f in range(7)]
        tiles[x] = y_tiles([zero if a is None else a for a in v] + [zero])
    for at, (x, sharer, shift) in enumerate(CORNERS):
        ups, downs = tiles[x]
        if sharer is not None:
            other_ups, other_downs = tiles[sharer]
            ups = [jnp.where(row >= 4 - shift, a, roll(b, -shift, 0)) for a, b in zip(ups, other_ups)]
            downs = [jnp.where(row < shift, a, roll(b, shift, 0)) for a, b in zip(downs, other_downs)]
        put_y_tiles((ups, downs), halo.first, fwd, bwd, at)


def y_halo(first, got, at, pair):
    gy = lax.axis_index("gy")
    part = pl.ds(8 * pair, 8)
    f, b = got[0][at, part], got[1][at, part]
    lower = jnp.where(gy > 0, jnp.where(first, f, b), 0.0)
    upper = jnp.where(gy < lax.axis_size("gy") - 1, jnp.where(first, b, f), 0.0)
    return lower, upper


CORNERS = (
    (-3, None, 0), (-2, None, 0), (-1, None, 0), (16, None, 0), (17, None, 0), (19, -4, 2), (18, 20, 3),
)
HALO_X = tuple(range(-LOW, 0)) + tuple(range(16, 16 + HIGH))
X_ALL = LOW + 16 + HIGH
BLOCKS = 5
Y_LANES = LOW + 16 + HIGH
X_PAIRS = (X_ALL + 1) // 2


def y_slabs(first, got, at, v, shift=0):
    low_half = rows((8, 128)) < 4
    window = lanes((24, 128)) // 16
    slabs, acc = [], None
    for pair in range(4):
        lower, upper = y_halo(first, got, at, pair)
        lower, upper = roll(lower, shift, 0), roll(upper, -shift, 0)
        ends = [jnp.where(low_half, upper, lower)]
        if pair < 3:
            ends.append(roll(jnp.where(low_half, lower, upper), 4, 0))
        else:
            ends.append(roll(upper, 3, 0))
        for f, tile in zip((2 * pair, 2 * pair + 1), ends):
            slabs.append(jnp.concatenate([v[f], tile], axis=0))
            moved = roll(slabs[f], 16 * f + 8, 1)
            acc = moved if acc is None else jnp.where(window == f, moved, acc)
    return slabs, acc


def z_tiles(a, b):
    half = (lanes((24, 128)) // 8) % 2 == 0
    return jnp.where(half, a, roll(b, 8, 1)), jnp.where(half, roll(a, -8, 1), b)


def pack_inner(
    field, scaled, warmth, storage, xf, xb, yf, yb, whole, packed, up, down, began, padded
):
    first, gx = on_first_core(), lax.axis_index("gx")
    low_at, high_at = UP_AT[7, -1], DOWN_AT[7, 16]
    padded[0] = jnp.where(gx > 0, jnp.where(first, xf[low_at], xb[low_at]), 0.0)
    padded[17] = jnp.where(
        gx < lax.axis_size("gx") - 1, jnp.where(first, xb[high_at], xf[high_at]), 0.0
    )
    padded[1:17] = warmth[...]
    row, lane = rows((16, 128)), lanes((16, 128))

    def step(k, carry):
        windows = []
        for x in (2 * k, 2 * k + 1):
            t = warmth[x]
            lower, upper = y_halo(first, (yf, yb), x, 3)
            total = padded[x] + padded[x + 2]
            total = total + jnp.where(row == 0, lower[3:4], roll(t, 1, 0))
            total = total + jnp.where(row == 15, upper[4:5], roll(t, -1, 0))
            total = total + jnp.where(lane == 0, 0.0, roll(t, 1, 1))
            total = total + jnp.where(lane == 127, 0.0, roll(t, -1, 1))
            weight = HEAT_WEIGHTS[0] / (6.0 + storage[x])
            start = t + weight * (total - 6.0 * t)
            began[x] = start
            t = jnp.where(lane == 126, roll(start, -1, 1), t)
            t = jnp.where(lane == 125, roll(weight, -2, 1), t)
            t = jnp.where(lane == 1, roll(start, 1, 1), t)
            t = jnp.where(lane == 2, roll(weight, 2, 1), t)
            v = [field[f, x] for f in range(3)] + [scaled[f, x] for f in range(4)] + [t]
            slabs, acc = y_slabs(first, (yf, yb), x, v)
            for f in range(8):
                whole[f, x] = slabs[f]
            packed[x] = acc
            windows.append(acc)
        up[k], down[k] = z_tiles(*windows)
        return carry

    lax.fori_loop(0, 8, step, 0, unroll=4)


def pack_outer(xf, xb, cf, cb, inner_up, inner_down, swept, whole, packed, up, down):
    del swept
    halo = Halo(xf, xb)
    zero = jnp.zeros((16, 128), F32)
    windows = []
    place_of = {}
    for at, (x, sharer, shift) in enumerate(CORNERS):
        place_of[x], place_of[sharer] = (at, 0), (at, shift)
    for number, x in enumerate(HALO_X):
        v = [halo.layer(f, x) for f in range(7)]
        at, shift = place_of[x]
        slabs, acc = y_slabs(
            halo.first, (cf, cb), at, [zero if a is None else a for a in v] + [zero], shift
        )
        for f in range(8):
            whole[f, number] = slabs[f]
        packed[number] = acc
        windows.append(acc)
    windows.append(jnp.zeros((24, 128), F32))
    for pair in range(len(windows) // 2):
        k = pair if pair < LOW // 2 else pair + 8
        up[k], down[k] = z_tiles(windows[2 * pair], windows[2 * pair + 1])
    up[LOW // 2 : LOW // 2 + 8] = inner_up[...]
    down[LOW // 2 : LOW // 2 + 8] = inner_down[...]


def twist(a, b, c, d):
    return (a - b) - (c - d)


def curls(e, e_up_y, e_up_z, e_up_x):
    (ex, ey, ez), (ex_y, ez_y), (ex_z, ey_z), (ey_x, ez_x) = e, e_up_y, e_up_z, e_up_x
    return twist(ez_y, ez, ey_z, ey), twist(ex_z, ex, ez_x, ez), twist(ey_x, ey, ex_y, ex)


def relaxed(weight, e, h, g, c, c_down_x, c_down_y, c_down_z):
    (cx, cy, cz), (cy_x, cz_x), (cx_y, cz_y), (cx_z, cy_z) = c, c_down_x, c_down_y, c_down_z
    k = twist(cz, cz_y, cy, cy_z), twist(cx, cx_z, cz, cz_x), twist(cy, cy_x, cx, cx_y)
    g = g * weight
    keep = (1.0 - weight) + 4.0 * g
    return [keep * e[f] + weight * h[f] - g * k[f] for f in range(3)]


def lane_curls(get, source, at):
    row = rows((24, 128))
    e = [get(source, f, at) for f in range(3)]
    up_y = roll(e[0], -1, 0), roll(e[2], -1, 0)
    if source == 0:
        up_y = [jnp.where(row == 19, get(0, 7, at)[16 + n : 17 + n], up_y[n]) for n in range(2)]
    up_z = roll(e[0], -1, 1), roll(e[1], -1, 1)
    return e, curls(e, up_y, up_z, (get(source, 1, at + 1), get(source, 2, at + 1)))


def lane_sweep(get, source, at, carry):
    e, c = lane_curls(get, source, at)
    h, g = [get(0, 3 + f, at) for f in range(3)], get(0, 6, at)
    down_y = roll(c[0], 1, 0), roll(c[2], 1, 0)
    down_z = roll(c[0], 1, 1), roll(c[1], 1, 1)
    new = relaxed(EM_WEIGHTS[source], e, h, g, c, carry, down_y, down_z)
    return new, (c[1], c[2])


def bulk(whole, swept):
    def get(number, f, x):
        return whole[f, x] if number == 0 else swept[number - 1, f, x]

    for number in range(EM_SWEEPS - 1):

        def step(x, carry, number=number):
            new, carry = lane_sweep(get, number, x, carry)
            for f in range(3):
                swept[number, f, x] = new[f]
            return carry

        _, c = lane_curls(get, number, number)
        lax.fori_loop(number + 1, 15 - number, step, (c[1], c[2]), unroll=6)


def swept_low(number):
    return range(number - LOW, number)


def swept_high(number):
    return range(16 - number, 21 - number)


def rest_of_bulk(inner, outer, swept, final, whole_sum, shifted, others):
    def get(number, f, x):
        if number == 0:
            return inner[f, x] if 0 <= x < 16 else outer[f, HALO_X.index(x)]
        if number == EM_SWEEPS:
            return final[f, x]
        if number <= x <= 15 - number:
            return swept[number - 1, f, x]
        low, high = swept_low(number), swept_high(number)
        return others[number - 1, f, low.index(x) if x < number else len(low) + high.index(x)]

    for number in range(EM_SWEEPS):
        at = 0
        ranges = (swept_low(number + 1), swept_high(number + 1))
        if number == EM_SWEEPS - 1:
            ranges = (range(17),)
        for layers in ranges:
            _, c = lane_curls(get, number, layers[0] - 1)
            carry = c[1], c[2]
            for x in layers:
                new, carry = lane_sweep(get, number, x, carry)
                for f in range(3):
                    if number == EM_SWEEPS - 1:
                        final[f, x] = new[f]
                    else:
                        others[number, f, at] = new[f]
                at += 1

    for x in range(16):
        ex, ey, ez = (get(EM_SWEEPS, f, x) for f in range(3))
        ey_x, ez_x = (get(EM_SWEEPS, f, x + 1) for f in (1, 2))
        ex, upright = ex * ex, ez * ez + ez_x * ez_x
        flat = (ex + roll(ex, -1, 0)) + (ey * ey + ey_x * ey_x)
        upright = upright + roll(upright, -1, 0)
        whole_sum[x] = flat[0:16] + upright[0:16]
        shifted[x] = roll(flat[0:16], -1, 1)


def of_layer(at):
    return at % BLOCKS, Y_LANES * (at // BLOCKS)


def clear_gaps(stack):
    for block in range(BLOCKS):
        for n in range(BLOCKS):
            at = Y_LANES * n + 24
            stack[block, at : at + 1, :] = jnp.zeros((1, 128), F32)
        stack[block, 125:128, :] = jnp.zeros((3, 128), F32)


def put_layer(stack, at, windows):
    block, lane_at = of_layer(at)
    stack[block, lane_at : lane_at + 24, :] = roll(windows, 4, 0)


def turn(inner, outer, turned, stack):
    clear_gaps(stack)
    for at in range(X_ALL):
        x = at - LOW
        put_layer(stack, at, inner[x] if 0 <= x < 16 else outer[HALO_X.index(x)])
    for block in range(BLOCKS):
        turned[block] = stack[block].T


def edge(
    own, below_z, above_z, whole_sum, shifted, sigma, targets, spread_rows, into, nodes,
    final, send, beside, stack, fields, spare, last, heat,
):
    gz = lax.axis_index("gz")
    half = (lanes((24, 128)) // 8) % 2 == 0
    has_below, has_above = gz > 0, gz < lax.axis_size("gz") - 1
    clear_gaps(stack)
    for k in range(X_PAIRS):
        lower = jnp.where(has_below, below_z[k], 0.0)
        upper = jnp.where(has_above, above_z[k], 0.0)
        for at in range(2 * k, min(2 * k + 2, X_ALL)):
            if at % 2:
                came = jnp.where(half, roll(lower, -8, 1), upper)
            else:
                came = jnp.where(half, lower, roll(upper, 8, 1))
            if 0 <= at - LOW < 16:
                beside[at - LOW] = came[0:16]
            put_layer(stack, at, came)
    for block in range(BLOCKS):
        came = stack[block].T
        for f in range(8):
            for n, part in enumerate((own, came, came, own)):
                at = 16 * f + 8 * (n % 2)
                values = part[block, at : at + 8, :] if part is own else part[at : at + 8]
                fields[block, f, 8 * n : 8 * n + 8, :] = values
    top = lanes((32, 128)) % Y_LANES == 24
    for block in range(BLOCKS):
        extra = fields[block, 7]
        for f, by in ((0, 4), (2, 3)):
            fields[block, f] = jnp.where(top, roll(extra, by, 1), fields[block, f])

    buffers = (fields, spare, final, spare, final)

    def ahead(source, block, f):
        if block < BLOCKS - 1:
            return source[block + 1, f]
        return roll(source[0, f], -Y_LANES, 1)

    def curls_at(source, block):
        e = [source[block, f] for f in range(3)]
        up_y = roll(e[0], -1, 1), roll(e[2], -1, 1)
        up_z = roll(e[0], -1, 0), roll(e[1], -1, 0)
        return e, curls(e, up_y, up_z, (ahead(source, block, 1), ahead(source, block, 2)))

    for number, weight in enumerate(EM_WEIGHTS):
        source, target = buffers[number], buffers[number + 1]
        _, c = curls_at(source, BLOCKS - 1)
        for f in range(3):
            last[f] = c[f]
        before = roll(c[1], Y_LANES, 1), roll(c[2], Y_LANES, 1)
        for block in range(BLOCKS):
            if block < BLOCKS - 1:
                e, c = curls_at(source, block)
            else:
                e, c = [source[block, f] for f in range(3)], [last[f] for f in range(3)]
            h, g = [fields[block, 3 + f] for f in range(3)], fields[block, 6]
            down_y = roll(c[0], 1, 1), roll(c[2], 1, 1)
            down_z = roll(c[0], 1, 0), roll(c[1], 1, 0)
            new = relaxed(weight, e, h, g, c, before, down_y, down_z)
            for f in range(3):
                target[block, f] = new[f]
            before = c[1], c[2]

    for block in range(BLOCKS):
        ex, ey, ez = (final[block, f] * final[block, f] for f in range(3))
        ey_x, ez_x = (ahead(final, block, f) for f in (1, 2))
        flat, upright = (ex + roll(ex, -1, 1)) + (ey + ey_x * ey_x), ez + ez_x * ez_x
        both = flat + (upright + roll(upright, -1, 1))
        stack[block, 0:8, :] = both[24:32]
        stack[block, 120:128, :] = both[0:8]
        stack[block, 59:64, :] = flat[4:9]
        stack[block, 64:67, :] = flat[25:28]
    for block in range(BLOCKS):
        stack[block] = stack[block].T
    lane = lanes((16, 128))
    for x in range(16):
        block, lane_at = of_layer(x + LOW)
        near = stack[block, lane_at + LOW : lane_at + LOW + 16, :]
        here = jnp.where((lane < 4) | (lane >= 124), near, whole_sum[x])
        above = jnp.where((lane < 3) | (lane >= 123), roll(near, 64, 1), shifted[x])
        heat[x] = sigma[x] * (0.25 * (here + above))

    def spread_out(hit, columns, total):
        for _ in range(3):
            piece = columns.astype(jnp.bfloat16)
            columns = columns - piece.astype(F32)
            term = jnp.dot(hit, piece, preferred_element_type=F32)
            total = term if total is None else total + term
        return total

    columns = heat[...].reshape(256, 128)
    send[...] = spread_out(spread_rows[...], columns, None)
    ends = jnp.concatenate([columns[:, 127:128] * into[0], columns[:, 0:1] * into[1]], axis=0)
    target = jnp.concatenate([targets[0:1, :], targets[1:2, :]], axis=1)
    groups = nodes.shape[0]
    hit = (rows((groups, 512)) == target).astype(jnp.bfloat16)
    send[pl.ds(CAP, groups, stride=CAP + 1), :] = spread_out(hit, ends, nodes[...])


def merge(final, near, got, beside, warmth, storage, heat, mid, out, beyond, rest, stack):
    beyond_z(got, beside, warmth, beyond)
    own_part(mid, heat, warmth, storage, rest)
    for block in range(BLOCKS):
        for f in range(3):
            stack[block, 32 * f : 32 * f + 8, :] = near[block, f, 24:32, :]
            at = (32 * f - 8) % 128
            stack[block, at : at + 8, :] = near[block, f, 0:8, :]
    for block in range(BLOCKS):
        stack[block] = stack[block].T
    lane = lanes((16, 128))
    outer = (lane < 4) | (lane >= 124)
    for x in range(16):
        block, lane_at = of_layer(x + LOW)
        windows = stack[block, lane_at + LOW : lane_at + LOW + 16, :]
        for f in range(3):
            inner = final[f, x, 0:16, :]
            out[f, x] = jnp.where(outer, roll(windows, -32 * f, 1), inner)


BELOW, ABOVE = CAP, 3 * CAP


def place(owners, columns, targets, spread_rows, into, nodes):
    planes = lax.axis_size("gz")
    groups = lax.axis_size("gy") * planes
    owner, column = owners[...], columns[...]
    member = rows((groups, 256)) == owner
    earlier = (rows((256, 256)) < lanes((256, 256))).astype(jnp.bfloat16)
    before = jnp.dot(member.astype(jnp.bfloat16), earlier, preferred_element_type=F32)
    rank = jnp.sum(jnp.where(member, before, 0.0), axis=0, keepdims=True).astype(jnp.int32)
    depth = lax.rem(owner, planes)
    to_above = jnp.where(depth < planes - 1, owner + 1, -1)
    to_below = jnp.where(depth > 0, owner - 1, -1)
    count = spread_rows.shape[0]
    spread_rows[...] = (rows((count, 256)) == owner * (CAP + 1) + rank).astype(jnp.bfloat16)
    targets[0:1, :] = to_above
    targets[1:2, :] = to_below
    total = None
    for target, start in ((owner, 0), (to_above, BELOW), (to_below, ABOVE)):
        spread = (rows((groups, 256)) == target).astype(jnp.bfloat16)
        listed = jnp.where(rows((128, 256)) == rank + start, column + 1, 0).astype(F32)
        term = lax.dot_general(
            spread,
            listed.astype(jnp.bfloat16),
            (((1,), (1,)), ((), ())),
            preferred_element_type=F32,
        )
        total = term if total is None else total + term
    nodes[...] = total
    for n, start in enumerate((BELOW + CAP, ABOVE + CAP)):
        into[n] = (rows((128, 256)) == rank + start).astype(F32).T


def warm(got, beside, began, storage, xf, xb, yf, yb, heat, mid):
    first = on_first_core()
    groups = got.shape[0] // (CAP + 1)
    ids = got[pl.ds(CAP, groups, stride=CAP + 1), :].T
    node = rows((256, 1)) + 1
    per = max(1, 128 // groups)
    total = None
    for r in range(0, CAP, per):
        number = jnp.concatenate([ids[r + n : r + n + 1, :] for n in range(per)], axis=1)
        hit = (number == node.astype(F32)).astype(jnp.bfloat16)
        left = jnp.concatenate(
            [got[pl.ds(r + n, groups, stride=CAP + 1), :] for n in range(per)], axis=0
        )
        for _ in range(3):
            piece = left.astype(jnp.bfloat16)
            left = left - piece.astype(F32)
            term = jnp.dot(hit, piece, preferred_element_type=F32)
            total = term if total is None else total + term
    heat[...] = total.reshape(16, 16, 128)
    lane = lanes((16, 128))
    for x in range(16):
        ends = beside[x]
        halo = jnp.where(lane == 0, roll(ends, 9, 1), jnp.where(lane == 127, roll(ends, 7, 1), 0.0))
        mid[x] = began[x] + HEAT_WEIGHTS[0] * (heat[x] + halo) / (6.0 + storage[x])
    xf[...] = jnp.where(first, mid[15], mid[0])
    xb[...] = jnp.where(first, mid[0], mid[15])
    for x in range(16):
        t = mid[x]
        top, end = t[15:16], t[0:1]
        yf[x : x + 1] = jnp.where(first, top, end)
        yb[x : x + 1] = jnp.where(first, end, top)


def own_part(mid, heat, warmth, storage, rest):
    lane, row = lanes((16, 128)), rows((16, 128))
    for x in range(16):
        t = mid[x]
        near = jnp.where(row == 0, 0.0, roll(t, 1, 0)) + jnp.where(row == 15, 0.0, roll(t, -1, 0))
        near = near + jnp.where(lane == 0, 0.0, roll(t, 1, 1))
        near = near + jnp.where(lane == 127, 0.0, roll(t, -1, 1))
        if x > 0:
            near = near + mid[x - 1]
        if x < 15:
            near = near + mid[x + 1]
        s = storage[x]
        push = s * warmth[x] + heat[x] - (6.0 + s) * t + near
        rest[x] = t + HEAT_WEIGHTS[1] * push / (6.0 + s)


def beyond_z(got, beside, warmth, out):
    groups = got.shape[0] // (CAP + 1)
    listing = got[pl.ds(CAP, groups, stride=CAP + 1), :].T
    node = (rows((256, 1)) + 1).astype(F32)
    per = max(1, 128 // groups)

    def beside_rows(at):
        return jnp.concatenate([listing[at + n : at + n + 1, :] for n in range(per)], axis=1)

    heat = []
    for start in (BELOW, ABOVE):
        total = None
        for r in range(0, CAP, per):
            hit = beside_rows(start + r) == node
            term = jnp.where(hit, beside_rows(start + CAP + r), 0.0)
            total = term if total is None else total + term
        heat.append(jnp.sum(total, axis=1, keepdims=True))
    lane = lanes((16, 128))
    for x in range(16):
        ends, t = beside[x], warmth[x]
        part = slice(16 * x, 16 * x + 16)
        low = ends[:, 118:119] + ends[:, 117:118] * (t[:, 0:1] + heat[0][part])
        high = ends[:, 121:122] + ends[:, 122:123] * (t[:, 127:128] + heat[1][part])
        out[x] = jnp.where(lane == 0, low, jnp.where(lane == 127, high, 0.0))


def finish(rest, storage, xf, xb, yf, yb, beyond, out):
    first = on_first_core()
    gx, gy = lax.axis_index("gx"), lax.axis_index("gy")
    f, b = xf[...], xb[...]
    x_low = jnp.where(gx > 0, jnp.where(first, f, b), 0.0)
    x_high = jnp.where(gx < lax.axis_size("gx") - 1, jnp.where(first, b, f), 0.0)
    f, b = yf[...], yb[...]
    y_low = jnp.where(gy > 0, jnp.where(first, f, b), 0.0)
    y_high = jnp.where(gy < lax.axis_size("gy") - 1, jnp.where(first, b, f), 0.0)
    row = rows((16, 128))
    for x in range(16):
        near = beyond[x] + jnp.where(row == 0, y_low[x : x + 1], 0.0)
        near = near + jnp.where(row == 15, y_high[x : x + 1], 0.0)
        if x == 0:
            near = near + x_low
        if x == 15:
            near = near + x_high
        out[x] = rest[x] + HEAT_WEIGHTS[1] * near / (6.0 + storage[x])


def around(axis):
    n, m = lax.axis_size(axis), lax.axis_size("gz")

    def target(a, c):
        to = a + (1 if c % 2 == 0 else -1)
        return (to, c) if 0 <= to < n else (a, c ^ 1)

    forward = []
    for a in range(n):
        for c in range(m):
            to = target(a, c)
            forward.append((a * m + c, to[0] * m + to[1]))
    return forward, [(j, i) for i, j in forward]


def exchange(axis, fwd, bwd):
    forward, backward = around(axis)
    names = (axis, "gz")
    return lax.ppermute(fwd, names, forward), lax.ppermute(bwd, names, backward)


def exchange_z(up, down):
    m = lax.axis_size("gz")
    ring = [(i, (i + 1) % m) for i in range(m)]
    return lax.ppermute(up, "gz", ring), lax.ppermute(down, "gz", [(j, i) for i, j in ring])


def local(field, source, sigma, warmth, storage, partition, column):
    groups = lax.axis_size("gy") * lax.axis_size("gz")
    count = groups * (CAP + 1)
    cube = (16, 16, 128)
    face = (16, 128)
    x_message, y_message, corners = (X_LAYERS, 16, 128), (16, 32, 128), (len(CORNERS), 32, 128)
    here = (field, sigma, warmth, storage, source)
    xf, xb, scaled, field, sigma, warmth, storage = call(
        pack_x,
        [x_message, x_message, (4, *cube), (3, *cube), cube, cube, cube],
        [(3, *cube), pltpu.SemaphoreType.DMA((5,))],
        name="pack_x",
        near=True,
        in_specs=[pl.BlockSpec(memory_space=pltpu.HBM)] * 5,
    )(*(pltpu.with_memory_space_constraint(v, pltpu.HBM) for v in here))
    xf, xb = exchange("gx", xf, xb)
    yf, yb = call(pack_y, [y_message, y_message], name="pack_y", near=True)(field, scaled, warmth)
    yf, yb = exchange("gy", yf, yb)
    targets, spread_rows, into, nodes = pl.pallas_call(
        place,
        out_shape=[
            jax.ShapeDtypeStruct((2, 256), jnp.int32),
            jax.ShapeDtypeStruct((count, 256), jnp.bfloat16),
            jax.ShapeDtypeStruct((2, 256, 128), F32),
            jax.ShapeDtypeStruct((groups, 128), F32),
        ],
        compiler_params=pltpu.CompilerParams(vmem_limit_bytes=8 << 20),
        name="place",
    )(partition.reshape(1, 256), column.reshape(1, 256))
    cf, cb = call(pack_corners, [corners, corners], name="pack_corners")(
        xf, xb, targets
    )
    cf, cb = exchange("gy", cf, cb)
    layer, halo = (24, 128), len(HALO_X)
    inner, inner_packed, inner_up, inner_down, began = call(
        pack_inner,
        [(8, 16, *layer), (16, *layer), (8, *layer), (8, *layer), cube],
        [(18, 16, 128)],
        name="pack_inner",
        near=True,
    )(field, scaled, warmth, storage, xf, xb, yf, yb)
    (swept,) = call(
        bulk,
        [(EM_SWEEPS - 1, 3, 16, *layer)],
        name="bulk",
        near=True,
        cost_estimate=pl.CostEstimate(flops=10**9, bytes_accessed=10**7, transcendentals=0),
    )(inner)
    outer, outer_packed, up, down = call(
        pack_outer,
        [(8, halo, *layer), (halo, *layer), (X_PAIRS, *layer), (X_PAIRS, *layer)],
        name="pack_outer",
        near=True,
    )(xf, xb, cf, cb, inner_up, inner_down, swept)
    below_z, above_z = exchange_z(up, down)
    final, whole_sum, shifted = call(
        rest_of_bulk,
        [(3, 17, *layer), cube, cube],
        [(EM_SWEEPS - 1, 3, halo, *layer)],
        name="rest_of_bulk",
        near=True,
        cost_estimate=pl.CostEstimate(flops=10**9, bytes_accessed=10**7, transcendentals=0),
    )(inner, outer, swept)
    (own,) = call(
        turn,
        [(BLOCKS, 128, 128)],
        [(BLOCKS, 128, 128)],
        name="turn",
        near=True,
        cost_estimate=pl.CostEstimate(flops=10**8, bytes_accessed=10**6, transcendentals=0),
    )(inner_packed, outer_packed)
    near, send, beside = call(
        edge,
        [(BLOCKS, 3, 32, 128), (count, 128), cube],
        [
            (BLOCKS, 128, 128),
            (BLOCKS, 8, 32, 128),
            (BLOCKS, 3, 32, 128),
            (3, 32, 128),
            cube,
        ],
        name="edge",
        near=True,
    )(
        own, below_z, above_z, whole_sum, shifted, sigma, targets, spread_rows, into, nodes
    )
    got = lax.all_to_all(
        send.reshape(count, 1, 128), ("gy", "gz"), split_axis=0, concat_axis=0, tiled=True
    ).reshape(count, 128)
    xf, xb, yf, yb, heat, mid = call(
        warm, [face, face, face, face, cube, cube], name="warm", near=True
    )(got, beside, began, storage)
    xf, xb = exchange("gx", xf, xb)
    yf, yb = exchange("gy", yf, yb)
    out, beyond, rest = call(
        merge,
        [(3, *cube), cube, cube],
        [(BLOCKS, 128, 128)],
        name="merge",
        cost_estimate=pl.CostEstimate(flops=10**9, bytes_accessed=10**6, transcendentals=0),
    )(final, near, got, beside, warmth, storage, heat, mid)
    (updated,) = call(finish, [cube], name="finish")(rest, storage, xf, xb, yf, yb, beyond)
    return out, updated


def solution(mesh):
    in_specs = (
        P(None, "gx", "gy", "gz"),
        P(None, "gx", "gy", "gz"),
        P("gx", "gy", "gz"),
        P("gx", "gy", "gz"),
        P("gx", "gy", "gz"),
        P("gx", "gy", "gz", None, None),
        P("gx", "gy", "gz", None),
    )
    out_specs = (P(None, "gx", "gy", "gz"), P("gx", "gy", "gz"))
    return jax.shard_map(local, mesh=mesh, in_specs=in_specs, out_specs=out_specs, check_vma=False)
```

```python
import functools
import math

import jax
import jax.numpy as jnp
from jax import lax
from jax.experimental import pallas as pl
from jax.experimental.pallas import tpu as pltpu
from jax.sharding import PartitionSpec as P

EM_SWEEPS = 4
HEAT_SWEEPS = 2
CAP = 8
LOW, HIGH = 4, 5
F32 = jnp.float32

em_lower = 0.02
em_upper = 3.0
heat_lower = 0.07
heat_upper = 2.0

UP_LAYERS = ((0, 12, 4), (1, 12, 4), (2, 12, 4), (3, 13, 3), (4, 13, 3), (5, 13, 3), (6, 13, 3), (7, 15, 1))
DOWN_LAYERS = ((0, 0, 4), (1, 0, 5), (2, 0, 5), (3, 0, 3), (4, 0, 4), (5, 0, 4), (6, 0, 4), (7, 0, 1))


def spots(layers, shift):
    where, at = {}, 0
    for field, first, count in layers:
        for x in range(first, first + count):
            where[field, x + shift] = at
            at += 1
    return where, at


UP_AT, UP_COUNT = spots(UP_LAYERS, -16)
DOWN_AT, DOWN_COUNT = spots(DOWN_LAYERS, 16)
X_LAYERS = max(UP_COUNT, DOWN_COUNT)


def chebyshev_weights(lower_end, upper_end, sweep_count):
    middle = 0.5 * (upper_end + lower_end)
    radius = 0.5 * (upper_end - lower_end)
    return [
        1.0 / (middle + radius * math.cos(math.pi * (2 * number + 1) / (2 * sweep_count)))
        for number in range(sweep_count)
    ]


EM_WEIGHTS = chebyshev_weights(em_lower, em_upper, EM_SWEEPS)
HEAT_WEIGHTS = chebyshev_weights(heat_lower, heat_upper, HEAT_SWEEPS)


def on_first_core():
    return lax.rem(lax.axis_index("gz"), 2) == 0


def lanes(shape):
    return lax.broadcasted_iota(jnp.int32, shape, len(shape) - 1)


def rows(shape):
    return lax.broadcasted_iota(jnp.int32, shape, len(shape) - 2)


def roll(values, by, axis):
    size = values.shape[axis]
    by = by % size
    return values if by == 0 else pltpu.roll(values, by, axis)


def call(body, out_shapes, scratch=(), name=None, limit=8 << 20, near=False, **options):
    return pl.pallas_call(
        body,
        out_shape=[
            pltpu.VMEM(s, F32) if near else jax.ShapeDtypeStruct(s, F32) for s in out_shapes
        ],
        scratch_shapes=[pltpu.VMEM(s, F32) if isinstance(s, tuple) else s for s in scratch],
        compiler_params=pltpu.CompilerParams(vmem_limit_bytes=limit),
        name=name,
        **options,
    )


def swap_store(first, fwd, bwd, at, up, down):
    fwd[at] = jnp.where(first, up, down)
    bwd[at] = jnp.where(first, down, up)


def y_tiles(v):
    row = rows((8, 128))
    low_half = row < 4
    tops = [a[8:16] for a in v]
    ends = [a[0:8] for a in v]
    ups, downs = [], []
    for pair in range(4):
        a, b = 2 * pair, 2 * pair + 1
        ups.append(jnp.where(low_half, roll(tops[b], 4, 0), tops[a]))
        down = jnp.where(low_half, ends[a], roll(ends[b], 4, 0))
        if pair == 3:
            down = jnp.where(row == 5, roll(ends[0], 1, 0), down)
            down = jnp.where(row == 6, roll(ends[2], 2, 0), down)
        downs.append(down)
    return ups, downs


def put_y_tiles(tiles, first, fwd, bwd, at):
    for pair, (up, down) in enumerate(zip(*tiles)):
        part = pl.ds(8 * pair, 8)
        fwd[at, part] = jnp.where(first, up, down)
        bwd[at, part] = jnp.where(first, down, up)


def pack_x(*refs):
    far, (xf, xb, scaled), near, arrived = refs[:5], refs[5:8], refs[8:13], refs[13]
    copies = [
        pltpu.make_async_copy(a, b, arrived.at[n]) for n, (a, b) in enumerate(zip(far, near))
    ]
    for copy in copies:
        copy.start()
    field, sigma, warmth, storage, source = near
    del storage
    first = on_first_core()
    for at in (0, 1, 2, 4):
        copies[at].wait()
    inverse = 1.0 / (4.0 + sigma[...])
    scaled[3] = inverse
    for c in range(3):
        scaled[c] = source[c] * inverse

    def layer(f, x):
        if f < 3:
            return field[f, x]
        return warmth[x] if f == 7 else scaled[f - 3, x]

    ups = [(f, x) for f, start, n in UP_LAYERS for x in range(start, start + n)]
    downs = [(f, x) for f, start, n in DOWN_LAYERS for x in range(start, start + n)]
    for at in range(X_LAYERS):
        up = layer(*ups[min(at, len(ups) - 1)])
        down = layer(*downs[min(at, len(downs) - 1)])
        swap_store(first, xf, xb, at, up, down)
    copies[3].wait()


def pack_y(field, scaled, warmth, targets, yf, yb):
    del targets
    first = on_first_core()

    def step(x, carry):
        v = [field[f, x] for f in range(3)] + [scaled[f, x] for f in range(4)] + [warmth[x]]
        put_y_tiles(y_tiles(v), first, yf, yb, x)
        return carry

    lax.fori_loop(0, 16, step, 0, unroll=4)


class Halo:
    def __init__(self, got_fwd, got_bwd):
        self.got_fwd, self.got_bwd = got_fwd, got_bwd
        self.first = on_first_core()
        gx = lax.axis_index("gx")
        self.below, self.above = gx > 0, gx < lax.axis_size("gx") - 1

    def layer(self, f, x):
        if x < 0:
            at, near, far, inside = UP_AT.get((f, x)), self.got_fwd, self.got_bwd, self.below
        else:
            at, near, far, inside = DOWN_AT.get((f, x)), self.got_bwd, self.got_fwd, self.above
        if at is None:
            return None
        return jnp.where(inside, jnp.where(self.first, near[at], far[at]), 0.0)


def pack_corners(xf, xb, targets, fwd, bwd):
    del targets
    halo = Halo(xf, xb)
    zero = jnp.zeros((16, 128), F32)
    row = rows((8, 128)) % 4
    tiles = {}
    for x in HALO_X:
        v = [halo.layer(f, x) for f in range(7)]
        tiles[x] = y_tiles([zero if a is None else a for a in v] + [zero])
    for at, (x, sharer, shift) in enumerate(CORNERS):
        ups, downs = tiles[x]
        if sharer is not None:
            other_ups, other_downs = tiles[sharer]
            ups = [jnp.where(row >= 4 - shift, a, roll(b, -shift, 0)) for a, b in zip(ups, other_ups)]
            downs = [jnp.where(row < shift, a, roll(b, shift, 0)) for a, b in zip(downs, other_downs)]
        put_y_tiles((ups, downs), halo.first, fwd, bwd, at)


def y_halo(first, got, at, pair):
    gy = lax.axis_index("gy")
    part = pl.ds(8 * pair, 8)
    f, b = got[0][at, part], got[1][at, part]
    lower = jnp.where(gy > 0, jnp.where(first, f, b), 0.0)
    upper = jnp.where(gy < lax.axis_size("gy") - 1, jnp.where(first, b, f), 0.0)
    return lower, upper


CORNERS = (
    (-3, None, 0), (-2, None, 0), (-1, None, 0), (16, None, 0), (17, None, 0), (19, -4, 2), (18, 20, 3),
)
HALO_X = tuple(range(-LOW, 0)) + tuple(range(16, 16 + HIGH))
X_ALL = LOW + 16 + HIGH
BLOCKS = 5
Y_LANES = LOW + 16 + HIGH
X_PAIRS = (X_ALL + 1) // 2


def y_slabs(first, got, at, v, shift=0):
    low_half = rows((8, 128)) < 4
    window = lanes((24, 128)) // 16
    slabs, acc = [], None
    for pair in range(4):
        lower, upper = y_halo(first, got, at, pair)
        lower, upper = roll(lower, shift, 0), roll(upper, -shift, 0)
        ends = [jnp.where(low_half, upper, lower)]
        if pair < 3:
            ends.append(roll(jnp.where(low_half, lower, upper), 4, 0))
        else:
            ends.append(roll(upper, 3, 0))
        for f, tile in zip((2 * pair, 2 * pair + 1), ends):
            slabs.append(jnp.concatenate([v[f], tile], axis=0))
            moved = roll(slabs[f], 16 * f + 8, 1)
            acc = moved if acc is None else jnp.where(window == f, moved, acc)
    return slabs, acc


def z_tiles(a, b):
    half = (lanes((24, 128)) // 8) % 2 == 0
    return jnp.where(half, a, roll(b, 8, 1)), jnp.where(half, roll(a, -8, 1), b)


def pack_inner(
    field, scaled, warmth, storage, xf, xb, yf, yb, whole, packed, up, down, began, padded
):
    first, gx = on_first_core(), lax.axis_index("gx")
    low_at, high_at = UP_AT[7, -1], DOWN_AT[7, 16]
    padded[0] = jnp.where(gx > 0, jnp.where(first, xf[low_at], xb[low_at]), 0.0)
    padded[17] = jnp.where(
        gx < lax.axis_size("gx") - 1, jnp.where(first, xb[high_at], xf[high_at]), 0.0
    )
    padded[1:17] = warmth[...]
    row, lane = rows((16, 128)), lanes((16, 128))

    def step(k, carry):
        windows = []
        for x in (2 * k, 2 * k + 1):
            t = warmth[x]
            lower, upper = y_halo(first, (yf, yb), x, 3)
            total = padded[x] + padded[x + 2]
            total = total + jnp.where(row == 0, lower[3:4], roll(t, 1, 0))
            total = total + jnp.where(row == 15, upper[4:5], roll(t, -1, 0))
            total = total + jnp.where(lane == 0, 0.0, roll(t, 1, 1))
            total = total + jnp.where(lane == 127, 0.0, roll(t, -1, 1))
            weight = HEAT_WEIGHTS[0] / (6.0 + storage[x])
            start = t + weight * (total - 6.0 * t)
            began[x] = start
            t = jnp.where(lane == 126, roll(start, -1, 1), t)
            t = jnp.where(lane == 125, roll(weight, -2, 1), t)
            t = jnp.where(lane == 1, roll(start, 1, 1), t)
            t = jnp.where(lane == 2, roll(weight, 2, 1), t)
            v = [field[f, x] for f in range(3)] + [scaled[f, x] for f in range(4)] + [t]
            slabs, acc = y_slabs(first, (yf, yb), x, v)
            for f in range(8):
                whole[f, x] = slabs[f]
            packed[x] = acc
            windows.append(acc)
        up[k], down[k] = z_tiles(*windows)
        return carry

    lax.fori_loop(0, 8, step, 0, unroll=4)


def pack_outer(xf, xb, cf, cb, inner_up, inner_down, swept, whole, packed, up, down):
    del swept
    halo = Halo(xf, xb)
    zero = jnp.zeros((16, 128), F32)
    windows = []
    place_of = {}
    for at, (x, sharer, shift) in enumerate(CORNERS):
        place_of[x], place_of[sharer] = (at, 0), (at, shift)
    for number, x in enumerate(HALO_X):
        v = [halo.layer(f, x) for f in range(7)]
        at, shift = place_of[x]
        slabs, acc = y_slabs(
            halo.first, (cf, cb), at, [zero if a is None else a for a in v] + [zero], shift
        )
        for f in range(8):
            whole[f, number] = slabs[f]
        packed[number] = acc
        windows.append(acc)
    windows.append(jnp.zeros((24, 128), F32))
    for pair in range(len(windows) // 2):
        k = pair if pair < LOW // 2 else pair + 8
        up[k], down[k] = z_tiles(windows[2 * pair], windows[2 * pair + 1])
    up[LOW // 2 : LOW // 2 + 8] = inner_up[...]
    down[LOW // 2 : LOW // 2 + 8] = inner_down[...]


def twist(a, b, c, d):
    return (a - b) - (c - d)


def curls(e, e_up_y, e_up_z, e_up_x):
    (ex, ey, ez), (ex_y, ez_y), (ex_z, ey_z), (ey_x, ez_x) = e, e_up_y, e_up_z, e_up_x
    return twist(ez_y, ez, ey_z, ey), twist(ex_z, ex, ez_x, ez), twist(ey_x, ey, ex_y, ex)


def relaxed(weight, e, h, g, c, c_down_x, c_down_y, c_down_z):
    (cx, cy, cz), (cy_x, cz_x), (cx_y, cz_y), (cx_z, cy_z) = c, c_down_x, c_down_y, c_down_z
    k = twist(cz, cz_y, cy, cy_z), twist(cx, cx_z, cz, cz_x), twist(cy, cy_x, cx, cx_y)
    g = g * weight
    keep = (1.0 - weight) + 4.0 * g
    return [keep * e[f] + weight * h[f] - g * k[f] for f in range(3)]


def lane_curls(get, source, at):
    row = rows((24, 128))
    e = [get(source, f, at) for f in range(3)]
    up_y = roll(e[0], -1, 0), roll(e[2], -1, 0)
    if source == 0:
        up_y = [jnp.where(row == 19, get(0, 7, at)[16 + n : 17 + n], up_y[n]) for n in range(2)]
    up_z = roll(e[0], -1, 1), roll(e[1], -1, 1)
    return e, curls(e, up_y, up_z, (get(source, 1, at + 1), get(source, 2, at + 1)))


def lane_sweep(get, source, at, carry):
    e, c = lane_curls(get, source, at)
    h, g = [get(0, 3 + f, at) for f in range(3)], get(0, 6, at)
    down_y = roll(c[0], 1, 0), roll(c[2], 1, 0)
    down_z = roll(c[0], 1, 1), roll(c[1], 1, 1)
    new = relaxed(EM_WEIGHTS[source], e, h, g, c, carry, down_y, down_z)
    return new, (c[1], c[2])


def bulk(whole, swept):
    def get(number, f, x):
        return whole[f, x] if number == 0 else swept[number - 1, f, x]

    for number in range(EM_SWEEPS - 1):

        def step(x, carry, number=number):
            new, carry = lane_sweep(get, number, x, carry)
            for f in range(3):
                swept[number, f, x] = new[f]
            return carry

        _, c = lane_curls(get, number, number)
        lax.fori_loop(number + 1, 15 - number, step, (c[1], c[2]), unroll=6)


def swept_low(number):
    return range(number - LOW, number)


def swept_high(number):
    return range(16 - number, 21 - number)


def rest_of_bulk(inner, outer, swept, final, whole_sum, shifted, others):
    def get(number, f, x):
        if number == 0:
            return inner[f, x] if 0 <= x < 16 else outer[f, HALO_X.index(x)]
        if number == EM_SWEEPS:
            return final[f, x]
        if number <= x <= 15 - number:
            return swept[number - 1, f, x]
        low, high = swept_low(number), swept_high(number)
        return others[number - 1, f, low.index(x) if x < number else len(low) + high.index(x)]

    for number in range(EM_SWEEPS):
        at = 0
        ranges = (swept_low(number + 1), swept_high(number + 1))
        if number == EM_SWEEPS - 1:
            ranges = (range(17),)
        for layers in ranges:
            _, c = lane_curls(get, number, layers[0] - 1)
            carry = c[1], c[2]
            for x in layers:
                new, carry = lane_sweep(get, number, x, carry)
                for f in range(3):
                    if number == EM_SWEEPS - 1:
                        final[f, x] = new[f]
                    else:
                        others[number, f, at] = new[f]
                at += 1

    for x in range(16):
        ex, ey, ez = (get(EM_SWEEPS, f, x) for f in range(3))
        ey_x, ez_x = (get(EM_SWEEPS, f, x + 1) for f in (1, 2))
        ex, upright = ex * ex, ez * ez + ez_x * ez_x
        flat = (ex + roll(ex, -1, 0)) + (ey * ey + ey_x * ey_x)
        upright = upright + roll(upright, -1, 0)
        whole_sum[x] = flat[0:16] + upright[0:16]
        shifted[x] = roll(flat[0:16], -1, 1)


def of_layer(at):
    return at % BLOCKS, Y_LANES * (at // BLOCKS)


def clear_gaps(stack):
    for block in range(BLOCKS):
        for n in range(BLOCKS):
            at = Y_LANES * n + 24
            stack[block, at : at + 1, :] = jnp.zeros((1, 128), F32)
        stack[block, 125:128, :] = jnp.zeros((3, 128), F32)


def put_layer(stack, at, windows):
    block, lane_at = of_layer(at)
    stack[block, lane_at : lane_at + 24, :] = roll(windows, 4, 0)


def turn(inner, outer, turned, stack):
    clear_gaps(stack)
    for at in range(X_ALL):
        x = at - LOW
        put_layer(stack, at, inner[x] if 0 <= x < 16 else outer[HALO_X.index(x)])
    for block in range(BLOCKS):
        turned[block] = stack[block].T


def edge(
    own, below_z, above_z, whole_sum, shifted, sigma, targets, spread_rows, into, nodes,
    final, send, beside, stack, fields, spare, last, heat,
):
    gz = lax.axis_index("gz")
    half = (lanes((24, 128)) // 8) % 2 == 0
    has_below, has_above = gz > 0, gz < lax.axis_size("gz") - 1
    clear_gaps(stack)
    for k in range(X_PAIRS):
        lower = jnp.where(has_below, below_z[k], 0.0)
        upper = jnp.where(has_above, above_z[k], 0.0)
        for at in range(2 * k, min(2 * k + 2, X_ALL)):
            if at % 2:
                came = jnp.where(half, roll(lower, -8, 1), upper)
            else:
                came = jnp.where(half, lower, roll(upper, 8, 1))
            if 0 <= at - LOW < 16:
                beside[at - LOW] = came[0:16]
            put_layer(stack, at, came)
    for block in range(BLOCKS):
        came = stack[block].T
        for f in range(8):
            for n, part in enumerate((own, came, came, own)):
                at = 16 * f + 8 * (n % 2)
                values = part[block, at : at + 8, :] if part is own else part[at : at + 8]
                fields[block, f, 8 * n : 8 * n + 8, :] = values
    top = lanes((32, 128)) % Y_LANES == 24
    for block in range(BLOCKS):
        extra = fields[block, 7]
        for f, by in ((0, 4), (2, 3)):
            fields[block, f] = jnp.where(top, roll(extra, by, 1), fields[block, f])

    buffers = (fields, spare, final, spare, final)

    def ahead(source, block, f):
        if block < BLOCKS - 1:
            return source[block + 1, f]
        return roll(source[0, f], -Y_LANES, 1)

    def curls_at(source, block):
        e = [source[block, f] for f in range(3)]
        up_y = roll(e[0], -1, 1), roll(e[2], -1, 1)
        up_z = roll(e[0], -1, 0), roll(e[1], -1, 0)
        return e, curls(e, up_y, up_z, (ahead(source, block, 1), ahead(source, block, 2)))

    for number, weight in enumerate(EM_WEIGHTS):
        source, target = buffers[number], buffers[number + 1]
        _, c = curls_at(source, BLOCKS - 1)
        for f in range(3):
            last[f] = c[f]
        before = roll(c[1], Y_LANES, 1), roll(c[2], Y_LANES, 1)
        for block in range(BLOCKS):
            if block < BLOCKS - 1:
                e, c = curls_at(source, block)
            else:
                e, c = [source[block, f] for f in range(3)], [last[f] for f in range(3)]
            h, g = [fields[block, 3 + f] for f in range(3)], fields[block, 6]
            down_y = roll(c[0], 1, 1), roll(c[2], 1, 1)
            down_z = roll(c[0], 1, 0), roll(c[1], 1, 0)
            new = relaxed(weight, e, h, g, c, before, down_y, down_z)
            for f in range(3):
                target[block, f] = new[f]
            before = c[1], c[2]

    for block in range(BLOCKS):
        ex, ey, ez = (final[block, f] * final[block, f] for f in range(3))
        ey_x, ez_x = (ahead(final, block, f) for f in (1, 2))
        flat, upright = (ex + roll(ex, -1, 1)) + (ey + ey_x * ey_x), ez + ez_x * ez_x
        both = flat + (upright + roll(upright, -1, 1))
        stack[block, 0:8, :] = both[24:32]
        stack[block, 120:128, :] = both[0:8]
        stack[block, 59:64, :] = flat[4:9]
        stack[block, 64:67, :] = flat[25:28]
    for block in range(BLOCKS):
        stack[block] = stack[block].T
    lane = lanes((16, 128))
    for x in range(16):
        block, lane_at = of_layer(x + LOW)
        near = stack[block, lane_at + LOW : lane_at + LOW + 16, :]
        here = jnp.where((lane < 4) | (lane >= 124), near, whole_sum[x])
        above = jnp.where((lane < 3) | (lane >= 123), roll(near, 64, 1), shifted[x])
        heat[x] = sigma[x] * (0.25 * (here + above))

    def spread_out(hit, columns, total):
        for _ in range(3):
            piece = columns.astype(jnp.bfloat16)
            columns = columns - piece.astype(F32)
            term = jnp.dot(hit, piece, preferred_element_type=F32)
            total = term if total is None else total + term
        return total

    columns = heat[...].reshape(256, 128)
    send[...] = spread_out(spread_rows[...], columns, None)
    ends = jnp.concatenate([columns[:, 127:128] * into[0], columns[:, 0:1] * into[1]], axis=0)
    target = jnp.concatenate([targets[0:1, :], targets[1:2, :]], axis=1)
    groups = nodes.shape[0]
    hit = (rows((groups, 512)) == target).astype(jnp.bfloat16)
    send[pl.ds(CAP, groups, stride=CAP + 1), :] = spread_out(hit, ends, nodes[...])


def merge(final, near, got, beside, warmth, storage, heat, mid, out, beyond, rest, stack):
    beyond_z(got, beside, warmth, beyond)
    own_part(mid, heat, warmth, storage, rest)
    for block in range(BLOCKS):
        for f in range(3):
            stack[block, 32 * f : 32 * f + 8, :] = near[block, f, 24:32, :]
            at = (32 * f - 8) % 128
            stack[block, at : at + 8, :] = near[block, f, 0:8, :]
    for block in range(BLOCKS):
        stack[block] = stack[block].T
    lane = lanes((16, 128))
    outer = (lane < 4) | (lane >= 124)
    for x in range(16):
        block, lane_at = of_layer(x + LOW)
        windows = stack[block, lane_at + LOW : lane_at + LOW + 16, :]
        for f in range(3):
            inner = final[f, x, 0:16, :]
            out[f, x] = jnp.where(outer, roll(windows, -32 * f, 1), inner)


BELOW, ABOVE = CAP, 3 * CAP


def place(owners, columns, targets, spread_rows, into, nodes):
    planes = lax.axis_size("gz")
    groups = lax.axis_size("gy") * planes
    owner, column = owners[...], columns[...]
    member = rows((groups, 256)) == owner
    earlier = (rows((256, 256)) < lanes((256, 256))).astype(jnp.bfloat16)
    before = jnp.dot(member.astype(jnp.bfloat16), earlier, preferred_element_type=F32)
    rank = jnp.sum(jnp.where(member, before, 0.0), axis=0, keepdims=True).astype(jnp.int32)
    depth = lax.rem(owner, planes)
    to_above = jnp.where(depth < planes - 1, owner + 1, -1)
    to_below = jnp.where(depth > 0, owner - 1, -1)
    count = spread_rows.shape[0]
    spread_rows[...] = (rows((count, 256)) == owner * (CAP + 1) + rank).astype(jnp.bfloat16)
    targets[0:1, :] = to_above
    targets[1:2, :] = to_below
    total = None
    for target, start in ((owner, 0), (to_above, BELOW), (to_below, ABOVE)):
        spread = (rows((groups, 256)) == target).astype(jnp.bfloat16)
        listed = jnp.where(rows((128, 256)) == rank + start, column + 1, 0).astype(F32)
        term = lax.dot_general(
            spread,
            listed.astype(jnp.bfloat16),
            (((1,), (1,)), ((), ())),
            preferred_element_type=F32,
        )
        total = term if total is None else total + term
    nodes[...] = total
    for n, start in enumerate((BELOW + CAP, ABOVE + CAP)):
        into[n] = (rows((128, 256)) == rank + start).astype(F32).T


def warm(got, beside, began, storage, xf, xb, yf, yb, heat, mid):
    first = on_first_core()
    groups = got.shape[0] // (CAP + 1)
    ids = got[pl.ds(CAP, groups, stride=CAP + 1), :].T
    node = rows((256, 1)) + 1
    per = max(1, 128 // groups)
    total = None
    for r in range(0, CAP, per):
        number = jnp.concatenate([ids[r + n : r + n + 1, :] for n in range(per)], axis=1)
        hit = (number == node.astype(F32)).astype(jnp.bfloat16)
        left = jnp.concatenate(
            [got[pl.ds(r + n, groups, stride=CAP + 1), :] for n in range(per)], axis=0
        )
        for _ in range(3):
            piece = left.astype(jnp.bfloat16)
            left = left - piece.astype(F32)
            term = jnp.dot(hit, piece, preferred_element_type=F32)
            total = term if total is None else total + term
    heat[...] = total.reshape(16, 16, 128)
    lane = lanes((16, 128))
    for x in range(16):
        ends = beside[x]
        halo = jnp.where(lane == 0, roll(ends, 9, 1), jnp.where(lane == 127, roll(ends, 7, 1), 0.0))
        mid[x] = began[x] + HEAT_WEIGHTS[0] * (heat[x] + halo) / (6.0 + storage[x])
    xf[...] = jnp.where(first, mid[15], mid[0])
    xb[...] = jnp.where(first, mid[0], mid[15])
    for x in range(16):
        t = mid[x]
        top, end = t[15:16], t[0:1]
        yf[x : x + 1] = jnp.where(first, top, end)
        yb[x : x + 1] = jnp.where(first, end, top)


def own_part(mid, heat, warmth, storage, rest):
    lane, row = lanes((16, 128)), rows((16, 128))
    for x in range(16):
        t = mid[x]
        near = jnp.where(row == 0, 0.0, roll(t, 1, 0)) + jnp.where(row == 15, 0.0, roll(t, -1, 0))
        near = near + jnp.where(lane == 0, 0.0, roll(t, 1, 1))
        near = near + jnp.where(lane == 127, 0.0, roll(t, -1, 1))
        if x > 0:
            near = near + mid[x - 1]
        if x < 15:
            near = near + mid[x + 1]
        s = storage[x]
        push = s * warmth[x] + heat[x] - (6.0 + s) * t + near
        rest[x] = t + HEAT_WEIGHTS[1] * push / (6.0 + s)


def beyond_z(got, beside, warmth, out):
    groups = got.shape[0] // (CAP + 1)
    listing = got[pl.ds(CAP, groups, stride=CAP + 1), :].T
    node = (rows((256, 1)) + 1).astype(F32)
    per = max(1, 128 // groups)

    def beside_rows(at):
        return jnp.concatenate([listing[at + n : at + n + 1, :] for n in range(per)], axis=1)

    heat = []
    for start in (BELOW, ABOVE):
        total = None
        for r in range(0, CAP, per):
            hit = beside_rows(start + r) == node
            term = jnp.where(hit, beside_rows(start + CAP + r), 0.0)
            total = term if total is None else total + term
        heat.append(jnp.sum(total, axis=1, keepdims=True))
    lane = lanes((16, 128))
    for x in range(16):
        ends, t = beside[x], warmth[x]
        part = slice(16 * x, 16 * x + 16)
        low = ends[:, 118:119] + ends[:, 117:118] * (t[:, 0:1] + heat[0][part])
        high = ends[:, 121:122] + ends[:, 122:123] * (t[:, 127:128] + heat[1][part])
        out[x] = jnp.where(lane == 0, low, jnp.where(lane == 127, high, 0.0))


def finish(rest, storage, xf, xb, yf, yb, beyond, out):
    first = on_first_core()
    gx, gy = lax.axis_index("gx"), lax.axis_index("gy")
    f, b = xf[...], xb[...]
    x_low = jnp.where(gx > 0, jnp.where(first, f, b), 0.0)
    x_high = jnp.where(gx < lax.axis_size("gx") - 1, jnp.where(first, b, f), 0.0)
    f, b = yf[...], yb[...]
    y_low = jnp.where(gy > 0, jnp.where(first, f, b), 0.0)
    y_high = jnp.where(gy < lax.axis_size("gy") - 1, jnp.where(first, b, f), 0.0)
    row = rows((16, 128))
    for x in range(16):
        near = beyond[x] + jnp.where(row == 0, y_low[x : x + 1], 0.0)
        near = near + jnp.where(row == 15, y_high[x : x + 1], 0.0)
        if x == 0:
            near = near + x_low
        if x == 15:
            near = near + x_high
        out[x] = rest[x] + HEAT_WEIGHTS[1] * near / (6.0 + storage[x])


def around(axis):
    n, m = lax.axis_size(axis), lax.axis_size("gz")

    def target(a, c):
        to = a + (1 if c % 2 == 0 else -1)
        return (to, c) if 0 <= to < n else (a, c ^ 1)

    forward = []
    for a in range(n):
        for c in range(m):
            to = target(a, c)
            forward.append((a * m + c, to[0] * m + to[1]))
    return forward, [(j, i) for i, j in forward]


def exchange(axis, fwd, bwd):
    forward, backward = around(axis)
    names = (axis, "gz")
    return lax.ppermute(fwd, names, forward), lax.ppermute(bwd, names, backward)


def exchange_z(up, down):
    m = lax.axis_size("gz")
    ring = [(i, (i + 1) % m) for i in range(m)]
    return lax.ppermute(up, "gz", ring), lax.ppermute(down, "gz", [(j, i) for i, j in ring])


def local(field, source, sigma, warmth, storage, partition, column):
    groups = lax.axis_size("gy") * lax.axis_size("gz")
    count = groups * (CAP + 1)
    cube = (16, 16, 128)
    face = (16, 128)
    x_message, y_message, corners = (X_LAYERS, 16, 128), (16, 32, 128), (len(CORNERS), 32, 128)
    here = (field, sigma, warmth, storage, source)
    xf, xb, scaled, field, sigma, warmth, storage = call(
        pack_x,
        [x_message, x_message, (4, *cube), (3, *cube), cube, cube, cube],
        [(3, *cube), pltpu.SemaphoreType.DMA((5,))],
        name="pack_x",
        near=True,
        in_specs=[pl.BlockSpec(memory_space=pltpu.HBM)] * 5,
    )(*(pltpu.with_memory_space_constraint(v, pltpu.HBM) for v in here))
    xf, xb = exchange("gx", xf, xb)
    targets, spread_rows, into, nodes = pl.pallas_call(
        place,
        out_shape=[
            jax.ShapeDtypeStruct((2, 256), jnp.int32),
            jax.ShapeDtypeStruct((count, 256), jnp.bfloat16),
            jax.ShapeDtypeStruct((2, 256, 128), F32),
            jax.ShapeDtypeStruct((groups, 128), F32),
        ],
        compiler_params=pltpu.CompilerParams(vmem_limit_bytes=8 << 20),
        name="place",
    )(partition.reshape(1, 256), column.reshape(1, 256))
    yf, yb = call(pack_y, [y_message, y_message], name="pack_y", near=True)(
        field, scaled, warmth, targets
    )
    yf, yb = exchange("gy", yf, yb)
    cf, cb = call(pack_corners, [corners, corners], name="pack_corners")(
        xf, xb, targets
    )
    cf, cb = exchange("gy", cf, cb)
    layer, halo = (24, 128), len(HALO_X)
    inner, inner_packed, inner_up, inner_down, began = call(
        pack_inner,
        [(8, 16, *layer), (16, *layer), (8, *layer), (8, *layer), cube],
        [(18, 16, 128)],
        name="pack_inner",
        near=True,
    )(field, scaled, warmth, storage, xf, xb, yf, yb)
    (swept,) = call(
        bulk,
        [(EM_SWEEPS - 1, 3, 16, *layer)],
        name="bulk",
        near=True,
        cost_estimate=pl.CostEstimate(flops=10**9, bytes_accessed=10**7, transcendentals=0),
    )(inner)
    outer, outer_packed, up, down = call(
        pack_outer,
        [(8, halo, *layer), (halo, *layer), (X_PAIRS, *layer), (X_PAIRS, *layer)],
        name="pack_outer",
        near=True,
    )(xf, xb, cf, cb, inner_up, inner_down, swept)
    below_z, above_z = exchange_z(up, down)
    final, whole_sum, shifted = call(
        rest_of_bulk,
        [(3, 17, *layer), cube, cube],
        [(EM_SWEEPS - 1, 3, halo, *layer)],
        name="rest_of_bulk",
        near=True,
        cost_estimate=pl.CostEstimate(flops=10**9, bytes_accessed=10**7, transcendentals=0),
    )(inner, outer, swept)
    (own,) = call(
        turn,
        [(BLOCKS, 128, 128)],
        [(BLOCKS, 128, 128)],
        name="turn",
        near=True,
        cost_estimate=pl.CostEstimate(flops=10**8, bytes_accessed=10**6, transcendentals=0),
    )(inner_packed, outer_packed)
    near, send, beside = call(
        edge,
        [(BLOCKS, 3, 32, 128), (count, 128), cube],
        [
            (BLOCKS, 128, 128),
            (BLOCKS, 8, 32, 128),
            (BLOCKS, 3, 32, 128),
            (3, 32, 128),
            cube,
        ],
        name="edge",
        near=True,
    )(
        own, below_z, above_z, whole_sum, shifted, sigma, targets, spread_rows, into, nodes
    )
    got = lax.all_to_all(
        send.reshape(count, 1, 128), ("gy", "gz"), split_axis=0, concat_axis=0, tiled=True
    ).reshape(count, 128)
    xf, xb, yf, yb, heat, mid = call(
        warm, [face, face, face, face, cube, cube], name="warm", near=True
    )(got, beside, began, storage)
    xf, xb = exchange("gx", xf, xb)
    yf, yb = exchange("gy", yf, yb)
    out, beyond, rest = call(
        merge,
        [(3, *cube), cube, cube],
        [(BLOCKS, 128, 128)],
        name="merge",
        cost_estimate=pl.CostEstimate(flops=10**9, bytes_accessed=10**6, transcendentals=0),
    )(final, near, got, beside, warmth, storage, heat, mid)
    (updated,) = call(finish, [cube], name="finish")(rest, storage, xf, xb, yf, yb, beyond)
    return out, updated


def solution(mesh):
    in_specs = (
        P(None, "gx", "gy", "gz"),
        P(None, "gx", "gy", "gz"),
        P("gx", "gy", "gz"),
        P("gx", "gy", "gz"),
        P("gx", "gy", "gz"),
        P("gx", "gy", "gz", None, None),
        P("gx", "gy", "gz", None),
    )
    out_specs = (P(None, "gx", "gy", "gz"), P("gx", "gy", "gz"))
    return jax.shard_map(local, mesh=mesh, in_specs=in_specs, out_specs=out_specs, check_vma=False)
```

```python
import functools
import math

import jax
import jax.numpy as jnp
from jax import lax
from jax.experimental import pallas as pl
from jax.experimental.pallas import tpu as pltpu
from jax.sharding import PartitionSpec as P

EM_SWEEPS = 4
HEAT_SWEEPS = 2
CAP = 8
LOW, HIGH = 4, 5
F32 = jnp.float32

em_lower = 0.02
em_upper = 3.0
heat_lower = 0.07
heat_upper = 2.0

UP_LAYERS = ((0, 12, 4), (1, 12, 4), (2, 12, 4), (3, 13, 3), (4, 13, 3), (5, 13, 3), (6, 13, 3), (7, 15, 1))
DOWN_LAYERS = ((0, 0, 4), (1, 0, 5), (2, 0, 5), (3, 0, 3), (4, 0, 4), (5, 0, 4), (6, 0, 4), (7, 0, 1))


def spots(layers, shift):
    where, at = {}, 0
    for field, first, count in layers:
        for x in range(first, first + count):
            where[field, x + shift] = at
            at += 1
    return where, at


UP_AT, UP_COUNT = spots(UP_LAYERS, -16)
DOWN_AT, DOWN_COUNT = spots(DOWN_LAYERS, 16)
X_LAYERS = max(UP_COUNT, DOWN_COUNT)


def chebyshev_weights(lower_end, upper_end, sweep_count):
    middle = 0.5 * (upper_end + lower_end)
    radius = 0.5 * (upper_end - lower_end)
    return [
        1.0 / (middle + radius * math.cos(math.pi * (2 * number + 1) / (2 * sweep_count)))
        for number in range(sweep_count)
    ]


EM_WEIGHTS = chebyshev_weights(em_lower, em_upper, EM_SWEEPS)
HEAT_WEIGHTS = chebyshev_weights(heat_lower, heat_upper, HEAT_SWEEPS)


def on_first_core():
    return lax.rem(lax.axis_index("gz"), 2) == 0


def lanes(shape):
    return lax.broadcasted_iota(jnp.int32, shape, len(shape) - 1)


def rows(shape):
    return lax.broadcasted_iota(jnp.int32, shape, len(shape) - 2)


def roll(values, by, axis):
    size = values.shape[axis]
    by = by % size
    return values if by == 0 else pltpu.roll(values, by, axis)


def call(body, out_shapes, scratch=(), name=None, limit=8 << 20, near=False, **options):
    return pl.pallas_call(
        body,
        out_shape=[
            pltpu.VMEM(s, F32) if near else jax.ShapeDtypeStruct(s, F32) for s in out_shapes
        ],
        scratch_shapes=[pltpu.VMEM(s, F32) if isinstance(s, tuple) else s for s in scratch],
        compiler_params=pltpu.CompilerParams(vmem_limit_bytes=limit),
        name=name,
        **options,
    )


def swap_store(first, fwd, bwd, at, up, down):
    fwd[at] = jnp.where(first, up, down)
    bwd[at] = jnp.where(first, down, up)


def y_tiles(v):
    row = rows((8, 128))
    low_half = row < 4
    tops = [a[8:16] for a in v]
    ends = [a[0:8] for a in v]
    ups, downs = [], []
    for pair in range(4):
        a, b = 2 * pair, 2 * pair + 1
        ups.append(jnp.where(low_half, roll(tops[b], 4, 0), tops[a]))
        down = jnp.where(low_half, ends[a], roll(ends[b], 4, 0))
        if pair == 3:
            down = jnp.where(row == 5, roll(ends[0], 1, 0), down)
            down = jnp.where(row == 6, roll(ends[2], 2, 0), down)
        downs.append(down)
    return ups, downs


def put_y_tiles(tiles, first, fwd, bwd, at):
    for pair, (up, down) in enumerate(zip(*tiles)):
        part = pl.ds(8 * pair, 8)
        fwd[at, part] = jnp.where(first, up, down)
        bwd[at, part] = jnp.where(first, down, up)


def pack_first(*refs):
    far, (yf, yb, scaled), near, arrived = refs[:5], refs[5:8], refs[8:13], refs[13]
    copies = [
        pltpu.make_async_copy(a, b, arrived.at[n]) for n, (a, b) in enumerate(zip(far, near))
    ]
    for copy in copies:
        copy.start()
    field, sigma, warmth, storage, source = near
    del storage
    first = on_first_core()
    for at in (0, 1, 2, 4):
        copies[at].wait()
    inverse = 1.0 / (4.0 + sigma[...])
    scaled[3] = inverse
    for c in range(3):
        scaled[c] = source[c] * inverse

    def step(x, carry):
        v = [field[f, x] for f in range(3)] + [scaled[f, x] for f in range(4)] + [warmth[x]]
        put_y_tiles(y_tiles(v), first, yf, yb, x)
        return carry

    lax.fori_loop(0, 16, step, 0, unroll=4)
    copies[3].wait()


def pack_second(field, scaled, warmth, xf, xb):
    first = on_first_core()

    def layer(f, x):
        if f < 3:
            return field[f, x]
        return warmth[x] if f == 7 else scaled[f - 3, x]

    ups = [(f, x) for f, start, n in UP_LAYERS for x in range(start, start + n)]
    downs = [(f, x) for f, start, n in DOWN_LAYERS for x in range(start, start + n)]
    for at in range(X_LAYERS):
        up = layer(*ups[min(at, len(ups) - 1)])
        down = layer(*downs[min(at, len(downs) - 1)])
        swap_store(first, xf, xb, at, up, down)


class Halo:
    def __init__(self, got_fwd, got_bwd):
        self.got_fwd, self.got_bwd = got_fwd, got_bwd
        self.first = on_first_core()
        gx = lax.axis_index("gx")
        self.below, self.above = gx > 0, gx < lax.axis_size("gx") - 1

    def layer(self, f, x):
        if x < 0:
            at, near, far, inside = UP_AT.get((f, x)), self.got_fwd, self.got_bwd, self.below
        else:
            at, near, far, inside = DOWN_AT.get((f, x)), self.got_bwd, self.got_fwd, self.above
        if at is None:
            return None
        return jnp.where(inside, jnp.where(self.first, near[at], far[at]), 0.0)


def pack_corners(xf, xb, targets, fwd, bwd):
    del targets
    halo = Halo(xf, xb)
    zero = jnp.zeros((16, 128), F32)
    row = rows((8, 128)) % 4
    tiles = {}
    for x in HALO_X:
        v = [halo.layer(f, x) for f in range(7)]
        tiles[x] = y_tiles([zero if a is None else a for a in v] + [zero])
    for at, (x, sharer, shift) in enumerate(CORNERS):
        ups, downs = tiles[x]
        if sharer is not None:
            other_ups, other_downs = tiles[sharer]
            ups = [jnp.where(row >= 4 - shift, a, roll(b, -shift, 0)) for a, b in zip(ups, other_ups)]
            downs = [jnp.where(row < shift, a, roll(b, shift, 0)) for a, b in zip(downs, other_downs)]
        put_y_tiles((ups, downs), halo.first, fwd, bwd, at)


def y_halo(first, got, at, pair):
    gy = lax.axis_index("gy")
    part = pl.ds(8 * pair, 8)
    f, b = got[0][at, part], got[1][at, part]
    lower = jnp.where(gy > 0, jnp.where(first, f, b), 0.0)
    upper = jnp.where(gy < lax.axis_size("gy") - 1, jnp.where(first, b, f), 0.0)
    return lower, upper


CORNERS = (
    (-3, None, 0), (-2, None, 0), (-1, None, 0), (16, None, 0), (17, None, 0), (19, -4, 2), (18, 20, 3),
)
HALO_X = tuple(range(-LOW, 0)) + tuple(range(16, 16 + HIGH))
X_ALL = LOW + 16 + HIGH
BLOCKS = 5
Y_LANES = LOW + 16 + HIGH
X_PAIRS = (X_ALL + 1) // 2


def y_slabs(first, got, at, v, shift=0):
    low_half = rows((8, 128)) < 4
    window = lanes((24, 128)) // 16
    slabs, acc = [], None
    for pair in range(4):
        lower, upper = y_halo(first, got, at, pair)
        lower, upper = roll(lower, shift, 0), roll(upper, -shift, 0)
        ends = [jnp.where(low_half, upper, lower)]
        if pair < 3:
            ends.append(roll(jnp.where(low_half, lower, upper), 4, 0))
        else:
            ends.append(roll(upper, 3, 0))
        for f, tile in zip((2 * pair, 2 * pair + 1), ends):
            slabs.append(jnp.concatenate([v[f], tile], axis=0))
            moved = roll(slabs[f], 16 * f + 8, 1)
            acc = moved if acc is None else jnp.where(window == f, moved, acc)
    return slabs, acc


def z_tiles(a, b):
    half = (lanes((24, 128)) // 8) % 2 == 0
    return jnp.where(half, a, roll(b, 8, 1)), jnp.where(half, roll(a, -8, 1), b)


def pack_inner(
    field, scaled, warmth, storage, xf, xb, yf, yb, whole, packed, up, down, began, padded
):
    first, gx = on_first_core(), lax.axis_index("gx")
    low_at, high_at = UP_AT[7, -1], DOWN_AT[7, 16]
    padded[0] = jnp.where(gx > 0, jnp.where(first, xf[low_at], xb[low_at]), 0.0)
    padded[17] = jnp.where(
        gx < lax.axis_size("gx") - 1, jnp.where(first, xb[high_at], xf[high_at]), 0.0
    )
    padded[1:17] = warmth[...]
    row, lane = rows((16, 128)), lanes((16, 128))

    def step(k, carry):
        windows = []
        for x in (2 * k, 2 * k + 1):
            t = warmth[x]
            lower, upper = y_halo(first, (yf, yb), x, 3)
            total = padded[x] + padded[x + 2]
            total = total + jnp.where(row == 0, lower[3:4], roll(t, 1, 0))
            total = total + jnp.where(row == 15, upper[4:5], roll(t, -1, 0))
            total = total + jnp.where(lane == 0, 0.0, roll(t, 1, 1))
            total = total + jnp.where(lane == 127, 0.0, roll(t, -1, 1))
            weight = HEAT_WEIGHTS[0] / (6.0 + storage[x])
            start = t + weight * (total - 6.0 * t)
            began[x] = start
            t = jnp.where(lane == 126, roll(start, -1, 1), t)
            t = jnp.where(lane == 125, roll(weight, -2, 1), t)
            t = jnp.where(lane == 1, roll(start, 1, 1), t)
            t = jnp.where(lane == 2, roll(weight, 2, 1), t)
            v = [field[f, x] for f in range(3)] + [scaled[f, x] for f in range(4)] + [t]
            slabs, acc = y_slabs(first, (yf, yb), x, v)
            for f in range(8):
                whole[f, x] = slabs[f]
            packed[x] = acc
            windows.append(acc)
        up[k], down[k] = z_tiles(*windows)
        return carry

    lax.fori_loop(0, 8, step, 0, unroll=4)


def pack_outer(xf, xb, cf, cb, inner_up, inner_down, swept, whole, packed, up, down):
    del swept
    halo = Halo(xf, xb)
    zero = jnp.zeros((16, 128), F32)
    windows = []
    place_of = {}
    for at, (x, sharer, shift) in enumerate(CORNERS):
        place_of[x], place_of[sharer] = (at, 0), (at, shift)
    for number, x in enumerate(HALO_X):
        v = [halo.layer(f, x) for f in range(7)]
        at, shift = place_of[x]
        slabs, acc = y_slabs(
            halo.first, (cf, cb), at, [zero if a is None else a for a in v] + [zero], shift
        )
        for f in range(8):
            whole[f, number] = slabs[f]
        packed[number] = acc
        windows.append(acc)
    windows.append(jnp.zeros((24, 128), F32))
    for pair in range(len(windows) // 2):
        k = pair if pair < LOW // 2 else pair + 8
        up[k], down[k] = z_tiles(windows[2 * pair], windows[2 * pair + 1])
    up[LOW // 2 : LOW // 2 + 8] = inner_up[...]
    down[LOW // 2 : LOW // 2 + 8] = inner_down[...]


def twist(a, b, c, d):
    return (a - b) - (c - d)


def curls(e, e_up_y, e_up_z, e_up_x):
    (ex, ey, ez), (ex_y, ez_y), (ex_z, ey_z), (ey_x, ez_x) = e, e_up_y, e_up_z, e_up_x
    return twist(ez_y, ez, ey_z, ey), twist(ex_z, ex, ez_x, ez), twist(ey_x, ey, ex_y, ex)


def relaxed(weight, e, h, g, c, c_down_x, c_down_y, c_down_z):
    (cx, cy, cz), (cy_x, cz_x), (cx_y, cz_y), (cx_z, cy_z) = c, c_down_x, c_down_y, c_down_z
    k = twist(cz, cz_y, cy, cy_z), twist(cx, cx_z, cz, cz_x), twist(cy, cy_x, cx, cx_y)
    g = g * weight
    keep = (1.0 - weight) + 4.0 * g
    return [keep * e[f] + weight * h[f] - g * k[f] for f in range(3)]


def lane_curls(get, source, at):
    row = rows((24, 128))
    e = [get(source, f, at) for f in range(3)]
    up_y = roll(e[0], -1, 0), roll(e[2], -1, 0)
    if source == 0:
        up_y = [jnp.where(row == 19, get(0, 7, at)[16 + n : 17 + n], up_y[n]) for n in range(2)]
    up_z = roll(e[0], -1, 1), roll(e[1], -1, 1)
    return e, curls(e, up_y, up_z, (get(source, 1, at + 1), get(source, 2, at + 1)))


def lane_sweep(get, source, at, carry):
    e, c = lane_curls(get, source, at)
    h, g = [get(0, 3 + f, at) for f in range(3)], get(0, 6, at)
    down_y = roll(c[0], 1, 0), roll(c[2], 1, 0)
    down_z = roll(c[0], 1, 1), roll(c[1], 1, 1)
    new = relaxed(EM_WEIGHTS[source], e, h, g, c, carry, down_y, down_z)
    return new, (c[1], c[2])


def bulk(whole, swept):
    def get(number, f, x):
        return whole[f, x] if number == 0 else swept[number - 1, f, x]

    for number in range(EM_SWEEPS - 1):

        def step(x, carry, number=number):
            new, carry = lane_sweep(get, number, x, carry)
            for f in range(3):
                swept[number, f, x] = new[f]
            return carry

        _, c = lane_curls(get, number, number)
        lax.fori_loop(number + 1, 15 - number, step, (c[1], c[2]), unroll=6)


def swept_low(number):
    return range(number - LOW, number)


def swept_high(number):
    return range(16 - number, 21 - number)


def rest_of_bulk(inner, outer, swept, final, whole_sum, shifted, others):
    def get(number, f, x):
        if number == 0:
            return inner[f, x] if 0 <= x < 16 else outer[f, HALO_X.index(x)]
        if number == EM_SWEEPS:
            return final[f, x]
        if number <= x <= 15 - number:
            return swept[number - 1, f, x]
        low, high = swept_low(number), swept_high(number)
        return others[number - 1, f, low.index(x) if x < number else len(low) + high.index(x)]

    for number in range(EM_SWEEPS):
        at = 0
        ranges = (swept_low(number + 1), swept_high(number + 1))
        if number == EM_SWEEPS - 1:
            ranges = (range(17),)
        for layers in ranges:
            _, c = lane_curls(get, number, layers[0] - 1)
            carry = c[1], c[2]
            for x in layers:
                new, carry = lane_sweep(get, number, x, carry)
                for f in range(3):
                    if number == EM_SWEEPS - 1:
                        final[f, x] = new[f]
                    else:
                        others[number, f, at] = new[f]
                at += 1

    for x in range(16):
        ex, ey, ez = (get(EM_SWEEPS, f, x) for f in range(3))
        ey_x, ez_x = (get(EM_SWEEPS, f, x + 1) for f in (1, 2))
        ex, upright = ex * ex, ez * ez + ez_x * ez_x
        flat = (ex + roll(ex, -1, 0)) + (ey * ey + ey_x * ey_x)
        upright = upright + roll(upright, -1, 0)
        whole_sum[x] = flat[0:16] + upright[0:16]
        shifted[x] = roll(flat[0:16], -1, 1)


def of_layer(at):
    return at % BLOCKS, Y_LANES * (at // BLOCKS)


def clear_gaps(stack):
    for block in range(BLOCKS):
        for n in range(BLOCKS):
            at = Y_LANES * n + 24
            stack[block, at : at + 1, :] = jnp.zeros((1, 128), F32)
        stack[block, 125:128, :] = jnp.zeros((3, 128), F32)


def put_layer(stack, at, windows):
    block, lane_at = of_layer(at)
    stack[block, lane_at : lane_at + 24, :] = roll(windows, 4, 0)


def turn(inner, outer, turned, stack):
    clear_gaps(stack)
    for at in range(X_ALL):
        x = at - LOW
        put_layer(stack, at, inner[x] if 0 <= x < 16 else outer[HALO_X.index(x)])
    for block in range(BLOCKS):
        turned[block] = stack[block].T


def edge(
    own, below_z, above_z, whole_sum, shifted, sigma, targets, spread_rows, into, nodes,
    final, send, beside, stack, fields, spare, last, heat,
):
    gz = lax.axis_index("gz")
    half = (lanes((24, 128)) // 8) % 2 == 0
    has_below, has_above = gz > 0, gz < lax.axis_size("gz") - 1
    clear_gaps(stack)
    for k in range(X_PAIRS):
        lower = jnp.where(has_below, below_z[k], 0.0)
        upper = jnp.where(has_above, above_z[k], 0.0)
        for at in range(2 * k, min(2 * k + 2, X_ALL)):
            if at % 2:
                came = jnp.where(half, roll(lower, -8, 1), upper)
            else:
                came = jnp.where(half, lower, roll(upper, 8, 1))
            if 0 <= at - LOW < 16:
                beside[at - LOW] = came[0:16]
            put_layer(stack, at, came)
    for block in range(BLOCKS):
        came = stack[block].T
        for f in range(8):
            for n, part in enumerate((own, came, came, own)):
                at = 16 * f + 8 * (n % 2)
                values = part[block, at : at + 8, :] if part is own else part[at : at + 8]
                fields[block, f, 8 * n : 8 * n + 8, :] = values
    top = lanes((32, 128)) % Y_LANES == 24
    for block in range(BLOCKS):
        extra = fields[block, 7]
        for f, by in ((0, 4), (2, 3)):
            fields[block, f] = jnp.where(top, roll(extra, by, 1), fields[block, f])

    buffers = (fields, spare, final, spare, final)

    def ahead(source, block, f):
        if block < BLOCKS - 1:
            return source[block + 1, f]
        return roll(source[0, f], -Y_LANES, 1)

    def curls_at(source, block):
        e = [source[block, f] for f in range(3)]
        up_y = roll(e[0], -1, 1), roll(e[2], -1, 1)
        up_z = roll(e[0], -1, 0), roll(e[1], -1, 0)
        return e, curls(e, up_y, up_z, (ahead(source, block, 1), ahead(source, block, 2)))

    for number, weight in enumerate(EM_WEIGHTS):
        source, target = buffers[number], buffers[number + 1]
        _, c = curls_at(source, BLOCKS - 1)
        for f in range(3):
            last[f] = c[f]
        before = roll(c[1], Y_LANES, 1), roll(c[2], Y_LANES, 1)
        for block in range(BLOCKS):
            if block < BLOCKS - 1:
                e, c = curls_at(source, block)
            else:
                e, c = [source[block, f] for f in range(3)], [last[f] for f in range(3)]
            h, g = [fields[block, 3 + f] for f in range(3)], fields[block, 6]
            down_y = roll(c[0], 1, 1), roll(c[2], 1, 1)
            down_z = roll(c[0], 1, 0), roll(c[1], 1, 0)
            new = relaxed(weight, e, h, g, c, before, down_y, down_z)
            for f in range(3):
                target[block, f] = new[f]
            before = c[1], c[2]

    for block in range(BLOCKS):
        ex, ey, ez = (final[block, f] * final[block, f] for f in range(3))
        ey_x, ez_x = (ahead(final, block, f) for f in (1, 2))
        flat, upright = (ex + roll(ex, -1, 1)) + (ey + ey_x * ey_x), ez + ez_x * ez_x
        both = flat + (upright + roll(upright, -1, 1))
        stack[block, 0:8, :] = both[24:32]
        stack[block, 120:128, :] = both[0:8]
        stack[block, 59:64, :] = flat[4:9]
        stack[block, 64:67, :] = flat[25:28]
    for block in range(BLOCKS):
        stack[block] = stack[block].T
    lane = lanes((16, 128))
    for x in range(16):
        block, lane_at = of_layer(x + LOW)
        near = stack[block, lane_at + LOW : lane_at + LOW + 16, :]
        here = jnp.where((lane < 4) | (lane >= 124), near, whole_sum[x])
        above = jnp.where((lane < 3) | (lane >= 123), roll(near, 64, 1), shifted[x])
        heat[x] = sigma[x] * (0.25 * (here + above))

    def spread_out(hit, columns, total):
        for _ in range(3):
            piece = columns.astype(jnp.bfloat16)
            columns = columns - piece.astype(F32)
            term = jnp.dot(hit, piece, preferred_element_type=F32)
            total = term if total is None else total + term
        return total

    columns = heat[...].reshape(256, 128)
    send[...] = spread_out(spread_rows[...], columns, None)
    ends = jnp.concatenate([columns[:, 127:128] * into[0], columns[:, 0:1] * into[1]], axis=0)
    target = jnp.concatenate([targets[0:1, :], targets[1:2, :]], axis=1)
    groups = nodes.shape[0]
    hit = (rows((groups, 512)) == target).astype(jnp.bfloat16)
    send[pl.ds(CAP, groups, stride=CAP + 1), :] = spread_out(hit, ends, nodes[...])


def merge(final, near, got, beside, warmth, storage, heat, mid, out, beyond, rest, stack):
    beyond_z(got, beside, warmth, beyond)
    own_part(mid, heat, warmth, storage, rest)
    for block in range(BLOCKS):
        for f in range(3):
            stack[block, 32 * f : 32 * f + 8, :] = near[block, f, 24:32, :]
            at = (32 * f - 8) % 128
            stack[block, at : at + 8, :] = near[block, f, 0:8, :]
    for block in range(BLOCKS):
        stack[block] = stack[block].T
    lane = lanes((16, 128))
    outer = (lane < 4) | (lane >= 124)
    for x in range(16):
        block, lane_at = of_layer(x + LOW)
        windows = stack[block, lane_at + LOW : lane_at + LOW + 16, :]
        for f in range(3):
            inner = final[f, x, 0:16, :]
            out[f, x] = jnp.where(outer, roll(windows, -32 * f, 1), inner)


BELOW, ABOVE = CAP, 3 * CAP


def place(owners, columns, targets, spread_rows, into, nodes):
    planes = lax.axis_size("gz")
    groups = lax.axis_size("gy") * planes
    owner, column = owners[...], columns[...]
    member = rows((groups, 256)) == owner
    earlier = (rows((256, 256)) < lanes((256, 256))).astype(jnp.bfloat16)
    before = jnp.dot(member.astype(jnp.bfloat16), earlier, preferred_element_type=F32)
    rank = jnp.sum(jnp.where(member, before, 0.0), axis=0, keepdims=True).astype(jnp.int32)
    depth = lax.rem(owner, planes)
    to_above = jnp.where(depth < planes - 1, owner + 1, -1)
    to_below = jnp.where(depth > 0, owner - 1, -1)
    count = spread_rows.shape[0]
    spread_rows[...] = (rows((count, 256)) == owner * (CAP + 1) + rank).astype(jnp.bfloat16)
    targets[0:1, :] = to_above
    targets[1:2, :] = to_below
    total = None
    for target, start in ((owner, 0), (to_above, BELOW), (to_below, ABOVE)):
        spread = (rows((groups, 256)) == target).astype(jnp.bfloat16)
        listed = jnp.where(rows((128, 256)) == rank + start, column + 1, 0).astype(F32)
        term = lax.dot_general(
            spread,
            listed.astype(jnp.bfloat16),
            (((1,), (1,)), ((), ())),
            preferred_element_type=F32,
        )
        total = term if total is None else total + term
    nodes[...] = total
    for n, start in enumerate((BELOW + CAP, ABOVE + CAP)):
        into[n] = (rows((128, 256)) == rank + start).astype(F32).T


def warm(got, beside, began, storage, xf, xb, yf, yb, heat, mid):
    first = on_first_core()
    groups = got.shape[0] // (CAP + 1)
    ids = got[pl.ds(CAP, groups, stride=CAP + 1), :].T
    node = rows((256, 1)) + 1
    per = max(1, 128 // groups)
    total = None
    for r in range(0, CAP, per):
        number = jnp.concatenate([ids[r + n : r + n + 1, :] for n in range(per)], axis=1)
        hit = (number == node.astype(F32)).astype(jnp.bfloat16)
        left = jnp.concatenate(
            [got[pl.ds(r + n, groups, stride=CAP + 1), :] for n in range(per)], axis=0
        )
        for _ in range(3):
            piece = left.astype(jnp.bfloat16)
            left = left - piece.astype(F32)
            term = jnp.dot(hit, piece, preferred_element_type=F32)
            total = term if total is None else total + term
    heat[...] = total.reshape(16, 16, 128)
    lane = lanes((16, 128))
    for x in range(16):
        ends = beside[x]
        halo = jnp.where(lane == 0, roll(ends, 9, 1), jnp.where(lane == 127, roll(ends, 7, 1), 0.0))
        mid[x] = began[x] + HEAT_WEIGHTS[0] * (heat[x] + halo) / (6.0 + storage[x])
    xf[...] = jnp.where(first, mid[15], mid[0])
    xb[...] = jnp.where(first, mid[0], mid[15])
    for x in range(16):
        t = mid[x]
        top, end = t[15:16], t[0:1]
        yf[x : x + 1] = jnp.where(first, top, end)
        yb[x : x + 1] = jnp.where(first, end, top)


def own_part(mid, heat, warmth, storage, rest):
    lane, row = lanes((16, 128)), rows((16, 128))
    for x in range(16):
        t = mid[x]
        near = jnp.where(row == 0, 0.0, roll(t, 1, 0)) + jnp.where(row == 15, 0.0, roll(t, -1, 0))
        near = near + jnp.where(lane == 0, 0.0, roll(t, 1, 1))
        near = near + jnp.where(lane == 127, 0.0, roll(t, -1, 1))
        if x > 0:
            near = near + mid[x - 1]
        if x < 15:
            near = near + mid[x + 1]
        s = storage[x]
        push = s * warmth[x] + heat[x] - (6.0 + s) * t + near
        rest[x] = t + HEAT_WEIGHTS[1] * push / (6.0 + s)


def beyond_z(got, beside, warmth, out):
    groups = got.shape[0] // (CAP + 1)
    listing = got[pl.ds(CAP, groups, stride=CAP + 1), :].T
    node = (rows((256, 1)) + 1).astype(F32)
    per = max(1, 128 // groups)

    def beside_rows(at):
        return jnp.concatenate([listing[at + n : at + n + 1, :] for n in range(per)], axis=1)

    heat = []
    for start in (BELOW, ABOVE):
        total = None
        for r in range(0, CAP, per):
            hit = beside_rows(start + r) == node
            term = jnp.where(hit, beside_rows(start + CAP + r), 0.0)
            total = term if total is None else total + term
        heat.append(jnp.sum(total, axis=1, keepdims=True))
    lane = lanes((16, 128))
    for x in range(16):
        ends, t = beside[x], warmth[x]
        part = slice(16 * x, 16 * x + 16)
        low = ends[:, 118:119] + ends[:, 117:118] * (t[:, 0:1] + heat[0][part])
        high = ends[:, 121:122] + ends[:, 122:123] * (t[:, 127:128] + heat[1][part])
        out[x] = jnp.where(lane == 0, low, jnp.where(lane == 127, high, 0.0))


def finish(rest, storage, xf, xb, yf, yb, beyond, out):
    first = on_first_core()
    gx, gy = lax.axis_index("gx"), lax.axis_index("gy")
    f, b = xf[...], xb[...]
    x_low = jnp.where(gx > 0, jnp.where(first, f, b), 0.0)
    x_high = jnp.where(gx < lax.axis_size("gx") - 1, jnp.where(first, b, f), 0.0)
    f, b = yf[...], yb[...]
    y_low = jnp.where(gy > 0, jnp.where(first, f, b), 0.0)
    y_high = jnp.where(gy < lax.axis_size("gy") - 1, jnp.where(first, b, f), 0.0)
    row = rows((16, 128))
    for x in range(16):
        near = beyond[x] + jnp.where(row == 0, y_low[x : x + 1], 0.0)
        near = near + jnp.where(row == 15, y_high[x : x + 1], 0.0)
        if x == 0:
            near = near + x_low
        if x == 15:
            near = near + x_high
        out[x] = rest[x] + HEAT_WEIGHTS[1] * near / (6.0 + storage[x])


def around(axis):
    n, m = lax.axis_size(axis), lax.axis_size("gz")

    def target(a, c):
        to = a + (1 if c % 2 == 0 else -1)
        return (to, c) if 0 <= to < n else (a, c ^ 1)

    forward = []
    for a in range(n):
        for c in range(m):
            to = target(a, c)
            forward.append((a * m + c, to[0] * m + to[1]))
    return forward, [(j, i) for i, j in forward]


def exchange(axis, fwd, bwd):
    forward, backward = around(axis)
    names = (axis, "gz")
    return lax.ppermute(fwd, names, forward), lax.ppermute(bwd, names, backward)


def exchange_z(up, down):
    m = lax.axis_size("gz")
    ring = [(i, (i + 1) % m) for i in range(m)]
    return lax.ppermute(up, "gz", ring), lax.ppermute(down, "gz", [(j, i) for i, j in ring])


def local(field, source, sigma, warmth, storage, partition, column):
    groups = lax.axis_size("gy") * lax.axis_size("gz")
    count = groups * (CAP + 1)
    cube = (16, 16, 128)
    face = (16, 128)
    x_message, y_message, corners = (X_LAYERS, 16, 128), (16, 32, 128), (len(CORNERS), 32, 128)
    here = (field, sigma, warmth, storage, source)
    yf, yb, scaled, field, sigma, warmth, storage = call(
        pack_first,
        [y_message, y_message, (4, *cube), (3, *cube), cube, cube, cube],
        [(3, *cube), pltpu.SemaphoreType.DMA((5,))],
        name="pack_first",
        near=True,
        in_specs=[pl.BlockSpec(memory_space=pltpu.HBM)] * 5,
    )(*(pltpu.with_memory_space_constraint(v, pltpu.HBM) for v in here))
    yf, yb = exchange("gy", yf, yb)
    xf, xb = call(pack_second, [x_message, x_message], name="pack_second", near=True)(
        field, scaled, warmth
    )
    xf, xb = exchange("gx", xf, xb)
    targets, spread_rows, into, nodes = pl.pallas_call(
        place,
        out_shape=[
            jax.ShapeDtypeStruct((2, 256), jnp.int32),
            jax.ShapeDtypeStruct((count, 256), jnp.bfloat16),
            jax.ShapeDtypeStruct((2, 256, 128), F32),
            jax.ShapeDtypeStruct((groups, 128), F32),
        ],
        compiler_params=pltpu.CompilerParams(vmem_limit_bytes=8 << 20),
        name="place",
    )(partition.reshape(1, 256), column.reshape(1, 256))
    cf, cb = call(pack_corners, [corners, corners], name="pack_corners")(
        xf, xb, targets
    )
    cf, cb = exchange("gy", cf, cb)
    layer, halo = (24, 128), len(HALO_X)
    inner, inner_packed, inner_up, inner_down, began = call(
        pack_inner,
        [(8, 16, *layer), (16, *layer), (8, *layer), (8, *layer), cube],
        [(18, 16, 128)],
        name="pack_inner",
        near=True,
    )(field, scaled, warmth, storage, xf, xb, yf, yb)
    (swept,) = call(
        bulk,
        [(EM_SWEEPS - 1, 3, 16, *layer)],
        name="bulk",
        near=True,
        cost_estimate=pl.CostEstimate(flops=10**9, bytes_accessed=10**7, transcendentals=0),
    )(inner)
    outer, outer_packed, up, down = call(
        pack_outer,
        [(8, halo, *layer), (halo, *layer), (X_PAIRS, *layer), (X_PAIRS, *layer)],
        name="pack_outer",
        near=True,
    )(xf, xb, cf, cb, inner_up, inner_down, swept)
    below_z, above_z = exchange_z(up, down)
    final, whole_sum, shifted = call(
        rest_of_bulk,
        [(3, 17, *layer), cube, cube],
        [(EM_SWEEPS - 1, 3, halo, *layer)],
        name="rest_of_bulk",
        near=True,
        cost_estimate=pl.CostEstimate(flops=10**9, bytes_accessed=10**7, transcendentals=0),
    )(inner, outer, swept)
    (own,) = call(
        turn,
        [(BLOCKS, 128, 128)],
        [(BLOCKS, 128, 128)],
        name="turn",
        near=True,
        cost_estimate=pl.CostEstimate(flops=10**8, bytes_accessed=10**6, transcendentals=0),
    )(inner_packed, outer_packed)
    near, send, beside = call(
        edge,
        [(BLOCKS, 3, 32, 128), (count, 128), cube],
        [
            (BLOCKS, 128, 128),
            (BLOCKS, 8, 32, 128),
            (BLOCKS, 3, 32, 128),
            (3, 32, 128),
            cube,
        ],
        name="edge",
        near=True,
    )(
        own, below_z, above_z, whole_sum, shifted, sigma, targets, spread_rows, into, nodes
    )
    got = lax.all_to_all(
        send.reshape(count, 1, 128), ("gy", "gz"), split_axis=0, concat_axis=0, tiled=True
    ).reshape(count, 128)
    xf, xb, yf, yb, heat, mid = call(
        warm, [face, face, face, face, cube, cube], name="warm", near=True
    )(got, beside, began, storage)
    xf, xb = exchange("gx", xf, xb)
    yf, yb = exchange("gy", yf, yb)
    out, beyond, rest = call(
        merge,
        [(3, *cube), cube, cube],
        [(BLOCKS, 128, 128)],
        name="merge",
        cost_estimate=pl.CostEstimate(flops=10**9, bytes_accessed=10**6, transcendentals=0),
    )(final, near, got, beside, warmth, storage, heat, mid)
    (updated,) = call(finish, [cube], name="finish")(rest, storage, xf, xb, yf, yb, beyond)
    return out, updated


def solution(mesh):
    in_specs = (
        P(None, "gx", "gy", "gz"),
        P(None, "gx", "gy", "gz"),
        P("gx", "gy", "gz"),
        P("gx", "gy", "gz"),
        P("gx", "gy", "gz"),
        P("gx", "gy", "gz", None, None),
        P("gx", "gy", "gz", None),
    )
    out_specs = (P(None, "gx", "gy", "gz"), P("gx", "gy", "gz"))
    return jax.shard_map(local, mesh=mesh, in_specs=in_specs, out_specs=out_specs, check_vma=False)
```
